32 devices in a mesh: rep: 8 (over z, core), shard: 4 (over y, x).
Axes of the slice: x: 2, y: 2, z: 4, core: 2. Of those that a mesh axis runs over, the one named last changes fastest.
Arguments:
- tokens: bfloat16 [16, 1536, 1280], P('rep', 'shard'), may hold values from -6 to 6
- lengths: int32 [16], P('rep'), may hold values from 1200 to 1500, as said below
- cotangent: bfloat16 [16, 1536, 1280], P('rep', 'shard'), may hold values from -6 to 6
- first_gain: bfloat16 [1280], P('shard'), may hold values from 0.5 to 1.5
- first_shift: bfloat16 [1280], P('shard'), may hold values from -1 to 1
- query_weight: bfloat16 [1280, 1280], P('shard'), may hold values from -0.3125 to 0.3125
- query_bias: bfloat16 [1280], P('shard'), may hold values from -1 to 1
- key_weight: bfloat16 [1280, 1280], P('shard'), may hold values from -0.15625 to 0.15625
- value_weight: bfloat16 [1280, 1280], P('shard'), may hold values from -0.15625 to 0.15625
- value_bias: bfloat16 [1280], P('shard'), may hold values from -1 to 1
- out_weight: bfloat16 [1280, 1280], P('shard'), may hold values from -1 to 1
- out_bias: bfloat16 [1280], P('shard'), may hold values from -1 to 1
- second_gain: bfloat16 [1280], P('shard'), may hold values from 0.5 to 1.5
- second_shift: bfloat16 [1280], P('shard'), may hold values from -1 to 1
- up_weight: bfloat16 [1280, 5120], P('shard'), may hold values from -0.15625 to 0.15625
- up_bias: bfloat16 [5120], P('shard'), may hold values from -1 to 1
- down_weight: bfloat16 [5120, 1280], P('shard'), may hold values from -0.078125 to 0.078125
- down_bias: bfloat16 [1280], P('shard'), may hold values from -1 to 1
Outputs:
- layer_out: bfloat16 [16, 1536, 1280], P('rep', 'shard')
- tokens_grad: bfloat16 [16, 1536, 1280], P('rep', 'shard')
- first_gain_grad: float32 [1280], P('shard')
- first_shift_grad: float32 [1280], P('shard')
- query_weight_grad: float32 [1280, 1280], P('shard')
- query_bias_grad: float32 [1280], P('shard')
- key_weight_grad: float32 [1280, 1280], P('shard')
- value_weight_grad: float32 [1280, 1280], P('shard')
- value_bias_grad: float32 [1280], P('shard')
- out_weight_grad: float32 [1280, 1280], P('shard')
- out_bias_grad: float32 [1280], P('shard')
- second_gain_grad: float32 [1280], P('shard')
- second_shift_grad: float32 [1280], P('shard')
- up_weight_grad: float32 [1280, 5120], P('shard')
- up_bias_grad: float32 [5120], P('shard')
- down_weight_grad: float32 [5120, 1280], P('shard')
- down_bias_grad: float32 [1280], P('shard')
The draws below stay inside these ranges and needn't reach their ends.
Inputs may be any that keep to these rules, and one draw needn't show every extreme that they name: `lengths`: in each aligned block of 2 clips (those of one index of rep) at least one clip has more than 1152 live tokens; some clip of the whole array has exactly 1500.
All inputs are finite; a program needn't handle non-finite values.
Results may differ from the reference program's by a relative error of at most 0.02.
Values may be sent and summed in bfloat16 or wider, within the bound.
A program may use at most 320 MiB of HBM per device.

```python
import jax
import jax.numpy as jnp
from jax import lax

D = 1280
FF = 5120
HEADS = 16
HEAD = 80
PAD = 1536
TOK_DEV = 768
CLIPS_GRP = 2
CLIPS = 16
LEN_LO = 1200
LEN_HI = 1500


def draw_lengths(key, part):
    key = jax.random.fold_in(key, 11)
    base_key, pick_key, far_key, top_key = jax.random.split(key, 4)
    groups = CLIPS // CLIPS_GRP
    group_width = CLIPS_GRP * PAD // TOK_DEV
    far_low = max(LEN_LO, PAD - PAD // group_width + 1)
    drawn = jax.random.randint(base_key, (groups, CLIPS_GRP), LEN_LO, LEN_HI + 1)
    far_drawn = jax.random.randint(far_key, (groups, 1), far_low, LEN_HI + 1)
    chosen = jax.random.randint(pick_key, (groups, 1), 0, CLIPS_GRP)
    filled = jnp.where(jnp.arange(CLIPS_GRP)[None, :] == chosen, far_drawn, drawn).reshape(CLIPS)
    top_clip = jax.random.randint(top_key, (), 0, CLIPS)
    filled = jnp.where(jnp.arange(CLIPS) == top_clip, LEN_HI, filled)
    return filled.astype(jnp.int32)


def shard_levels(key, shape, pieces, low, high):
    def one(position, blocks):
        steps = jax.random.uniform(jax.random.fold_in(jax.random.fold_in(key, 6), position), (blocks,), jnp.float32, low / len(pieces), high / len(pieces))
        return jnp.repeat(jnp.exp(steps), shape[position] // blocks).reshape((-1,) + (1,) * (len(shape) - position - 1))

    level = one(*pieces[0])
    for cut in pieces[1:]:
        level = level * one(*cut)
    return level


def scatter_about(key, shape, width, reach, cuts=(), dtype=jnp.bfloat16):
    result = width * jax.random.normal(key, shape, jnp.float32)
    if cuts:
        result = result * shard_levels(key, shape, cuts, -0.22, 0.18)
    return jnp.clip(result, -reach, reach).astype(dtype)


def setup_inputs(seed: int = 0) -> dict:
    keys = jax.random.split(jax.random.key(seed), 19)
    return {
        "tokens": scatter_about(keys[0], (CLIPS, PAD, D), 1.0, 6.0, ((0, 8), (1, 4))),
        "lengths": draw_lengths(jax.random.fold_in(keys[18], 71), 0),
        "cotangent": scatter_about(keys[2], (CLIPS, PAD, D), 1.0, 6.0, ((0, 8), (1, 4))),
        "first_gain": jnp.clip(1.0 + 0.1 * jax.random.normal(keys[3], (D,), jnp.float32), 0.5, 1.5).astype(jnp.bfloat16),
        "first_shift": scatter_about(keys[4], (D,), 0.2, 1.0, ((0, 4),)),
        "query_weight": scatter_about(keys[5], (D, D), (D // 4) ** -0.5, 0.3125, ((0, 4),)),
        "query_bias": scatter_about(keys[6], (D,), 0.2, 1.0, ((0, 4),)),
        "key_weight": scatter_about(keys[7], (D, D), D ** -0.5, 0.15625, ((0, 4),)),
        "value_weight": scatter_about(keys[8], (D, D), D ** -0.5, 0.15625, ((0, 4),)),
        "value_bias": scatter_about(keys[9], (D,), 0.2, 1.0, ((0, 4),)),
        "out_weight": scatter_about(keys[10], (D, D), (D // 32) ** -0.5, 1.0, ((0, 4),)),
        "out_bias": scatter_about(keys[11], (D,), 0.2, 1.0, ((0, 4),)),
        "second_gain": jnp.clip(1.0 + 0.1 * jax.random.normal(keys[12], (D,), jnp.float32), 0.5, 1.5).astype(jnp.bfloat16),
        "second_shift": scatter_about(keys[13], (D,), 0.2, 1.0, ((0, 4),)),
        "up_weight": scatter_about(keys[14], (D, FF), D ** -0.5, 0.15625, ((0, 4),)),
        "up_bias": scatter_about(keys[15], (FF,), 0.2, 1.0, ((0, 4),)),
        "down_weight": scatter_about(keys[16], (FF, D), FF ** -0.5, 0.078125, ((0, 4),)),
        "down_bias": scatter_about(keys[17], (D,), 0.2, 1.0, ((0, 4),)),
    }


@jax.custom_vjp
def low(v):
    return lax.optimization_barrier(v.astype(jnp.bfloat16)).astype(jnp.float32)

@jax.custom_vjp
def low_back(v):
    return v

def low_keep(v):
    return (low(v), None)

def low_pass(kept, grad):
    return (grad,)

def back_keep(v):
    return (v, None)

def back_low(kept, grad):
    return (low(grad),)
low.defvjp(low_keep, low_pass)
low_back.defvjp(back_keep, back_low)
masked_score = -1e+30

def norm_rows(rows_in, gain, shift):
    centre = lax.optimization_barrier(jnp.mean(rows_in, axis=-1, keepdims=True))
    centred = rows_in - centre
    spread = lax.optimization_barrier(jnp.mean(centred * centred, axis=-1, keepdims=True))
    return centred * lax.rsqrt(spread + 1e-05) * gain + shift

def precise_dot(left, right):
    return jnp.dot(left, right, precision=lax.Precision.HIGHEST)

def clip_layer(params, clip, length):
    first_gain, first_shift, query_weight, query_bias, key_weight, value_weight, value_bias, out_weight, out_bias, second_gain, second_shift, up_weight, up_bias, down_weight, down_bias = params
    normed_one = low(norm_rows(clip, first_gain, first_shift))
    query_rows = low(low_back(precise_dot(normed_one, query_weight) + query_bias))
    key_rows = low(low_back(precise_dot(normed_one, key_weight)))
    value_rows = low(low_back(precise_dot(normed_one, value_weight) + value_bias))
    query_heads = query_rows.reshape(PAD, HEADS, HEAD).transpose(1, 0, 2)
    key_heads = key_rows.reshape(PAD, HEADS, HEAD).transpose(1, 0, 2)
    value_heads = value_rows.reshape(PAD, HEADS, HEAD).transpose(1, 0, 2)
    raw_scores = jnp.einsum('hqd,hkd->hqk', query_heads, key_heads, precision=lax.Precision.HIGHEST)
    key_live = jnp.arange(PAD).astype(jnp.int32) < length
    scores = jnp.where(key_live[None, None, :], low_back(raw_scores) * HEAD ** (-0.5), masked_score)
    peak = lax.optimization_barrier(jnp.max(scores, axis=-1, keepdims=True))
    expo = jnp.exp(scores - peak)
    attention = expo / lax.optimization_barrier(jnp.sum(expo, axis=-1, keepdims=True))
    mixed_heads = jnp.einsum('hqk,hkd->hqd', low(attention), value_heads, precision=lax.Precision.HIGHEST)
    attended = low(low_back(mixed_heads.transpose(1, 0, 2).reshape(PAD, D)))
    middle = clip + low_back(precise_dot(attended, out_weight) + out_bias)
    normed_two = low(norm_rows(middle, second_gain, second_shift))
    hidden_pre = low_back(precise_dot(normed_two, up_weight) + up_bias)
    hidden_act = low(jax.nn.gelu(hidden_pre, approximate=False))
    return middle + (precise_dot(hidden_act, down_weight) + down_bias)

def reference(tokens, lengths, cotangent, first_gain, first_shift, query_weight, query_bias, key_weight, value_weight, value_bias, out_weight, out_bias, second_gain, second_shift, up_weight, up_bias, down_weight, down_bias):
    params = tuple((tensor.astype(jnp.float32) for tensor in (first_gain, first_shift, query_weight, query_bias, key_weight, value_weight, value_bias, out_weight, out_bias, second_gain, second_shift, up_weight, up_bias, down_weight, down_bias)))

    def forward(all_clips, layer_params):

        def one_clip(clip_pair):
            return clip_layer(layer_params, clip_pair[0], clip_pair[1])
        return lax.map(jax.checkpoint(one_clip), (all_clips, lengths))
    layer_out, pull_back = jax.vjp(forward, tokens.astype(jnp.float32), params)
    live_rows = jnp.arange(PAD).astype(jnp.int32)[None, :] < lengths[:, None]
    masked_cot = jnp.where(live_rows[:, :, None], cotangent.astype(jnp.float32), jnp.float32(0.0))
    tokens_grad, grads = pull_back(masked_cot)
    g_one, s_one, g_query, b_query, g_key, g_value, b_value, g_out, b_out, g_two, s_two, g_up, b_up, g_down, b_down = grads
    return (layer_out.astype(jnp.bfloat16), tokens_grad.astype(jnp.bfloat16), g_one, s_one, g_query, b_query, g_key, g_value, b_value, g_out, b_out, g_two, s_two, g_up, b_up, g_down, b_down)
```

```python
import functools
import math

import jax
import jax.numpy as jnp
from jax import lax
from jax.experimental import pallas as pl
from jax.experimental.pallas import tpu as pltpu
from jax.sharding import PartitionSpec as P

HEAD = 80
WIN = 256
AUG = 192
EPS = 1e-5
SCALE = HEAD**-0.5
SCALE2 = SCALE * math.log2(math.e)
DEAD = -1e30
ROWS = 256
f32 = jnp.float32
bf16 = jnp.bfloat16

ERF_P = 0.35
ERF_C = (0.19458996, 0.23381038, -0.00165479, 0.67243411, -0.66868964, 0.76616445, -0.19665448)


def params(limit=60):
    return pltpu.CompilerParams(vmem_limit_bytes=limit * 2**20)


def cost(flops, size):
    return pl.CostEstimate(flops=int(flops), bytes_accessed=int(size), transcendentals=0)


def dot(a, b):
    return jnp.dot(a, b, preferred_element_type=f32)


def dot_nt(a, b):
    return lax.dot_general(a, b, (((1,), (1,)), ((), ())), preferred_element_type=f32)


def dot_tn(a, b):
    return lax.dot_general(a, b, (((0,), (0,)), ((), ())), preferred_element_type=f32)


def gelu_pair(a):
    expo = jnp.exp2(a * a * (-0.5 * math.log2(math.e)))
    t = 1.0 / (1.0 + jnp.abs(a) * (ERF_P * math.sqrt(0.5)))
    total = ERF_C[-1]
    for c in ERF_C[-2::-1]:
        total = total * t + c
    tail = 0.5 * expo * (total * t)
    cdf = jnp.where(a >= 0, 1.0 - tail, tail)
    return a * cdf, cdf + a * (expo * (1.0 / math.sqrt(2.0 * math.pi)))


def whole(shape):
    return pl.BlockSpec(shape, lambda *_: (0,) * len(shape))


def row_block(rows, cols):
    return pl.BlockSpec((rows, cols), lambda i: (i, 0))


def standardize(x):
    centred = x - jnp.mean(x, axis=-1, keepdims=True)
    inv = lax.rsqrt(jnp.mean(centred * centred, axis=-1, keepdims=True) + EPS)
    return centred * inv, inv


def qkv_kernel(x_ref, g_ref, b_ref, w_ref, bias_ref, h_ref, q_ref, k_ref, v_ref):
    xhat, _ = standardize(x_ref[...].astype(f32))
    h = (xhat * g_ref[...] + b_ref[...]).astype(bf16)
    h_ref[...] = h
    z = dot(h, w_ref[...]) + bias_ref[...]
    width = z.shape[1] // 3
    for i, ref in enumerate((q_ref, k_ref, v_ref)):
        ref[:, :width] = z[:, i * width : (i + 1) * width].astype(bf16)
        ref[:, width:] = jnp.zeros((ref.shape[0], ref.shape[1] - width), bf16)


def qkv_call(x, gain, shift, w, bias, wide):
    n, d = x.shape
    out = jax.ShapeDtypeStruct((n, wide), bf16)
    return pl.pallas_call(
        qkv_kernel,
        grid=(n // ROWS,),
        in_specs=[
            row_block(ROWS, d),
            whole((1, d)),
            whole((1, d)),
            whole(w.shape),
            whole(bias.shape),
        ],
        out_specs=[row_block(ROWS, d)] + [row_block(ROWS, wide)] * 3,
        out_shape=[jax.ShapeDtypeStruct((n, d), bf16), out, out, out],
        compiler_params=params(),
        cost_estimate=cost(2 * n * d * w.shape[1], 4 * n * d + 2 * w.size + 6 * n * wide),
        name="project",
    )(x, gain, shift, w, bias)


def head_window(h):
    start = h * HEAD
    base = (start // 128) * 128
    off = start - base
    lane = lax.broadcasted_iota(jnp.int32, (1, WIN), 1)
    keep = jnp.where((lane >= off) & (lane < off + HEAD), 1.0, 0.0)
    return pl.ds(pl.multiple_of(base, 128), WIN), keep, lane


def put3(x, lane, first, value):
    hi = value.astype(bf16).astype(f32)
    rest = value - hi
    mid = rest.astype(bf16).astype(f32)
    low = rest - mid
    return jnp.where(
        lane == first,
        hi,
        jnp.where(lane == first + 1, mid, jnp.where(lane == first + 2, low, x)),
    )


def key_extra(rows, length):
    lane = lax.broadcasted_iota(jnp.int32, (rows, WIN), 1)
    row = lax.broadcasted_iota(jnp.int32, (rows, WIN), 0)
    dead = jnp.where(row >= length, DEAD, 0.0)
    minus = jnp.where((lane > AUG) & (lane <= AUG + 3), -1.0, 0.0)
    return jnp.where(lane == AUG, dead, minus).astype(bf16)


def attn_fwd_kernel(len_ref, q_ref, k_ref, v_ref, o_ref, lse_ref, acc, kx, *, bq):
    h = pl.program_id(0)
    n = q_ref.shape[0]
    width = o_ref.shape[1]

    @pl.when(h == 0)
    def _():
        acc[...] = jnp.zeros_like(acc)
        lse_ref[...] = jnp.zeros_like(lse_ref)
        kx[...] = key_extra(n, len_ref[0])

    win, keep, lane = head_window(h)
    low = keep.astype(bf16)
    q_one = jnp.where(lane == AUG, 1.0, 0.0).astype(bf16)
    v_one = jnp.where((lane >= AUG) & (lane < AUG + 3), 1.0, 0.0).astype(bf16)
    k = k_ref[:, win] * low + kx[...]
    v = v_ref[:, win] * low + v_one
    for i in range(n // bq):
        rows = slice(i * bq, (i + 1) * bq)
        s = dot_nt(q_ref[rows, win] * low + q_one, k)
        peak = jnp.max(s, axis=-1, keepdims=True)
        p = jnp.exp2((s - peak) * SCALE2).astype(bf16)
        o = dot(p, v)
        total = o[:, AUG : AUG + 1]
        acc[rows, win] += o * (keep * (1.0 / total))
        here = lax.broadcasted_iota(jnp.int32, (bq, 128), 1) == h
        lse = peak + jnp.log(total) * (1.0 / SCALE)
        lse_ref[rows, :] = jnp.where(here, lse, lse_ref[rows, :])

    @pl.when(h == pl.num_programs(0) - 1)
    def _():
        o_ref[...] = acc[:, :width].astype(bf16)


def attn_fwd_call(length, q, k, v, width, heads):
    n, wide = q.shape
    return pl.pallas_call(
        functools.partial(attn_fwd_kernel, bq=256),
        grid=(heads,),
        in_specs=[pl.BlockSpec(memory_space=pltpu.SMEM)] + [whole((n, wide))] * 3,
        out_specs=[whole((n, width)), whole((n, 128))],
        out_shape=[jax.ShapeDtypeStruct((n, width), bf16), jax.ShapeDtypeStruct((n, 128), f32)],
        scratch_shapes=[pltpu.VMEM((n, wide), f32), pltpu.VMEM((n, WIN), bf16)],
        compiler_params=params(),
        cost_estimate=cost(4 * n * n * WIN * heads, 8 * n * wide),
        name="attend",
    )(length, q, k, v)


def attn_bwd_kernel(
    len_ref, q_ref, k_ref, v_ref, o_ref, do_ref, lse_ref, g_ref, sum_ref, dq, dk, dv, part, qa, da, kx, *, bk
):
    h = pl.program_id(0)
    n = q_ref.shape[0]
    width = o_ref.shape[1]

    @pl.when(h == 0)
    def _():
        for ref in (dq, dk, dv):
            ref[...] = jnp.zeros_like(ref)
        kx[...] = key_extra(n, len_ref[0])

    win, keep, lane = head_window(h)
    low = keep.astype(bf16)
    v_one = jnp.where((lane >= AUG) & (lane < AUG + 3), 1.0, 0.0).astype(bf16)
    for i in range(n // ROWS):
        rows = slice(i * ROWS, (i + 1) * ROWS)
        here = lax.broadcasted_iota(jnp.int32, (ROWS, 128), 1) == h
        lse = jnp.sum(jnp.where(here, lse_ref[rows, :], 0.0), axis=-1, keepdims=True)
        q = q_ref[rows, win].astype(f32) * keep
        qa[rows, :] = jnp.where(lane == AUG, 1.0, put3(q, lane, AUG + 1, lse)).astype(bf16)
        d = do_ref[rows, win].astype(f32) * keep
        delta = jnp.sum(d * o_ref[rows, win].astype(f32), axis=-1, keepdims=True)
        da[rows, :] = put3(d, lane, AUG, -delta).astype(bf16)
    for i in range(n // bk):
        rows = slice(i * bk, (i + 1) * bk)
        k = k_ref[rows, win] * low + kx[rows, :]
        v = v_ref[rows, win] * low + v_one
        p = jnp.exp2(dot_nt(k, qa[...]) * SCALE2)
        ds = (p * dot_nt(v, da[...])).astype(bf16)
        dv[rows, win] += dot(p.astype(bf16), da[...]) * keep
        dk[rows, win] += dot(ds, qa[...]) * keep
        new = dot_tn(ds, k)
        part[...] = new if i == 0 else part[...] + new
    dq[:, win] += part[...] * keep

    @pl.when(h == pl.num_programs(0) - 1)
    def _():
        for i, (ref, factor) in enumerate(((dq, SCALE), (dk, SCALE), (dv, 1.0))):
            value = (ref[:, : g_ref.shape[1] // 3] * factor).astype(bf16)
            cols = slice(i * value.shape[1], (i + 1) * value.shape[1])
            g_ref[:, cols] = value
            sum_ref[:, cols] = jnp.sum(value.astype(f32), axis=0, keepdims=True)


def attn_bwd_call(length, q, k, v, o, do, lse, width, heads):
    n, wide = q.shape
    return pl.pallas_call(
        functools.partial(attn_bwd_kernel, bk=256),
        grid=(heads,),
        in_specs=[pl.BlockSpec(memory_space=pltpu.SMEM)]
        + [whole((n, wide))] * 5
        + [whole((n, 128))],
        out_specs=[whole((n, 3 * width)), whole((1, 3 * width))],
        out_shape=[
            jax.ShapeDtypeStruct((n, 3 * width), bf16),
            jax.ShapeDtypeStruct((1, 3 * width), f32),
        ],
        scratch_shapes=[pltpu.VMEM((n, wide), f32)] * 3
        + [pltpu.VMEM((n, WIN), f32)]
        + [pltpu.VMEM((n, WIN), bf16)] * 3,
        compiler_params=params(),
        cost_estimate=cost(10 * n * n * WIN * heads, 20 * n * wide),
        name="attend_back",
    )(length, q, k, v, o, do, lse)


def matmul_kernel(a_ref, w_ref, out_ref):
    out_ref[...] = dot(a_ref[...], w_ref[...]).astype(out_ref.dtype)


def matmul_nt_kernel(a_ref, w_ref, out_ref):
    out_ref[...] = dot_nt(a_ref[...], w_ref[...]).astype(out_ref.dtype)


def matmul_call(kernel, a, w, cols, name):
    n = a.shape[0]
    return pl.pallas_call(
        kernel,
        grid=(n // ROWS,),
        in_specs=[row_block(ROWS, a.shape[1]), whole(w.shape)],
        out_specs=row_block(ROWS, cols),
        out_shape=jax.ShapeDtypeStruct((n, cols), bf16),
        compiler_params=params(),
        cost_estimate=cost(2 * n * w.size, 2 * (a.size + w.size + n * cols)),
        name=name,
    )(a, w)


def middle_kernel(x_ref, y_ref, z_ref, bias_ref, g_ref, b_ref, mid_ref, h_ref):
    mid = x_ref[...].astype(f32) + (y_ref[...].astype(f32) + z_ref[...].astype(f32) + bias_ref[...])
    mid_ref[...] = mid
    xhat, _ = standardize(mid)
    h_ref[...] = (xhat * g_ref[...] + b_ref[...]).astype(bf16)


def middle_call(x, y, z, bias, gain, shift):
    n, d = x.shape
    block = row_block(ROWS, d)
    return pl.pallas_call(
        middle_kernel,
        grid=(n // ROWS,),
        in_specs=[block] * 3 + [whole((1, d))] * 3,
        out_specs=[block] * 2,
        out_shape=[jax.ShapeDtypeStruct((n, d), f32), jax.ShapeDtypeStruct((n, d), bf16)],
        compiler_params=params(),
        cost_estimate=cost(20 * n * d, 12 * n * d),
        name="middle",
    )(x, y, z, bias, gain, shift)


def ffn_kernel(*refs, chained, mc):
    h_ref, dz_ref, up_ref, ub_ref, dn_ref = refs[:5]
    refs = refs[5:]
    if chained:
        old_out, old_dh = refs[:2]
        refs = refs[2:]
    out_ref, dh_ref, dup_ref, ddn_ref, dub_ref, acc, dh, ht, act, grad = refs[:10]
    t = pl.program_id(0)
    n = h_ref.shape[0]

    @pl.when(t == 0)
    def _():
        ht[...] = h_ref[...].T
        if chained:
            sem = refs[10]
            copies = [
                pltpu.make_async_copy(src, dst, sem.at[i])
                for i, (src, dst) in enumerate(((old_out, acc), (old_dh, dh)))
            ]
            for c in copies:
                c.start()
            for c in copies:
                c.wait()
        else:
            acc[...] = jnp.zeros_like(acc)
            dh[...] = jnp.zeros_like(dh)

    def step(i, carry):
        rows = pl.ds(pl.multiple_of(i * mc, mc), mc)
        g, slope = gelu_pair(dot(h_ref[rows, :], up_ref[...]) + ub_ref[...])
        g = g.astype(bf16)
        da = (dot_nt(dz_ref[rows, :], dn_ref[...]) * slope).astype(bf16)
        act[rows, :] = g
        grad[rows, :] = da
        acc[rows, :] += dot(g, dn_ref[...])
        dh[rows, :] += dot_nt(da, up_ref[...])
        return carry

    lax.fori_loop(0, n // mc, step, 0)
    dub_ref[...] = jnp.sum(grad[...].astype(f32), axis=0, keepdims=True)
    dup_ref[...] = dot(ht[...], grad[...]).astype(bf16)
    ddn_ref[...] = dot_tn(act[...], dz_ref[...]).astype(bf16)

    @pl.when(t == pl.num_programs(0) - 1)
    def _():
        out_ref[...] = acc[...].astype(out_ref.dtype)
        dh_ref[...] = dh[...].astype(dh_ref.dtype)


def ffn_call(h, dz, up, bias, down, old, last, name):
    n, d = h.shape
    hidden = up.shape[1]
    bt = 256
    out = jax.ShapeDtypeStruct((n, d), bf16 if last else f32)
    chained = old is not None
    scratch = [pltpu.VMEM((n, d), f32)] * 2 + [pltpu.VMEM((d, n), bf16)] + [pltpu.VMEM((n, bt), bf16)] * 2
    once = pl.BlockSpec((n, d), lambda t: (0, 0), pipeline_mode=pl.Buffered(1))
    return pl.pallas_call(
        functools.partial(ffn_kernel, chained=chained, mc=384),
        grid=(hidden // bt,),
        in_specs=[
            once,
            once,
            pl.BlockSpec((d, bt), lambda t: (0, t)),
            pl.BlockSpec((1, bt), lambda t: (0, t)),
            pl.BlockSpec((bt, d), lambda t: (t, 0)),
        ]
        + ([pl.BlockSpec(memory_space=pl.ANY)] * 2 if chained else []),
        out_specs=[
            once,
            once,
            pl.BlockSpec((d, bt), lambda t: (0, t)),
            pl.BlockSpec((bt, d), lambda t: (t, 0)),
            pl.BlockSpec((1, bt), lambda t: (0, t)),
        ],
        out_shape=[
            out,
            out,
            jax.ShapeDtypeStruct((d, hidden), bf16),
            jax.ShapeDtypeStruct((hidden, d), bf16),
            jax.ShapeDtypeStruct((1, hidden), f32),
        ],
        scratch_shapes=scratch + ([pltpu.SemaphoreType.DMA((2,))] if chained else []),
        compiler_params=params(),
        cost_estimate=cost(12 * n * d * hidden, 8 * d * hidden + 12 * n * d),
        name=name,
    )(h, dz, up, bias, down, *(old if chained else ()))


def second_back_kernel(
    mid_ref, dh1_ref, dh2_ref, dz_ref, g_ref, w_ref, o_ref, dmid_ref, do_ref, dw_ref, sums_ref, acc
):
    i = pl.program_id(0)
    xhat, inv = standardize(mid_ref[...])
    dh = dh1_ref[...].astype(f32) + dh2_ref[...].astype(f32)
    dx = dh * g_ref[...]
    dz = dz_ref[...].astype(f32)
    dmid = dz + inv * (
        dx - jnp.mean(dx, axis=-1, keepdims=True) - xhat * jnp.mean(dx * xhat, axis=-1, keepdims=True)
    )
    dmid_ref[...] = dmid
    dy = dmid.astype(bf16)
    width = w_ref.shape[0]
    do_ref[:, :width] = dot_nt(dy, w_ref[...]).astype(bf16)
    do_ref[:, width:] = jnp.zeros((do_ref.shape[0], do_ref.shape[1] - width), bf16)

    @pl.when(i == 0)
    def _():
        acc[...] = jnp.zeros_like(acc)
        sums_ref[...] = jnp.zeros_like(sums_ref)

    acc[...] += dot_tn(o_ref[...], dy)
    for row, value in enumerate((dh * xhat, dh, dy.astype(f32), dz)):
        sums_ref[row : row + 1, :] += jnp.sum(value, axis=0, keepdims=True)

    @pl.when(i == pl.num_programs(0) - 1)
    def _():
        dw_ref[...] = acc[...].astype(bf16)


def second_back_call(mid, dh1, dh2, dz, gain, w, o, wide):
    n, d = mid.shape
    width = w.shape[0]
    block = row_block(ROWS, d)
    return pl.pallas_call(
        second_back_kernel,
        grid=(n // ROWS,),
        in_specs=[block] * 4 + [whole((1, d)), whole(w.shape), row_block(ROWS, width)],
        out_specs=[block, row_block(ROWS, wide), whole((width, d)), whole((8, d))],
        out_shape=[
            jax.ShapeDtypeStruct((n, d), f32),
            jax.ShapeDtypeStruct((n, wide), bf16),
            jax.ShapeDtypeStruct((width, d), bf16),
            jax.ShapeDtypeStruct((8, d), f32),
        ],
        scratch_shapes=[pltpu.VMEM((width, d), f32)],
        compiler_params=params(),
        cost_estimate=cost(4 * n * d * width, 14 * n * d),
        name="second_back",
    )(mid, dh1, dh2, dz, gain, w, o)


def dw_kernel(h_ref, g_ref, out_ref):
    out_ref[...] = dot_tn(h_ref[...], g_ref[...]).astype(bf16)


def dw_call(h, grads):
    n, d = h.shape
    cols = grads.shape[1]
    return pl.pallas_call(
        dw_kernel,
        grid=(d // 256,),
        in_specs=[pl.BlockSpec((n, 256), lambda i: (0, i)), whole((n, cols))],
        out_specs=row_block(256, cols),
        out_shape=jax.ShapeDtypeStruct((d, cols), bf16),
        compiler_params=params(),
        cost_estimate=cost(2 * n * d * cols, 2 * (n * d + n * cols + d * cols)),
        name="project_grad",
    )(h, grads)


def first_back_kernel(x_ref, dh1_ref, dh2_ref, dmid_ref, g_ref, dx_ref, sums_ref):
    xhat, inv = standardize(x_ref[...].astype(f32))
    dh = dh1_ref[...].astype(f32) + dh2_ref[...].astype(f32)
    dx = dh * g_ref[...]
    dx_ref[...] = (
        dmid_ref[...]
        + inv * (dx - jnp.mean(dx, axis=-1, keepdims=True) - xhat * jnp.mean(dx * xhat, axis=-1, keepdims=True))
    ).astype(bf16)

    @pl.when(pl.program_id(0) == 0)
    def _():
        sums_ref[...] = jnp.zeros_like(sums_ref)

    for row, value in enumerate((dh * xhat, dh)):
        sums_ref[row : row + 1, :] += jnp.sum(value, axis=0, keepdims=True)


def first_back_call(x, dh1, dh2, dmid, gain):
    n, d = x.shape
    block = row_block(ROWS, d)
    return pl.pallas_call(
        first_back_kernel,
        grid=(n // ROWS,),
        in_specs=[block] * 4 + [whole((1, d))],
        out_specs=[block, whole((8, d))],
        out_shape=[jax.ShapeDtypeStruct((n, d), bf16), jax.ShapeDtypeStruct((8, d), f32)],
        compiler_params=params(),
        cost_estimate=cost(20 * n * d, 12 * n * d),
        name="first_back",
    )(x, dh1, dh2, dmid, gain)


class Place:
    def __init__(self):
        self.groups = lax.axis_size("shard")
        self.reps = lax.axis_size("rep")
        self.shard = lax.axis_index("shard")
        self.rep = lax.axis_index("rep")
        self.core = lax.rem(self.rep, 2)

    def swap_core(self, x):
        return lax.ppermute(x, "rep", [(r, r ^ 1) for r in range(self.reps)])

    def swap(self, x, bit):
        return lax.ppermute(x, "shard", [(s, s ^ bit) for s in range(self.groups)])

    def gather(self, block):
        if self.groups != 4:
            return lax.all_gather(block, "shard", axis=0)
        half = block.shape[0] // 2
        one = self.swap(block, 1)
        two = self.swap(block, 2)
        three = jnp.concatenate([self.swap(one[:half], 2), self.swap(two[half:], 1)], axis=0)
        out = jnp.zeros((4,) + block.shape, block.dtype)
        for i, part in enumerate((block, one, two, three)):
            out = lax.dynamic_update_index_in_dim(out, part, self.shard ^ i, 0)
        return out

    def reduce(self, blocks):
        groups, rows, cols = blocks.shape
        if groups != 4:
            return lax.psum_scatter(blocks.reshape(groups * rows, cols), "shard", scatter_dimension=0, tiled=True)
        half = rows // 2
        low, high = slice(0, half), slice(half, rows)

        def part(i, rows_of):
            return lax.dynamic_index_in_dim(blocks, self.shard ^ i, 0, keepdims=False)[rows_of]

        a = self.swap(jnp.stack([part(1, low), part(3, low)]), 1)
        b = self.swap(jnp.stack([part(2, high), part(3, high)]), 2)
        c = self.swap(part(2, low) + a[1], 2)
        d = self.swap(part(1, high) + b[1], 1)
        return jnp.concatenate([part(0, low) + a[0] + c, part(0, high) + b[0] + d], axis=0)

    def over_reps(self, own):
        planes = self.reps // 2
        sums = lax.psum_scatter(
            own,
            "rep",
            scatter_dimension=0,
            tiled=True,
            axis_index_groups=[[2 * z + c for z in range(planes)] for c in range(2)],
        )
        both = lax.all_gather(sums, "rep", axis=0)
        rows, cols = sums.shape
        return both.reshape(planes, 2, rows, cols).transpose(1, 0, 2, 3).reshape(2, planes * rows, cols)

    def clip_perm(self, k):
        g, cl = self.groups, self.groups // 2
        pairs = []
        for r in range(self.reps):
            for s in range(g):
                to = ((r & ~1) | (s // cl)) * g + (r & 1) * cl + (s + k) % cl
                pairs.append((r * g + s, to))
        return pairs

    def to_clip(self, x):
        cl = self.groups // 2
        parts = []
        for k in range(cl):
            send = lax.dynamic_index_in_dim(x, lax.rem(self.shard + k, cl), 0, keepdims=False)
            parts.append(lax.ppermute(send, ("rep", "shard"), self.clip_perm(k)))
        out = jnp.zeros((cl,) + x.shape[1:], x.dtype)
        for k, part in enumerate(parts):
            out = lax.dynamic_update_index_in_dim(out, part, lax.rem(self.shard + cl - k, cl), 0)
        return out.reshape((-1,) + x.shape[2:])

    def from_clip(self, x):
        cl = self.groups // 2
        x = x.reshape((cl, -1) + x.shape[1:])
        out = jnp.zeros_like(x)
        for k in range(cl):
            send = lax.dynamic_index_in_dim(x, lax.rem(self.shard + cl - k, cl), 0, keepdims=False)
            part = lax.ppermute(send, ("rep", "shard"), [(b, a) for a, b in self.clip_perm(k)])
            out = lax.dynamic_update_index_in_dim(out, part, lax.rem(self.shard + k, cl), 0)
        return out

    def both_halves(self, mine):
        other = self.swap_core(mine)
        n = mine.shape[0]
        out = jnp.zeros((2,) + mine.shape, mine.dtype)
        out = lax.dynamic_update_index_in_dim(out, mine, self.core, 0)
        out = lax.dynamic_update_index_in_dim(out, other, 1 - self.core, 0)
        return out.reshape((2 * n,) + mine.shape[1:])

    def half(self, x, which):
        n = x.shape[0] // 2
        return lax.dynamic_slice_in_dim(x, which * n, n, 0)


def on_device(
    tokens,
    lengths,
    cotangent,
    first_gain,
    first_shift,
    query_weight,
    query_bias,
    key_weight,
    value_weight,
    value_bias,
    out_weight,
    out_bias,
    second_gain,
    second_shift,
    up_weight,
    up_bias,
    down_weight,
    down_bias,
):
    at = Place()
    g, core, shard = at.groups, at.core, at.shard
    cl = g // 2
    d = tokens.shape[2]
    ff = up_weight.shape[1]
    own_d = d // g
    own_f = ff // g
    attn_cols = own_d // 2
    ffn_cols = own_f // 2
    width = d // 2
    heads = width // HEAD
    wide = pl.cdiv(width, 128) * 128 + 128
    first_n = ffn_cols * 2 // 5
    pieces = ((0, first_n), (first_n, ffn_cols))

    def core_cols(w, size):
        return lax.dynamic_index_in_dim(w.reshape(w.shape[0], g, 2, size), core, 2, keepdims=False)

    vectors = (first_gain, first_shift, query_bias, value_bias, out_bias, second_gain, second_shift, down_bias)
    small = jnp.concatenate([jnp.stack(vectors), up_bias.reshape(-1, own_d)], axis=0)
    small = lax.all_gather(small, "shard", axis=0).astype(f32)
    full = [small[:, i].reshape(1, d) for i in range(len(vectors))]
    gain1, shift1, qbias, vbias, obias, gain2, shift2, dbias = full
    ubias = small[:, len(vectors) :].reshape(g, 2, ffn_cols)

    lens = lengths.astype(f32)
    other_lens = at.swap_core(lens)
    mine = shard // cl == core
    length = jnp.where(mine, lens, other_lens)[lax.rem(shard, cl)].astype(jnp.int32).reshape(1)

    x = at.both_halves(at.to_clip(tokens))
    n = x.shape[0]

    qkv_own = jnp.concatenate(
        [core_cols(w, attn_cols).reshape(own_d, width) for w in (query_weight, key_weight, value_weight)], axis=1
    )
    w_qkv = at.gather(qkv_own).reshape(d, 3 * width)
    w_out = at.gather(at.half(out_weight, core)).reshape(width, d)

    def bias_cols(b):
        return core_cols(b, attn_cols).reshape(1, width)

    bias = jnp.concatenate([bias_cols(qbias), jnp.zeros((1, width), f32), bias_cols(vbias)], axis=1)
    up_own = core_cols(up_weight, ffn_cols)
    down_own = at.half(down_weight, core)
    ub_own = lax.dynamic_index_in_dim(ubias, core, 1, keepdims=False)

    cot = at.both_halves(at.to_clip(cotangent))
    live = jnp.arange(n, dtype=jnp.int32)[:, None] < length
    dz = jnp.where(live, cot, jnp.zeros_like(cot))

    ups, downs, ubs = [], [], []
    for a, b in pieces:
        ups.append(at.gather(up_own[:, :, a:b].reshape(own_d, -1)).reshape(d, -1))
        downs.append(at.gather(down_own[a:b]).reshape(-1, d))
        ubs.append(ub_own[:, a:b].reshape(1, -1))

    h1, q, k, v = qkv_call(x, gain1, shift1, w_qkv, bias, wide)
    o, lse = attn_fwd_call(length, q, k, v, width, heads)
    y = matmul_call(matmul_kernel, o, w_out, d, "out_project")
    mid, h2 = middle_call(x, y, at.swap_core(y), obias, gain2, shift2)

    old = None
    up_own_grads, down_own_grads, ub_grads = [], [], []
    for i in range(len(pieces)):
        last = i == len(pieces) - 1
        out, dh2, dup, ddn, dub = ffn_call(h2, dz, ups[i], ubs[i], downs[i], old, last, "hidden" + str(i))
        old = (out, dh2)
        up_own_grads.append(at.reduce(dup.reshape(g, own_d, -1)))
        down_own_grads.append(at.reduce(ddn.reshape(g, -1, d)))
        ub_grads.append(dub.reshape(g, -1))
    other_out = at.swap_core(at.half(out, 1 - core))
    layer_own = at.half(mid, core) + (at.half(out, core).astype(f32) + other_out.astype(f32) + dbias)
    layer_out = at.from_clip(layer_own.astype(bf16))

    dmid, do, dwo, sums2 = second_back_call(mid, dh2, at.swap_core(dh2), dz, gain2, w_out, o, wide)
    out_own_grad = at.reduce(dwo.reshape(g, -1, d))

    o_wide = jnp.pad(o, ((0, 0), (0, wide - width)))
    grads, bias_sums = attn_bwd_call(length, q, k, v, o_wide, do, lse, width, heads)
    dwqkv = dw_call(h1, grads)
    qkv_own_grad = at.reduce(dwqkv.reshape(g, own_d, 3 * width))
    dh1 = matmul_call(matmul_nt_kernel, grads, w_qkv, d, "project_back")
    other_dh1 = at.swap_core(at.half(dh1, 1 - core))
    dx, sums1 = first_back_call(at.half(x, core), at.half(dh1, core), other_dh1, at.half(dmid, core), gain1)
    tokens_grad = at.from_clip(dx)

    up_all = at.over_reps(jnp.concatenate([u.reshape(own_d, g, -1) for u in up_own_grads], axis=2).reshape(own_d, -1))
    up_grad = up_all.reshape(2, own_d, g, ffn_cols).transpose(1, 2, 0, 3).reshape(own_d, ff).astype(f32)
    down_grad = at.over_reps(jnp.concatenate(down_own_grads, axis=0)).reshape(own_f, d).astype(f32)
    out_grad = at.over_reps(out_own_grad).reshape(own_d, d).astype(f32)
    qkv_all = at.over_reps(qkv_own_grad).reshape(2, own_d, 3, g, attn_cols)
    qkv_grads = [qkv_all[:, :, i].transpose(1, 2, 0, 3).reshape(own_d, d).astype(f32) for i in range(3)]

    def spread(v, size):
        out = jnp.zeros((g, 2, size), f32)
        return lax.dynamic_update_index_in_dim(out, v.reshape(g, size), core, 1).reshape(-1, own_d)

    pieces_small = [
        sums1[0].reshape(g, own_d),
        sums1[1].reshape(g, own_d),
        spread(bias_sums[0, :width], attn_cols),
        spread(bias_sums[0, 2 * width :], attn_cols),
        (sums2[2] * 0.5).reshape(g, own_d),
        (sums2[0] * 0.5).reshape(g, own_d),
        (sums2[1] * 0.5).reshape(g, own_d),
        (sums2[3] * 0.5).reshape(g, own_d),
    ]
    ub_sum = jnp.zeros((g, 2, ffn_cols), f32)
    ub_sum = lax.dynamic_update_index_in_dim(ub_sum, jnp.concatenate(ub_grads, axis=1), core, 1)
    packed = jnp.concatenate(
        [jnp.stack(pieces_small, axis=1), ub_sum.reshape(g, -1, own_d)], axis=1
    )
    packed = lax.psum(packed, ("rep", "shard"))
    mine_small = lax.dynamic_index_in_dim(packed, shard, 0, keepdims=False)
    s_gain1, s_shift1, s_qb, s_vb, s_ob, s_gain2, s_shift2, s_db = [mine_small[i] for i in range(8)]
    s_ub = mine_small[8:].reshape(-1)

    return (
        layer_out,
        tokens_grad,
        s_gain1,
        s_shift1,
        qkv_grads[0],
        s_qb,
        qkv_grads[1],
        qkv_grads[2],
        s_vb,
        out_grad,
        s_ob,
        s_gain2,
        s_shift2,
        up_grad,
        s_ub,
        down_grad,
        s_db,
    )


def solution(mesh):
    row, mat, vec = P("rep", "shard", None), P("shard", None), P("shard")
    return jax.shard_map(
        on_device,
        mesh=mesh,
        in_specs=(row, P("rep"), row, vec, vec, mat, vec, mat, mat, vec, mat, vec, vec, vec, mat, vec, mat, vec),
        out_specs=(row, row, vec, vec, mat, vec, mat, mat, vec, mat, vec, vec, vec, mat, vec, mat, vec),
        check_vma=False,
    )
```

```python
import functools
import math

import jax
import jax.numpy as jnp
from jax import lax
from jax.experimental import pallas as pl
from jax.experimental.pallas import tpu as pltpu
from jax.sharding import PartitionSpec as P

HEAD = 80
WIN = 256
AUG = 192
EPS = 1e-5
SCALE = HEAD**-0.5
SCALE2 = SCALE * math.log2(math.e)
DEAD = -1e30
ROWS = 256
GAIN1, SHIFT1, QBIAS, VBIAS, OBIAS, GAIN2, SHIFT2, DBIAS, LENGTHS = [slice(i, i + 1) for i in range(9)]
UBIAS = 9
FFN_TILE = 256
FFN_ROWS = 384
f32 = jnp.float32
bf16 = jnp.bfloat16
MESH = pl.DeviceIdType.MESH

ERF_P = 0.35
ERF_C = (0.19458996, 0.23381038, -0.00165479, 0.67243411, -0.66868964, 0.76616445, -0.19665448)


def params(limit=60):
    return pltpu.CompilerParams(vmem_limit_bytes=limit * 2**20)


def cost(flops, size):
    return pl.CostEstimate(flops=int(flops), bytes_accessed=int(size), transcendentals=0)


def dot(a, b):
    return jnp.dot(a, b, preferred_element_type=f32)


def dot_nt(a, b):
    return lax.dot_general(a, b, (((1,), (1,)), ((), ())), preferred_element_type=f32)


def dot_tn(a, b):
    return lax.dot_general(a, b, (((0,), (0,)), ((), ())), preferred_element_type=f32)


def gelu_pair(a):
    expo = jnp.exp2(a * a * (-0.5 * math.log2(math.e)))
    t = 1.0 / (1.0 + jnp.abs(a) * (ERF_P * math.sqrt(0.5)))
    total = ERF_C[-1]
    for c in ERF_C[-2::-1]:
        total = total * t + c
    tail = 0.5 * expo * (total * t)
    cdf = jnp.where(a >= 0, 1.0 - tail, tail)
    return a * cdf, cdf + a * (expo * (1.0 / math.sqrt(2.0 * math.pi)))


def whole(shape):
    return pl.BlockSpec(shape, lambda *_: (0,) * len(shape))


def row_block(rows, cols):
    return pl.BlockSpec((rows, cols), lambda i: (i, 0))


def standardize(x):
    centred = x - jnp.mean(x, axis=-1, keepdims=True)
    inv = lax.rsqrt(jnp.mean(centred * centred, axis=-1, keepdims=True) + EPS)
    return centred * inv, inv


class Link:
    def __init__(self, sems):
        self.send, self.recv, self.local = sems
        self.next = 0
        self.next_local = 0
        self.groups = lax.axis_size("shard")
        self.rep = lax.axis_index("rep")
        self.shard = lax.axis_index("shard")
        self.core = lax.rem(self.rep, 2)
        self.half = self.groups // 2

    def meet_plane(self):
        barrier = pltpu.get_barrier_semaphore()
        base = self.rep - self.core
        for c in range(2):
            for p in range(self.groups):
                if c or p:
                    to = (base + (self.core ^ c), self.shard ^ p)
                    pl.semaphore_signal(barrier, inc=1, device_id=to, device_id_type=MESH)
        pl.semaphore_wait(barrier, 2 * self.groups - 1)

    def meet_core(self):
        barrier = pltpu.get_barrier_semaphore()
        pl.semaphore_signal(barrier, inc=1, device_id=self.sibling(), device_id_type=MESH)
        pl.semaphore_wait(barrier, 1)

    def sibling(self):
        return (self.rep ^ 1, self.shard)

    def slots(self, count):
        first = self.next
        self.next += count
        return first

    def local_slots(self, count):
        first = self.next_local
        self.next_local += count
        return first

    def remote(self, src, dst, send, recv, to):
        return pltpu.make_async_remote_copy(
            src_ref=src,
            dst_ref=dst,
            send_sem=self.send.at[send],
            recv_sem=self.recv.at[recv],
            device_id=to,
            device_id_type=MESH,
        )

    def here(self, src, dst, slot):
        return pltpu.make_async_copy(src, dst, self.local.at[slot])


class Gather:
    def __init__(self, link, src, dst):
        self.link, self.src, self.dst = link, src, dst
        self.rows = src.shape[0]
        self.base = link.slots(max(4, link.groups - 1))
        self.keep = link.here(src, dst.at[link.shard], link.local_slots(1))

    def first(self):
        link = self.link
        peers = (1, 2) if link.groups == 4 else range(1, link.groups)
        return [
            link.remote(self.src, self.dst.at[link.shard], self.base + i, self.base + i, (link.rep, link.shard ^ p))
            for i, p in enumerate(peers)
        ]

    def second(self):
        link = self.link
        if link.groups != 4:
            return []
        cut = self.rows // 2
        parts = ((1, 2, pl.ds(0, cut)), (2, 1, pl.ds(cut, self.rows - cut)))
        out = []
        for i, (origin, to, rows) in enumerate(parts):
            ref = self.dst.at[link.shard ^ origin, rows]
            out.append(link.remote(ref, ref, self.base + 2 + i, self.base + 2 + i, (link.rep, link.shard ^ to)))
        return out

    def start(self):
        self.keep.start()
        for c in self.first():
            c.start()

    def forward(self):
        for c, d in zip(self.first(), self.second()):
            c.wait_recv()
            d.start()

    def finish(self):
        second = self.second()
        for c in self.first():
            if not second:
                c.wait_recv()
            c.wait_send()
        for c in second:
            c.wait()
        self.keep.wait()


class ToClip:
    def __init__(self, link, src, dst):
        self.link, self.src, self.dst = link, src, dst
        self.rows = src.shape[1]
        self.base = link.slots(link.half + 1)
        self.keep = link.local_slots(1)

    def copy(self, j):
        link = self.link
        core = lax.div(link.shard, link.half)
        to = (link.rep - link.core + core, link.core * link.half + j)
        mine = (core == link.core) & (link.core * link.half + j == link.shard)
        dst = self.dst.at[pl.ds(pl.multiple_of(link.shard * self.rows, self.rows), self.rows)]
        there = link.remote(self.src.at[j], dst, self.base + j, self.base + lax.rem(link.shard, link.half), to)
        return mine, there, link.here(self.src.at[j], dst, self.keep)

    def arrival(self, t):
        link = self.link
        source = link.core * link.half + t
        mine = (lax.div(link.shard, link.half) == link.core) & (source == link.shard)
        dst = self.dst.at[pl.ds(pl.multiple_of(source * self.rows, self.rows), self.rows)]
        there = link.remote(self.src.at[0], dst, self.base, self.base + t, link.sibling())
        return mine, there, link.here(self.src.at[0], dst, self.keep)

    def to_sibling(self):
        link = self.link
        size = link.half * self.rows
        rows = pl.ds(pl.multiple_of(link.core * size, size), size)
        slot = self.base + link.half
        return link.remote(self.dst.at[rows], self.dst.at[rows], slot, slot, link.sibling())

    def start(self):
        for j in range(self.link.half):
            mine, there, here = self.copy(j)
            pl.when(mine)(here.start)
            pl.when(jnp.logical_not(mine))(there.start)

    def forward(self):
        for t in range(self.link.half):
            mine, there, here = self.arrival(t)
            pl.when(mine)(here.wait)
            pl.when(jnp.logical_not(mine))(there.wait_recv)
        self.to_sibling().start()

    def finish(self):
        self.to_sibling().wait()
        for j in range(self.link.half):
            mine, there, _ = self.copy(j)
            pl.when(jnp.logical_not(mine))(there.wait_send)


class FromClip:
    def __init__(self, link, src, dst):
        self.link, self.src, self.dst = link, src, dst
        self.rows = dst.shape[1]
        self.base = link.slots(link.half)
        self.keep = link.local_slots(1)

    def copy(self, t):
        link = self.link
        core = lax.div(link.shard, link.half)
        shard = link.core * link.half + t
        mine = (core == link.core) & (shard == link.shard)
        clip = lax.rem(link.shard, link.half)
        src = self.src.at[pl.ds(t * self.rows, self.rows)]
        dst = self.dst.at[clip]
        there = link.remote(src, dst, self.base + t, self.base + clip, (link.rep - link.core + core, shard))
        return mine, there, link.here(src, dst, self.keep)

    def arrival(self, j):
        link = self.link
        mine = (lax.div(link.shard, link.half) == link.core) & (link.core * link.half + j == link.shard)
        src = self.src.at[pl.ds(0, self.rows)]
        there = link.remote(src, self.dst.at[j], self.base, self.base + j, link.sibling())
        return mine, there, link.here(src, self.dst.at[j], self.keep)

    def start(self):
        for t in range(self.link.half):
            mine, there, here = self.copy(t)
            pl.when(mine)(here.start)
            pl.when(jnp.logical_not(mine))(there.start)

    def forward(self):
        pass

    def finish(self):
        for t in range(self.link.half):
            mine, there, here = self.copy(t)
            pl.when(jnp.logical_not(mine))(there.wait_send)
        for j in range(self.link.half):
            mine, there, here = self.arrival(j)
            pl.when(mine)(here.wait)
            pl.when(jnp.logical_not(mine))(there.wait_recv)


class Owners:
    def __init__(self, link, src, dst):
        self.link, self.src, self.dst = link, src, dst
        self.base = link.slots(link.groups - 1)

    def copies(self):
        link = self.link
        return [
            link.remote(
                self.src.at[link.shard ^ p],
                self.dst.at[p - 1],
                self.base + p - 1,
                self.base + p - 1,
                (link.rep, link.shard ^ p),
            )
            for p in range(1, link.groups)
        ]

    def start(self):
        for c in self.copies():
            c.start()

    def forward(self):
        pass

    def finish(self):
        for c in self.copies():
            c.wait()


class Jobs:
    def __init__(self, *jobs):
        self.jobs = jobs

    def sources(self):
        return [a for _, a, _ in self.jobs]

    def in_specs(self):
        return [pl.BlockSpec(memory_space=pl.ANY)] * len(self.jobs)

    def out_shapes(self):
        return [jax.ShapeDtypeStruct(shape, a.dtype) for _, a, shape in self.jobs]

    def scratch(self, extra=0):
        groups = lax.axis_size("shard")
        remote = len(self.jobs) * max(4, groups) + extra
        return [
            pltpu.SemaphoreType.DMA((remote,)),
            pltpu.SemaphoreType.DMA((remote,)),
            pltpu.SemaphoreType.DMA((len(self.jobs) + extra + 1,)),
        ]

    def bind(self, sems, srcs, dsts):
        link = Link(sems)
        return link, [kind(link, a, b) for (kind, _, _), a, b in zip(self.jobs, srcs, dsts)]


def comm_params(number, limit=60):
    return pltpu.CompilerParams(
        vmem_limit_bytes=limit * 2**20, collective_id=number, has_side_effects=True
    )


def exchange_call(jobs, sibling, number, name):
    count = len(jobs.jobs)

    def kernel(*refs):
        srcs, mine = refs[:count], refs[count]
        dsts, other = refs[count + 1 : 2 * count + 1], refs[2 * count + 1]
        link, bound = jobs.bind(refs[2 * count + 2 :], srcs, dsts)
        slot = link.slots(1)
        swap = link.remote(mine, other, slot, slot, link.sibling())
        link.meet_plane()
        swap.start()
        for job in bound:
            job.start()
        for job in bound:
            job.forward()
        for job in bound:
            job.finish()
        swap.wait()

    return pl.pallas_call(
        kernel,
        in_specs=jobs.in_specs() + [pl.BlockSpec(memory_space=pl.ANY)],
        out_specs=[pl.BlockSpec(memory_space=pl.ANY)] * (count + 1),
        out_shape=jobs.out_shapes() + [jax.ShapeDtypeStruct(sibling.shape, sibling.dtype)],
        scratch_shapes=jobs.scratch(1),
        compiler_params=comm_params(number),
        name=name,
    )(*jobs.sources(), sibling)


def qkv_kernel(x_ref, vec_ref, w_ref, bias_ref, h_ref, q_ref, k_ref, v_ref):
    xhat, _ = standardize(x_ref[...].astype(f32))
    h = (xhat * vec_ref[GAIN1] + vec_ref[SHIFT1]).astype(bf16)
    h_ref[...] = h
    z = dot(h, w_ref[...]) + bias_ref[...]
    width = z.shape[1] // 3
    for i, ref in enumerate((q_ref, k_ref, v_ref)):
        ref[:, :width] = z[:, i * width : (i + 1) * width].astype(bf16)
        ref[:, width:] = jnp.zeros((ref.shape[0], ref.shape[1] - width), bf16)


def qkv_call(x, vec, w, bias, wide):
    n, d = x.shape
    out = jax.ShapeDtypeStruct((n, wide), bf16)
    return pl.pallas_call(
        qkv_kernel,
        grid=(n // ROWS,),
        in_specs=[row_block(ROWS, d), whole(vec.shape), whole(w.shape), whole(bias.shape)],
        out_specs=[row_block(ROWS, d)] + [row_block(ROWS, wide)] * 3,
        out_shape=[jax.ShapeDtypeStruct((n, d), bf16), out, out, out],
        compiler_params=params(),
        cost_estimate=cost(2 * n * d * w.shape[1], 4 * n * d + 2 * w.size + 6 * n * wide),
        name="project",
    )(x, vec, w, bias)


def head_window(h):
    start = h * HEAD
    base = (start // 128) * 128
    off = start - base
    lane = lax.broadcasted_iota(jnp.int32, (1, WIN), 1)
    keep = jnp.where((lane >= off) & (lane < off + HEAD), 1.0, 0.0)
    return pl.ds(pl.multiple_of(base, 128), WIN), keep, lane


def put3(x, lane, first, value):
    hi = value.astype(bf16).astype(f32)
    rest = value - hi
    mid = rest.astype(bf16).astype(f32)
    low = rest - mid
    return jnp.where(
        lane == first,
        hi,
        jnp.where(lane == first + 1, mid, jnp.where(lane == first + 2, low, x)),
    )


def key_extra(rows, length):
    lane = lax.broadcasted_iota(jnp.int32, (rows, WIN), 1)
    row = lax.broadcasted_iota(jnp.int32, (rows, WIN), 0)
    dead = jnp.where(row >= length, DEAD, 0.0)
    minus = jnp.where((lane > AUG) & (lane <= AUG + 3), -1.0, 0.0)
    return jnp.where(lane == AUG, dead, minus).astype(bf16)


def attn_fwd_kernel(*refs, bq, jobs):
    count = len(jobs.jobs)
    len_ref, q_ref, k_ref, v_ref = refs[:4]
    o_ref, lse_ref = refs[4 + count : 6 + count]
    acc, kx = refs[6 + 2 * count : 8 + 2 * count]
    link, bound = jobs.bind(refs[8 + 2 * count :], refs[4 : 4 + count], refs[6 + count : 6 + 2 * count])
    h = pl.program_id(0)
    heads = pl.num_programs(0)
    n = q_ref.shape[0]
    width = o_ref.shape[1]

    @pl.when(h == 0)
    def _():
        link.meet_plane()
        for job in bound:
            job.start()
        acc[...] = jnp.zeros_like(acc)
        lse_ref[...] = jnp.zeros_like(lse_ref)
        kx[...] = key_extra(n, len_ref[0])

    @pl.when(h == heads - 2)
    def _():
        for job in bound:
            job.forward()

    win, keep, lane = head_window(h)
    low = keep.astype(bf16)
    q_one = jnp.where(lane == AUG, 1.0, 0.0).astype(bf16)
    v_one = jnp.where((lane >= AUG) & (lane < AUG + 3), 1.0, 0.0).astype(bf16)
    k = k_ref[:, win] * low + kx[...]
    v = v_ref[:, win] * low + v_one
    for i in range(n // bq):
        rows = slice(i * bq, (i + 1) * bq)
        s = dot_nt(q_ref[rows, win] * low + q_one, k)
        peak = jnp.max(s, axis=-1, keepdims=True)
        p = jnp.exp2((s - peak) * SCALE2).astype(bf16)
        o = dot(p, v)
        total = o[:, AUG : AUG + 1]
        acc[rows, win] += o * (keep * (1.0 / total))
        here = lax.broadcasted_iota(jnp.int32, (bq, 128), 1) == h
        lse = peak + jnp.log(total) * (1.0 / SCALE)
        lse_ref[rows, :] = jnp.where(here, lse, lse_ref[rows, :])

    @pl.when(h == heads - 1)
    def _():
        o_ref[:, :width] = acc[:, :width].astype(bf16)
        for job in bound:
            job.finish()


def attn_fwd_call(length, q, k, v, width, heads, jobs, number):
    n, wide = q.shape
    return pl.pallas_call(
        functools.partial(attn_fwd_kernel, bq=256, jobs=jobs),
        grid=(heads,),
        in_specs=[pl.BlockSpec(memory_space=pltpu.SMEM)] + [whole((n, wide))] * 3 + jobs.in_specs(),
        out_specs=[whole((n, width)), whole((n, 128))] + jobs.in_specs(),
        out_shape=[jax.ShapeDtypeStruct((n, width), bf16), jax.ShapeDtypeStruct((n, 128), f32)] + jobs.out_shapes(),
        scratch_shapes=[pltpu.VMEM((n, wide), f32), pltpu.VMEM((n, WIN), bf16)] + jobs.scratch(),
        compiler_params=comm_params(number),
        cost_estimate=cost(4 * n * n * WIN * heads, 8 * n * wide),
        name="attend",
    )(length, q, k, v, *jobs.sources())


def attn_bwd_kernel(*refs, bk, jobs):
    count = len(jobs.jobs)
    len_ref, q_ref, k_ref, v_ref, o_ref, do_ref, lse_ref = refs[:7]
    g_ref, sum_ref = refs[7 + count : 9 + count]
    dq, dk, dv, part, qa, da, kx = refs[9 + 2 * count : 16 + 2 * count]
    link, bound = jobs.bind(refs[16 + 2 * count :], refs[7 : 7 + count], refs[9 + count : 9 + 2 * count])
    h = pl.program_id(0)
    n = q_ref.shape[0]

    @pl.when(h == 0)
    def _():
        link.meet_plane()
        for job in bound:
            job.start()
        for ref in (dq, dk, dv):
            ref[...] = jnp.zeros_like(ref)
        kx[...] = key_extra(n, len_ref[0])

    win, keep, lane = head_window(h)
    low = keep.astype(bf16)
    v_one = jnp.where((lane >= AUG) & (lane < AUG + 3), 1.0, 0.0).astype(bf16)
    for i in range(n // ROWS):
        rows = slice(i * ROWS, (i + 1) * ROWS)
        here = lax.broadcasted_iota(jnp.int32, (ROWS, 128), 1) == h
        lse = jnp.sum(jnp.where(here, lse_ref[rows, :], 0.0), axis=-1, keepdims=True)
        q = q_ref[rows, win].astype(f32) * keep
        qa[rows, :] = jnp.where(lane == AUG, 1.0, put3(q, lane, AUG + 1, lse)).astype(bf16)
        d = do_ref[rows, win].astype(f32) * keep
        delta = jnp.sum(d * o_ref[rows, win].astype(f32), axis=-1, keepdims=True)
        da[rows, :] = put3(d, lane, AUG, -delta).astype(bf16)
    for i in range(n // bk):
        rows = slice(i * bk, (i + 1) * bk)
        k = k_ref[rows, win] * low + kx[rows, :]
        v = v_ref[rows, win] * low + v_one
        p = jnp.exp2(dot_nt(k, qa[...]) * SCALE2)
        ds = (p * dot_nt(v, da[...])).astype(bf16)
        dv[rows, win] += dot(p.astype(bf16), da[...]) * keep
        dk[rows, win] += dot(ds, qa[...]) * keep
        new = dot_tn(ds, k)
        part[...] = new if i == 0 else part[...] + new
    dq[:, win] += part[...] * keep

    @pl.when(h == pl.num_programs(0) - 1)
    def _():
        for i, (ref, factor) in enumerate(((dq, SCALE), (dk, SCALE), (dv, 1.0))):
            value = (ref[:, : g_ref.shape[1] // 3] * factor).astype(bf16)
            cols = slice(i * value.shape[1], (i + 1) * value.shape[1])
            g_ref[:, cols] = value
            sum_ref[:, cols] = jnp.sum(value.astype(f32), axis=0, keepdims=True)
        for job in bound:
            job.finish()


def attn_bwd_call(length, q, k, v, o, do, lse, width, heads, jobs, number):
    n, wide = q.shape
    return pl.pallas_call(
        functools.partial(attn_bwd_kernel, bk=256, jobs=jobs),
        grid=(heads,),
        in_specs=[pl.BlockSpec(memory_space=pltpu.SMEM)]
        + [whole((n, wide))] * 5
        + [whole((n, 128))]
        + jobs.in_specs(),
        out_specs=[whole((n, 3 * width)), whole((1, 3 * width))] + jobs.in_specs(),
        out_shape=[
            jax.ShapeDtypeStruct((n, 3 * width), bf16),
            jax.ShapeDtypeStruct((1, 3 * width), f32),
        ]
        + jobs.out_shapes(),
        scratch_shapes=[pltpu.VMEM((n, wide), f32)] * 3
        + [pltpu.VMEM((n, WIN), f32)]
        + [pltpu.VMEM((n, WIN), bf16)] * 3
        + jobs.scratch(),
        compiler_params=comm_params(number),
        cost_estimate=cost(10 * n * n * WIN * heads, 20 * n * wide),
        name="attend_back",
    )(length, q, k, v, o, do, lse, *jobs.sources())


def middle_kernel(o_ref, w_ref, x_ref, vec_ref, mid_ref, h_ref, owide_ref, mine, other, *sems):
    link = Link(sems)
    n = x_ref.shape[0]
    width = o_ref.shape[1]
    link.meet_core()

    def swap(i):
        rows = pl.ds(pl.multiple_of(i * ROWS, ROWS), ROWS)
        return rows, link.remote(mine.at[rows], other.at[rows], i, i, link.sibling())

    def project(i, carry):
        rows, copy = swap(i)
        mine[rows, :] = dot(o_ref[rows, :], w_ref[...]).astype(bf16)
        copy.start()
        return carry

    def norm(i, carry):
        rows, copy = swap(i)
        copy.wait_recv()
        mid = x_ref[rows, :].astype(f32) + (
            mine[rows, :].astype(f32) + other[rows, :].astype(f32) + vec_ref[OBIAS]
        )
        mid_ref[rows, :] = mid
        xhat, _ = standardize(mid)
        h_ref[rows, :] = (xhat * vec_ref[GAIN2] + vec_ref[SHIFT2]).astype(bf16)
        return carry

    lax.fori_loop(0, n // ROWS, project, 0)
    owide_ref[:, :width] = o_ref[...]
    owide_ref[:, width:] = jnp.zeros((n, owide_ref.shape[1] - width), bf16)
    lax.fori_loop(0, n // ROWS, norm, 0)
    for i in range(n // ROWS):
        swap(i)[1].wait_send()


def middle_call(o, w, x, vec, wide, number):
    n, d = x.shape
    sems = [pltpu.SemaphoreType.DMA((n // ROWS,))] * 2 + [pltpu.SemaphoreType.DMA((1,))]
    vmem = pl.BlockSpec(memory_space=pltpu.VMEM)
    return pl.pallas_call(
        middle_kernel,
        in_specs=[vmem] * 4,
        out_specs=[vmem] * 3,
        out_shape=[
            jax.ShapeDtypeStruct((n, d), f32),
            jax.ShapeDtypeStruct((n, d), bf16),
            jax.ShapeDtypeStruct((n, wide), bf16),
        ],
        scratch_shapes=[pltpu.VMEM((n, d), bf16)] * 2 + sems,
        compiler_params=comm_params(number),
        cost_estimate=cost(2 * n * w.size, 14 * n * d),
        name="middle",
    )(o, w, x, vec)


def ffn_kernel(*refs, chained, last, mc, jobs):
    count = len(jobs.jobs)
    h_ref, dz_ref, up_ref, ub_ref, dn_ref = refs[:5]
    refs = refs[5:]
    if chained:
        old_out, old_dh = refs[:2]
        refs = refs[2:]
    srcs, refs = refs[:count], refs[count:]
    out_ref, dh_ref, dup_ref, ddn_ref, dub_ref = refs[:5]
    dsts, refs = refs[5 : 5 + count], refs[5 + count :]
    ht, act, grad = refs[:3]
    acc, dh = refs[3:5] if last else (out_ref, dh_ref)
    refs = refs[5:] if last else refs[3:]
    link, bound = jobs.bind(refs[:3], srcs, dsts)
    t = pl.program_id(0)
    tiles = pl.num_programs(0)
    n = h_ref.shape[0]

    @pl.when(t == 0)
    def _():
        link.meet_plane()
        for job in bound:
            job.start()
        if chained:
            sem = refs[3]
            copies = [
                pltpu.make_async_copy(src, dst, sem.at[i])
                for i, (src, dst) in enumerate(((old_out, acc), (old_dh, dh)))
            ]
            for c in copies:
                c.start()
            ht[...] = h_ref[...].T
            for c in copies:
                c.wait()
        else:
            ht[...] = h_ref[...].T
            acc[...] = jnp.zeros_like(acc)
            dh[...] = jnp.zeros_like(dh)

    @pl.when(t == tiles - 1)
    def _():
        for job in bound:
            job.forward()

    def step(i, carry):
        rows = pl.ds(pl.multiple_of(i * mc, mc), mc)
        g, slope = gelu_pair(dot(h_ref[rows, :], up_ref[...]) + ub_ref[...])
        g = g.astype(bf16)
        da = (dot_nt(dz_ref[rows, :], dn_ref[...]) * slope).astype(bf16)
        act[rows, :] = g
        grad[rows, :] = da
        acc[rows, :] += dot(g, dn_ref[...])
        dh[rows, :] += dot_nt(da, up_ref[...])
        return carry

    lax.fori_loop(0, n // mc, step, 0)
    dub_ref[...] = jnp.sum(grad[...].astype(f32), axis=0, keepdims=True)
    dup_ref[...] = dot(ht[...], grad[...]).astype(bf16)
    ddn_ref[...] = dot_tn(act[...], dz_ref[...]).astype(bf16)

    @pl.when(t == tiles - 1)
    def _():
        if last:
            out_ref[...] = acc[...].astype(out_ref.dtype)
            dh_ref[...] = dh[...].astype(dh_ref.dtype)
        for job in bound:
            job.finish()


def ffn_call(h, dz, up, bias, down, old, last, jobs, number, name):
    n, d = h.shape
    hidden = up.shape[1]
    bt = FFN_TILE
    out = jax.ShapeDtypeStruct((n, d), bf16 if last else f32)
    chained = old is not None
    once = pl.BlockSpec((n, d), lambda t: (0, 0), pipeline_mode=pl.Buffered(1))
    return pl.pallas_call(
        functools.partial(ffn_kernel, chained=chained, last=last, mc=FFN_ROWS, jobs=jobs),
        grid=(hidden // bt,),
        in_specs=[
            once,
            once,
            pl.BlockSpec((d, bt), lambda t: (0, t)),
            pl.BlockSpec((1, bt), lambda t: (0, t)),
            pl.BlockSpec((bt, d), lambda t: (t, 0)),
        ]
        + ([pl.BlockSpec(memory_space=pl.ANY)] * 2 if chained else [])
        + jobs.in_specs(),
        out_specs=[
            once,
            once,
            pl.BlockSpec((d, bt), lambda t: (0, t)),
            pl.BlockSpec((bt, d), lambda t: (t, 0)),
            pl.BlockSpec((1, bt), lambda t: (0, t)),
        ]
        + jobs.in_specs(),
        out_shape=[
            out,
            out,
            jax.ShapeDtypeStruct((d, hidden), bf16),
            jax.ShapeDtypeStruct((hidden, d), bf16),
            jax.ShapeDtypeStruct((1, hidden), f32),
        ]
        + jobs.out_shapes(),
        scratch_shapes=[pltpu.VMEM((d, n), bf16)]
        + [pltpu.VMEM((n, bt), bf16)] * 2
        + ([pltpu.VMEM((n, d), f32)] * 2 if last else [])
        + jobs.scratch()
        + ([pltpu.SemaphoreType.DMA((2,))] if chained else []),
        compiler_params=comm_params(number),
        cost_estimate=cost(12 * n * d * hidden, 8 * d * hidden + 12 * n * d),
        name=name,
    )(h, dz, up, bias, down, *(old if chained else ()), *jobs.sources())


def second_back_kernel(
    mid_ref, dh_ref, out_ref, dz_ref, vec_ref, w_ref, o_ref, dh_any, out_any,
    dmid_ref, do_ref, dw_ref, sums_ref, layer_ref,
    acc, dh_other, out_other, *sems
):
    i = pl.program_id(0)
    blocks = pl.num_programs(0)
    link = Link(sems)
    half = layer_ref.shape[0] // ROWS
    width = w_ref.shape[0]

    def swap_dh(j):
        rows = pl.ds(pl.multiple_of(j * ROWS, ROWS), ROWS)
        return link.remote(dh_any.at[rows], dh_other.at[rows], j, j, link.sibling())

    def swap_out(j):
        src = pl.ds(pl.multiple_of(((1 - link.core) * half + j) * ROWS, ROWS), ROWS)
        dst = pl.ds(pl.multiple_of(j * ROWS, ROWS), ROWS)
        slot = 2 * half + j
        return link.remote(out_any.at[src], out_other.at[dst], slot, slot, link.sibling())

    @pl.when(i == 0)
    def _():
        link.meet_core()
        for j in range(2 * half):
            swap_dh(j).start()
        for j in range(half):
            swap_out(j).start()
        acc[...] = jnp.zeros_like(acc)
        sums_ref[...] = jnp.zeros_like(sums_ref)

    mid = mid_ref[...]
    xhat, inv = standardize(mid)
    swap_dh(i).wait_recv()
    rows = pl.ds(pl.multiple_of(i * ROWS, ROWS), ROWS)
    dh = dh_ref[...].astype(f32) + dh_other[rows, :].astype(f32)
    dx = dh * vec_ref[GAIN2]
    dz = dz_ref[...].astype(f32)
    dmid = dz + inv * (
        dx - jnp.mean(dx, axis=-1, keepdims=True) - xhat * jnp.mean(dx * xhat, axis=-1, keepdims=True)
    )
    dmid_ref[...] = dmid
    dy = dmid.astype(bf16)
    do_ref[:, :width] = dot_nt(dy, w_ref[...]).astype(bf16)
    do_ref[:, width:] = jnp.zeros((do_ref.shape[0], do_ref.shape[1] - width), bf16)
    acc[...] += dot_tn(o_ref[...], dy)
    for row, value in enumerate((dh * xhat, dh, dy.astype(f32), dz)):
        sums_ref[row : row + 1, :] += jnp.sum(value, axis=0, keepdims=True)

    j = i - link.core * half

    @pl.when((j >= 0) & (j < half))
    def _():
        swap_out(j).wait_recv()
        here = pl.ds(pl.multiple_of(j * ROWS, ROWS), ROWS)
        layer_ref[here, :] = (
            mid + (out_ref[...].astype(f32) + out_other[here, :].astype(f32) + vec_ref[DBIAS])
        ).astype(bf16)

    @pl.when(i == blocks - 1)
    def _():
        dw_ref[...] = acc[...].astype(bf16)
        for j in range(2 * half):
            swap_dh(j).wait_send()
        for j in range(half):
            swap_out(j).wait_send()


def second_back_call(mid, dh, out, dz, vec, w, o, wide, number):
    n, d = mid.shape
    width = w.shape[0]
    block = row_block(ROWS, d)
    count = 3 * n // ROWS // 2
    return pl.pallas_call(
        second_back_kernel,
        grid=(n // ROWS,),
        in_specs=[block] * 4
        + [whole(vec.shape), whole(w.shape), row_block(ROWS, width)]
        + [pl.BlockSpec(memory_space=pl.ANY)] * 2,
        out_specs=[block, row_block(ROWS, wide), whole((width, d)), whole((8, d)), whole((n // 2, d))],
        out_shape=[
            jax.ShapeDtypeStruct((n, d), f32),
            jax.ShapeDtypeStruct((n, wide), bf16),
            jax.ShapeDtypeStruct((width, d), bf16),
            jax.ShapeDtypeStruct((8, d), f32),
            jax.ShapeDtypeStruct((n // 2, d), bf16),
        ],
        scratch_shapes=[
            pltpu.VMEM((width, d), f32),
            pltpu.VMEM((n, d), bf16),
            pltpu.VMEM((n // 2, d), bf16),
            pltpu.SemaphoreType.DMA((count,)),
            pltpu.SemaphoreType.DMA((count,)),
            pltpu.SemaphoreType.DMA((1,)),
        ],
        compiler_params=comm_params(number),
        cost_estimate=cost(4 * n * d * width, 14 * n * d),
        name="second_back",
    )(mid, dh, out, dz, vec, w, o, dh, out)


def dw_kernel(h_ref, g_ref, out_ref):
    out_ref[...] = dot_tn(h_ref[...], g_ref[...]).astype(bf16)


def dw_call(h, grads):
    n, d = h.shape
    cols = grads.shape[1]
    return pl.pallas_call(
        dw_kernel,
        grid=(d // 256,),
        in_specs=[pl.BlockSpec((n, 256), lambda i: (0, i)), whole((n, cols))],
        out_specs=row_block(256, cols),
        out_shape=jax.ShapeDtypeStruct((d, cols), bf16),
        compiler_params=params(),
        cost_estimate=cost(2 * n * d * cols, 2 * (n * d + n * cols + d * cols)),
        name="project_grad",
    )(h, grads)


def first_back_kernel(*refs, jobs):
    count = len(jobs.jobs)
    g_ref, w_ref, vec_ref, x_any, dmid_any = refs[:5]
    dx_ref, sums_ref = refs[5 + count : 7 + count]
    x, dmid, mine, other = refs[7 + 2 * count : 11 + 2 * count]
    link, bound = jobs.bind(refs[11 + 2 * count :], refs[5 : 5 + count], refs[7 + count : 7 + 2 * count])
    size = dx_ref.shape[0]
    half = size // ROWS
    base = link.slots(half)
    keep = link.local_slots(2)
    own = pl.ds(pl.multiple_of(link.core * size, size), size)
    loads = [link.here(x_any.at[own], x, keep), link.here(dmid_any.at[own], dmid, keep + 1)]
    for c in loads:
        c.start()
    link.meet_plane()
    for job in bound:
        job.start()

    def product(j):
        rows = pl.ds(pl.multiple_of(j * ROWS, ROWS), ROWS)
        return dot_nt(g_ref[rows, :], w_ref[...])

    def swap(j):
        rows = pl.ds(pl.multiple_of(j * ROWS, ROWS), ROWS)
        return rows, link.remote(mine.at[rows], other.at[rows], base + j, base + j, link.sibling())

    def send(j, carry):
        rows, copy = swap(j)
        mine[rows, :] = product((1 - link.core) * half + j).astype(bf16)
        copy.start()
        return carry

    def norm(j, carry):
        rows, copy = swap(j)
        part = product(link.core * half + j)
        copy.wait_recv()
        xhat, inv = standardize(x[rows, :].astype(f32))
        dh = part + other[rows, :].astype(f32)
        dx = dh * vec_ref[GAIN1]
        dx_ref[rows, :] = (
            dmid[rows, :]
            + inv
            * (dx - jnp.mean(dx, axis=-1, keepdims=True) - xhat * jnp.mean(dx * xhat, axis=-1, keepdims=True))
        ).astype(bf16)
        for row, value in enumerate((dh * xhat, dh)):
            sums_ref[row : row + 1, :] += jnp.sum(value, axis=0, keepdims=True)
        return carry

    sums_ref[...] = jnp.zeros_like(sums_ref)
    lax.fori_loop(0, half, send, 0)
    for c in loads:
        c.wait()
    lax.fori_loop(0, half, norm, 0)
    for j in range(half):
        swap(j)[1].wait_send()
    for job in bound:
        job.forward()
    for job in bound:
        job.finish()


def first_back_call(grads, w, vec, x, dmid, jobs, number):
    n, d = x.shape
    size = n // 2
    vmem = pl.BlockSpec(memory_space=pltpu.VMEM)
    hbm = pl.BlockSpec(memory_space=pl.ANY)
    return pl.pallas_call(
        functools.partial(first_back_kernel, jobs=jobs),
        in_specs=[vmem] * 3 + [hbm] * 2 + jobs.in_specs(),
        out_specs=[vmem] * 2 + jobs.in_specs(),
        out_shape=[jax.ShapeDtypeStruct((size, d), bf16), jax.ShapeDtypeStruct((8, d), f32)] + jobs.out_shapes(),
        scratch_shapes=[
            pltpu.VMEM((size, d), bf16),
            pltpu.VMEM((size, d), f32),
            pltpu.VMEM((size, d), bf16),
            pltpu.VMEM((size, d), bf16),
        ]
        + jobs.scratch(size // ROWS),
        compiler_params=comm_params(number),
        cost_estimate=cost(2 * n * w.size, 12 * n * d),
        name="first_back",
    )(grads, w, vec, x, dmid, *jobs.sources())


def own_sum(blocks, others):
    shard = lax.axis_index("shard")
    total = lax.dynamic_index_in_dim(blocks, shard, 0, keepdims=False).astype(f32)
    for i in range(others.shape[0]):
        total = total + others[i].astype(f32)
    return total.astype(bf16)


def over_reps(own):
    planes = lax.axis_size("rep") // 2
    sums = lax.psum_scatter(
        own,
        "rep",
        scatter_dimension=0,
        tiled=True,
        axis_index_groups=[[2 * z + c for z in range(planes)] for c in range(2)],
    )
    both = lax.all_gather(sums, "rep", axis=0)
    rows, cols = sums.shape
    return both.reshape(planes, 2, rows, cols).transpose(1, 0, 2, 3).reshape(2, planes * rows, cols)


def on_device(
    tokens,
    lengths,
    cotangent,
    first_gain,
    first_shift,
    query_weight,
    query_bias,
    key_weight,
    value_weight,
    value_bias,
    out_weight,
    out_bias,
    second_gain,
    second_shift,
    up_weight,
    up_bias,
    down_weight,
    down_bias,
):
    g = lax.axis_size("shard")
    shard = lax.axis_index("shard")
    core = lax.rem(lax.axis_index("rep"), 2)
    cl, rows, d = tokens.shape
    n = 2 * cl * rows
    ff = up_weight.shape[1]
    own_d = d // g
    own_f = ff // g
    attn_cols = own_d // 2
    ffn_cols = own_f // 2
    width = d // 2
    heads = width // HEAD
    wide = pl.cdiv(width, 128) * 128 + 128
    first_n = ffn_cols * 2 // 5
    pieces = ((0, first_n), (first_n, ffn_cols))

    def core_cols(w, size, a, b):
        def of(c):
            return jnp.concatenate([w[:, (2 * s + c) * size + a : (2 * s + c) * size + b] for s in range(g)], axis=1)

        return jnp.where(core == 0, of(0), of(1))

    def core_rows(w):
        half = w.shape[0] // 2
        return lax.dynamic_slice_in_dim(w, core * half, half, 0)

    vectors = (first_gain, first_shift, query_bias, value_bias, out_bias, second_gain, second_shift, down_bias)
    lens = jnp.pad(lengths.astype(f32), (0, own_d - cl)).reshape(1, own_d)
    small = jnp.concatenate(
        [jnp.stack(vectors).astype(f32), lens, up_bias.astype(f32).reshape(-1, own_d)], axis=0
    )
    small = jnp.pad(small, ((0, 16 - small.shape[0]), (0, -own_d % 128)))
    qkv_own = jnp.concatenate(
        [core_cols(w, attn_cols, 0, attn_cols) for w in (query_weight, key_weight, value_weight)], axis=1
    )
    jobs = Jobs(
        (ToClip, tokens, (n, d)),
        (Gather, qkv_own, (g,) + qkv_own.shape),
        (Gather, small, (g,) + small.shape),
    )
    x, w_qkv, smalls, other_small = exchange_call(jobs, small, 0, "first_exchange")
    w_qkv = w_qkv.reshape(d, 3 * width)
    vec = smalls[:, :, :own_d].transpose(1, 0, 2).reshape(16, d)
    near = lax.div(shard, cl) == core
    lens = jnp.where(near, small[LENGTHS], other_small[LENGTHS])[0]
    length = lens[lax.rem(shard, cl)].astype(jnp.int32).reshape(1)

    def bias_cols(b):
        return lax.dynamic_index_in_dim(vec[b].reshape(1, g, 2, attn_cols), core, 2).reshape(1, width)

    bias = jnp.concatenate([bias_cols(QBIAS), jnp.zeros((1, width), f32), bias_cols(VBIAS)], axis=1)
    ubias = lax.dynamic_index_in_dim(
        vec[UBIAS : UBIAS + own_f // own_d].reshape(-1, g, own_d).transpose(1, 0, 2).reshape(g, 2, ffn_cols),
        core,
        1,
        keepdims=False,
    )
    ups = [core_cols(up_weight, ffn_cols, a, b) for a, b in pieces]
    down_own = core_rows(down_weight)
    downs = [down_own[a:b] for a, b in pieces]
    out_own = core_rows(out_weight)

    def gathered(a):
        return (Gather, a, (g,) + a.shape)

    h1, q, k, v = qkv_call(x, vec, w_qkv, bias, wide)
    jobs = Jobs(gathered(out_own), (ToClip, cotangent, (n, d)), gathered(ups[0]), gathered(downs[0]))
    o, lse, w_out, cot, up, down = attn_fwd_call(length, q, k, v, width, heads, jobs, 1)
    w_out = w_out.reshape(width, d)
    mid, h2, o_wide = middle_call(o, w_out, x, vec, wide, 2)
    live = jnp.arange(n, dtype=jnp.int32)[:, None] < length
    dz = jnp.where(live, cot, jnp.zeros_like(cot))

    def hidden_bias(piece):
        return ubias[:, piece[0] : piece[1]].reshape(1, -1)

    def to_owners(a):
        return (Owners, a, (g - 1,) + a.shape[1:])

    jobs = Jobs(gathered(ups[1]), gathered(downs[1]))
    out, dh2, dup0, ddn0, dub0, up1, down1 = ffn_call(
        h2, dz, up.reshape(d, -1), hidden_bias(pieces[0]), down.reshape(-1, d), None, False, jobs, 3, "hidden0"
    )
    dup0, ddn0 = dup0.reshape(g, own_d, -1), ddn0.reshape(g, -1, d)
    jobs = Jobs(to_owners(dup0), to_owners(ddn0))
    out, dh2, dup1, ddn1, dub1, dup0_in, ddn0_in = ffn_call(
        h2, dz, up1.reshape(d, -1), hidden_bias(pieces[1]), down1.reshape(-1, d), (out, dh2), True, jobs, 4, "hidden1"
    )
    dup1, ddn1 = dup1.reshape(g, own_d, -1), ddn1.reshape(g, -1, d)
    up0_all = over_reps(own_sum(dup0, dup0_in))
    down0_all = over_reps(own_sum(ddn0, ddn0_in))

    dmid, do, dwo, sums2, layer_own = second_back_call(mid, dh2, out, dz, vec, w_out, o, wide, 5)
    dwo = dwo.reshape(g, -1, d)

    jobs = Jobs(to_owners(dup1), to_owners(ddn1), to_owners(dwo), (FromClip, layer_own, (cl, rows, d)))
    grads, bias_sums, dup1_in, ddn1_in, dwo_in, layer_out = attn_bwd_call(
        length, q, k, v, o_wide, do, lse, width, heads, jobs, 6
    )
    up1_all = over_reps(own_sum(dup1, dup1_in))
    down1_all = over_reps(own_sum(ddn1, ddn1_in))
    out_grad = over_reps(own_sum(dwo, dwo_in)).reshape(own_d, d).astype(f32)
    dwqkv = dw_call(h1, grads).reshape(g, own_d, 3 * width)
    jobs = Jobs(to_owners(dwqkv))
    dx, sums1, dwqkv_in = first_back_call(grads, w_qkv, vec, x, dmid, jobs, 7)
    qkv_all = over_reps(own_sum(dwqkv, dwqkv_in)).reshape(2, own_d, 3, g, attn_cols)
    jobs = Jobs((FromClip, dx, (cl, rows, d)))
    tokens_grad, _ = exchange_call(jobs, sums1, 8, "last_exchange")

    up_all = jnp.concatenate([up0_all.reshape(2, own_d, g, -1), up1_all.reshape(2, own_d, g, -1)], axis=3)
    up_grad = up_all.transpose(1, 2, 0, 3).reshape(own_d, ff).astype(f32)
    down_grad = jnp.concatenate([down0_all, down1_all], axis=1).reshape(own_f, d).astype(f32)
    qkv_grads = [qkv_all[:, :, i].transpose(1, 2, 0, 3).reshape(own_d, d).astype(f32) for i in range(3)]

    def spread(v, size):
        out = jnp.zeros((g, 2, size), f32)
        return lax.dynamic_update_index_in_dim(out, v.reshape(g, size), core, 1).reshape(-1, own_d)

    pieces_small = [
        sums1[0].reshape(g, own_d),
        sums1[1].reshape(g, own_d),
        spread(bias_sums[0, :width], attn_cols),
        spread(bias_sums[0, 2 * width :], attn_cols),
        (sums2[2] * 0.5).reshape(g, own_d),
        (sums2[0] * 0.5).reshape(g, own_d),
        (sums2[1] * 0.5).reshape(g, own_d),
        (sums2[3] * 0.5).reshape(g, own_d),
    ]
    ub_sum = jnp.zeros((g, 2, ffn_cols), f32)
    ub_sum = lax.dynamic_update_index_in_dim(ub_sum, jnp.concatenate([dub0.reshape(g, -1), dub1.reshape(g, -1)], axis=1), core, 1)
    packed = jnp.concatenate(
        [jnp.stack(pieces_small, axis=1), ub_sum.reshape(g, -1, own_d)], axis=1
    )
    packed = lax.psum(packed, ("rep", "shard"))
    mine_small = lax.dynamic_index_in_dim(packed, shard, 0, keepdims=False)
    s_gain1, s_shift1, s_qb, s_vb, s_ob, s_gain2, s_shift2, s_db = [mine_small[i] for i in range(8)]
    s_ub = mine_small[8:].reshape(-1)

    return (
        layer_out,
        tokens_grad,
        s_gain1,
        s_shift1,
        qkv_grads[0],
        s_qb,
        qkv_grads[1],
        qkv_grads[2],
        s_vb,
        out_grad,
        s_ob,
        s_gain2,
        s_shift2,
        up_grad,
        s_ub,
        down_grad,
        s_db,
    )


def solution(mesh):
    row, mat, vec = P("rep", "shard", None), P("shard", None), P("shard")
    return jax.shard_map(
        on_device,
        mesh=mesh,
        in_specs=(row, P("rep"), row, vec, vec, mat, vec, mat, mat, vec, mat, vec, vec, vec, mat, vec, mat, vec),
        out_specs=(row, row, vec, vec, mat, vec, mat, mat, vec, mat, vec, vec, vec, mat, vec, mat, vec),
        check_vma=False,
    )
```

```python
import functools
import math

import jax
import jax.numpy as jnp
from jax import lax
from jax.experimental import pallas as pl
from jax.experimental.pallas import tpu as pltpu
from jax.sharding import PartitionSpec as P

HEAD = 80
WIN = 256
AUG = 192
EPS = 1e-5
SCALE = HEAD**-0.5
SCALE2 = SCALE * math.log2(math.e)
DEAD = -1e30
ROWS = 256
GAIN1, SHIFT1, QBIAS, VBIAS, OBIAS, GAIN2, SHIFT2, DBIAS, LENGTHS = [slice(i, i + 1) for i in range(9)]
UBIAS = 9
FFN_TILE = 256
FFN_ROWS = 384
f32 = jnp.float32
bf16 = jnp.bfloat16
MESH = pl.DeviceIdType.MESH

ERF_P = 0.35
ERF_C = (0.19458996, 0.23381038, -0.00165479, 0.67243411, -0.66868964, 0.76616445, -0.19665448)


def params(limit=60):
    return pltpu.CompilerParams(vmem_limit_bytes=limit * 2**20)


def cost(flops, size):
    return pl.CostEstimate(flops=int(flops), bytes_accessed=int(size), transcendentals=0)


def dot(a, b):
    return jnp.dot(a, b, preferred_element_type=f32)


def dot_nt(a, b):
    return lax.dot_general(a, b, (((1,), (1,)), ((), ())), preferred_element_type=f32)


def dot_tn(a, b):
    return lax.dot_general(a, b, (((0,), (0,)), ((), ())), preferred_element_type=f32)


def gelu_pair(a):
    expo = jnp.exp2(a * a * (-0.5 * math.log2(math.e)))
    t = 1.0 / (1.0 + jnp.abs(a) * (ERF_P * math.sqrt(0.5)))
    total = ERF_C[-1]
    for c in ERF_C[-2::-1]:
        total = total * t + c
    tail = 0.5 * expo * (total * t)
    cdf = jnp.where(a >= 0, 1.0 - tail, tail)
    return a * cdf, cdf + a * (expo * (1.0 / math.sqrt(2.0 * math.pi)))


def whole(shape):
    return pl.BlockSpec(shape, lambda *_: (0,) * len(shape))


def once(shape):
    return pl.BlockSpec(shape, lambda *_: (0,) * len(shape), pipeline_mode=pl.Buffered(1))


def row_block(rows, cols):
    return pl.BlockSpec((rows, cols), lambda i: (i, 0))


def standardize(x):
    centred = x - jnp.mean(x, axis=-1, keepdims=True)
    inv = lax.rsqrt(jnp.mean(centred * centred, axis=-1, keepdims=True) + EPS)
    return centred * inv, inv


class Link:
    def __init__(self, sems):
        self.send, self.recv, self.local = sems
        self.next = 0
        self.next_local = 0
        self.groups = lax.axis_size("shard")
        self.rep = lax.axis_index("rep")
        self.shard = lax.axis_index("shard")
        self.core = lax.rem(self.rep, 2)
        self.half = self.groups // 2

    def meet_plane(self):
        barrier = pltpu.get_barrier_semaphore()
        base = self.rep - self.core
        for c in range(2):
            for p in range(self.groups):
                if c or p:
                    to = (base + (self.core ^ c), self.shard ^ p)
                    pl.semaphore_signal(barrier, inc=1, device_id=to, device_id_type=MESH)
        pl.semaphore_wait(barrier, 2 * self.groups - 1)

    def meet_all(self):
        barrier = pltpu.get_barrier_semaphore()
        base = self.rep - self.core
        for c in range(2):
            for p in range(self.groups):
                if c or p:
                    to = (base + (self.core ^ c), self.shard ^ p)
                    pl.semaphore_signal(barrier, inc=1, device_id=to, device_id_type=MESH)
        pl.semaphore_signal(barrier, inc=1, device_id=self.inward(), device_id_type=MESH)

        @pl.when(self.inner())
        def _():
            pl.semaphore_signal(barrier, inc=1, device_id=self.outward(), device_id_type=MESH)
            pl.semaphore_wait(barrier, 2 * self.groups + 1)

        @pl.when(jnp.logical_not(self.inner()))
        def _():
            pl.semaphore_wait(barrier, 2 * self.groups)

    def inner(self):
        plane = lax.div(self.rep, 2)
        return (plane == 1) | (plane == 2)

    def inward(self):
        return (self.rep + jnp.where(self.rep < 4, 2, -2), self.shard)

    def outward(self):
        return (self.rep - jnp.where(self.rep < 4, 2, -2), self.shard)

    def meet_core(self):
        barrier = pltpu.get_barrier_semaphore()
        pl.semaphore_signal(barrier, inc=1, device_id=self.sibling(), device_id_type=MESH)
        pl.semaphore_wait(barrier, 1)

    def sibling(self):
        return (self.rep ^ 1, self.shard)

    def slots(self, count):
        first = self.next
        self.next += count
        return first

    def local_slots(self, count):
        first = self.next_local
        self.next_local += count
        return first

    def remote(self, src, dst, send, recv, to):
        return pltpu.make_async_remote_copy(
            src_ref=src,
            dst_ref=dst,
            send_sem=self.send.at[send],
            recv_sem=self.recv.at[recv],
            device_id=to,
            device_id_type=MESH,
        )

    def here(self, src, dst, slot):
        return pltpu.make_async_copy(src, dst, self.local.at[slot])


class Job:
    @staticmethod
    def buffers(source):
        return []

    def forward(self):
        pass

    def inward(self):
        pass

    def across(self):
        pass

    def outward(self):
        pass


class Gather(Job):
    def __init__(self, link, src, dst, bufs):
        self.link, self.src, self.dst = link, src, dst
        self.rows = src.shape[0]
        self.base = link.slots(max(4, link.groups - 1))
        self.keep = link.here(src, dst.at[link.shard], link.local_slots(1))

    def first(self):
        link = self.link
        peers = (1, 2) if link.groups == 4 else range(1, link.groups)
        return [
            link.remote(self.src, self.dst.at[link.shard], self.base + i, self.base + i, (link.rep, link.shard ^ p))
            for i, p in enumerate(peers)
        ]

    def second(self):
        link = self.link
        if link.groups != 4:
            return []
        cut = self.rows // 2
        parts = ((1, 2, pl.ds(0, cut)), (2, 1, pl.ds(cut, self.rows - cut)))
        out = []
        for i, (origin, to, rows) in enumerate(parts):
            ref = self.dst.at[link.shard ^ origin, rows]
            out.append(link.remote(ref, ref, self.base + 2 + i, self.base + 2 + i, (link.rep, link.shard ^ to)))
        return out

    def start(self):
        self.keep.start()
        for c in self.first():
            c.start()

    def forward(self):
        for c, d in zip(self.first(), self.second()):
            c.wait_recv()
            d.start()

    def finish(self):
        second = self.second()
        for c in self.first():
            if not second:
                c.wait_recv()
            c.wait_send()
        for c in second:
            c.wait()
        self.keep.wait()


class ToClip(Job):
    def __init__(self, link, src, dst, bufs):
        self.link, self.src, self.dst = link, src, dst
        self.rows = src.shape[1]
        self.base = link.slots(link.half + 1)
        self.keep = link.local_slots(1)

    def copy(self, j):
        link = self.link
        core = lax.div(link.shard, link.half)
        to = (link.rep - link.core + core, link.core * link.half + j)
        mine = (core == link.core) & (link.core * link.half + j == link.shard)
        dst = self.dst.at[pl.ds(pl.multiple_of(link.shard * self.rows, self.rows), self.rows)]
        there = link.remote(self.src.at[j], dst, self.base + j, self.base + lax.rem(link.shard, link.half), to)
        return mine, there, link.here(self.src.at[j], dst, self.keep)

    def arrival(self, t):
        link = self.link
        source = link.core * link.half + t
        mine = (lax.div(link.shard, link.half) == link.core) & (source == link.shard)
        dst = self.dst.at[pl.ds(pl.multiple_of(source * self.rows, self.rows), self.rows)]
        there = link.remote(self.src.at[0], dst, self.base, self.base + t, link.sibling())
        return mine, there, link.here(self.src.at[0], dst, self.keep)

    def to_sibling(self):
        link = self.link
        size = link.half * self.rows
        rows = pl.ds(pl.multiple_of(link.core * size, size), size)
        slot = self.base + link.half
        return link.remote(self.dst.at[rows], self.dst.at[rows], slot, slot, link.sibling())

    def start(self):
        for j in range(self.link.half):
            mine, there, here = self.copy(j)
            pl.when(mine)(here.start)
            pl.when(jnp.logical_not(mine))(there.start)

    def forward(self):
        for t in range(self.link.half):
            mine, there, here = self.arrival(t)
            pl.when(mine)(here.wait)
            pl.when(jnp.logical_not(mine))(there.wait_recv)
        self.to_sibling().start()

    def finish(self):
        self.to_sibling().wait()
        for j in range(self.link.half):
            mine, there, _ = self.copy(j)
            pl.when(jnp.logical_not(mine))(there.wait_send)


class FromClip(Job):
    def __init__(self, link, src, dst, bufs):
        self.link, self.src, self.dst = link, src, dst
        self.rows = dst.shape[1]
        self.base = link.slots(link.half)
        self.keep = link.local_slots(1)

    def copy(self, t):
        link = self.link
        core = lax.div(link.shard, link.half)
        shard = link.core * link.half + t
        mine = (core == link.core) & (shard == link.shard)
        clip = lax.rem(link.shard, link.half)
        src = self.src.at[pl.ds(t * self.rows, self.rows)]
        dst = self.dst.at[clip]
        there = link.remote(src, dst, self.base + t, self.base + clip, (link.rep - link.core + core, shard))
        return mine, there, link.here(src, dst, self.keep)

    def arrival(self, j):
        link = self.link
        mine = (lax.div(link.shard, link.half) == link.core) & (link.core * link.half + j == link.shard)
        src = self.src.at[pl.ds(0, self.rows)]
        there = link.remote(src, self.dst.at[j], self.base, self.base + j, link.sibling())
        return mine, there, link.here(src, self.dst.at[j], self.keep)

    def start(self):
        for t in range(self.link.half):
            mine, there, here = self.copy(t)
            pl.when(mine)(here.start)
            pl.when(jnp.logical_not(mine))(there.start)

    def finish(self):
        for t in range(self.link.half):
            mine, there, here = self.copy(t)
            pl.when(jnp.logical_not(mine))(there.wait_send)
        for j in range(self.link.half):
            mine, there, here = self.arrival(j)
            pl.when(mine)(here.wait)
            pl.when(jnp.logical_not(mine))(there.wait_recv)


class Owners(Job):
    def __init__(self, link, src, dst, bufs):
        self.link, self.src, self.dst = link, src, dst
        self.base = link.slots(link.groups - 1)

    def copies(self):
        link = self.link
        return [
            link.remote(
                self.src.at[link.shard ^ p],
                self.dst.at[p - 1],
                self.base + p - 1,
                self.base + p - 1,
                (link.rep, link.shard ^ p),
            )
            for p in range(1, link.groups)
        ]

    def start(self):
        for c in self.copies():
            c.start()

    def finish(self):
        for c in self.copies():
            c.wait()


def add_low(a, b):
    return (a.astype(f32) + b.astype(f32)).astype(bf16)


class Reduce(Job):
    def __init__(self, link, src, dst, bufs):
        self.link, self.src, self.dst = link, src, dst
        self.a, self.b, self.low, self.high = bufs
        self.base = link.slots(6)
        self.keep = link.local_slots(2)
        self.half = dst.shape[1]

    @staticmethod
    def buffers(source):
        half = pltpu.VMEM((source.shape[1] // 2, source.shape[2]), source.dtype)
        return [half] * 4

    def block(self, i, part):
        rows = pl.ds(part * self.half, self.half)
        return self.src.at[self.link.shard ^ i, rows]

    def hops(self):
        link = self.link
        x, y = (link.rep, link.shard ^ 1), (link.rep, link.shard ^ 2)
        plan = (
            (self.block(3, 0), self.a, x),
            (self.block(3, 1), self.b, y),
            (self.block(1, 0), self.dst.at[0], x),
            (self.block(2, 1), self.dst.at[2], y),
        )
        return [link.remote(s, d, self.base + i, self.base + i, to) for i, (s, d, to) in enumerate(plan)]

    def later(self):
        link = self.link
        x, y = (link.rep, link.shard ^ 1), (link.rep, link.shard ^ 2)
        plan = ((self.low, self.dst.at[1], y), (self.high, self.dst.at[3], x))
        return [link.remote(s, d, self.base + 4 + i, self.base + 4 + i, to) for i, (s, d, to) in enumerate(plan)]

    def loads(self):
        link = self.link
        return (
            link.here(self.block(2, 0), self.low, self.keep),
            link.here(self.block(1, 1), self.high, self.keep + 1),
        )

    def start(self):
        for c in self.hops():
            c.start()
        for c in self.loads():
            c.start()

    def forward(self):
        hops, loads, later = self.hops(), self.loads(), self.later()
        for i, (total, part) in enumerate(((self.low, self.a), (self.high, self.b))):
            loads[i].wait()
            hops[i].wait_recv()
            total[...] = add_low(total[...], part[...])
            later[i].start()

    def finish(self):
        hops, later = self.hops(), self.later()
        for i in range(4):
            hops[i].wait_send()
        for i in (2, 3):
            hops[i].wait_recv()
        for c in later:
            c.wait()


class Chain(Job):
    def __init__(self, link, src, dst, bufs):
        self.link, self.src, self.dst = link, src, dst
        self.own, self.one, self.two = bufs
        self.base = link.slots(4)
        self.keep = link.local_slots(2)

    @staticmethod
    def buffers(source):
        return [pltpu.VMEM(source.shape, source.dtype)] * 3

    def step(self, src, dst, slot, to):
        return self.link.remote(src, dst, self.base + slot, self.base + slot, to)

    def steps(self):
        link = self.link
        return (
            self.step(self.src, self.one, 0, link.inward()),
            self.step(self.own, self.two, 1, link.inward()),
            self.step(self.one, self.two, 2, link.outward()),
        )

    def share(self, ref):
        link = self.link
        place = self.dst.at[link.core]
        return self.step(ref, place, 3, link.sibling()), link.here(ref, place, self.keep + 1)

    def start(self):
        inner = self.link.inner()
        pl.when(inner)(self.link.here(self.src, self.own, self.keep).start)
        pl.when(jnp.logical_not(inner))(self.steps()[0].start)

    def add(self, a, b):
        return (a[...].astype(f32) + b[...].astype(f32)).astype(a.dtype)

    def inward(self):
        @pl.when(self.link.inner())
        def _():
            steps = self.steps()
            self.link.here(self.src, self.own, self.keep).wait()
            steps[0].wait_recv()
            self.own[...] = self.add(self.own, self.one)
            steps[1].start()

    def across(self):
        @pl.when(self.link.inner())
        def _():
            steps = self.steps()
            steps[1].wait_recv()
            self.one[...] = self.add(self.own, self.two)
            steps[2].start()
            for c in self.share(self.one):
                c.start()

    def outward(self):
        @pl.when(jnp.logical_not(self.link.inner()))
        def _():
            self.steps()[2].wait_recv()
            for c in self.share(self.two):
                c.start()

    def finish(self):
        swap, here = self.share(self.one)
        swap.wait()
        here.wait()
        inner = self.link.inner()

        @pl.when(inner)
        def _():
            self.steps()[1].wait_send()
            self.steps()[2].wait_send()

        pl.when(jnp.logical_not(inner))(self.steps()[0].wait_send)


def run_chains(chains):
    for i in range(len(chains) + 1):
        if i < len(chains):
            chains[i].inward()
        if i:
            chains[i - 1].across()
    for c in chains:
        c.outward()


class Jobs:
    def __init__(self, *jobs):
        self.jobs = jobs
        self.bufs = [kind.buffers(a) for kind, a, _ in jobs]

    def sources(self):
        return [a for _, a, _ in self.jobs]

    def in_specs(self):
        return [pl.BlockSpec(memory_space=pl.ANY)] * len(self.jobs)

    def out_shapes(self):
        return [jax.ShapeDtypeStruct(shape, a.dtype) for _, a, shape in self.jobs]

    def scratch(self, extra=0):
        groups = lax.axis_size("shard")
        remote = len(self.jobs) * max(6, groups) + extra
        return [b for bufs in self.bufs for b in bufs] + [
            pltpu.SemaphoreType.DMA((remote,)),
            pltpu.SemaphoreType.DMA((remote,)),
            pltpu.SemaphoreType.DMA((2 * len(self.jobs) + extra + 1,)),
        ]

    def bind(self, rest, srcs, dsts):
        rest = list(rest)
        bufs = []
        for shapes in self.bufs:
            bufs.append([rest.pop(0) for _ in shapes])
        link = Link(rest[:3])
        bound = [kind(link, a, b, c) for (kind, _, _), a, b, c in zip(self.jobs, srcs, dsts, bufs)]
        return link, bound, rest[3:]


def comm_params(number, limit=60):
    return pltpu.CompilerParams(
        vmem_limit_bytes=limit * 2**20, collective_id=number, has_side_effects=True
    )


def exchange_call(jobs, sibling, number, name):
    count = len(jobs.jobs)

    def kernel(*refs):
        srcs, mine = refs[:count], refs[count]
        dsts, other = refs[count + 1 : 2 * count + 1], refs[2 * count + 1]
        link, bound, _ = jobs.bind(refs[2 * count + 2 :], srcs, dsts)
        slot = link.slots(1)
        swap = link.remote(mine, other, slot, slot, link.sibling())
        link.meet_plane()
        swap.start()
        for job in bound:
            job.start()
        for job in bound:
            job.forward()
        for job in bound:
            job.finish()
        swap.wait()

    return pl.pallas_call(
        kernel,
        in_specs=jobs.in_specs() + [pl.BlockSpec(memory_space=pl.ANY)],
        out_specs=[pl.BlockSpec(memory_space=pl.ANY)] * (count + 1),
        out_shape=jobs.out_shapes() + [jax.ShapeDtypeStruct(sibling.shape, sibling.dtype)],
        scratch_shapes=jobs.scratch(1),
        compiler_params=comm_params(number),
        name=name,
    )(*jobs.sources(), sibling)


def qkv_kernel(x_ref, vec_ref, w_ref, bias_ref, h_ref, q_ref, k_ref, v_ref):
    xhat, _ = standardize(x_ref[...].astype(f32))
    h = (xhat * vec_ref[GAIN1] + vec_ref[SHIFT1]).astype(bf16)
    h_ref[...] = h
    z = dot(h, w_ref[...]) + bias_ref[...]
    width = z.shape[1] // 3
    for i, ref in enumerate((q_ref, k_ref, v_ref)):
        ref[:, :width] = z[:, i * width : (i + 1) * width].astype(bf16)
        ref[:, width:] = jnp.zeros((ref.shape[0], ref.shape[1] - width), bf16)


def qkv_call(x, vec, w, bias, wide):
    n, d = x.shape
    out = jax.ShapeDtypeStruct((n, wide), bf16)
    return pl.pallas_call(
        qkv_kernel,
        grid=(n // ROWS,),
        in_specs=[row_block(ROWS, d), whole(vec.shape), whole(w.shape), whole(bias.shape)],
        out_specs=[row_block(ROWS, d)] + [row_block(ROWS, wide)] * 3,
        out_shape=[jax.ShapeDtypeStruct((n, d), bf16), out, out, out],
        compiler_params=params(),
        cost_estimate=cost(2 * n * d * w.shape[1], 4 * n * d + 2 * w.size + 6 * n * wide),
        name="project",
    )(x, vec, w, bias)


def head_window(h):
    start = h * HEAD
    base = (start // 128) * 128
    off = start - base
    lane = lax.broadcasted_iota(jnp.int32, (1, WIN), 1)
    keep = jnp.where((lane >= off) & (lane < off + HEAD), 1.0, 0.0)
    return pl.ds(pl.multiple_of(base, 128), WIN), keep, lane


def put3(x, lane, first, value):
    hi = value.astype(bf16).astype(f32)
    rest = value - hi
    mid = rest.astype(bf16).astype(f32)
    low = rest - mid
    return jnp.where(
        lane == first,
        hi,
        jnp.where(lane == first + 1, mid, jnp.where(lane == first + 2, low, x)),
    )


def key_extra(rows, length):
    lane = lax.broadcasted_iota(jnp.int32, (rows, WIN), 1)
    row = lax.broadcasted_iota(jnp.int32, (rows, WIN), 0)
    dead = jnp.where(row >= length, DEAD, 0.0)
    minus = jnp.where((lane > AUG) & (lane <= AUG + 3), -1.0, 0.0)
    return jnp.where(lane == AUG, dead, minus).astype(bf16)


def attn_fwd_kernel(*refs, bq, jobs):
    count = len(jobs.jobs)
    len_ref, q_ref, k_ref, v_ref = refs[:4]
    o_ref, lse_ref = refs[4 + count : 6 + count]
    acc, kx = refs[6 + 2 * count : 8 + 2 * count]
    link, bound, _ = jobs.bind(refs[8 + 2 * count :], refs[4 : 4 + count], refs[6 + count : 6 + 2 * count])
    h = pl.program_id(0)
    heads = pl.num_programs(0)
    n = q_ref.shape[0]
    width = o_ref.shape[1]

    @pl.when(h == 0)
    def _():
        link.meet_plane()
        for job in bound:
            job.start()
        acc[...] = jnp.zeros_like(acc)
        lse_ref[...] = jnp.zeros_like(lse_ref)
        kx[...] = key_extra(n, len_ref[0])

    @pl.when(h == heads - 2)
    def _():
        for job in bound:
            job.forward()

    win, keep, lane = head_window(h)
    low = keep.astype(bf16)
    q_one = jnp.where(lane == AUG, 1.0, 0.0).astype(bf16)
    v_one = jnp.where((lane >= AUG) & (lane < AUG + 3), 1.0, 0.0).astype(bf16)
    k = k_ref[:, win] * low + kx[...]
    v = v_ref[:, win] * low + v_one
    for i in range(n // bq):
        rows = slice(i * bq, (i + 1) * bq)
        s = dot_nt(q_ref[rows, win] * low + q_one, k)
        peak = jnp.max(s, axis=-1, keepdims=True)
        p = jnp.exp2((s - peak) * SCALE2).astype(bf16)
        o = dot(p, v)
        total = o[:, AUG : AUG + 1]
        acc[rows, win] += o * (keep * (1.0 / total))
        here = lax.broadcasted_iota(jnp.int32, (bq, 128), 1) == h
        lse = peak + jnp.log(total) * (1.0 / SCALE)
        lse_ref[rows, :] = jnp.where(here, lse, lse_ref[rows, :])

    @pl.when(h == heads - 1)
    def _():
        o_ref[:, :width] = acc[:, :width].astype(bf16)
        for job in bound:
            job.finish()


def attn_fwd_call(length, q, k, v, width, heads, jobs, number):
    n, wide = q.shape
    return pl.pallas_call(
        functools.partial(attn_fwd_kernel, bq=256, jobs=jobs),
        grid=(heads,),
        in_specs=[pl.BlockSpec(memory_space=pltpu.SMEM)] + [whole((n, wide))] * 3 + jobs.in_specs(),
        out_specs=[whole((n, width)), whole((n, 128))] + jobs.in_specs(),
        out_shape=[jax.ShapeDtypeStruct((n, width), bf16), jax.ShapeDtypeStruct((n, 128), f32)] + jobs.out_shapes(),
        scratch_shapes=[pltpu.VMEM((n, wide), f32), pltpu.VMEM((n, WIN), bf16)] + jobs.scratch(),
        compiler_params=comm_params(number),
        cost_estimate=cost(4 * n * n * WIN * heads, 8 * n * wide),
        name="attend",
    )(length, q, k, v, *jobs.sources())


def attn_bwd_kernel(*refs, bk, jobs):
    count = len(jobs.jobs)
    len_ref, q_ref, k_ref, v_ref, o_ref, do_ref, lse_ref = refs[:7]
    g_ref, sum_ref = refs[7 + count : 9 + count]
    dq, dk, dv, part, qa, da, kx = refs[9 + 2 * count : 16 + 2 * count]
    link, bound, _ = jobs.bind(refs[16 + 2 * count :], refs[7 : 7 + count], refs[9 + count : 9 + 2 * count])
    chains = [job for job in bound if isinstance(job, Chain)]
    h = pl.program_id(0)
    n = q_ref.shape[0]

    @pl.when(h == 0)
    def _():
        if chains:
            link.meet_all()
        else:
            link.meet_plane()
        for job in bound:
            job.start()
        for ref in (dq, dk, dv):
            ref[...] = jnp.zeros_like(ref)
        kx[...] = key_extra(n, len_ref[0])

    heads = pl.num_programs(0)

    def at_head(number, steps):
        @pl.when(h == number)
        def _():
            for step in steps:
                step()

    if chains:
        at_head(2, [c.inward for c in chains[:1]])
        at_head(4, [c.inward for c in chains[1:]] + [c.across for c in chains[:1]])
    at_head(heads - 2, [job.forward for job in bound] + [c.across for c in chains[1:]])

    win, keep, lane = head_window(h)
    low = keep.astype(bf16)
    v_one = jnp.where((lane >= AUG) & (lane < AUG + 3), 1.0, 0.0).astype(bf16)
    for i in range(n // ROWS):
        rows = slice(i * ROWS, (i + 1) * ROWS)
        here = lax.broadcasted_iota(jnp.int32, (ROWS, 128), 1) == h
        lse = jnp.sum(jnp.where(here, lse_ref[rows, :], 0.0), axis=-1, keepdims=True)
        q = q_ref[rows, win].astype(f32) * keep
        qa[rows, :] = jnp.where(lane == AUG, 1.0, put3(q, lane, AUG + 1, lse)).astype(bf16)
        d = do_ref[rows, win].astype(f32) * keep
        delta = jnp.sum(d * o_ref[rows, win].astype(f32), axis=-1, keepdims=True)
        da[rows, :] = put3(d, lane, AUG, -delta).astype(bf16)
    for i in range(n // bk):
        rows = slice(i * bk, (i + 1) * bk)
        k = k_ref[rows, win] * low + kx[rows, :]
        v = v_ref[rows, win] * low + v_one
        p = jnp.exp2(dot_nt(k, qa[...]) * SCALE2)
        ds = (p * dot_nt(v, da[...])).astype(bf16)
        dv[rows, win] += dot(p.astype(bf16), da[...]) * keep
        dk[rows, win] += dot(ds, qa[...]) * keep
        new = dot_tn(ds, k)
        part[...] = new if i == 0 else part[...] + new
    dq[:, win] += part[...] * keep

    @pl.when(h == heads - 1)
    def _():
        for i, (ref, factor) in enumerate(((dq, SCALE), (dk, SCALE), (dv, 1.0))):
            value = (ref[:, : g_ref.shape[1] // 3] * factor).astype(bf16)
            cols = slice(i * value.shape[1], (i + 1) * value.shape[1])
            g_ref[:, cols] = value
            sum_ref[:, cols] = jnp.sum(value.astype(f32), axis=0, keepdims=True)
        for job in bound:
            job.outward()
        for job in bound:
            job.finish()


def attn_bwd_call(length, q, k, v, o, do, lse, width, heads, jobs, number):
    n, wide = q.shape
    return pl.pallas_call(
        functools.partial(attn_bwd_kernel, bk=256, jobs=jobs),
        grid=(heads,),
        in_specs=[pl.BlockSpec(memory_space=pltpu.SMEM)]
        + [once((n, wide))] * 5
        + [once((n, 128))]
        + jobs.in_specs(),
        out_specs=[whole((n, 3 * width)), whole((1, 3 * width))] + jobs.in_specs(),
        out_shape=[
            jax.ShapeDtypeStruct((n, 3 * width), bf16),
            jax.ShapeDtypeStruct((1, 3 * width), f32),
        ]
        + jobs.out_shapes(),
        scratch_shapes=[pltpu.VMEM((n, wide), f32)] * 3
        + [pltpu.VMEM((n, WIN), f32)]
        + [pltpu.VMEM((n, WIN), bf16)] * 3
        + jobs.scratch(),
        compiler_params=comm_params(number),
        cost_estimate=cost(10 * n * n * WIN * heads, 20 * n * wide),
        name="attend_back",
    )(length, q, k, v, o, do, lse, *jobs.sources())


def middle_kernel(o_ref, w_ref, x_ref, vec_ref, mid_ref, h_ref, owide_ref, mine, other, *sems):
    link = Link(sems)
    n = x_ref.shape[0]
    width = o_ref.shape[1]
    link.meet_core()

    def swap(i):
        rows = pl.ds(pl.multiple_of(i * ROWS, ROWS), ROWS)
        return rows, link.remote(mine.at[rows], other.at[rows], i, i, link.sibling())

    def project(i, carry):
        rows, copy = swap(i)
        mine[rows, :] = dot(o_ref[rows, :], w_ref[...]).astype(bf16)
        copy.start()
        return carry

    def norm(i, carry):
        rows, copy = swap(i)
        copy.wait_recv()
        mid = x_ref[rows, :].astype(f32) + (
            mine[rows, :].astype(f32) + other[rows, :].astype(f32) + vec_ref[OBIAS]
        )
        mid_ref[rows, :] = mid
        xhat, _ = standardize(mid)
        h_ref[rows, :] = (xhat * vec_ref[GAIN2] + vec_ref[SHIFT2]).astype(bf16)
        return carry

    lax.fori_loop(0, n // ROWS, project, 0)
    owide_ref[:, :width] = o_ref[...]
    owide_ref[:, width:] = jnp.zeros((n, owide_ref.shape[1] - width), bf16)
    lax.fori_loop(0, n // ROWS, norm, 0)
    for i in range(n // ROWS):
        swap(i)[1].wait_send()


def middle_call(o, w, x, vec, wide, number):
    n, d = x.shape
    sems = [pltpu.SemaphoreType.DMA((n // ROWS,))] * 2 + [pltpu.SemaphoreType.DMA((1,))]
    vmem = pl.BlockSpec(memory_space=pltpu.VMEM)
    return pl.pallas_call(
        middle_kernel,
        in_specs=[vmem] * 4,
        out_specs=[vmem] * 3,
        out_shape=[
            jax.ShapeDtypeStruct((n, d), f32),
            jax.ShapeDtypeStruct((n, d), bf16),
            jax.ShapeDtypeStruct((n, wide), bf16),
        ],
        scratch_shapes=[pltpu.VMEM((n, d), bf16)] * 2 + sems,
        compiler_params=comm_params(number),
        cost_estimate=cost(2 * n * w.size, 14 * n * d),
        name="middle",
    )(o, w, x, vec)


def ffn_kernel(*refs, chained, last, mc, jobs):
    count = len(jobs.jobs)
    h_ref, dz_ref, up_ref, ub_ref, dn_ref = refs[:5]
    refs = refs[5:]
    if chained:
        old_out, old_dh = refs[:2]
        refs = refs[2:]
    srcs, refs = refs[:count], refs[count:]
    out_ref, dh_ref, dup_ref, ddn_ref, dub_ref = refs[:5]
    dsts, refs = refs[5 : 5 + count], refs[5 + count :]
    ht, act, grad = refs[:3]
    acc, dh = refs[3:5] if last else (out_ref, dh_ref)
    refs = refs[5:] if last else refs[3:]
    link, bound, refs = jobs.bind(refs, srcs, dsts)
    t = pl.program_id(0)
    tiles = pl.num_programs(0)
    n = h_ref.shape[0]

    @pl.when(t == 0)
    def _():
        link.meet_plane()
        for job in bound:
            job.start()
        if chained:
            sem = refs[0]
            copies = [
                pltpu.make_async_copy(src, dst, sem.at[i])
                for i, (src, dst) in enumerate(((old_out, acc), (old_dh, dh)))
            ]
            for c in copies:
                c.start()
            ht[...] = h_ref[...].T
            for c in copies:
                c.wait()
        else:
            ht[...] = h_ref[...].T
            acc[...] = jnp.zeros_like(acc)
            dh[...] = jnp.zeros_like(dh)

    @pl.when(t == tiles - 1)
    def _():
        for job in bound:
            job.forward()

    def step(i, carry):
        rows = pl.ds(pl.multiple_of(i * mc, mc), mc)
        g, slope = gelu_pair(dot(h_ref[rows, :], up_ref[...]) + ub_ref[...])
        g = g.astype(bf16)
        da = (dot_nt(dz_ref[rows, :], dn_ref[...]) * slope).astype(bf16)
        act[rows, :] = g
        grad[rows, :] = da
        acc[rows, :] += dot(g, dn_ref[...])
        dh[rows, :] += dot_nt(da, up_ref[...])
        return carry

    lax.fori_loop(0, n // mc, step, 0)
    dub_ref[...] = jnp.sum(grad[...].astype(f32), axis=0, keepdims=True)
    dup_ref[...] = dot(ht[...], grad[...]).astype(bf16)
    ddn_ref[...] = dot_tn(act[...], dz_ref[...]).astype(bf16)

    @pl.when(t == tiles - 1)
    def _():
        if last:
            out_ref[...] = acc[...].astype(out_ref.dtype)
            dh_ref[...] = dh[...].astype(dh_ref.dtype)
        for job in bound:
            job.finish()


def ffn_call(h, dz, up, bias, down, old, last, jobs, number, name):
    n, d = h.shape
    hidden = up.shape[1]
    bt = FFN_TILE
    out = jax.ShapeDtypeStruct((n, d), bf16 if last else f32)
    chained = old is not None
    kept = once((n, d))
    return pl.pallas_call(
        functools.partial(ffn_kernel, chained=chained, last=last, mc=FFN_ROWS, jobs=jobs),
        grid=(hidden // bt,),
        in_specs=[
            kept,
            kept,
            pl.BlockSpec((d, bt), lambda t: (0, t)),
            pl.BlockSpec((1, bt), lambda t: (0, t)),
            pl.BlockSpec((bt, d), lambda t: (t, 0)),
        ]
        + ([pl.BlockSpec(memory_space=pl.ANY)] * 2 if chained else [])
        + jobs.in_specs(),
        out_specs=[
            kept,
            kept,
            pl.BlockSpec((d, bt), lambda t: (0, t)),
            pl.BlockSpec((bt, d), lambda t: (t, 0)),
            pl.BlockSpec((1, bt), lambda t: (0, t)),
        ]
        + jobs.in_specs(),
        out_shape=[
            out,
            out,
            jax.ShapeDtypeStruct((d, hidden), bf16),
            jax.ShapeDtypeStruct((hidden, d), bf16),
            jax.ShapeDtypeStruct((1, hidden), f32),
        ]
        + jobs.out_shapes(),
        scratch_shapes=[pltpu.VMEM((d, n), bf16)]
        + [pltpu.VMEM((n, bt), bf16)] * 2
        + ([pltpu.VMEM((n, d), f32)] * 2 if last else [])
        + jobs.scratch()
        + ([pltpu.SemaphoreType.DMA((2,))] if chained else []),
        compiler_params=comm_params(number),
        cost_estimate=cost(12 * n * d * hidden, 8 * d * hidden + 12 * n * d),
        name=name,
    )(h, dz, up, bias, down, *(old if chained else ()), *jobs.sources())


def second_back_kernel(
    mid_ref, dh_ref, out_ref, dz_ref, vec_ref, w_ref, o_ref, dh_any, out_any,
    dmid_ref, do_ref, dw_ref, sums_ref, layer_ref,
    acc, dh_other, out_other, *sems
):
    i = pl.program_id(0)
    blocks = pl.num_programs(0)
    link = Link(sems)
    half = layer_ref.shape[0] // ROWS
    width = w_ref.shape[0]

    def swap_dh(j):
        rows = pl.ds(pl.multiple_of(j * ROWS, ROWS), ROWS)
        return link.remote(dh_any.at[rows], dh_other.at[rows], j, j, link.sibling())

    def swap_out(j):
        src = pl.ds(pl.multiple_of(((1 - link.core) * half + j) * ROWS, ROWS), ROWS)
        dst = pl.ds(pl.multiple_of(j * ROWS, ROWS), ROWS)
        slot = 2 * half + j
        return link.remote(out_any.at[src], out_other.at[dst], slot, slot, link.sibling())

    @pl.when(i == 0)
    def _():
        link.meet_core()
        for j in range(2 * half):
            swap_dh(j).start()
        for j in range(half):
            swap_out(j).start()
        acc[...] = jnp.zeros_like(acc)
        sums_ref[...] = jnp.zeros_like(sums_ref)

    mid = mid_ref[...]
    xhat, inv = standardize(mid)
    swap_dh(i).wait_recv()
    rows = pl.ds(pl.multiple_of(i * ROWS, ROWS), ROWS)
    dh = dh_ref[...].astype(f32) + dh_other[rows, :].astype(f32)
    dx = dh * vec_ref[GAIN2]
    dz = dz_ref[...].astype(f32)
    dmid = dz + inv * (
        dx - jnp.mean(dx, axis=-1, keepdims=True) - xhat * jnp.mean(dx * xhat, axis=-1, keepdims=True)
    )
    dmid_ref[...] = dmid
    dy = dmid.astype(bf16)
    do_ref[:, :width] = dot_nt(dy, w_ref[...]).astype(bf16)
    do_ref[:, width:] = jnp.zeros((do_ref.shape[0], do_ref.shape[1] - width), bf16)
    acc[...] += dot_tn(o_ref[...], dy)
    for row, value in enumerate((dh * xhat, dh, dy.astype(f32), dz)):
        sums_ref[row : row + 1, :] += jnp.sum(value, axis=0, keepdims=True)

    j = i - link.core * half

    @pl.when((j >= 0) & (j < half))
    def _():
        swap_out(j).wait_recv()
        here = pl.ds(pl.multiple_of(j * ROWS, ROWS), ROWS)
        layer_ref[here, :] = (
            mid + (out_ref[...].astype(f32) + out_other[here, :].astype(f32) + vec_ref[DBIAS])
        ).astype(bf16)

    @pl.when(i == blocks - 1)
    def _():
        dw_ref[...] = acc[...].astype(bf16)
        for j in range(2 * half):
            swap_dh(j).wait_send()
        for j in range(half):
            swap_out(j).wait_send()


def second_back_call(mid, dh, out, dz, vec, w, o, wide, number):
    n, d = mid.shape
    width = w.shape[0]
    block = row_block(ROWS, d)
    count = 3 * n // ROWS // 2
    return pl.pallas_call(
        second_back_kernel,
        grid=(n // ROWS,),
        in_specs=[block] * 4
        + [whole(vec.shape), whole(w.shape), row_block(ROWS, width)]
        + [pl.BlockSpec(memory_space=pl.ANY)] * 2,
        out_specs=[block, row_block(ROWS, wide), whole((width, d)), whole((8, d)), whole((n // 2, d))],
        out_shape=[
            jax.ShapeDtypeStruct((n, d), f32),
            jax.ShapeDtypeStruct((n, wide), bf16),
            jax.ShapeDtypeStruct((width, d), bf16),
            jax.ShapeDtypeStruct((8, d), f32),
            jax.ShapeDtypeStruct((n // 2, d), bf16),
        ],
        scratch_shapes=[
            pltpu.VMEM((width, d), f32),
            pltpu.VMEM((n, d), bf16),
            pltpu.VMEM((n // 2, d), bf16),
            pltpu.SemaphoreType.DMA((count,)),
            pltpu.SemaphoreType.DMA((count,)),
            pltpu.SemaphoreType.DMA((1,)),
        ],
        compiler_params=comm_params(number),
        cost_estimate=cost(4 * n * d * width, 14 * n * d),
        name="second_back",
    )(mid, dh, out, dz, vec, w, o, dh, out)


def dw_kernel(h_ref, g_ref, out_ref):
    out_ref[...] = dot_tn(h_ref[...], g_ref[...]).astype(bf16)


def dw_call(h, grads):
    n, d = h.shape
    cols = grads.shape[1]
    return pl.pallas_call(
        dw_kernel,
        grid=(d // 256,),
        in_specs=[pl.BlockSpec((n, 256), lambda i: (0, i)), whole((n, cols))],
        out_specs=row_block(256, cols),
        out_shape=jax.ShapeDtypeStruct((d, cols), bf16),
        compiler_params=params(),
        cost_estimate=cost(2 * n * d * cols, 2 * (n * d + n * cols + d * cols)),
        name="project_grad",
    )(h, grads)


def first_back_kernel(*refs, jobs):
    count = len(jobs.jobs)
    g_ref, w_ref, vec_ref, x_any, dmid_any = refs[:5]
    dx_ref, sums_ref = refs[5 + count : 7 + count]
    x, dmid, mine, other = refs[7 + 2 * count : 11 + 2 * count]
    link, bound, _ = jobs.bind(refs[11 + 2 * count :], refs[5 : 5 + count], refs[7 + count : 7 + 2 * count])
    size = dx_ref.shape[0]
    half = size // ROWS
    base = link.slots(half)
    keep = link.local_slots(2)
    own = pl.ds(pl.multiple_of(link.core * size, size), size)
    loads = [link.here(x_any.at[own], x, keep), link.here(dmid_any.at[own], dmid, keep + 1)]
    for c in loads:
        c.start()
    link.meet_plane()
    for job in bound:
        job.start()

    def product(j):
        rows = pl.ds(pl.multiple_of(j * ROWS, ROWS), ROWS)
        return dot_nt(g_ref[rows, :], w_ref[...])

    def swap(j):
        rows = pl.ds(pl.multiple_of(j * ROWS, ROWS), ROWS)
        return rows, link.remote(mine.at[rows], other.at[rows], base + j, base + j, link.sibling())

    def send(j, carry):
        rows, copy = swap(j)
        mine[rows, :] = product((1 - link.core) * half + j).astype(bf16)
        copy.start()
        return carry

    def norm(j, carry):
        rows, copy = swap(j)
        part = product(link.core * half + j)
        copy.wait_recv()
        xhat, inv = standardize(x[rows, :].astype(f32))
        dh = part + other[rows, :].astype(f32)
        dx = dh * vec_ref[GAIN1]
        dx_ref[rows, :] = (
            dmid[rows, :]
            + inv
            * (dx - jnp.mean(dx, axis=-1, keepdims=True) - xhat * jnp.mean(dx * xhat, axis=-1, keepdims=True))
        ).astype(bf16)
        for row, value in enumerate((dh * xhat, dh)):
            sums_ref[row : row + 1, :] += jnp.sum(value, axis=0, keepdims=True)
        return carry

    sums_ref[...] = jnp.zeros_like(sums_ref)
    lax.fori_loop(0, half, send, 0)
    for c in loads:
        c.wait()
    lax.fori_loop(0, half, norm, 0)
    for j in range(half):
        swap(j)[1].wait_send()
    for job in bound:
        job.forward()
    for job in bound:
        job.finish()


def first_back_call(grads, w, vec, x, dmid, jobs, number):
    n, d = x.shape
    size = n // 2
    vmem = pl.BlockSpec(memory_space=pltpu.VMEM)
    hbm = pl.BlockSpec(memory_space=pl.ANY)
    return pl.pallas_call(
        functools.partial(first_back_kernel, jobs=jobs),
        in_specs=[vmem] * 3 + [hbm] * 2 + jobs.in_specs(),
        out_specs=[vmem] * 2 + jobs.in_specs(),
        out_shape=[jax.ShapeDtypeStruct((size, d), bf16), jax.ShapeDtypeStruct((8, d), f32)] + jobs.out_shapes(),
        scratch_shapes=[
            pltpu.VMEM((size, d), bf16),
            pltpu.VMEM((size, d), f32),
            pltpu.VMEM((size, d), bf16),
            pltpu.VMEM((size, d), bf16),
        ]
        + jobs.scratch(size // ROWS),
        compiler_params=comm_params(number),
        cost_estimate=cost(2 * n * w.size, 12 * n * d),
        name="first_back",
    )(grads, w, vec, x, dmid, *jobs.sources())


class Blocks:
    def __init__(self, ref, rows):
        self.ref, self.rows = ref, rows

    @property
    def at(self):
        return self

    def __getitem__(self, index):
        block, part = index
        first = pl.multiple_of(block * self.rows + part.start, 16)
        return self.ref.at[pl.ds(first, part.size)]


def back_kernel(*refs, jobs):
    count = len(jobs.jobs)
    g_ref, w_ref, vec_ref, h_ref, x_any, dmid_any = refs[:6]
    dx_ref, sums_ref, own_ref = refs[6 + count : 9 + count]
    x, dmid, mine, other, dw, left = refs[9 + 2 * count : 15 + 2 * count]
    bufs = refs[15 + 2 * count : 19 + 2 * count]
    link, chains, _ = jobs.bind(refs[19 + 2 * count :], refs[6 : 6 + count], refs[9 + count : 9 + 2 * count])
    size, d = dx_ref.shape
    half = size // ROWS
    owned = own_ref.shape[0]
    reduce = Reduce(link, Blocks(dw, owned), left, bufs)
    base = link.slots(half)
    keep = link.local_slots(2)
    own = pl.ds(pl.multiple_of(link.core * size, size), size)
    loads = [link.here(x_any.at[own], x, keep), link.here(dmid_any.at[own], dmid, keep + 1)]
    for c in loads:
        c.start()
    link.meet_all()
    for job in chains:
        job.start()

    def weight(i, carry):
        part = pl.ds(pl.multiple_of(i * 256, 256), 256)
        dw[part, :] = dot_tn(h_ref[:, part], g_ref[...]).astype(bf16)
        return carry

    lax.fori_loop(0, d // 256, weight, 0)
    reduce.start()

    def product(j):
        rows = pl.ds(pl.multiple_of(j * ROWS, ROWS), ROWS)
        return dot_nt(g_ref[rows, :], w_ref[...])

    def swap(j):
        rows = pl.ds(pl.multiple_of(j * ROWS, ROWS), ROWS)
        return rows, link.remote(mine.at[rows], other.at[rows], base + j, base + j, link.sibling())

    def send(j, carry):
        rows, copy = swap(j)
        mine[rows, :] = product((1 - link.core) * half + j).astype(bf16)
        copy.start()
        return carry

    def norm(j, carry):
        rows, copy = swap(j)
        part = product(link.core * half + j)
        copy.wait_recv()
        xhat, inv = standardize(x[rows, :].astype(f32))
        dh = part + other[rows, :].astype(f32)
        dx = dh * vec_ref[GAIN1]
        dx_ref[rows, :] = (
            dmid[rows, :]
            + inv
            * (dx - jnp.mean(dx, axis=-1, keepdims=True) - xhat * jnp.mean(dx * xhat, axis=-1, keepdims=True))
        ).astype(bf16)
        for row, value in enumerate((dh * xhat, dh)):
            sums_ref[row : row + 1, :] += jnp.sum(value, axis=0, keepdims=True)
        return carry

    sums_ref[...] = jnp.zeros_like(sums_ref)
    lax.fori_loop(0, half, send, 0)
    for c in loads:
        c.wait()
    chains[0].inward()
    lax.fori_loop(0, half, norm, 0)
    for j in range(half):
        swap(j)[1].wait_send()
    reduce.forward()
    for i in range(1, len(chains) + 1):
        if i < len(chains):
            chains[i].inward()
        chains[i - 1].across()
    reduce.finish()
    cut = owned // 2
    for part in range(2):
        first = pl.multiple_of(link.shard * owned + part * cut, 16)
        block = dw[pl.ds(first, cut), :].astype(f32)
        own_ref[part * cut : (part + 1) * cut, :] = (
            block + left[2 * part].astype(f32) + left[2 * part + 1].astype(f32)
        ).astype(bf16)
    for job in chains:
        job.outward()
    for job in chains:
        job.finish()


def back_call(grads, w, vec, h, x, dmid, jobs, number):
    n, d = x.shape
    size = n // 2
    cols = grads.shape[1]
    owned = d // lax.axis_size("shard")
    part = pltpu.VMEM((owned // 2, cols), bf16)
    vmem = pl.BlockSpec(memory_space=pltpu.VMEM)
    hbm = pl.BlockSpec(memory_space=pl.ANY)
    return pl.pallas_call(
        functools.partial(back_kernel, jobs=jobs),
        in_specs=[vmem] * 4 + [hbm] * 2 + jobs.in_specs(),
        out_specs=[vmem] * 3 + jobs.in_specs(),
        out_shape=[
            jax.ShapeDtypeStruct((size, d), bf16),
            jax.ShapeDtypeStruct((8, d), f32),
            jax.ShapeDtypeStruct((owned, cols), bf16),
        ]
        + jobs.out_shapes(),
        scratch_shapes=[
            pltpu.VMEM((size, d), bf16),
            pltpu.VMEM((size, d), f32),
            pltpu.VMEM((size, d), bf16),
            pltpu.VMEM((size, d), bf16),
            pltpu.VMEM((d, cols), bf16),
            pltpu.VMEM((4, owned // 2, cols), bf16),
        ]
        + [part] * 4
        + jobs.scratch(size // ROWS + 8),
        compiler_params=comm_params(number, 62),
        cost_estimate=cost(4 * n * w.size, 20 * n * d),
        name="back",
    )(grads, w, vec, h, x, dmid, *jobs.sources())


def finish_kernel(*refs, jobs, parts):
    count = len(jobs.jobs)
    early_ref, late_ref, own_any = refs[:3]
    small_ref, both_any = refs[3 + count : 5 + count]
    rest = refs[5 + 2 * count :]
    total, came, chain_bufs, rest = rest[0], rest[1], rest[2:5], rest[5:]
    own_bufs, rest = rest[: 3 * parts], rest[3 * parts :]
    link, bound, _ = jobs.bind(rest, refs[3 : 3 + count], refs[5 + count : 5 + 2 * count])
    size = own_any.shape[0] // parts
    chains = []
    for i in range(parts):
        rows = pl.ds(i * size, size)
        chains.append(Chain(link, own_any.at[rows], both_any.at[:, rows], own_bufs[3 * i : 3 * i + 3]))
    base = link.slots(3)
    peers = [link.sibling()] + [(link.rep, link.shard ^ bit) for bit in (1, 2)]
    swaps = [link.remote(total, came.at[i], base + i, base + i, to) for i, to in enumerate(peers)]
    small = Chain(link, total, small_ref, chain_bufs)
    first = early_ref.shape[0]
    total[:first, :] = early_ref[...]
    total[first:, :] = late_ref[...]
    link.meet_all()
    swaps[0].start()
    for c in chains:
        c.start()
    for job in bound:
        job.start()
    for i in range(parts + 1):
        if i < 3:
            swaps[i].wait()
            total[...] += came[i]
            if i < 2:
                swaps[i + 1].start()
            else:
                small.start()
        if i < parts:
            chains[i].inward()
        if i:
            chains[i - 1].across()
        if i == 3:
            small.inward()
    small.across()
    for c in chains:
        c.outward()
    small.outward()
    for c in chains:
        c.finish()
    small.finish()
    for job in bound:
        job.finish()


def finish_call(early, late, own, jobs, number):
    rows = early.shape[0] + late.shape[0]
    d = early.shape[1]
    parts = 4
    small = pltpu.VMEM((rows, d), f32)
    vmem = pl.BlockSpec(memory_space=pltpu.VMEM)
    hbm = pl.BlockSpec(memory_space=pl.ANY)
    return pl.pallas_call(
        functools.partial(finish_kernel, jobs=jobs, parts=parts),
        in_specs=[vmem] * 2 + [hbm] + jobs.in_specs(),
        out_specs=[vmem, hbm] + jobs.in_specs(),
        out_shape=[
            jax.ShapeDtypeStruct((2, rows, d), f32),
            jax.ShapeDtypeStruct((2,) + own.shape, bf16),
        ]
        + jobs.out_shapes(),
        scratch_shapes=[small, pltpu.VMEM((3, rows, d), f32)]
        + [small] * 3
        + [pltpu.VMEM((own.shape[0] // parts, own.shape[1]), bf16)] * (3 * parts)
        + jobs.scratch(6 * parts + 8),
        compiler_params=comm_params(number),
        name="finish",
    )(early, late, own, *jobs.sources())


def place_up_kernel(a_ref, b_ref, out_ref):
    first, second = a_ref.shape[2], b_ref.shape[2]
    for c in range(2):
        base = c * (first + second)
        out_ref[:, base : base + first] = a_ref[c].astype(f32)
        out_ref[:, base + first : base + first + second] = b_ref[c].astype(f32)


def place_up_call(a, b, groups):
    rows = a.shape[1]
    first, second = a.shape[2] // groups, b.shape[2] // groups
    return pl.pallas_call(
        place_up_kernel,
        grid=(groups,),
        in_specs=[
            pl.BlockSpec((2, rows, first), lambda i: (0, 0, i)),
            pl.BlockSpec((2, rows, second), lambda i: (0, 0, i)),
        ],
        out_specs=pl.BlockSpec((rows, 2 * (first + second)), lambda i: (0, i)),
        out_shape=jax.ShapeDtypeStruct((rows, 2 * (first + second) * groups), f32),
        compiler_params=params(),
        name="place_up",
    )(a, b)


def place_down_kernel(a_ref, b_ref, out_ref):
    first, second = a_ref.shape[1], b_ref.shape[1]
    for c in range(2):
        base = c * (first + second)
        out_ref[base : base + first, :] = a_ref[c].astype(f32)
        out_ref[base + first : base + first + second, :] = b_ref[c].astype(f32)


def place_down_call(a, b):
    d = a.shape[2]
    first, second = a.shape[1], b.shape[1]
    return pl.pallas_call(
        place_down_kernel,
        grid=(d // 256,),
        in_specs=[
            pl.BlockSpec((2, first, 256), lambda i: (0, 0, i)),
            pl.BlockSpec((2, second, 256), lambda i: (0, 0, i)),
        ],
        out_specs=pl.BlockSpec((2 * (first + second), 256), lambda i: (0, i)),
        out_shape=jax.ShapeDtypeStruct((2 * (first + second), d), f32),
        compiler_params=params(),
        name="place_down",
    )(a, b)


def place_qkv_kernel(in_ref, *outs, groups):
    rows = in_ref.shape[1]
    width = in_ref.shape[2] // 3
    part = width // groups
    row = lax.broadcasted_iota(jnp.int32, (width, 2 * width), 0)
    ahead = lax.broadcasted_iota(jnp.int32, (width, 2 * width), 1) - row
    places = []
    for c in range(2):
        place = jnp.zeros((width, 2 * width), f32)
        for s in range(groups):
            here = (row >= s * part) & (row < (s + 1) * part) & (ahead == (s + c) * part)
            place = jnp.where(here, 1.0, place)
        places.append(place.astype(bf16))
    for i, out in enumerate(outs):
        cols = slice(i * width, (i + 1) * width)
        out[...] = dot(in_ref[0, :, cols], places[0]) + dot(in_ref[1, :, cols], places[1])


def place_qkv_call(both, groups):
    _, rows, cols = both.shape
    vmem = pl.BlockSpec(memory_space=pltpu.VMEM)
    return pl.pallas_call(
        functools.partial(place_qkv_kernel, groups=groups),
        in_specs=[vmem],
        out_specs=[vmem] * 3,
        out_shape=[jax.ShapeDtypeStruct((rows, 2 * cols // 3), f32)] * 3,
        compiler_params=params(),
        name="place_qkv",
    )(both)


def own_sum(blocks, others):
    shard = lax.axis_index("shard")
    total = lax.dynamic_index_in_dim(blocks, shard, 0, keepdims=False).astype(f32)
    for i in range(others.shape[0]):
        total = total + others[i].astype(f32)
    return total.astype(bf16)


def own_sum2(blocks, left):
    shard = lax.axis_index("shard")
    block = lax.dynamic_index_in_dim(blocks, shard, 0, keepdims=False).astype(f32)
    cut = block.shape[0] // 2
    left = left.astype(f32)
    return jnp.concatenate(
        [block[:cut] + left[0] + left[1], block[cut:] + left[2] + left[3]], axis=0
    ).astype(bf16)


def over_reps(own):
    planes = lax.axis_size("rep") // 2
    sums = lax.psum_scatter(
        own,
        "rep",
        scatter_dimension=0,
        tiled=True,
        axis_index_groups=[[2 * z + c for z in range(planes)] for c in range(2)],
    )
    both = lax.all_gather(sums, "rep", axis=0)
    rows, cols = sums.shape
    return both.reshape(planes, 2, rows, cols).transpose(1, 0, 2, 3).reshape(2, planes * rows, cols)


def on_device(
    tokens,
    lengths,
    cotangent,
    first_gain,
    first_shift,
    query_weight,
    query_bias,
    key_weight,
    value_weight,
    value_bias,
    out_weight,
    out_bias,
    second_gain,
    second_shift,
    up_weight,
    up_bias,
    down_weight,
    down_bias,
):
    g = lax.axis_size("shard")
    shard = lax.axis_index("shard")
    core = lax.rem(lax.axis_index("rep"), 2)
    cl, rows, d = tokens.shape
    n = 2 * cl * rows
    ff = up_weight.shape[1]
    own_d = d // g
    own_f = ff // g
    attn_cols = own_d // 2
    ffn_cols = own_f // 2
    width = d // 2
    heads = width // HEAD
    wide = pl.cdiv(width, 128) * 128 + 128
    first_n = ffn_cols * 2 // 5
    pieces = ((0, first_n), (first_n, ffn_cols))

    def core_cols(w, size, a, b):
        def of(c):
            return jnp.concatenate([w[:, (2 * s + c) * size + a : (2 * s + c) * size + b] for s in range(g)], axis=1)

        return jnp.where(core == 0, of(0), of(1))

    def core_rows(w):
        half = w.shape[0] // 2
        return lax.dynamic_slice_in_dim(w, core * half, half, 0)

    vectors = (first_gain, first_shift, query_bias, value_bias, out_bias, second_gain, second_shift, down_bias)
    lens = jnp.pad(lengths.astype(f32), (0, own_d - cl)).reshape(1, own_d)
    small = jnp.concatenate(
        [jnp.stack(vectors).astype(f32), lens, up_bias.astype(f32).reshape(-1, own_d)], axis=0
    )
    small = jnp.pad(small, ((0, 16 - small.shape[0]), (0, -own_d % 128)))
    qkv_own = jnp.concatenate(
        [core_cols(w, attn_cols, 0, attn_cols) for w in (query_weight, key_weight, value_weight)], axis=1
    )
    jobs = Jobs(
        (ToClip, tokens, (n, d)),
        (Gather, qkv_own, (g,) + qkv_own.shape),
        (Gather, small, (g,) + small.shape),
    )
    x, w_qkv, smalls, other_small = exchange_call(jobs, small, 0, "first_exchange")
    w_qkv = w_qkv.reshape(d, 3 * width)
    vec = smalls[:, :, :own_d].transpose(1, 0, 2).reshape(16, d)
    near = lax.div(shard, cl) == core
    lens = jnp.where(near, small[LENGTHS], other_small[LENGTHS])[0]
    length = lens[lax.rem(shard, cl)].astype(jnp.int32).reshape(1)

    def bias_cols(b):
        return lax.dynamic_index_in_dim(vec[b].reshape(1, g, 2, attn_cols), core, 2).reshape(1, width)

    bias = jnp.concatenate([bias_cols(QBIAS), jnp.zeros((1, width), f32), bias_cols(VBIAS)], axis=1)
    ubias = lax.dynamic_index_in_dim(
        vec[UBIAS : UBIAS + own_f // own_d].reshape(-1, g, own_d).transpose(1, 0, 2).reshape(g, 2, ffn_cols),
        core,
        1,
        keepdims=False,
    )
    ups = [core_cols(up_weight, ffn_cols, a, b) for a, b in pieces]
    down_own = core_rows(down_weight)
    downs = [down_own[a:b] for a, b in pieces]
    out_own = core_rows(out_weight)

    def gathered(a):
        return (Gather, a, (g,) + a.shape)

    h1, q, k, v = qkv_call(x, vec, w_qkv, bias, wide)
    jobs = Jobs(gathered(out_own), (ToClip, cotangent, (n, d)), gathered(ups[0]), gathered(downs[0]))
    o, lse, w_out, cot, up, down = attn_fwd_call(length, q, k, v, width, heads, jobs, 1)
    w_out = w_out.reshape(width, d)
    mid, h2, o_wide = middle_call(o, w_out, x, vec, wide, 2)
    live = jnp.arange(n, dtype=jnp.int32)[:, None] < length
    dz = jnp.where(live, cot, jnp.zeros_like(cot))

    def hidden_bias(piece):
        return ubias[:, piece[0] : piece[1]].reshape(1, -1)

    fast = g == 4 and lax.axis_size("rep") == 8

    def to_owners(a):
        if fast:
            return (Reduce, a, (4, a.shape[1] // 2, a.shape[2]))
        return (Owners, a, (g - 1,) + a.shape[1:])

    def owned(a, came):
        return own_sum2(a, came) if fast else own_sum(a, came)

    def chained(a):
        return (Chain, a, (2,) + a.shape)

    jobs = Jobs(gathered(ups[1]), gathered(downs[1]))
    out, dh2, dup0, ddn0, dub0, up1, down1 = ffn_call(
        h2, dz, up.reshape(d, -1), hidden_bias(pieces[0]), down.reshape(-1, d), None, False, jobs, 3, "hidden0"
    )
    dup0, ddn0 = dup0.reshape(g, own_d, -1), ddn0.reshape(g, -1, d)
    jobs = Jobs(to_owners(dup0), to_owners(ddn0))
    out, dh2, dup1, ddn1, dub1, dup0_in, ddn0_in = ffn_call(
        h2, dz, up1.reshape(d, -1), hidden_bias(pieces[1]), down1.reshape(-1, d), (out, dh2), True, jobs, 4, "hidden1"
    )
    dup1, ddn1 = dup1.reshape(g, own_d, -1), ddn1.reshape(g, -1, d)
    up0_own, down0_own = owned(dup0, dup0_in), owned(ddn0, ddn0_in)

    dmid, do, dwo, sums2, layer_own = second_back_call(mid, dh2, out, dz, vec, w_out, o, wide, 5)
    dwo = dwo.reshape(g, -1, d)

    jobs = [to_owners(dup1), to_owners(ddn1), to_owners(dwo), (FromClip, layer_own, (cl, rows, d))]
    if fast:
        jobs += [chained(up0_own), chained(down0_own)]
    grads, bias_sums, dup1_in, ddn1_in, dwo_in, layer_out, *sums0 = attn_bwd_call(
        length, q, k, v, o_wide, do, lse, width, heads, Jobs(*jobs), 6
    )
    up1_own, down1_own, out_own_grad = owned(dup1, dup1_in), owned(ddn1, ddn1_in), owned(dwo, dwo_in)

    def spread(v, size):
        out = jnp.zeros((g, 2, size), f32)
        return lax.dynamic_update_index_in_dim(out, v.reshape(g, size), core, 1)

    ub_sums = jnp.concatenate([dub0.reshape(g, -1), dub1.reshape(g, -1)], axis=1)
    early = jnp.concatenate(
        [
            spread(bias_sums[0, :width], attn_cols).reshape(1, d),
            spread(bias_sums[0, 2 * width :], attn_cols).reshape(1, d),
            sums2[:4] * 0.5,
            spread(ub_sums, ffn_cols).reshape(-1, d),
        ],
        axis=0,
    )
    early = jnp.pad(early, ((0, -early.shape[0] % 8), (0, 0)))

    def to_halves(a):
        return [a[i * a.shape[0] // 2 : (i + 1) * a.shape[0] // 2] for i in range(2)]

    if fast:
        pieces_own = to_halves(up1_own) + to_halves(down1_own) + [out_own_grad]
        jobs = Jobs(*[chained(a) for a in pieces_own])
        dx, sums1, qkv_own_grad, *sums = back_call(grads, w_qkv, vec, h1, x, dmid, jobs, 7)
        jobs = Jobs((FromClip, dx, (cl, rows, d)))
        smalls, qkv_all, tokens_grad = finish_call(early, sums1, qkv_own_grad, jobs, 8)
        up_grad = place_up_call(sums0[0], jnp.concatenate(sums[:2], axis=1), g)
        down_grad = place_down_call(sums0[1], jnp.concatenate(sums[2:4], axis=1))
        out_grad = sums[4].reshape(own_d, d).astype(f32)
        qkv_grads = place_qkv_call(qkv_all, g)
        smalls = lax.dynamic_index_in_dim(smalls, core, 0, keepdims=False)
    else:
        dwqkv = dw_call(h1, grads).reshape(g, own_d, 3 * width)
        jobs = Jobs(to_owners(dwqkv))
        dx, sums1, dwqkv_in = first_back_call(grads, w_qkv, vec, x, dmid, jobs, 7)
        jobs = Jobs((FromClip, dx, (cl, rows, d)))
        tokens_grad, _ = exchange_call(jobs, sums1, 8, "last_exchange")
        ups_all = [over_reps(a).reshape(2, own_d, g, -1) for a in (up0_own, up1_own)]
        up_grad = jnp.concatenate(ups_all, axis=3).transpose(1, 2, 0, 3).reshape(own_d, ff).astype(f32)
        downs_all = [over_reps(a) for a in (down0_own, down1_own)]
        down_grad = jnp.concatenate(downs_all, axis=1).reshape(own_f, d).astype(f32)
        out_grad = over_reps(out_own_grad).reshape(own_d, d).astype(f32)
        qkv_all = over_reps(owned(dwqkv, dwqkv_in)).reshape(2, own_d, 3, g, attn_cols)
        qkv_grads = [qkv_all[:, :, i].transpose(1, 2, 0, 3).reshape(own_d, d).astype(f32) for i in range(3)]
        smalls = lax.psum(jnp.concatenate([early, sums1], axis=0), ("rep", "shard"))

    mine = lax.dynamic_slice_in_dim(smalls, shard * own_d, own_d, 1)
    s_qb, s_vb, s_gain2, s_shift2, s_ob, s_db = [mine[i] for i in range(6)]
    s_gain1, s_shift1 = [mine[early.shape[0] + i] for i in range(2)]
    s_ub = lax.dynamic_slice_in_dim(smalls[6 : 6 + ff // d].reshape(-1), shard * own_f, own_f, 0)

    return (
        layer_out,
        tokens_grad,
        s_gain1,
        s_shift1,
        qkv_grads[0],
        s_qb,
        qkv_grads[1],
        qkv_grads[2],
        s_vb,
        out_grad,
        s_ob,
        s_gain2,
        s_shift2,
        up_grad,
        s_ub,
        down_grad,
        s_db,
    )


def solution(mesh):
    row, mat, vec = P("rep", "shard", None), P("shard", None), P("shard")
    return jax.shard_map(
        on_device,
        mesh=mesh,
        in_specs=(row, P("rep"), row, vec, vec, mat, vec, mat, mat, vec, mat, vec, vec, vec, mat, vec, mat, vec),
        out_specs=(row, row, vec, vec, mat, vec, mat, mat, vec, mat, vec, vec, vec, mat, vec, mat, vec),
        check_vma=False,
    )
```

```python
import functools
import math

import jax
import jax.numpy as jnp
from jax import lax
from jax.experimental import pallas as pl
from jax.experimental.pallas import tpu as pltpu
from jax.sharding import PartitionSpec as P

HEAD = 80
WIN = 256
AUG = 192
EPS = 1e-5
SCALE = HEAD**-0.5
SCALE2 = SCALE * math.log2(math.e)
DEAD = -1e30
ROWS = 256
GAIN1, SHIFT1, QBIAS, VBIAS, OBIAS, GAIN2, SHIFT2, DBIAS, LENGTHS = [slice(i, i + 1) for i in range(9)]
UBIAS = 9
FFN_TILE = 512
FFN_ROWS = 768
f32 = jnp.float32
bf16 = jnp.bfloat16
MESH = pl.DeviceIdType.MESH

ERF_P = 0.35
ERF_C = (0.19458996, 0.23381038, -0.00165479, 0.67243411, -0.66868964, 0.76616445, -0.19665448)


def params(limit=60):
    return pltpu.CompilerParams(vmem_limit_bytes=limit * 2**20)


def cost(flops, size):
    return pl.CostEstimate(flops=int(flops), bytes_accessed=int(size), transcendentals=0)


def dot(a, b):
    return jnp.dot(a, b, preferred_element_type=f32)


def dot_nt(a, b):
    return lax.dot_general(a, b, (((1,), (1,)), ((), ())), preferred_element_type=f32)


def dot_tn(a, b):
    return lax.dot_general(a, b, (((0,), (0,)), ((), ())), preferred_element_type=f32)


def gelu_pair(a):
    expo = jnp.exp2(a * a * (-0.5 * math.log2(math.e)))
    t = 1.0 / (1.0 + jnp.abs(a) * (ERF_P * math.sqrt(0.5)))
    total = ERF_C[-1]
    for c in ERF_C[-2::-1]:
        total = total * t + c
    tail = 0.5 * expo * (total * t)
    cdf = jnp.where(a >= 0, 1.0 - tail, tail)
    return a * cdf, cdf + a * (expo * (1.0 / math.sqrt(2.0 * math.pi)))


def whole(shape):
    return pl.BlockSpec(shape, lambda *_: (0,) * len(shape))


def once(shape):
    return pl.BlockSpec(shape, lambda *_: (0,) * len(shape), pipeline_mode=pl.Buffered(1))


def row_block(rows, cols):
    return pl.BlockSpec((rows, cols), lambda i: (i, 0))


def standardize(x):
    centred = x - jnp.mean(x, axis=-1, keepdims=True)
    inv = lax.rsqrt(jnp.mean(centred * centred, axis=-1, keepdims=True) + EPS)
    return centred * inv, inv


class Link:
    def __init__(self, sems):
        self.send, self.recv, self.local = sems
        self.next = 0
        self.next_local = 0
        self.groups = lax.axis_size("shard")
        self.rep = lax.axis_index("rep")
        self.shard = lax.axis_index("shard")
        self.core = lax.rem(self.rep, 2)
        self.half = self.groups // 2

    def meet_plane(self):
        barrier = pltpu.get_barrier_semaphore()
        base = self.rep - self.core
        for c in range(2):
            for p in range(self.groups):
                if c or p:
                    to = (base + (self.core ^ c), self.shard ^ p)
                    pl.semaphore_signal(barrier, inc=1, device_id=to, device_id_type=MESH)
        pl.semaphore_wait(barrier, 2 * self.groups - 1)

    def meet_all(self):
        barrier = pltpu.get_barrier_semaphore()
        base = self.rep - self.core
        for c in range(2):
            for p in range(self.groups):
                if c or p:
                    to = (base + (self.core ^ c), self.shard ^ p)
                    pl.semaphore_signal(barrier, inc=1, device_id=to, device_id_type=MESH)
        pl.semaphore_signal(barrier, inc=1, device_id=self.inward(), device_id_type=MESH)

        @pl.when(self.inner())
        def _():
            pl.semaphore_signal(barrier, inc=1, device_id=self.outward(), device_id_type=MESH)
            pl.semaphore_wait(barrier, 2 * self.groups + 1)

        @pl.when(jnp.logical_not(self.inner()))
        def _():
            pl.semaphore_wait(barrier, 2 * self.groups)

    def inner(self):
        plane = lax.div(self.rep, 2)
        return (plane == 1) | (plane == 2)

    def inward(self):
        return (self.rep + jnp.where(self.rep < 4, 2, -2), self.shard)

    def outward(self):
        return (self.rep - jnp.where(self.rep < 4, 2, -2), self.shard)

    def meet_core(self):
        barrier = pltpu.get_barrier_semaphore()
        pl.semaphore_signal(barrier, inc=1, device_id=self.sibling(), device_id_type=MESH)
        pl.semaphore_wait(barrier, 1)

    def sibling(self):
        return (self.rep ^ 1, self.shard)

    def slots(self, count):
        first = self.next
        self.next += count
        return first

    def local_slots(self, count):
        first = self.next_local
        self.next_local += count
        return first

    def remote(self, src, dst, send, recv, to):
        return pltpu.make_async_remote_copy(
            src_ref=src,
            dst_ref=dst,
            send_sem=self.send.at[send],
            recv_sem=self.recv.at[recv],
            device_id=to,
            device_id_type=MESH,
        )

    def here(self, src, dst, slot):
        return pltpu.make_async_copy(src, dst, self.local.at[slot])


class Job:
    @staticmethod
    def buffers(source):
        return []

    def forward(self):
        pass

    def inward(self):
        pass

    def across(self):
        pass

    def outward(self):
        pass


class Gather(Job):
    def __init__(self, link, src, dst, bufs):
        self.link, self.src, self.dst = link, src, dst
        self.rows = src.shape[0]
        self.base = link.slots(max(4, link.groups - 1))
        self.keep = link.here(src, dst.at[link.shard], link.local_slots(1))

    def first(self):
        link = self.link
        peers = (1, 2) if link.groups == 4 else range(1, link.groups)
        return [
            link.remote(self.src, self.dst.at[link.shard], self.base + i, self.base + i, (link.rep, link.shard ^ p))
            for i, p in enumerate(peers)
        ]

    def second(self):
        link = self.link
        if link.groups != 4:
            return []
        cut = self.rows // 2
        parts = ((1, 2, pl.ds(0, cut)), (2, 1, pl.ds(cut, self.rows - cut)))
        out = []
        for i, (origin, to, rows) in enumerate(parts):
            ref = self.dst.at[link.shard ^ origin, rows]
            out.append(link.remote(ref, ref, self.base + 2 + i, self.base + 2 + i, (link.rep, link.shard ^ to)))
        return out

    def start(self):
        self.keep.start()
        for c in self.first():
            c.start()

    def forward(self):
        for c, d in zip(self.first(), self.second()):
            c.wait_recv()
            d.start()

    def finish(self):
        second = self.second()
        for c in self.first():
            if not second:
                c.wait_recv()
            c.wait_send()
        for c in second:
            c.wait()
        self.keep.wait()


class ToClip(Job):
    def __init__(self, link, src, dst, bufs):
        self.link, self.src, self.dst = link, src, dst
        self.rows = src.shape[1]
        self.base = link.slots(link.half + 1)
        self.keep = link.local_slots(1)

    def copy(self, j):
        link = self.link
        core = lax.div(link.shard, link.half)
        to = (link.rep - link.core + core, link.core * link.half + j)
        mine = (core == link.core) & (link.core * link.half + j == link.shard)
        dst = self.dst.at[pl.ds(pl.multiple_of(link.shard * self.rows, self.rows), self.rows)]
        there = link.remote(self.src.at[j], dst, self.base + j, self.base + lax.rem(link.shard, link.half), to)
        return mine, there, link.here(self.src.at[j], dst, self.keep)

    def arrival(self, t):
        link = self.link
        source = link.core * link.half + t
        mine = (lax.div(link.shard, link.half) == link.core) & (source == link.shard)
        dst = self.dst.at[pl.ds(pl.multiple_of(source * self.rows, self.rows), self.rows)]
        there = link.remote(self.src.at[0], dst, self.base, self.base + t, link.sibling())
        return mine, there, link.here(self.src.at[0], dst, self.keep)

    def to_sibling(self):
        link = self.link
        size = link.half * self.rows
        rows = pl.ds(pl.multiple_of(link.core * size, size), size)
        slot = self.base + link.half
        return link.remote(self.dst.at[rows], self.dst.at[rows], slot, slot, link.sibling())

    def start(self):
        for j in range(self.link.half):
            mine, there, here = self.copy(j)
            pl.when(mine)(here.start)
            pl.when(jnp.logical_not(mine))(there.start)

    def forward(self):
        for t in range(self.link.half):
            mine, there, here = self.arrival(t)
            pl.when(mine)(here.wait)
            pl.when(jnp.logical_not(mine))(there.wait_recv)
        self.to_sibling().start()

    def finish(self):
        self.to_sibling().wait()
        for j in range(self.link.half):
            mine, there, _ = self.copy(j)
            pl.when(jnp.logical_not(mine))(there.wait_send)


class FromClip(Job):
    def __init__(self, link, src, dst, bufs):
        self.link, self.src, self.dst = link, src, dst
        self.rows = dst.shape[1]
        self.base = link.slots(link.half)
        self.keep = link.local_slots(1)

    def copy(self, t):
        link = self.link
        core = lax.div(link.shard, link.half)
        shard = link.core * link.half + t
        mine = (core == link.core) & (shard == link.shard)
        clip = lax.rem(link.shard, link.half)
        src = self.src.at[pl.ds(t * self.rows, self.rows)]
        dst = self.dst.at[clip]
        there = link.remote(src, dst, self.base + t, self.base + clip, (link.rep - link.core + core, shard))
        return mine, there, link.here(src, dst, self.keep)

    def arrival(self, j):
        link = self.link
        mine = (lax.div(link.shard, link.half) == link.core) & (link.core * link.half + j == link.shard)
        src = self.src.at[pl.ds(0, self.rows)]
        there = link.remote(src, self.dst.at[j], self.base, self.base + j, link.sibling())
        return mine, there, link.here(src, self.dst.at[j], self.keep)

    def start(self):
        for t in range(self.link.half):
            mine, there, here = self.copy(t)
            pl.when(mine)(here.start)
            pl.when(jnp.logical_not(mine))(there.start)

    def finish(self):
        for t in range(self.link.half):
            mine, there, here = self.copy(t)
            pl.when(jnp.logical_not(mine))(there.wait_send)
        for j in range(self.link.half):
            mine, there, here = self.arrival(j)
            pl.when(mine)(here.wait)
            pl.when(jnp.logical_not(mine))(there.wait_recv)


class Owners(Job):
    def __init__(self, link, src, dst, bufs):
        self.link, self.src, self.dst = link, src, dst
        self.base = link.slots(link.groups - 1)

    def copies(self):
        link = self.link
        return [
            link.remote(
                self.src.at[link.shard ^ p],
                self.dst.at[p - 1],
                self.base + p - 1,
                self.base + p - 1,
                (link.rep, link.shard ^ p),
            )
            for p in range(1, link.groups)
        ]

    def start(self):
        for c in self.copies():
            c.start()

    def finish(self):
        for c in self.copies():
            c.wait()


def add_low(a, b):
    return (a.astype(f32) + b.astype(f32)).astype(bf16)


class Reduce(Job):
    def __init__(self, link, src, dst, bufs):
        self.link, self.src, self.dst = link, src, dst
        self.base = link.slots(6)
        self.keep = link.local_slots(4)
        self.half = dst.shape[0] // 2
        self.pass_in, self.pass_sum, self.near, self.far, self.own = (bufs[2 * i : 2 * i + 2] for i in range(5))

    @staticmethod
    def buffers(source):
        half = pltpu.VMEM((source.shape[1] // 2, source.shape[2]), source.dtype)
        return [half] * 10

    def block(self, i, part):
        rows = pl.ds(part * self.half, self.half)
        return self.src.at[self.link.shard ^ i, rows]

    def hops(self):
        link = self.link
        x, y = (link.rep, link.shard ^ 1), (link.rep, link.shard ^ 2)
        plan = (
            (self.block(3, 0), self.pass_in[0], x),
            (self.block(3, 1), self.pass_in[1], y),
            (self.block(1, 0), self.near[0], x),
            (self.block(2, 1), self.near[1], y),
        )
        return [link.remote(s, d, self.base + i, self.base + i, to) for i, (s, d, to) in enumerate(plan)]

    def later(self):
        link = self.link
        x, y = (link.rep, link.shard ^ 1), (link.rep, link.shard ^ 2)
        plan = zip(self.pass_sum, self.far, (y, x))
        return [link.remote(s, d, self.base + 4 + i, self.base + 4 + i, to) for i, (s, d, to) in enumerate(plan)]

    def loads(self):
        plan = (
            (self.block(2, 0), self.pass_sum[0]),
            (self.block(1, 1), self.pass_sum[1]),
            (self.block(0, 0), self.own[0]),
            (self.block(0, 1), self.own[1]),
        )
        return [self.link.here(s, d, self.keep + i) for i, (s, d) in enumerate(plan)]

    def store(self, part):
        rows = pl.ds(part * self.half, self.half)
        return self.link.here(self.own[part], self.dst.at[rows], self.keep + part)

    def start(self):
        for c in self.hops():
            c.start()
        for c in self.loads():
            c.start()

    def forward(self):
        hops, loads, later = self.hops(), self.loads(), self.later()
        for i in range(2):
            loads[i].wait()
            hops[i].wait_recv()
            self.pass_sum[i][...] = add_low(self.pass_sum[i][...], self.pass_in[i][...])
            later[i].start()

    def collect(self):
        hops, loads, later = self.hops(), self.loads(), self.later()
        for i in range(2):
            loads[2 + i].wait()
            hops[2 + i].wait_recv()
            later[i].wait_recv()
            total = self.own[i][...].astype(f32) + self.near[i][...].astype(f32) + self.far[i][...].astype(f32)
            self.own[i][...] = total.astype(bf16)
            self.store(i).start()
        for i in range(2):
            self.store(i).wait()

    def finish(self):
        self.collect()
        self.close()

    def close(self):
        for c in self.hops() + self.later():
            c.wait_send()


class Chain(Job):
    def __init__(self, link, src, dst, bufs):
        self.link, self.src, self.dst = link, src, dst
        self.own, self.one, self.two = bufs
        self.base = link.slots(4)
        self.keep = link.local_slots(2)

    @staticmethod
    def buffers(source):
        return [pltpu.VMEM(source.shape, source.dtype)] * 3

    def step(self, src, dst, slot, to):
        return self.link.remote(src, dst, self.base + slot, self.base + slot, to)

    def steps(self):
        link = self.link
        return (
            self.step(self.src, self.one, 0, link.inward()),
            self.step(self.own, self.two, 1, link.inward()),
            self.step(self.one, self.two, 2, link.outward()),
        )

    def share(self, ref):
        link = self.link
        place = self.dst.at[link.core]
        return self.step(ref, place, 3, link.sibling()), link.here(ref, place, self.keep + 1)

    def start(self):
        inner = self.link.inner()
        pl.when(inner)(self.link.here(self.src, self.own, self.keep).start)
        pl.when(jnp.logical_not(inner))(self.steps()[0].start)

    def add(self, a, b):
        return (a[...].astype(f32) + b[...].astype(f32)).astype(a.dtype)

    def inward(self):
        @pl.when(self.link.inner())
        def _():
            steps = self.steps()
            self.link.here(self.src, self.own, self.keep).wait()
            steps[0].wait_recv()
            self.own[...] = self.add(self.own, self.one)
            steps[1].start()

    def across(self):
        @pl.when(self.link.inner())
        def _():
            steps = self.steps()
            steps[1].wait_recv()
            self.one[...] = self.add(self.own, self.two)
            steps[2].start()
            for c in self.share(self.one):
                c.start()

    def outward(self):
        @pl.when(jnp.logical_not(self.link.inner()))
        def _():
            self.steps()[2].wait_recv()
            for c in self.share(self.two):
                c.start()

    def finish(self):
        swap, here = self.share(self.one)
        swap.wait()
        here.wait()
        inner = self.link.inner()

        @pl.when(inner)
        def _():
            self.steps()[1].wait_send()
            self.steps()[2].wait_send()

        pl.when(jnp.logical_not(inner))(self.steps()[0].wait_send)


def chain_steps(chains):
    lists = []
    for i in range(len(chains) + 1):
        lists.append([c.inward for c in chains[i : i + 1]] + [c.across for c in chains[max(i - 1, 0) : i]])
    return lists


class Jobs:
    def __init__(self, *jobs):
        self.jobs = [(job + (None,))[:4] for job in jobs]
        self.bufs = [kind.buffers(a) for kind, a, _, _ in self.jobs]

    def sources(self):
        return [a for _, a, _, _ in self.jobs]

    def in_specs(self):
        return [pl.BlockSpec(memory_space=pl.ANY)] * len(self.jobs)

    def out_shapes(self):
        return [jax.ShapeDtypeStruct(shape, a.dtype) for _, a, shape, _ in self.jobs]

    def scratch(self, extra=0):
        groups = lax.axis_size("shard")
        remote = len(self.jobs) * max(6, groups) + extra
        return [b for bufs in self.bufs for b in bufs] + [
            pltpu.SemaphoreType.DMA((remote,)),
            pltpu.SemaphoreType.DMA((remote,)),
            pltpu.SemaphoreType.DMA((4 * len(self.jobs) + extra + 1,)),
        ]

    def bind(self, rest, srcs, dsts):
        rest = list(rest)
        bufs = []
        for shapes in self.bufs:
            bufs.append([rest.pop(0) for _ in shapes])
        link = Link(rest[:3])
        bound = [
            kind(link, view(a) if view else a, b, c) for (kind, _, _, view), a, b, c in zip(self.jobs, srcs, dsts, bufs)
        ]
        return link, bound, rest[3:]


def comm_params(number, limit=60):
    return pltpu.CompilerParams(
        vmem_limit_bytes=limit * 2**20, collective_id=number, has_side_effects=True
    )


def exchange_call(jobs, sibling, number, name):
    count = len(jobs.jobs)

    def kernel(*refs):
        srcs, mine = refs[:count], refs[count]
        dsts, other = refs[count + 1 : 2 * count + 1], refs[2 * count + 1]
        link, bound, _ = jobs.bind(refs[2 * count + 2 :], srcs, dsts)
        slot = link.slots(1)
        swap = link.remote(mine, other, slot, slot, link.sibling())
        link.meet_plane()
        swap.start()
        for job in bound:
            job.start()
        for job in bound:
            job.forward()
        for job in bound:
            job.finish()
        swap.wait()

    return pl.pallas_call(
        kernel,
        in_specs=jobs.in_specs() + [pl.BlockSpec(memory_space=pl.ANY)],
        out_specs=[pl.BlockSpec(memory_space=pl.ANY)] * (count + 1),
        out_shape=jobs.out_shapes() + [jax.ShapeDtypeStruct(sibling.shape, sibling.dtype)],
        scratch_shapes=jobs.scratch(1),
        compiler_params=comm_params(number),
        name=name,
    )(*jobs.sources(), sibling)


def qkv_kernel(*refs, jobs):
    count = len(jobs.jobs)
    x_ref, vec_ref, w_ref, bias_ref = refs[:4]
    h_ref, q_ref, k_ref, v_ref = refs[4 + count : 8 + count]
    link, bound, _ = jobs.bind(refs[8 + 2 * count :], refs[4 : 4 + count], refs[8 + count : 8 + 2 * count])

    @pl.when(pl.program_id(0) == 0)
    def _():
        link.meet_plane()
        for job in bound:
            job.start()

    xhat, _ = standardize(x_ref[...].astype(f32))
    h = (xhat * vec_ref[GAIN1] + vec_ref[SHIFT1]).astype(bf16)
    h_ref[...] = h
    z = dot(h, w_ref[...]) + bias_ref[...]
    width = z.shape[1] // 3
    for i, ref in enumerate((q_ref, k_ref, v_ref)):
        ref[:, :width] = z[:, i * width : (i + 1) * width].astype(bf16)
        ref[:, width:] = jnp.zeros((ref.shape[0], ref.shape[1] - width), bf16)

    @pl.when(pl.program_id(0) == pl.num_programs(0) - 1)
    def _():
        for job in bound:
            job.forward()
        for job in bound:
            job.finish()


def qkv_call(x, vec, w, bias, wide, jobs, number):
    n, d = x.shape
    out = jax.ShapeDtypeStruct((n, wide), bf16)
    return pl.pallas_call(
        functools.partial(qkv_kernel, jobs=jobs),
        grid=(n // ROWS,),
        in_specs=[row_block(ROWS, d), whole(vec.shape), once(w.shape), whole(bias.shape)] + jobs.in_specs(),
        out_specs=[row_block(ROWS, d)] + [row_block(ROWS, wide)] * 3 + jobs.in_specs(),
        out_shape=[jax.ShapeDtypeStruct((n, d), bf16), out, out, out] + jobs.out_shapes(),
        scratch_shapes=jobs.scratch(),
        compiler_params=comm_params(number),
        cost_estimate=cost(2 * n * d * w.shape[1], 4 * n * d + 2 * w.size + 6 * n * wide),
        name="project",
    )(x, vec, w, bias, *jobs.sources())


def head_window(h):
    start = h * HEAD
    base = (start // 128) * 128
    off = start - base
    lane = lax.broadcasted_iota(jnp.int32, (1, WIN), 1)
    keep = jnp.where((lane >= off) & (lane < off + HEAD), 1.0, 0.0)
    return pl.ds(pl.multiple_of(base, 128), WIN), keep, lane


def put3(x, lane, first, value):
    hi = value.astype(bf16).astype(f32)
    rest = value - hi
    mid = rest.astype(bf16).astype(f32)
    low = rest - mid
    return jnp.where(
        lane == first,
        hi,
        jnp.where(lane == first + 1, mid, jnp.where(lane == first + 2, low, x)),
    )


def key_extra(rows, length):
    lane = lax.broadcasted_iota(jnp.int32, (rows, WIN), 1)
    row = lax.broadcasted_iota(jnp.int32, (rows, WIN), 0)
    dead = jnp.where(row >= length, DEAD, 0.0)
    minus = jnp.where((lane > AUG) & (lane <= AUG + 3), -1.0, 0.0)
    return jnp.where(lane == AUG, dead, minus).astype(bf16)


def attn_fwd_kernel(*refs, bq, jobs):
    count = len(jobs.jobs)
    len_ref, q_ref, k_ref, v_ref = refs[:4]
    o_ref, lse_ref = refs[4 + count : 6 + count]
    acc, kx = refs[6 + 2 * count : 8 + 2 * count]
    link, bound, _ = jobs.bind(refs[8 + 2 * count :], refs[4 : 4 + count], refs[6 + count : 6 + 2 * count])
    h = pl.program_id(0)
    heads = pl.num_programs(0)
    n = q_ref.shape[0]
    width = o_ref.shape[1]

    @pl.when(h == 0)
    def _():
        link.meet_plane()
        for job in bound:
            job.start()
        acc[...] = jnp.zeros_like(acc)
        lse_ref[...] = jnp.zeros_like(lse_ref)
        kx[...] = key_extra(n, len_ref[0])

    @pl.when(h == heads - 2)
    def _():
        for job in bound:
            job.forward()

    win, keep, lane = head_window(h)
    low = keep.astype(bf16)
    q_one = jnp.where(lane == AUG, 1.0, 0.0).astype(bf16)
    v_one = jnp.where((lane >= AUG) & (lane < AUG + 3), 1.0, 0.0).astype(bf16)
    k = k_ref[:, win] * low + kx[...]
    v = v_ref[:, win] * low + v_one
    for i in range(n // bq):
        rows = slice(i * bq, (i + 1) * bq)
        s = dot_nt(q_ref[rows, win] * low + q_one, k)
        peak = jnp.max(s, axis=-1, keepdims=True)
        p = jnp.exp2((s - peak) * SCALE2).astype(bf16)
        o = dot(p, v)
        total = o[:, AUG : AUG + 1]
        acc[rows, win] += o * (keep * (1.0 / total))
        here = lax.broadcasted_iota(jnp.int32, (bq, 128), 1) == h
        lse = peak + jnp.log(total) * (1.0 / SCALE)
        lse_ref[rows, :] = jnp.where(here, lse, lse_ref[rows, :])

    @pl.when(h == heads - 1)
    def _():
        o_ref[:, :width] = acc[:, :width].astype(bf16)
        for job in bound:
            job.finish()


def attn_fwd_call(length, q, k, v, width, heads, jobs, number):
    n, wide = q.shape
    return pl.pallas_call(
        functools.partial(attn_fwd_kernel, bq=256, jobs=jobs),
        grid=(heads,),
        in_specs=[pl.BlockSpec(memory_space=pltpu.SMEM)] + [whole((n, wide))] * 3 + jobs.in_specs(),
        out_specs=[whole((n, width)), whole((n, 128))] + jobs.in_specs(),
        out_shape=[jax.ShapeDtypeStruct((n, width), bf16), jax.ShapeDtypeStruct((n, 128), f32)] + jobs.out_shapes(),
        scratch_shapes=[pltpu.VMEM((n, wide), f32), pltpu.VMEM((n, WIN), bf16)] + jobs.scratch(),
        compiler_params=comm_params(number),
        cost_estimate=cost(4 * n * n * WIN * heads, 8 * n * wide),
        name="attend",
    )(length, q, k, v, *jobs.sources())


def attn_bwd_kernel(*refs, bk, jobs):
    count = len(jobs.jobs)
    len_ref, q_ref, k_ref, v_ref, o_ref, do_ref, lse_ref = refs[:7]
    g_ref, sum_ref = refs[7 + count : 9 + count]
    dq, dk, dv, part, qa, da, kx = refs[9 + 2 * count : 16 + 2 * count]
    link, bound, _ = jobs.bind(refs[16 + 2 * count :], refs[7 : 7 + count], refs[9 + count : 9 + 2 * count])
    chains = [job for job in bound if isinstance(job, Chain)]
    h = pl.program_id(0)
    n = q_ref.shape[0]

    @pl.when(h == 0)
    def _():
        if chains:
            link.meet_all()
        else:
            link.meet_plane()
        for job in bound:
            job.start()
        for ref in (dq, dk, dv):
            ref[...] = jnp.zeros_like(ref)
        kx[...] = key_extra(n, len_ref[0])

    heads = pl.num_programs(0)

    def at_head(number, steps):
        @pl.when(h == number)
        def _():
            for step in steps:
                step()

    steps = chain_steps(chains) if chains else []
    for number, some in zip((2, 4, 5, 6), steps):
        at_head(number, some)
    at_head(heads - 2, [job.forward for job in bound])

    win, keep, lane = head_window(h)
    low = keep.astype(bf16)
    v_one = jnp.where((lane >= AUG) & (lane < AUG + 3), 1.0, 0.0).astype(bf16)
    for i in range(n // ROWS):
        rows = slice(i * ROWS, (i + 1) * ROWS)
        here = lax.broadcasted_iota(jnp.int32, (ROWS, 128), 1) == h
        lse = jnp.sum(jnp.where(here, lse_ref[rows, :], 0.0), axis=-1, keepdims=True)
        q = q_ref[rows, win].astype(f32) * keep
        qa[rows, :] = jnp.where(lane == AUG, 1.0, put3(q, lane, AUG + 1, lse)).astype(bf16)
        d = do_ref[rows, win].astype(f32) * keep
        delta = jnp.sum(d * o_ref[rows, win].astype(f32), axis=-1, keepdims=True)
        da[rows, :] = put3(d, lane, AUG, -delta).astype(bf16)
    for i in range(n // bk):
        rows = slice(i * bk, (i + 1) * bk)
        k = k_ref[rows, win] * low + kx[rows, :]
        v = v_ref[rows, win] * low + v_one
        p = jnp.exp2(dot_nt(k, qa[...]) * SCALE2)
        ds = (p * dot_nt(v, da[...])).astype(bf16)
        dv[rows, win] += dot(p.astype(bf16), da[...]) * keep
        dk[rows, win] += dot(ds, qa[...]) * keep
        new = dot_tn(ds, k)
        part[...] = new if i == 0 else part[...] + new
    dq[:, win] += part[...] * keep

    @pl.when(h == heads - 1)
    def _():
        for i, (ref, factor) in enumerate(((dq, SCALE), (dk, SCALE), (dv, 1.0))):
            value = (ref[:, : g_ref.shape[1] // 3] * factor).astype(bf16)
            cols = slice(i * value.shape[1], (i + 1) * value.shape[1])
            g_ref[:, cols] = value
            sum_ref[:, cols] = jnp.sum(value.astype(f32), axis=0, keepdims=True)
        for some in steps[4:]:
            for step in some:
                step()
        for job in bound:
            job.outward()
        for job in bound:
            job.finish()


def attn_bwd_call(length, q, k, v, o, do, lse, width, heads, jobs, number):
    n, wide = q.shape
    return pl.pallas_call(
        functools.partial(attn_bwd_kernel, bk=256, jobs=jobs),
        grid=(heads,),
        in_specs=[pl.BlockSpec(memory_space=pltpu.SMEM)]
        + [once((n, wide))] * 5
        + [once((n, 128))]
        + jobs.in_specs(),
        out_specs=[once((n, 3 * width)), whole((1, 3 * width))] + jobs.in_specs(),
        out_shape=[
            jax.ShapeDtypeStruct((n, 3 * width), bf16),
            jax.ShapeDtypeStruct((1, 3 * width), f32),
        ]
        + jobs.out_shapes(),
        scratch_shapes=[pltpu.VMEM((n, wide), f32)] * 3
        + [pltpu.VMEM((n, WIN), f32)]
        + [pltpu.VMEM((n, WIN), bf16)] * 3
        + jobs.scratch(),
        compiler_params=comm_params(number),
        cost_estimate=cost(10 * n * n * WIN * heads, 20 * n * wide),
        name="attend_back",
    )(length, q, k, v, o, do, lse, *jobs.sources())


def middle_kernel(*refs, jobs):
    count = len(jobs.jobs)
    o_ref, w_ref, x_ref, vec_ref = refs[:4]
    mid_ref, h_ref, owide_ref = refs[4 + count : 7 + count]
    mine, other = refs[7 + 2 * count : 9 + 2 * count]
    link, bound, _ = jobs.bind(refs[9 + 2 * count :], refs[4 : 4 + count], refs[7 + count : 7 + 2 * count])
    n = x_ref.shape[0]
    width = o_ref.shape[1]
    base = link.slots(n // ROWS)
    link.meet_plane()
    for job in bound:
        job.start()

    def swap(i):
        rows = pl.ds(pl.multiple_of(i * ROWS, ROWS), ROWS)
        return rows, link.remote(mine.at[rows], other.at[rows], base + i, base + i, link.sibling())

    def project(i, carry):
        rows, copy = swap(i)
        mine[rows, :] = dot(o_ref[rows, :], w_ref[...]).astype(bf16)
        copy.start()
        return carry

    def norm(i, carry):
        rows, copy = swap(i)
        copy.wait_recv()
        mid = x_ref[rows, :].astype(f32) + (
            mine[rows, :].astype(f32) + other[rows, :].astype(f32) + vec_ref[OBIAS]
        )
        mid_ref[rows, :] = mid
        xhat, _ = standardize(mid)
        h_ref[rows, :] = (xhat * vec_ref[GAIN2] + vec_ref[SHIFT2]).astype(bf16)
        return carry

    lax.fori_loop(0, n // ROWS, project, 0)
    owide_ref[:, :width] = o_ref[...]
    owide_ref[:, width:] = jnp.zeros((n, owide_ref.shape[1] - width), bf16)
    lax.fori_loop(0, n // ROWS, norm, 0)
    for i in range(n // ROWS):
        swap(i)[1].wait_send()
    for job in bound:
        job.forward()
    for job in bound:
        job.finish()


def middle_call(o, w, x, vec, wide, jobs, number):
    n, d = x.shape
    vmem = pl.BlockSpec(memory_space=pltpu.VMEM)
    return pl.pallas_call(
        functools.partial(middle_kernel, jobs=jobs),
        in_specs=[vmem] * 4 + jobs.in_specs(),
        out_specs=[vmem] * 3 + jobs.in_specs(),
        out_shape=[
            jax.ShapeDtypeStruct((n, d), f32),
            jax.ShapeDtypeStruct((n, d), bf16),
            jax.ShapeDtypeStruct((n, wide), bf16),
        ]
        + jobs.out_shapes(),
        scratch_shapes=[pltpu.VMEM((n, d), bf16)] * 2 + jobs.scratch(n // ROWS),
        compiler_params=comm_params(number),
        cost_estimate=cost(2 * n * w.size, 14 * n * d),
        name="middle",
    )(o, w, x, vec, *jobs.sources())


def ffn_kernel(*refs, chained, last, mc, jobs):
    count = len(jobs.jobs)
    h_ref, dz_ref, up_ref, ub_ref, dn_ref = refs[:5]
    refs = refs[5:]
    if chained:
        old_out, old_dh = refs[:2]
        refs = refs[2:]
    srcs, refs = refs[:count], refs[count:]
    out_ref, dh_ref, dup_ref, ddn_ref, dub_ref = refs[:5]
    dsts, refs = refs[5 : 5 + count], refs[5 + count :]
    ht, act, grad = refs[:3]
    acc, dh = refs[3:5] if last else (out_ref, dh_ref)
    refs = refs[5:] if last else refs[3:]
    link, bound, refs = jobs.bind(refs, srcs, dsts)
    t = pl.program_id(0)
    tiles = pl.num_programs(0)
    n = h_ref.shape[0]

    @pl.when(t == 0)
    def _():
        link.meet_plane()
        for job in bound:
            job.start()
        if chained:
            sem = refs[0]
            copies = [
                pltpu.make_async_copy(src, dst, sem.at[i])
                for i, (src, dst) in enumerate(((old_out, acc), (old_dh, dh)))
            ]
            for c in copies:
                c.start()
            ht[...] = h_ref[...].T
            for c in copies:
                c.wait()
        else:
            ht[...] = h_ref[...].T
            acc[...] = jnp.zeros_like(acc)
            dh[...] = jnp.zeros_like(dh)

    @pl.when(t == tiles - 1)
    def _():
        for job in bound:
            job.forward()

    def step(i, carry):
        rows = pl.ds(pl.multiple_of(i * mc, mc), mc)
        g, slope = gelu_pair(dot(h_ref[rows, :], up_ref[...]) + ub_ref[...])
        g = g.astype(bf16)
        da = (dot_nt(dz_ref[rows, :], dn_ref[...]) * slope).astype(bf16)
        act[rows, :] = g
        grad[rows, :] = da
        acc[rows, :] += dot(g, dn_ref[...])
        dh[rows, :] += dot_nt(da, up_ref[...])
        return carry

    lax.fori_loop(0, n // mc, step, 0)
    dub_ref[...] = jnp.sum(grad[...].astype(f32), axis=0, keepdims=True)
    dup_ref[...] = dot(ht[...], grad[...]).astype(bf16)
    ddn_ref[...] = dot_tn(act[...], dz_ref[...]).astype(bf16)

    @pl.when(t == tiles - 1)
    def _():
        if last:
            out_ref[...] = acc[...].astype(out_ref.dtype)
            dh_ref[...] = dh[...].astype(dh_ref.dtype)
        for job in bound:
            job.finish()


def ffn_call(h, dz, up, bias, down, old, last, jobs, number, name):
    n, d = h.shape
    hidden = up.shape[1]
    bt = FFN_TILE
    out = jax.ShapeDtypeStruct((n, d), bf16 if last else f32)
    chained = old is not None
    kept = once((n, d))
    return pl.pallas_call(
        functools.partial(ffn_kernel, chained=chained, last=last, mc=FFN_ROWS, jobs=jobs),
        grid=(hidden // bt,),
        in_specs=[
            kept,
            kept,
            pl.BlockSpec((d, bt), lambda t: (0, t)),
            pl.BlockSpec((1, bt), lambda t: (0, t)),
            pl.BlockSpec((bt, d), lambda t: (t, 0)),
        ]
        + ([pl.BlockSpec(memory_space=pl.ANY)] * 2 if chained else [])
        + jobs.in_specs(),
        out_specs=[
            kept,
            kept,
            pl.BlockSpec((d, bt), lambda t: (0, t)),
            pl.BlockSpec((bt, d), lambda t: (t, 0)),
            pl.BlockSpec((1, bt), lambda t: (0, t)),
        ]
        + jobs.in_specs(),
        out_shape=[
            out,
            out,
            jax.ShapeDtypeStruct((d, hidden), bf16),
            jax.ShapeDtypeStruct((hidden, d), bf16),
            jax.ShapeDtypeStruct((1, hidden), f32),
        ]
        + jobs.out_shapes(),
        scratch_shapes=[pltpu.VMEM((d, n), bf16)]
        + [pltpu.VMEM((n, bt), bf16)] * 2
        + ([pltpu.VMEM((n, d), f32)] * 2 if last else [])
        + jobs.scratch()
        + ([pltpu.SemaphoreType.DMA((2,))] if chained else []),
        compiler_params=comm_params(number),
        cost_estimate=cost(12 * n * d * hidden, 8 * d * hidden + 12 * n * d),
        name=name,
    )(h, dz, up, bias, down, *(old if chained else ()), *jobs.sources())


def second_back_kernel(*refs, jobs):
    count = len(jobs.jobs)
    mid_ref, dh_ref, out_ref, dz_ref, vec_ref, w_ref, o_ref, dh_any, out_any = refs[:9]
    dmid_ref, do_ref, dw_ref, sums_ref, layer_ref = refs[9 + count : 14 + count]
    acc, dh_other, out_other = refs[14 + 2 * count : 17 + 2 * count]
    link, bound, _ = jobs.bind(refs[17 + 2 * count :], refs[9 : 9 + count], refs[14 + count : 14 + 2 * count])
    i = pl.program_id(0)
    blocks = pl.num_programs(0)
    half = layer_ref.shape[0] // ROWS
    width = w_ref.shape[0]
    base = link.slots(3 * half)

    def swap_dh(j):
        rows = pl.ds(pl.multiple_of(j * ROWS, ROWS), ROWS)
        return link.remote(dh_any.at[rows], dh_other.at[rows], base + j, base + j, link.sibling())

    def swap_out(j):
        src = pl.ds(pl.multiple_of(((1 - link.core) * half + j) * ROWS, ROWS), ROWS)
        dst = pl.ds(pl.multiple_of(j * ROWS, ROWS), ROWS)
        slot = base + 2 * half + j
        return link.remote(out_any.at[src], out_other.at[dst], slot, slot, link.sibling())

    @pl.when(i == 0)
    def _():
        link.meet_plane()
        for j in range(2 * half):
            swap_dh(j).start()
        for j in range(half):
            swap_out(j).start()
        for job in bound:
            job.start()
        acc[...] = jnp.zeros_like(acc)
        sums_ref[...] = jnp.zeros_like(sums_ref)

    @pl.when(i == blocks - 1)
    def _():
        for job in bound:
            job.forward()

    mid = mid_ref[...]
    xhat, inv = standardize(mid)
    swap_dh(i).wait_recv()
    rows = pl.ds(pl.multiple_of(i * ROWS, ROWS), ROWS)
    dh = dh_ref[...].astype(f32) + dh_other[rows, :].astype(f32)
    dx = dh * vec_ref[GAIN2]
    dz = dz_ref[...].astype(f32)
    dmid = dz + inv * (
        dx - jnp.mean(dx, axis=-1, keepdims=True) - xhat * jnp.mean(dx * xhat, axis=-1, keepdims=True)
    )
    dmid_ref[...] = dmid
    dy = dmid.astype(bf16)
    do_ref[:, :width] = dot_nt(dy, w_ref[...]).astype(bf16)
    do_ref[:, width:] = jnp.zeros((do_ref.shape[0], do_ref.shape[1] - width), bf16)
    acc[...] += dot_tn(o_ref[...], dy)
    for row, value in enumerate((dh * xhat, dh, dy.astype(f32), dz)):
        sums_ref[row : row + 1, :] += jnp.sum(value, axis=0, keepdims=True)

    j = i - link.core * half

    @pl.when((j >= 0) & (j < half))
    def _():
        swap_out(j).wait_recv()
        here = pl.ds(pl.multiple_of(j * ROWS, ROWS), ROWS)
        layer_ref[here, :] = (
            mid + (out_ref[...].astype(f32) + out_other[here, :].astype(f32) + vec_ref[DBIAS])
        ).astype(bf16)

    @pl.when(i == blocks - 1)
    def _():
        dw_ref[...] = acc[...].astype(bf16)
        for j in range(2 * half):
            swap_dh(j).wait_send()
        for j in range(half):
            swap_out(j).wait_send()
        for job in bound:
            job.finish()


def second_back_call(mid, dh, out, dz, vec, w, o, wide, jobs, number):
    n, d = mid.shape
    width = w.shape[0]
    block = row_block(ROWS, d)
    count = 3 * n // ROWS // 2
    return pl.pallas_call(
        functools.partial(second_back_kernel, jobs=jobs),
        grid=(n // ROWS,),
        in_specs=[block] * 4
        + [whole(vec.shape), whole(w.shape), row_block(ROWS, width)]
        + [pl.BlockSpec(memory_space=pl.ANY)] * 2
        + jobs.in_specs(),
        out_specs=[block, row_block(ROWS, wide), whole((width, d)), whole((8, d)), whole((n // 2, d))]
        + jobs.in_specs(),
        out_shape=[
            jax.ShapeDtypeStruct((n, d), f32),
            jax.ShapeDtypeStruct((n, wide), bf16),
            jax.ShapeDtypeStruct((width, d), bf16),
            jax.ShapeDtypeStruct((8, d), f32),
            jax.ShapeDtypeStruct((n // 2, d), bf16),
        ]
        + jobs.out_shapes(),
        scratch_shapes=[
            pltpu.VMEM((width, d), f32),
            pltpu.VMEM((n, d), bf16),
            pltpu.VMEM((n // 2, d), bf16),
        ]
        + jobs.scratch(count),
        compiler_params=comm_params(number),
        cost_estimate=cost(4 * n * d * width, 14 * n * d),
        name="second_back",
    )(mid, dh, out, dz, vec, w, o, dh, out, *jobs.sources())


def dw_kernel(h_ref, g_ref, out_ref):
    out_ref[...] = dot_tn(h_ref[...], g_ref[...]).astype(bf16)


def dw_call(h, grads):
    n, d = h.shape
    cols = grads.shape[1]
    return pl.pallas_call(
        dw_kernel,
        grid=(d // 256,),
        in_specs=[pl.BlockSpec((n, 256), lambda i: (0, i)), whole((n, cols))],
        out_specs=row_block(256, cols),
        out_shape=jax.ShapeDtypeStruct((d, cols), bf16),
        compiler_params=params(),
        cost_estimate=cost(2 * n * d * cols, 2 * (n * d + n * cols + d * cols)),
        name="project_grad",
    )(h, grads)


def first_back_kernel(*refs, jobs):
    count = len(jobs.jobs)
    g_ref, w_ref, vec_ref, x_any, dmid_any = refs[:5]
    dx_ref, sums_ref = refs[5 + count : 7 + count]
    x, dmid, mine, other = refs[7 + 2 * count : 11 + 2 * count]
    link, bound, _ = jobs.bind(refs[11 + 2 * count :], refs[5 : 5 + count], refs[7 + count : 7 + 2 * count])
    size = dx_ref.shape[0]
    half = size // ROWS
    base = link.slots(half)
    keep = link.local_slots(2)
    own = pl.ds(pl.multiple_of(link.core * size, size), size)
    loads = [link.here(x_any.at[own], x, keep), link.here(dmid_any.at[own], dmid, keep + 1)]
    for c in loads:
        c.start()
    link.meet_plane()
    for job in bound:
        job.start()

    def product(j):
        rows = pl.ds(pl.multiple_of(j * ROWS, ROWS), ROWS)
        return dot_nt(g_ref[rows, :], w_ref[...])

    def swap(j):
        rows = pl.ds(pl.multiple_of(j * ROWS, ROWS), ROWS)
        return rows, link.remote(mine.at[rows], other.at[rows], base + j, base + j, link.sibling())

    def send(j, carry):
        rows, copy = swap(j)
        mine[rows, :] = product((1 - link.core) * half + j).astype(bf16)
        copy.start()
        return carry

    def norm(j, carry):
        rows, copy = swap(j)
        part = product(link.core * half + j)
        copy.wait_recv()
        xhat, inv = standardize(x[rows, :].astype(f32))
        dh = part + other[rows, :].astype(f32)
        dx = dh * vec_ref[GAIN1]
        dx_ref[rows, :] = (
            dmid[rows, :]
            + inv
            * (dx - jnp.mean(dx, axis=-1, keepdims=True) - xhat * jnp.mean(dx * xhat, axis=-1, keepdims=True))
        ).astype(bf16)
        for row, value in enumerate((dh * xhat, dh)):
            sums_ref[row : row + 1, :] += jnp.sum(value, axis=0, keepdims=True)
        return carry

    sums_ref[...] = jnp.zeros_like(sums_ref)
    lax.fori_loop(0, half, send, 0)
    for c in loads:
        c.wait()
    lax.fori_loop(0, half, norm, 0)
    for j in range(half):
        swap(j)[1].wait_send()
    for job in bound:
        job.forward()
    for job in bound:
        job.finish()


def first_back_call(grads, w, vec, x, dmid, jobs, number):
    n, d = x.shape
    size = n // 2
    vmem = pl.BlockSpec(memory_space=pltpu.VMEM)
    hbm = pl.BlockSpec(memory_space=pl.ANY)
    return pl.pallas_call(
        functools.partial(first_back_kernel, jobs=jobs),
        in_specs=[vmem] * 3 + [hbm] * 2 + jobs.in_specs(),
        out_specs=[vmem] * 2 + jobs.in_specs(),
        out_shape=[jax.ShapeDtypeStruct((size, d), bf16), jax.ShapeDtypeStruct((8, d), f32)] + jobs.out_shapes(),
        scratch_shapes=[
            pltpu.VMEM((size, d), bf16),
            pltpu.VMEM((size, d), f32),
            pltpu.VMEM((size, d), bf16),
            pltpu.VMEM((size, d), bf16),
        ]
        + jobs.scratch(size // ROWS),
        compiler_params=comm_params(number),
        cost_estimate=cost(2 * n * w.size, 12 * n * d),
        name="first_back",
    )(grads, w, vec, x, dmid, *jobs.sources())


class Blocks:
    def __init__(self, ref, stride, first):
        self.ref, self.stride, self.first = ref, stride, first

    @property
    def at(self):
        return self

    def __getitem__(self, index):
        block, part = index
        start = pl.multiple_of(block * self.stride + (self.first + part.start), 16)
        return self.ref.at[pl.ds(start, part.size)]


def back_kernel(*refs, jobs, parts):
    count = len(jobs.jobs)
    g_ref, w_ref, vec_ref, h_ref, early_ref, x_any, dmid_any = refs[:7]
    tokens_any, small_ref, both_any = refs[7 + count : 10 + count]
    rest = list(refs[10 + 2 * count :])
    x, dmid, mine, other, dx, dw, own, total, came = rest[:9]
    rest = rest[9:]
    small_bufs, rest = rest[:3], rest[3:]
    reduce_bufs, rest = [rest[10 * i : 10 * i + 10] for i in range(parts)], rest[10 * parts :]
    chain_bufs, rest = [rest[3 * i : 3 * i + 3] for i in range(2 * parts)], rest[6 * parts :]
    link, chains, _ = jobs.bind(rest, refs[7 : 7 + count], refs[10 + count : 10 + 2 * count])
    size, d = dx.shape
    half = size // ROWS
    owned = own.shape[0]
    piece = owned // parts
    reduces = [
        Reduce(link, Blocks(dw, owned, i * piece), own.at[pl.ds(i * piece, piece)], reduce_bufs[i]) for i in range(parts)
    ]
    for i in range(2 * parts):
        rows = pl.ds(i * (piece // 2), piece // 2)
        chains.append(Chain(link, own.at[rows], both_any.at[:, rows], chain_bufs[i]))
    ready, last = chains[:count], chains[count:]
    to_owners = FromClip(link, dx, tokens_any, None)
    base = link.slots(half)
    keep = link.local_slots(2)
    swap_base = link.slots(3)
    peers = [link.sibling()] + [(link.rep, link.shard ^ bit) for bit in (1, 2)]
    swaps = [link.remote(total, came.at[i], swap_base + i, swap_base + i, to) for i, to in enumerate(peers)]
    small = Chain(link, total, small_ref, small_bufs)
    mine_rows = pl.ds(pl.multiple_of(link.core * size, size), size)
    loads = [link.here(x_any.at[mine_rows], x, keep), link.here(dmid_any.at[mine_rows], dmid, keep + 1)]
    for c in loads:
        c.start()
    link.meet_all()
    for job in ready:
        job.start()

    def weight(i, carry):
        part = pl.ds(pl.multiple_of(i * 256, 256), 256)
        dw[part, :] = dot_tn(h_ref[:, part], g_ref[...]).astype(bf16)
        return carry

    lax.fori_loop(0, d // 256, weight, 0)
    for job in reduces:
        job.start()

    def product(j):
        rows = pl.ds(pl.multiple_of(j * ROWS, ROWS), ROWS)
        return dot_nt(g_ref[rows, :], w_ref[...])

    def swap(j):
        rows = pl.ds(pl.multiple_of(j * ROWS, ROWS), ROWS)
        return rows, link.remote(mine.at[rows], other.at[rows], base + j, base + j, link.sibling())

    def send(j, carry):
        rows, copy = swap(j)
        mine[rows, :] = product((1 - link.core) * half + j).astype(bf16)
        copy.start()
        return carry

    first = early_ref.shape[0]

    def norm(j, carry):
        rows, copy = swap(j)
        part = product(link.core * half + j)
        copy.wait_recv()
        xhat, inv = standardize(x[rows, :].astype(f32))
        dh = part + other[rows, :].astype(f32)
        slope = dh * vec_ref[GAIN1]
        dx[rows, :] = (
            dmid[rows, :]
            + inv
            * (
                slope
                - jnp.mean(slope, axis=-1, keepdims=True)
                - xhat * jnp.mean(slope * xhat, axis=-1, keepdims=True)
            )
        ).astype(bf16)
        for row, value in enumerate((dh * xhat, dh)):
            total[first + row : first + row + 1, :] += jnp.sum(value, axis=0, keepdims=True)
        return carry

    total[:first, :] = early_ref[...]
    total[first:, :] = jnp.zeros((total.shape[0] - first, d), f32)
    lax.fori_loop(0, half, send, 0)
    for c in loads:
        c.wait()
    steps = chain_steps(ready)
    for step in steps[0]:
        step()
    reduces[0].forward()
    lax.fori_loop(0, half, norm, 0)
    swaps[0].start()
    for some in steps[1:]:
        for step in some:
            step()
    for job in reduces[1:]:
        job.forward()
    to_owners.start()
    swaps[0].wait()
    total[...] += came[0]
    swaps[1].start()
    reduces[0].collect()
    for c in last[:2]:
        c.start()
    swaps[1].wait()
    total[...] += came[1]
    swaps[2].start()
    for i in range(1, parts):
        reduces[i].collect()
        for c in last[2 * i : 2 * i + 2]:
            c.start()
    swaps[2].wait()
    total[...] += came[2]
    small.start()
    for some in chain_steps(last):
        for step in some:
            step()
    small.inward()
    for c in ready + last:
        c.outward()
    small.across()
    small.outward()
    for job in ready + last + [small]:
        job.finish()
    for job in reduces:
        job.close()
    for j in range(half):
        swap(j)[1].wait_send()
    to_owners.finish()


def back_call(grads, w, vec, h, early, x, dmid, jobs, clips, number):
    n, d = x.shape
    size = n // 2
    cols = grads.shape[1]
    groups = lax.axis_size("shard")
    owned = d // groups
    parts = 2
    rows = early.shape[0] + 8
    small = pltpu.VMEM((rows, d), f32)
    piece = owned // parts // 2
    vmem = pl.BlockSpec(memory_space=pltpu.VMEM)
    hbm = pl.BlockSpec(memory_space=pl.ANY)
    return pl.pallas_call(
        functools.partial(back_kernel, jobs=jobs, parts=parts),
        in_specs=[vmem] * 5 + [hbm] * 2 + jobs.in_specs(),
        out_specs=[hbm, vmem, hbm] + jobs.in_specs(),
        out_shape=[
            jax.ShapeDtypeStruct((clips, size // clips, d), bf16),
            jax.ShapeDtypeStruct((2, rows, d), f32),
            jax.ShapeDtypeStruct((2, owned, cols), bf16),
        ]
        + jobs.out_shapes(),
        scratch_shapes=[
            pltpu.VMEM((size, d), bf16),
            pltpu.VMEM((size, d), f32),
            pltpu.VMEM((size, d), bf16),
            pltpu.VMEM((size, d), bf16),
            pltpu.VMEM((size, d), bf16),
            pltpu.VMEM((d, cols), bf16),
            pltpu.VMEM((owned, cols), bf16),
            small,
            pltpu.VMEM((3, rows, d), f32),
        ]
        + [small] * 3
        + [pltpu.VMEM((piece, cols), bf16)] * (16 * parts)
        + jobs.scratch(64),
        compiler_params=comm_params(number, 62),
        cost_estimate=cost(4 * n * w.size, 20 * n * d),
        name="back",
    )(grads, w, vec, h, early, x, dmid, *jobs.sources())


def place_kernel(*refs, groups):
    up_refs, down_refs = refs[:3], refs[3:6]
    out_ref, in_ref = refs[6:8]
    up, down, wo = refs[8:11]
    qkv = refs[11:14]
    places = refs[14]
    t = pl.program_id(0)

    def put(target, axis, pieces):
        first = 0
        for value in pieces:
            size = value.shape[axis]
            span = slice(first, first + size)
            if axis:
                target[:, span] = value.astype(f32)
            else:
                target[span, :] = value.astype(f32)
            first += size

    halves = [jnp.concatenate([up_refs[1][c], up_refs[2][c]], axis=0) for c in range(2)]
    put(up, 1, [up_refs[0][0], halves[0], up_refs[0][1], halves[1]])
    put(down, 0, [r[c] for c in range(2) for r in down_refs])
    put(wo, 0, [out_ref[c] for c in range(2)])
    rows = in_ref.shape[1]
    width = in_ref.shape[2] // 3
    part = width // groups

    @pl.when(t == 0)
    def _():
        row = lax.broadcasted_iota(jnp.int32, (width, 2 * width), 0)
        ahead = lax.broadcasted_iota(jnp.int32, (width, 2 * width), 1) - row
        for c in range(2):
            place = jnp.zeros((width, 2 * width), f32)
            for s in range(groups):
                here = (row >= s * part) & (row < (s + 1) * part) & (ahead == (s + c) * part)
                place = jnp.where(here, 1.0, place)
            places[c] = place.astype(bf16)

    for i, out in enumerate(qkv):
        cols = slice(i * width, (i + 1) * width)
        out[...] = dot(in_ref[0, :, cols], places[0]) + dot(in_ref[1, :, cols], places[1])


def place_call(ups, downs, wo, qkv, groups):
    steps = 5
    own_d, cols = qkv.shape[1:]
    d = downs[0].shape[2]
    own_f = 2 * sum(a.shape[1] for a in downs)
    take = [pl.BlockSpec((2, a.shape[1], a.shape[2] // groups), lambda i: (0, 0, jnp.minimum(i, groups - 1))) for a in ups]
    wide = d // steps
    per = own_d // steps
    ff = 2 * ups[0].shape[2] + 2 * ups[1].shape[2]
    return pl.pallas_call(
        functools.partial(place_kernel, groups=groups),
        grid=(steps,),
        in_specs=take
        + [pl.BlockSpec((2, a.shape[1], wide), lambda i: (0, 0, i)) for a in downs]
        + [
            pl.BlockSpec((2, wo.shape[1], wide), lambda i: (0, 0, i)),
            pl.BlockSpec((2, per, cols), lambda i: (0, i, 0)),
        ],
        out_specs=[
            pl.BlockSpec((own_d, ff // groups), lambda i: (0, jnp.minimum(i, groups - 1))),
            pl.BlockSpec((own_f, wide), lambda i: (0, i)),
            pl.BlockSpec((own_d, wide), lambda i: (0, i)),
        ]
        + [pl.BlockSpec((per, d), lambda i: (i, 0))] * 3,
        out_shape=[
            jax.ShapeDtypeStruct((own_d, ff), f32),
            jax.ShapeDtypeStruct((own_f, d), f32),
            jax.ShapeDtypeStruct((own_d, d), f32),
        ]
        + [jax.ShapeDtypeStruct((own_d, d), f32)] * 3,
        scratch_shapes=[pltpu.VMEM((2, cols // 3, d), bf16)],
        compiler_params=params(),
        name="place",
    )(*ups, *downs, wo, qkv)


def own_sum(blocks, others):
    shard = lax.axis_index("shard")
    total = lax.dynamic_index_in_dim(blocks, shard, 0, keepdims=False).astype(f32)
    for i in range(others.shape[0]):
        total = total + others[i].astype(f32)
    return total.astype(bf16)


def over_reps(own):
    planes = lax.axis_size("rep") // 2
    sums = lax.psum_scatter(
        own,
        "rep",
        scatter_dimension=0,
        tiled=True,
        axis_index_groups=[[2 * z + c for z in range(planes)] for c in range(2)],
    )
    both = lax.all_gather(sums, "rep", axis=0)
    rows, cols = sums.shape
    return both.reshape(planes, 2, rows, cols).transpose(1, 0, 2, 3).reshape(2, planes * rows, cols)


def on_device(
    tokens,
    lengths,
    cotangent,
    first_gain,
    first_shift,
    query_weight,
    query_bias,
    key_weight,
    value_weight,
    value_bias,
    out_weight,
    out_bias,
    second_gain,
    second_shift,
    up_weight,
    up_bias,
    down_weight,
    down_bias,
):
    g = lax.axis_size("shard")
    shard = lax.axis_index("shard")
    core = lax.rem(lax.axis_index("rep"), 2)
    cl, rows, d = tokens.shape
    n = 2 * cl * rows
    ff = up_weight.shape[1]
    own_d = d // g
    own_f = ff // g
    attn_cols = own_d // 2
    ffn_cols = own_f // 2
    width = d // 2
    heads = width // HEAD
    wide = pl.cdiv(width, 128) * 128 + 128
    first_n = ffn_cols * 2 // 5
    pieces = ((0, first_n), (first_n, ffn_cols))

    positions = shard * rows + jnp.arange(rows, dtype=jnp.int32)
    live = positions[None, :] < lengths[:, None]
    masked = jnp.where(live[:, :, None], cotangent, jnp.zeros_like(cotangent))

    def core_of():
        return lax.rem(lax.axis_index("rep"), 2)

    def core_cols(w, size, a, b):
        def of(c):
            return jnp.concatenate([w[:, (2 * s + c) * size + a : (2 * s + c) * size + b] for s in range(g)], axis=1)

        return jnp.where(core == 0, of(0), of(1))

    vectors = (first_gain, first_shift, query_bias, value_bias, out_bias, second_gain, second_shift, down_bias)
    lens = jnp.pad(lengths.astype(f32), (0, own_d - cl)).reshape(1, own_d)
    small = jnp.concatenate(
        [jnp.stack(vectors).astype(f32), lens, up_bias.astype(f32).reshape(-1, own_d)], axis=0
    )
    small = jnp.pad(small, ((0, 16 - small.shape[0]), (0, -own_d % 128)))
    qkv_own = jnp.concatenate(
        [core_cols(w, attn_cols, 0, attn_cols) for w in (query_weight, key_weight, value_weight)], axis=1
    )
    jobs = Jobs(
        (ToClip, tokens, (n, d)),
        (Gather, qkv_own, (g,) + qkv_own.shape),
        (Gather, small, (g,) + small.shape),
    )
    x, w_qkv, smalls, other_small = exchange_call(jobs, small, 0, "first_exchange")
    w_qkv = w_qkv.reshape(d, 3 * width)
    vec = smalls[:, :, :own_d].transpose(1, 0, 2).reshape(16, d)
    near = lax.div(shard, cl) == core
    lens = jnp.where(near, small[LENGTHS], other_small[LENGTHS])[0]
    length = lens[lax.rem(shard, cl)].astype(jnp.int32).reshape(1)

    def bias_cols(b):
        return lax.dynamic_index_in_dim(vec[b].reshape(1, g, 2, attn_cols), core, 2).reshape(1, width)

    bias = jnp.concatenate([bias_cols(QBIAS), jnp.zeros((1, width), f32), bias_cols(VBIAS)], axis=1)
    ubias = lax.dynamic_index_in_dim(
        vec[UBIAS : UBIAS + own_f // own_d].reshape(-1, g, own_d).transpose(1, 0, 2).reshape(g, 2, ffn_cols),
        core,
        1,
        keepdims=False,
    )
    ups = [core_cols(up_weight, ffn_cols, a, b) for a, b in pieces]

    def half_rows(w, first=0, last=None):
        half = w.shape[0] // 2
        size = (half if last is None else last) - first

        def view(ref):
            return ref.at[pl.ds(pl.multiple_of(core_of() * half + first, 16), size)]

        return size, view

    def gathered(a, part=None):
        if part is None:
            return (Gather, a, (g,) + a.shape)
        return (Gather, a, (g, part[0]) + a.shape[1:], part[1])

    jobs = Jobs((ToClip, masked, (n, d)))
    h1, q, k, v, dz = qkv_call(x, vec, w_qkv, bias, wide, jobs, 9)
    jobs = Jobs(
        gathered(out_weight, half_rows(out_weight)),
        gathered(ups[0]),
        gathered(down_weight, half_rows(down_weight, *pieces[0])),
    )
    o, lse, w_out, up, down = attn_fwd_call(length, q, k, v, width, heads, jobs, 1)
    w_out = w_out.reshape(width, d)
    jobs = Jobs(gathered(ups[1]))
    mid, h2, o_wide, up1 = middle_call(o, w_out, x, vec, wide, jobs, 2)

    def hidden_bias(piece):
        return ubias[:, piece[0] : piece[1]].reshape(1, -1)

    fast = g == 4 and lax.axis_size("rep") == 8

    def to_owners(a):
        if fast:
            return (Reduce, a, a.shape[1:])
        return (Owners, a, (g - 1,) + a.shape[1:])

    def owned(a, came):
        return came if fast else own_sum(a, came)

    def chained(a):
        return (Chain, a, (2,) + a.shape)

    def upper(a):
        half = a.shape[0] // 2
        return [a[:half], a[half:]]

    jobs = Jobs(gathered(down_weight, half_rows(down_weight, *pieces[1])))
    out, dh2, dup0, ddn0, dub0, down1 = ffn_call(
        h2, dz, up.reshape(d, -1), hidden_bias(pieces[0]), down.reshape(-1, d), None, False, jobs, 3, "hidden0"
    )
    dup0, ddn0 = dup0.reshape(g, own_d, -1), ddn0.reshape(g, -1, d)
    jobs = Jobs(to_owners(dup0), to_owners(ddn0))
    out, dh2, dup1, ddn1, dub1, dup0_in, ddn0_in = ffn_call(
        h2, dz, up1.reshape(d, -1), hidden_bias(pieces[1]), down1.reshape(-1, d), (out, dh2), True, jobs, 4, "hidden1"
    )
    dup1, ddn1 = dup1.reshape(g, own_d, -1), ddn1.reshape(g, -1, d)
    up0_own, down0_own = owned(dup0, dup0_in), owned(ddn0, ddn0_in)

    jobs = Jobs(to_owners(dup1))
    dmid, do, dwo, sums2, layer_own, dup1_in = second_back_call(mid, dh2, out, dz, vec, w_out, o, wide, jobs, 5)
    dwo = dwo.reshape(g, -1, d)
    up1_own = owned(dup1, dup1_in)

    jobs = [to_owners(ddn1), to_owners(dwo), (FromClip, layer_own, (cl, rows, d))]
    if fast:
        jobs += [chained(a) for a in [up0_own, down0_own] + upper(up1_own)]
    grads, bias_sums, ddn1_in, dwo_in, layer_out, *sums0 = attn_bwd_call(
        length, q, k, v, o_wide, do, lse, width, heads, Jobs(*jobs), 6
    )
    down1_own, out_own_grad = owned(ddn1, ddn1_in), owned(dwo, dwo_in)

    def spread(v, size):
        out = jnp.zeros((g, 2, size), f32)
        return lax.dynamic_update_index_in_dim(out, v.reshape(g, size), core, 1)

    ub_sums = jnp.concatenate([dub0.reshape(g, -1), dub1.reshape(g, -1)], axis=1)
    early = jnp.concatenate(
        [
            spread(bias_sums[0, :width], attn_cols).reshape(1, d),
            spread(bias_sums[0, 2 * width :], attn_cols).reshape(1, d),
            sums2[:4] * 0.5,
            spread(ub_sums, ffn_cols).reshape(-1, d),
        ],
        axis=0,
    )
    early = jnp.pad(early, ((0, -early.shape[0] % 8), (0, 0)))

    if fast:
        jobs = Jobs(*[chained(a) for a in upper(down1_own) + [out_own_grad]])
        tokens_grad, smalls, qkv_all, *sums = back_call(grads, w_qkv, vec, h1, early, x, dmid, jobs, cl, 7)
        up_grad, down_grad, out_grad, *qkv_grads = place_call(
            (sums0[0], sums0[2], sums0[3]), (sums0[1], sums[0], sums[1]), sums[2], qkv_all, g
        )
        smalls = lax.dynamic_index_in_dim(smalls, core, 0, keepdims=False)
    else:
        dwqkv = dw_call(h1, grads).reshape(g, own_d, 3 * width)
        jobs = Jobs(to_owners(dwqkv))
        dx, sums1, dwqkv_in = first_back_call(grads, w_qkv, vec, x, dmid, jobs, 7)
        jobs = Jobs((FromClip, dx, (cl, rows, d)))
        tokens_grad, _ = exchange_call(jobs, sums1, 8, "last_exchange")
        ups_all = [over_reps(a).reshape(2, own_d, g, -1) for a in (up0_own, up1_own)]
        up_grad = jnp.concatenate(ups_all, axis=3).transpose(1, 2, 0, 3).reshape(own_d, ff).astype(f32)
        downs_all = [over_reps(a) for a in (down0_own, down1_own)]
        down_grad = jnp.concatenate(downs_all, axis=1).reshape(own_f, d).astype(f32)
        out_grad = over_reps(out_own_grad).reshape(own_d, d).astype(f32)
        qkv_all = over_reps(owned(dwqkv, dwqkv_in)).reshape(2, own_d, 3, g, attn_cols)
        qkv_grads = [qkv_all[:, :, i].transpose(1, 2, 0, 3).reshape(own_d, d).astype(f32) for i in range(3)]
        smalls = lax.psum(jnp.concatenate([early, sums1], axis=0), ("rep", "shard"))

    mine = lax.dynamic_slice_in_dim(smalls, shard * own_d, own_d, 1)
    s_qb, s_vb, s_gain2, s_shift2, s_ob, s_db = [mine[i] for i in range(6)]
    s_gain1, s_shift1 = [mine[early.shape[0] + i] for i in range(2)]
    s_ub = lax.dynamic_slice_in_dim(smalls[6 : 6 + ff // d].reshape(-1), shard * own_f, own_f, 0)

    return (
        layer_out,
        tokens_grad,
        s_gain1,
        s_shift1,
        qkv_grads[0],
        s_qb,
        qkv_grads[1],
        qkv_grads[2],
        s_vb,
        out_grad,
        s_ob,
        s_gain2,
        s_shift2,
        up_grad,
        s_ub,
        down_grad,
        s_db,
    )


def solution(mesh):
    row, mat, vec = P("rep", "shard", None), P("shard", None), P("shard")
    return jax.shard_map(
        on_device,
        mesh=mesh,
        in_specs=(row, P("rep"), row, vec, vec, mat, vec, mat, mat, vec, mat, vec, vec, vec, mat, vec, mat, vec),
        out_specs=(row, row, vec, vec, mat, vec, mat, mat, vec, mat, vec, vec, vec, mat, vec, mat, vec),
        check_vma=False,
    )
```

```python
import functools
import math

import jax
import jax.numpy as jnp
from jax import lax
from jax.experimental import pallas as pl
from jax.experimental.pallas import tpu as pltpu
from jax.sharding import PartitionSpec as P

HEAD = 80
WIN = 256
AUG = 192
EPS = 1e-5
SCALE = HEAD**-0.5
SCALE2 = SCALE * math.log2(math.e)
DEAD = -1e30
ROWS = 256
GAIN1, SHIFT1, QBIAS, VBIAS, OBIAS, GAIN2, SHIFT2, DBIAS, LENGTHS = [slice(i, i + 1) for i in range(9)]
UBIAS = 9
FFN_TILE = 512
FFN_ROWS = 768
PAIR_SHARE = 3
f32 = jnp.float32
bf16 = jnp.bfloat16
MESH = pl.DeviceIdType.MESH

ERF_P = 0.35
ERF_C = (0.19458996, 0.23381038, -0.00165479, 0.67243411, -0.66868964, 0.76616445, -0.19665448)


def params(limit=60):
    return pltpu.CompilerParams(vmem_limit_bytes=limit * 2**20)


def cost(flops, size):
    return pl.CostEstimate(flops=int(flops), bytes_accessed=int(size), transcendentals=0)


def dot(a, b):
    return jnp.dot(a, b, preferred_element_type=f32)


def dot_nt(a, b):
    return lax.dot_general(a, b, (((1,), (1,)), ((), ())), preferred_element_type=f32)


def dot_tn(a, b):
    return lax.dot_general(a, b, (((0,), (0,)), ((), ())), preferred_element_type=f32)


def gelu_pair(a):
    expo = jnp.exp2(a * a * (-0.5 * math.log2(math.e)))
    t = 1.0 / (1.0 + jnp.abs(a) * (ERF_P * math.sqrt(0.5)))
    total = ERF_C[-1]
    for c in ERF_C[-2::-1]:
        total = total * t + c
    tail = 0.5 * expo * (total * t)
    cdf = jnp.where(a >= 0, 1.0 - tail, tail)
    return a * cdf, cdf + a * (expo * (1.0 / math.sqrt(2.0 * math.pi)))


def whole(shape):
    return pl.BlockSpec(shape, lambda *_: (0,) * len(shape))


def once(shape):
    return pl.BlockSpec(shape, lambda *_: (0,) * len(shape), pipeline_mode=pl.Buffered(1))


def row_block(rows, cols):
    return pl.BlockSpec((rows, cols), lambda i: (i, 0))


def standardize(x):
    centred = x - jnp.mean(x, axis=-1, keepdims=True)
    inv = lax.rsqrt(jnp.mean(centred * centred, axis=-1, keepdims=True) + EPS)
    return centred * inv, inv


class Link:
    def __init__(self, sems):
        self.send, self.recv, self.local = sems
        self.next = 0
        self.next_local = 0
        self.groups = lax.axis_size("shard")
        self.rep = lax.axis_index("rep")
        self.shard = lax.axis_index("shard")
        self.core = lax.rem(self.rep, 2)
        self.half = self.groups // 2

    def meet_plane(self, pair=False):
        barrier = pltpu.get_barrier_semaphore()
        base = self.rep - self.core
        for c in range(2):
            for p in range(self.groups):
                if c or p:
                    to = (base + (self.core ^ c), self.shard ^ p)
                    pl.semaphore_signal(barrier, inc=1, device_id=to, device_id_type=MESH)
        if pair:
            pl.semaphore_signal(barrier, inc=1, device_id=self.pair(), device_id_type=MESH)
        pl.semaphore_wait(barrier, 2 * self.groups - 1 + int(pair))

    def pair(self):
        return (self.rep ^ 2, self.shard)

    def meet_all(self):
        barrier = pltpu.get_barrier_semaphore()
        base = self.rep - self.core
        for c in range(2):
            for p in range(self.groups):
                if c or p:
                    to = (base + (self.core ^ c), self.shard ^ p)
                    pl.semaphore_signal(barrier, inc=1, device_id=to, device_id_type=MESH)
        pl.semaphore_signal(barrier, inc=1, device_id=self.inward(), device_id_type=MESH)

        @pl.when(self.inner())
        def _():
            pl.semaphore_signal(barrier, inc=1, device_id=self.outward(), device_id_type=MESH)
            pl.semaphore_wait(barrier, 2 * self.groups + 1)

        @pl.when(jnp.logical_not(self.inner()))
        def _():
            pl.semaphore_wait(barrier, 2 * self.groups)

    def inner(self):
        plane = lax.div(self.rep, 2)
        return (plane == 1) | (plane == 2)

    def inward(self):
        return (self.rep + jnp.where(self.rep < 4, 2, -2), self.shard)

    def outward(self):
        return (self.rep - jnp.where(self.rep < 4, 2, -2), self.shard)

    def meet_core(self):
        barrier = pltpu.get_barrier_semaphore()
        pl.semaphore_signal(barrier, inc=1, device_id=self.sibling(), device_id_type=MESH)
        pl.semaphore_wait(barrier, 1)

    def sibling(self):
        return (self.rep ^ 1, self.shard)

    def slots(self, count):
        first = self.next
        self.next += count
        return first

    def local_slots(self, count):
        first = self.next_local
        self.next_local += count
        return first

    def remote(self, src, dst, send, recv, to):
        return pltpu.make_async_remote_copy(
            src_ref=src,
            dst_ref=dst,
            send_sem=self.send.at[send],
            recv_sem=self.recv.at[recv],
            device_id=to,
            device_id_type=MESH,
        )

    def here(self, src, dst, slot):
        return pltpu.make_async_copy(src, dst, self.local.at[slot])


class Job:
    @staticmethod
    def buffers(source, shape):
        return []

    def forward(self):
        pass

    def inward(self):
        pass

    def across(self):
        pass

    def outward(self):
        pass


class Staged:
    def __init__(self, link, src, dst, buf):
        slot = link.local_slots(1)
        self.load = link.here(src, buf, slot)
        self.store = link.here(buf, dst, slot)

    def start(self):
        self.load.start()

    def turn(self):
        self.load.wait()
        self.store.start()

    def wait(self):
        self.store.wait()


class Gather(Job):
    def __init__(self, link, src, dst, bufs):
        self.link, self.src, self.dst = link, src, dst
        self.rows = src.shape[0]
        self.base = link.slots(max(4, link.groups - 1))
        self.keep = Staged(link, src, dst.at[link.shard], bufs[0])

    @staticmethod
    def buffers(source, shape):
        return [pltpu.VMEM(shape[1:], source.dtype)]

    def first(self):
        link = self.link
        peers = (1, 2) if link.groups == 4 else range(1, link.groups)
        return [
            link.remote(self.src, self.dst.at[link.shard], self.base + i, self.base + i, (link.rep, link.shard ^ p))
            for i, p in enumerate(peers)
        ]

    def second(self):
        link = self.link
        if link.groups != 4:
            return []
        cut = self.rows // 2
        parts = ((1, 2, pl.ds(0, cut)), (2, 1, pl.ds(cut, self.rows - cut)))
        out = []
        for i, (origin, to, rows) in enumerate(parts):
            ref = self.dst.at[link.shard ^ origin, rows]
            out.append(link.remote(ref, ref, self.base + 2 + i, self.base + 2 + i, (link.rep, link.shard ^ to)))
        return out

    def start(self):
        self.keep.start()
        for c in self.first():
            c.start()

    def forward(self):
        self.keep.turn()
        for c, d in zip(self.first(), self.second()):
            c.wait_recv()
            d.start()

    def finish(self):
        second = self.second()
        for c in self.first():
            if not second:
                c.wait_recv()
            c.wait_send()
        for c in second:
            c.wait()
        self.keep.wait()


class PairGather(Job):
    def __init__(self, link, src, dst, bufs):
        self.link, self.src, self.dst = link, src, dst
        rows = src.shape[0]
        outer = max(rows // PAIR_SHARE // 16, 1) * 16
        second = lax.rem(lax.div(link.rep, 2), 2)
        self.part = pl.ds(pl.multiple_of(second * outer, 16), rows - outer)
        self.alone = pl.ds(pl.multiple_of(second * (rows - outer), 16), outer)
        self.both = pl.ds(outer, rows - 2 * outer)
        self.base = link.slots(7)
        self.keep = Staged(link, src, dst.at[link.shard], bufs[0])

    @staticmethod
    def buffers(source, shape):
        return [pltpu.VMEM(shape[1:], source.dtype)]

    def step(self, src, dst, slot, to):
        return self.link.remote(src, dst, self.base + slot, self.base + slot, to)

    def near(self, bit):
        return (self.link.rep, self.link.shard ^ bit)

    def first(self):
        mine = self.dst.at[self.link.shard, self.part]
        return [self.step(self.src.at[self.part], mine, i, self.near(i + 1)) for i in range(2)]

    def second(self):
        one = self.dst.at[self.link.shard ^ 1, self.alone]
        two = self.dst.at[self.link.shard ^ 2, self.both]
        return [self.step(one, one, 2, self.near(2)), self.step(two, two, 3, self.near(1))]

    def third(self):
        out = []
        for i in range(3):
            ref = self.dst.at[self.link.shard ^ (i + 1), self.alone]
            out.append(self.step(ref, ref, 4 + i, self.link.pair()))
        return out

    def start(self):
        self.keep.start()
        for c in self.first():
            c.start()

    def forward(self):
        self.keep.turn()
        for c, d, e in zip(self.first(), self.second(), self.third()):
            c.wait_recv()
            d.start()
            e.start()

    def inward(self):
        self.second()[0].wait_recv()
        self.third()[2].start()

    def finish(self):
        for c in self.first():
            c.wait_send()
        one, two = self.second()
        one.wait_send()
        two.wait()
        for c in self.third():
            c.wait()
        self.keep.wait()


class ToClip(Job):
    def __init__(self, link, src, dst, bufs):
        self.link, self.src, self.dst = link, src, dst
        self.rows = src.shape[1]
        self.base = link.slots(link.half + 1)
        self.keep = link.local_slots(1)
        self.buf = bufs[0]

    @staticmethod
    def buffers(source, shape):
        return [pltpu.VMEM(source.shape[1:], source.dtype)]

    def copy(self, j):
        link = self.link
        core = lax.div(link.shard, link.half)
        to = (link.rep - link.core + core, link.core * link.half + j)
        mine = (core == link.core) & (link.core * link.half + j == link.shard)
        dst = self.dst.at[pl.ds(pl.multiple_of(link.shard * self.rows, self.rows), self.rows)]
        there = link.remote(self.src.at[j], dst, self.base + j, self.base + lax.rem(link.shard, link.half), to)
        return mine, there, link.here(self.src.at[j], self.buf, self.keep)

    def arrival(self, t):
        link = self.link
        source = link.core * link.half + t
        mine = (lax.div(link.shard, link.half) == link.core) & (source == link.shard)
        dst = self.dst.at[pl.ds(pl.multiple_of(source * self.rows, self.rows), self.rows)]
        there = link.remote(self.src.at[0], dst, self.base, self.base + t, link.sibling())
        return mine, there, link.here(self.buf, dst, self.keep)

    def to_sibling(self):
        link = self.link
        size = link.half * self.rows
        rows = pl.ds(pl.multiple_of(link.core * size, size), size)
        slot = self.base + link.half
        return link.remote(self.dst.at[rows], self.dst.at[rows], slot, slot, link.sibling())

    def start(self):
        for j in range(self.link.half):
            mine, there, here = self.copy(j)
            pl.when(mine)(here.start)
            pl.when(jnp.logical_not(mine))(there.start)

    def forward(self):
        for t in range(self.link.half):
            mine, there, here = self.arrival(t)

            @pl.when(mine)
            def _():
                self.copy(0)[2].wait()
                here.start()
                here.wait()

            pl.when(jnp.logical_not(mine))(there.wait_recv)
        self.to_sibling().start()

    def finish(self):
        self.to_sibling().wait()
        for j in range(self.link.half):
            mine, there, _ = self.copy(j)
            pl.when(jnp.logical_not(mine))(there.wait_send)


class FromClip(Job):
    def __init__(self, link, src, dst, bufs):
        self.link, self.src, self.dst = link, src, dst
        self.rows = dst.shape[1]
        self.base = link.slots(link.half)
        self.keep = link.local_slots(1)
        self.buf = bufs[0]

    @staticmethod
    def buffers(source, shape):
        return [pltpu.VMEM(shape[1:], source.dtype)]

    def copy(self, t):
        link = self.link
        core = lax.div(link.shard, link.half)
        shard = link.core * link.half + t
        mine = (core == link.core) & (shard == link.shard)
        clip = lax.rem(link.shard, link.half)
        src = self.src.at[pl.ds(t * self.rows, self.rows)]
        dst = self.dst.at[clip]
        there = link.remote(src, dst, self.base + t, self.base + clip, (link.rep - link.core + core, shard))
        return mine, there, link.here(src, self.buf, self.keep)

    def arrival(self, j):
        link = self.link
        mine = (lax.div(link.shard, link.half) == link.core) & (link.core * link.half + j == link.shard)
        src = self.src.at[pl.ds(0, self.rows)]
        there = link.remote(src, self.dst.at[j], self.base, self.base + j, link.sibling())
        return mine, there, link.here(self.buf, self.dst.at[j], self.keep)

    def start(self):
        for t in range(self.link.half):
            mine, there, here = self.copy(t)
            pl.when(mine)(here.start)
            pl.when(jnp.logical_not(mine))(there.start)

    def finish(self):
        for t in range(self.link.half):
            mine, there, here = self.copy(t)
            pl.when(jnp.logical_not(mine))(there.wait_send)
        for j in range(self.link.half):
            mine, there, here = self.arrival(j)

            @pl.when(mine)
            def _():
                self.copy(0)[2].wait()
                here.start()
                here.wait()

            pl.when(jnp.logical_not(mine))(there.wait_recv)


class Owners(Job):
    def __init__(self, link, src, dst, bufs):
        self.link, self.src, self.dst = link, src, dst
        self.base = link.slots(link.groups - 1)

    def copies(self):
        link = self.link
        return [
            link.remote(
                self.src.at[link.shard ^ p],
                self.dst.at[p - 1],
                self.base + p - 1,
                self.base + p - 1,
                (link.rep, link.shard ^ p),
            )
            for p in range(1, link.groups)
        ]

    def start(self):
        for c in self.copies():
            c.start()

    def finish(self):
        for c in self.copies():
            c.wait()


def add_low(a, b):
    return (a.astype(f32) + b.astype(f32)).astype(bf16)


class Reduce(Job):
    def __init__(self, link, src, dst, bufs):
        self.link, self.src, self.dst = link, src, dst
        self.base = link.slots(6)
        self.keep = link.local_slots(4)
        self.half = dst.shape[0] // 2
        self.pass_in, self.pass_sum, self.near, self.far, self.own = (bufs[2 * i : 2 * i + 2] for i in range(5))

    @staticmethod
    def buffers(source, shape):
        half = pltpu.VMEM((source.shape[1] // 2, source.shape[2]), source.dtype)
        return [half] * 10

    def block(self, i, part):
        rows = pl.ds(part * self.half, self.half)
        return self.src.at[self.link.shard ^ i, rows]

    def hops(self):
        link = self.link
        x, y = (link.rep, link.shard ^ 1), (link.rep, link.shard ^ 2)
        plan = (
            (self.block(3, 0), self.pass_in[0], x),
            (self.block(3, 1), self.pass_in[1], y),
            (self.block(1, 0), self.near[0], x),
            (self.block(2, 1), self.near[1], y),
        )
        return [link.remote(s, d, self.base + i, self.base + i, to) for i, (s, d, to) in enumerate(plan)]

    def later(self):
        link = self.link
        x, y = (link.rep, link.shard ^ 1), (link.rep, link.shard ^ 2)
        plan = zip(self.pass_sum, self.far, (y, x))
        return [link.remote(s, d, self.base + 4 + i, self.base + 4 + i, to) for i, (s, d, to) in enumerate(plan)]

    def loads(self):
        plan = (
            (self.block(2, 0), self.pass_sum[0]),
            (self.block(1, 1), self.pass_sum[1]),
            (self.block(0, 0), self.own[0]),
            (self.block(0, 1), self.own[1]),
        )
        return [self.link.here(s, d, self.keep + i) for i, (s, d) in enumerate(plan)]

    def store(self, part):
        rows = pl.ds(part * self.half, self.half)
        return self.link.here(self.own[part], self.dst.at[rows], self.keep + part)

    def start(self):
        for c in self.hops():
            c.start()
        for c in self.loads():
            c.start()

    def forward(self):
        hops, loads, later = self.hops(), self.loads(), self.later()
        for i in range(2):
            loads[i].wait()
            hops[i].wait_recv()
            self.pass_sum[i][...] = add_low(self.pass_sum[i][...], self.pass_in[i][...])
            later[i].start()

    def collect(self):
        hops, loads, later = self.hops(), self.loads(), self.later()
        for i in range(2):
            loads[2 + i].wait()
            hops[2 + i].wait_recv()
            later[i].wait_recv()
            total = self.own[i][...].astype(f32) + self.near[i][...].astype(f32) + self.far[i][...].astype(f32)
            self.own[i][...] = total.astype(bf16)
            self.store(i).start()
        for i in range(2):
            self.store(i).wait()

    def finish(self):
        self.collect()
        self.close()

    def close(self):
        for c in self.hops() + self.later():
            c.wait_send()


class Chain(Job):
    def __init__(self, link, src, dst, bufs):
        self.link, self.src, self.dst = link, src, dst
        self.own, self.one, self.two = bufs
        self.base = link.slots(4)
        self.keep = link.local_slots(2)

    @staticmethod
    def buffers(source, shape):
        return [pltpu.VMEM(shape[1:], source.dtype)] * 3

    def step(self, src, dst, slot, to):
        return self.link.remote(src, dst, self.base + slot, self.base + slot, to)

    def steps(self):
        link = self.link
        return (
            self.step(self.src, self.one, 0, link.inward()),
            self.step(self.own, self.two, 1, link.inward()),
            self.step(self.one, self.two, 2, link.outward()),
        )

    def share(self, ref):
        link = self.link
        place = self.dst.at[link.core]
        return self.step(ref, place, 3, link.sibling()), link.here(ref, place, self.keep + 1)

    def start(self):
        inner = self.link.inner()
        pl.when(inner)(self.link.here(self.src, self.own, self.keep).start)
        pl.when(jnp.logical_not(inner))(self.steps()[0].start)

    def add(self, a, b):
        return (a[...].astype(f32) + b[...].astype(f32)).astype(a.dtype)

    def sent(self):
        pl.when(jnp.logical_not(self.link.inner()))(self.steps()[0].wait_send)

    def inward(self):
        @pl.when(self.link.inner())
        def _():
            steps = self.steps()
            self.link.here(self.src, self.own, self.keep).wait()
            steps[0].wait_recv()
            self.own[...] = self.add(self.own, self.one)
            steps[1].start()

    def across(self):
        @pl.when(self.link.inner())
        def _():
            steps = self.steps()
            steps[1].wait_recv()
            self.one[...] = self.add(self.own, self.two)
            steps[2].start()
            for c in self.share(self.one):
                c.start()

    def outward(self):
        @pl.when(jnp.logical_not(self.link.inner()))
        def _():
            self.steps()[2].wait_recv()
            for c in self.share(self.two):
                c.start()

    def finish(self):
        swap, here = self.share(self.one)
        swap.wait()
        here.wait()
        inner = self.link.inner()

        @pl.when(inner)
        def _():
            self.steps()[1].wait_send()
            self.steps()[2].wait_send()


def chain_steps(chains):
    lists = []
    for i in range(len(chains) + 1):
        lists.append(
            [step for c in chains[i : i + 1] for step in (c.inward, c.sent)]
            + [c.start for c in chains[i + 1 : i + 2]]
            + [c.across for c in chains[max(i - 1, 0) : i]]
        )
    return lists


def gather_steps(gathers):
    lists = []
    for i in range(len(gathers) + 2):
        lists.append(
            [c.start for c in gathers[i : i + 1]]
            + [c.forward for c in gathers[max(i - 1, 0) : i]]
            + [c.inward for c in gathers[max(i - 2, 0) : max(i - 1, 0)]]
        )
    return lists


def run(steps):
    for step in steps:
        step()


def split_gathers(bound):
    gathers = [job for job in bound if isinstance(job, (Gather, PairGather))]
    return gathers, [job for job in bound if job not in gathers]


class Jobs:
    def __init__(self, *jobs):
        self.jobs = [(job + (None,))[:4] for job in jobs]
        self.pairs = any(job[0] is PairGather for job in jobs)
        self.bufs = [kind.buffers(a, shape) for kind, a, shape, _ in self.jobs]

    def sources(self):
        return [a for _, a, _, _ in self.jobs]

    def in_specs(self):
        return [pl.BlockSpec(memory_space=pl.ANY)] * len(self.jobs)

    def out_shapes(self):
        return [jax.ShapeDtypeStruct(shape, a.dtype) for _, a, shape, _ in self.jobs]

    def scratch(self, extra=0):
        groups = lax.axis_size("shard")
        remote = len(self.jobs) * max(7, groups) + extra
        return [b for bufs in self.bufs for b in bufs] + [
            pltpu.SemaphoreType.DMA((remote,)),
            pltpu.SemaphoreType.DMA((remote,)),
            pltpu.SemaphoreType.DMA((4 * len(self.jobs) + extra + 1,)),
        ]

    def bind(self, rest, srcs, dsts):
        rest = list(rest)
        bufs = []
        for shapes in self.bufs:
            bufs.append([rest.pop(0) for _ in shapes])
        link = Link(rest[:3])
        bound = [
            kind(link, view(a) if view else a, b, c) for (kind, _, _, view), a, b, c in zip(self.jobs, srcs, dsts, bufs)
        ]
        return link, bound, rest[3:]


def comm_params(number, limit=60):
    return pltpu.CompilerParams(
        vmem_limit_bytes=limit * 2**20, collective_id=number, has_side_effects=True
    )


def exchange_call(jobs, sibling, number, name):
    count = len(jobs.jobs)

    def kernel(*refs):
        srcs, mine = refs[:count], refs[count]
        dsts, other = refs[count + 1 : 2 * count + 1], refs[2 * count + 1]
        link, bound, _ = jobs.bind(refs[2 * count + 2 :], srcs, dsts)
        slot = link.slots(1)
        swap = link.remote(mine, other, slot, slot, link.sibling())
        link.meet_plane(jobs.pairs)
        swap.start()
        gathers, others = split_gathers(bound)
        steps = gather_steps(gathers)
        run([job.start for job in others] + steps[0])
        for i, some in enumerate(steps[1:]):
            if i == 1:
                run([job.forward for job in others])
            run(some)
        run([job.finish for job in bound])
        swap.wait()

    return pl.pallas_call(
        kernel,
        in_specs=jobs.in_specs() + [pl.BlockSpec(memory_space=pl.ANY)],
        out_specs=[pl.BlockSpec(memory_space=pl.ANY)] * (count + 1),
        out_shape=jobs.out_shapes() + [jax.ShapeDtypeStruct(sibling.shape, sibling.dtype)],
        scratch_shapes=jobs.scratch(1),
        compiler_params=comm_params(number),
        name=name,
    )(*jobs.sources(), sibling)


def qkv_kernel(x_ref, vec_ref, bias_ref, wq_ref, wk_ref, wv_ref, h_ref, q_ref, k_ref, v_ref):
    xhat, _ = standardize(x_ref[...].astype(f32))
    h = (xhat * vec_ref[GAIN1] + vec_ref[SHIFT1]).astype(bf16)
    h_ref[...] = h
    for i, (w_ref, ref) in enumerate(((wq_ref, q_ref), (wk_ref, k_ref), (wv_ref, v_ref))):
        width = w_ref.shape[1]
        z = dot(h, w_ref[...]) + bias_ref[:, i * width : (i + 1) * width]
        ref[:, :width] = z.astype(bf16)
        ref[:, width:] = jnp.zeros((ref.shape[0], ref.shape[1] - width), bf16)


def qkv_call(x, vec, bias, weights, wide):
    n, d = x.shape
    out = jax.ShapeDtypeStruct((n, wide), bf16)
    return pl.pallas_call(
        qkv_kernel,
        grid=(n // ROWS,),
        in_specs=[row_block(ROWS, d), whole(vec.shape), whole(bias.shape)] + [once(w.shape) for w in weights],
        out_specs=[row_block(ROWS, d)] + [row_block(ROWS, wide)] * 3,
        out_shape=[jax.ShapeDtypeStruct((n, d), bf16), out, out, out],
        compiler_params=params(),
        cost_estimate=cost(6 * n * weights[0].size, 4 * n * d + 6 * weights[0].size + 6 * n * wide),
        name="project",
    )(x, vec, bias, *weights)


def head_window(h):
    start = h * HEAD
    base = (start // 128) * 128
    off = start - base
    lane = lax.broadcasted_iota(jnp.int32, (1, WIN), 1)
    keep = jnp.where((lane >= off) & (lane < off + HEAD), 1.0, 0.0)
    return pl.ds(pl.multiple_of(base, 128), WIN), keep, lane


def put3(x, lane, first, value):
    hi = value.astype(bf16).astype(f32)
    rest = value - hi
    mid = rest.astype(bf16).astype(f32)
    low = rest - mid
    return jnp.where(
        lane == first,
        hi,
        jnp.where(lane == first + 1, mid, jnp.where(lane == first + 2, low, x)),
    )


def key_extra(rows, length):
    lane = lax.broadcasted_iota(jnp.int32, (rows, WIN), 1)
    row = lax.broadcasted_iota(jnp.int32, (rows, WIN), 0)
    dead = jnp.where(row >= length, DEAD, 0.0)
    minus = jnp.where((lane > AUG) & (lane <= AUG + 3), -1.0, 0.0)
    return jnp.where(lane == AUG, dead, minus).astype(bf16)


def attn_fwd_kernel(*refs, bq, jobs):
    count = len(jobs.jobs)
    len_ref, q_ref, k_ref, v_ref = refs[:4]
    o_ref, lse_ref = refs[4 + count : 6 + count]
    acc, kx = refs[6 + 2 * count : 8 + 2 * count]
    link, bound, _ = jobs.bind(refs[8 + 2 * count :], refs[4 : 4 + count], refs[6 + count : 6 + 2 * count])
    h = pl.program_id(0)
    heads = pl.num_programs(0)
    n = q_ref.shape[0]
    width = o_ref.shape[1]

    gathers, others = split_gathers(bound)
    steps = gather_steps(gathers)

    @pl.when(h == 0)
    def _():
        link.meet_plane(jobs.pairs)
        run([job.start for job in others] + steps[0])
        acc[...] = jnp.zeros_like(acc)
        lse_ref[...] = jnp.zeros_like(lse_ref)
        kx[...] = key_extra(n, len_ref[0])

    for number, some in zip((2, 4, 6, 7), steps[1:]):

        @pl.when(h == number * heads // 8)
        def _():
            run(some)

    win, keep, lane = head_window(h)
    low = keep.astype(bf16)
    q_one = jnp.where(lane == AUG, 1.0, 0.0).astype(bf16)
    v_one = jnp.where((lane >= AUG) & (lane < AUG + 3), 1.0, 0.0).astype(bf16)
    k = k_ref[:, win] * low + kx[...]
    v = v_ref[:, win] * low + v_one
    for i in range(n // bq):
        rows = slice(i * bq, (i + 1) * bq)
        s = dot_nt(q_ref[rows, win] * low + q_one, k)
        peak = jnp.max(s, axis=-1, keepdims=True)
        p = jnp.exp2((s - peak) * SCALE2).astype(bf16)
        o = dot(p, v)
        total = o[:, AUG : AUG + 1]
        acc[rows, win] += o * (keep * (1.0 / total))
        here = lax.broadcasted_iota(jnp.int32, (bq, 128), 1) == h
        lse = peak + jnp.log(total) * (1.0 / SCALE)
        lse_ref[rows, :] = jnp.where(here, lse, lse_ref[rows, :])

    @pl.when(h == heads - 1)
    def _():
        o_ref[:, :width] = acc[:, :width].astype(bf16)
        for some in steps[5:]:
            run(some)
        run([job.finish for job in bound])


def attn_fwd_call(length, q, k, v, width, heads, jobs, number):
    n, wide = q.shape
    return pl.pallas_call(
        functools.partial(attn_fwd_kernel, bq=256, jobs=jobs),
        grid=(heads,),
        in_specs=[pl.BlockSpec(memory_space=pltpu.SMEM)] + [whole((n, wide))] * 3 + jobs.in_specs(),
        out_specs=[whole((n, width)), whole((n, 128))] + jobs.in_specs(),
        out_shape=[jax.ShapeDtypeStruct((n, width), bf16), jax.ShapeDtypeStruct((n, 128), f32)] + jobs.out_shapes(),
        scratch_shapes=[pltpu.VMEM((n, wide), f32), pltpu.VMEM((n, WIN), bf16)] + jobs.scratch(),
        compiler_params=comm_params(number),
        cost_estimate=cost(4 * n * n * WIN * heads, 8 * n * wide),
        name="attend",
    )(length, q, k, v, *jobs.sources())


def attn_bwd_kernel(*refs, bk, jobs):
    count = len(jobs.jobs)
    len_ref, q_ref, k_ref, v_ref, o_ref, do_ref, lse_ref = refs[:7]
    g_ref, sum_ref = refs[7 + count : 9 + count]
    dq, dk, dv, part, qa, da, kx = refs[9 + 2 * count : 16 + 2 * count]
    link, bound, _ = jobs.bind(refs[16 + 2 * count :], refs[7 : 7 + count], refs[9 + count : 9 + 2 * count])
    chains = [job for job in bound if isinstance(job, Chain)]
    h = pl.program_id(0)
    n = q_ref.shape[0]

    @pl.when(h == 0)
    def _():
        if chains:
            link.meet_all()
        else:
            link.meet_plane(jobs.pairs)
        for job in bound:
            if job not in chains[1:]:
                job.start()
        for ref in (dq, dk, dv):
            ref[...] = jnp.zeros_like(ref)
        kx[...] = key_extra(n, len_ref[0])

    heads = pl.num_programs(0)

    def at_head(number, steps):
        @pl.when(h == number)
        def _():
            for step in steps:
                step()

    steps = chain_steps(chains) if chains else []
    for number, some in zip((1, 2, 4, 6, 7), steps):
        at_head(number, some)
    at_head(heads - 3, [job.forward for job in bound])

    win, keep, lane = head_window(h)
    low = keep.astype(bf16)
    v_one = jnp.where((lane >= AUG) & (lane < AUG + 3), 1.0, 0.0).astype(bf16)
    for i in range(n // ROWS):
        rows = slice(i * ROWS, (i + 1) * ROWS)
        here = lax.broadcasted_iota(jnp.int32, (ROWS, 128), 1) == h
        lse = jnp.sum(jnp.where(here, lse_ref[rows, :], 0.0), axis=-1, keepdims=True)
        q = q_ref[rows, win].astype(f32) * keep
        qa[rows, :] = jnp.where(lane == AUG, 1.0, put3(q, lane, AUG + 1, lse)).astype(bf16)
        d = do_ref[rows, win].astype(f32) * keep
        delta = jnp.sum(d * o_ref[rows, win].astype(f32), axis=-1, keepdims=True)
        da[rows, :] = put3(d, lane, AUG, -delta).astype(bf16)
    for i in range(n // bk):
        rows = slice(i * bk, (i + 1) * bk)
        k = k_ref[rows, win] * low + kx[rows, :]
        v = v_ref[rows, win] * low + v_one
        p = jnp.exp2(dot_nt(k, qa[...]) * SCALE2)
        ds = (p * dot_nt(v, da[...])).astype(bf16)
        dv[rows, win] += dot(p.astype(bf16), da[...]) * keep
        dk[rows, win] += dot(ds, qa[...]) * keep
        new = dot_tn(ds, k)
        part[...] = new if i == 0 else part[...] + new
    dq[:, win] += part[...] * keep

    @pl.when(h == heads - 1)
    def _():
        for i, (ref, factor) in enumerate(((dq, SCALE), (dk, SCALE), (dv, 1.0))):
            value = (ref[:, : g_ref.shape[1] // 3] * factor).astype(bf16)
            cols = slice(i * value.shape[1], (i + 1) * value.shape[1])
            g_ref[:, cols] = value
            sum_ref[:, cols] = jnp.sum(value.astype(f32), axis=0, keepdims=True)
        for some in steps[5:]:
            run(some)
        for job in bound:
            job.outward()
        for job in bound:
            job.finish()


def attn_bwd_call(length, q, k, v, o, do, lse, width, heads, jobs, number):
    n, wide = q.shape
    return pl.pallas_call(
        functools.partial(attn_bwd_kernel, bk=256, jobs=jobs),
        grid=(heads,),
        in_specs=[pl.BlockSpec(memory_space=pltpu.SMEM)]
        + [once((n, wide))] * 5
        + [once((n, 128))]
        + jobs.in_specs(),
        out_specs=[once((n, 3 * width)), whole((1, 3 * width))] + jobs.in_specs(),
        out_shape=[
            jax.ShapeDtypeStruct((n, 3 * width), bf16),
            jax.ShapeDtypeStruct((1, 3 * width), f32),
        ]
        + jobs.out_shapes(),
        scratch_shapes=[pltpu.VMEM((n, wide), f32)] * 3
        + [pltpu.VMEM((n, WIN), f32)]
        + [pltpu.VMEM((n, WIN), bf16)] * 3
        + jobs.scratch(),
        compiler_params=comm_params(number),
        cost_estimate=cost(10 * n * n * WIN * heads, 20 * n * wide),
        name="attend_back",
    )(length, q, k, v, o, do, lse, *jobs.sources())


def middle_kernel(*refs, jobs):
    count = len(jobs.jobs)
    o_ref, w_ref, x_ref, vec_ref = refs[:4]
    mid_ref, h_ref, owide_ref = refs[4 + count : 7 + count]
    mine, other = refs[7 + 2 * count : 9 + 2 * count]
    link, bound, _ = jobs.bind(refs[9 + 2 * count :], refs[4 : 4 + count], refs[7 + count : 7 + 2 * count])
    n = x_ref.shape[0]
    width = o_ref.shape[1]
    base = link.slots(n // ROWS)
    link.meet_plane(jobs.pairs)
    for job in bound:
        job.start()

    def swap(i):
        rows = pl.ds(pl.multiple_of(i * ROWS, ROWS), ROWS)
        return rows, link.remote(mine.at[rows], other.at[rows], base + i, base + i, link.sibling())

    def project(i, carry):
        rows, copy = swap(i)
        mine[rows, :] = dot(o_ref[rows, :], w_ref[...]).astype(bf16)
        copy.start()
        return carry

    def norm(i, carry):
        rows, copy = swap(i)
        copy.wait_recv()
        mid = x_ref[rows, :].astype(f32) + (
            mine[rows, :].astype(f32) + other[rows, :].astype(f32) + vec_ref[OBIAS]
        )
        mid_ref[rows, :] = mid
        xhat, _ = standardize(mid)
        h_ref[rows, :] = (xhat * vec_ref[GAIN2] + vec_ref[SHIFT2]).astype(bf16)
        return carry

    lax.fori_loop(0, n // ROWS, project, 0)
    owide_ref[:, :width] = o_ref[...]
    owide_ref[:, width:] = jnp.zeros((n, owide_ref.shape[1] - width), bf16)
    lax.fori_loop(0, n // ROWS, norm, 0)
    for i in range(n // ROWS):
        swap(i)[1].wait_send()
    for job in bound:
        job.forward()
    for job in bound:
        job.inward()
    for job in bound:
        job.finish()


def middle_call(o, w, x, vec, wide, jobs, number):
    n, d = x.shape
    vmem = pl.BlockSpec(memory_space=pltpu.VMEM)
    return pl.pallas_call(
        functools.partial(middle_kernel, jobs=jobs),
        in_specs=[vmem] * 4 + jobs.in_specs(),
        out_specs=[vmem] * 3 + jobs.in_specs(),
        out_shape=[
            jax.ShapeDtypeStruct((n, d), f32),
            jax.ShapeDtypeStruct((n, d), bf16),
            jax.ShapeDtypeStruct((n, wide), bf16),
        ]
        + jobs.out_shapes(),
        scratch_shapes=[pltpu.VMEM((n, d), bf16)] * 2 + jobs.scratch(n // ROWS),
        compiler_params=comm_params(number),
        cost_estimate=cost(2 * n * w.size, 14 * n * d),
        name="middle",
    )(o, w, x, vec, *jobs.sources())


def ffn_kernel(*refs, chained, last, mc, jobs):
    count = len(jobs.jobs)
    h_ref, dz_ref, up_ref, ub_ref, dn_ref = refs[:5]
    refs = refs[5:]
    if chained:
        old_out, old_dh = refs[:2]
        refs = refs[2:]
    srcs, refs = refs[:count], refs[count:]
    out_ref, dh_ref, dup_ref, ddn_ref, dub_ref = refs[:5]
    dsts, refs = refs[5 : 5 + count], refs[5 + count :]
    ht, act, grad = refs[:3]
    acc, dh = refs[3:5] if last else (out_ref, dh_ref)
    refs = refs[5:] if last else refs[3:]
    link, bound, refs = jobs.bind(refs, srcs, dsts)
    gathers, others = split_gathers(bound)
    steps = gather_steps(gathers)
    t = pl.program_id(0)
    tiles = pl.num_programs(0)
    n = h_ref.shape[0]

    @pl.when(t == 0)
    def _():
        link.meet_plane(jobs.pairs)
        run([job.start for job in others] + steps[0])
        if chained:
            sem = refs[0]
            copies = [
                pltpu.make_async_copy(src, dst, sem.at[i])
                for i, (src, dst) in enumerate(((old_out, acc), (old_dh, dh)))
            ]
            for c in copies:
                c.start()
            ht[...] = h_ref[...].T
            for c in copies:
                c.wait()
        else:
            ht[...] = h_ref[...].T
            acc[...] = jnp.zeros_like(acc)
            dh[...] = jnp.zeros_like(dh)

    def at_tile(number, some):
        if some:

            @pl.when(t == number)
            def _():
                run(some)

    at_tile(tiles - 1, [job.forward for job in others])

    def step(i, carry):
        rows = pl.ds(pl.multiple_of(i * mc, mc), mc)
        g, slope = gelu_pair(dot(h_ref[rows, :], up_ref[...]) + ub_ref[...])
        g = g.astype(bf16)
        da = (dot_nt(dz_ref[rows, :], dn_ref[...]) * slope).astype(bf16)
        act[rows, :] = g
        grad[rows, :] = da
        acc[rows, :] += dot(g, dn_ref[...])
        dh[rows, :] += dot_nt(da, up_ref[...])
        return carry

    lax.fori_loop(0, n // mc, step, 0)

    at_tile(0, steps[1] if gathers else [])
    dub_ref[...] = jnp.sum(grad[...].astype(f32), axis=0, keepdims=True)
    dup_ref[...] = dot(ht[...], grad[...]).astype(bf16)
    at_tile(tiles - 1, steps[2] if gathers else [])
    ddn_ref[...] = dot_tn(act[...], dz_ref[...]).astype(bf16)

    @pl.when(t == tiles - 1)
    def _():
        if last:
            out_ref[...] = acc[...].astype(out_ref.dtype)
            dh_ref[...] = dh[...].astype(dh_ref.dtype)
        for some in steps[3:]:
            run(some)
        run([job.finish for job in bound])


def ffn_call(h, dz, up, bias, down, old, last, jobs, number, name):
    n, d = h.shape
    hidden = up.shape[1]
    bt = FFN_TILE
    out = jax.ShapeDtypeStruct((n, d), bf16 if last else f32)
    chained = old is not None
    kept = once((n, d))
    return pl.pallas_call(
        functools.partial(ffn_kernel, chained=chained, last=last, mc=FFN_ROWS, jobs=jobs),
        grid=(hidden // bt,),
        in_specs=[
            kept,
            kept,
            pl.BlockSpec((d, bt), lambda t: (0, t)),
            pl.BlockSpec((1, bt), lambda t: (0, t)),
            pl.BlockSpec((bt, d), lambda t: (t, 0)),
        ]
        + ([pl.BlockSpec(memory_space=pl.ANY)] * 2 if chained else [])
        + jobs.in_specs(),
        out_specs=[
            kept,
            kept,
            pl.BlockSpec((d, bt), lambda t: (0, t)),
            pl.BlockSpec((bt, d), lambda t: (t, 0)),
            pl.BlockSpec((1, bt), lambda t: (0, t)),
        ]
        + jobs.in_specs(),
        out_shape=[
            out,
            out,
            jax.ShapeDtypeStruct((d, hidden), bf16),
            jax.ShapeDtypeStruct((hidden, d), bf16),
            jax.ShapeDtypeStruct((1, hidden), f32),
        ]
        + jobs.out_shapes(),
        scratch_shapes=[pltpu.VMEM((d, n), bf16)]
        + [pltpu.VMEM((n, bt), bf16)] * 2
        + ([pltpu.VMEM((n, d), f32)] * 2 if last else [])
        + jobs.scratch()
        + ([pltpu.SemaphoreType.DMA((2,))] if chained else []),
        compiler_params=comm_params(number),
        cost_estimate=cost(12 * n * d * hidden, 8 * d * hidden + 12 * n * d),
        name=name,
    )(h, dz, up, bias, down, *(old if chained else ()), *jobs.sources())


def second_back_kernel(*refs, jobs):
    count = len(jobs.jobs)
    mid_ref, dh_ref, out_ref, dz_ref, vec_ref, w_ref, o_ref, dh_any, out_any = refs[:9]
    dmid_ref, do_ref, dw_ref, sums_ref, layer_ref = refs[9 + count : 14 + count]
    acc, dh_other, out_other = refs[14 + 2 * count : 17 + 2 * count]
    link, bound, _ = jobs.bind(refs[17 + 2 * count :], refs[9 : 9 + count], refs[14 + count : 14 + 2 * count])
    chains = [job for job in bound if isinstance(job, Chain)]
    others = [job for job in bound if job not in chains]
    steps = chain_steps(chains) if chains else []
    i = pl.program_id(0)
    blocks = pl.num_programs(0)
    half = layer_ref.shape[0] // ROWS
    width = w_ref.shape[0]
    base = link.slots(3 * half)

    def swap_dh(j):
        rows = pl.ds(pl.multiple_of(j * ROWS, ROWS), ROWS)
        return link.remote(dh_any.at[rows], dh_other.at[rows], base + j, base + j, link.sibling())

    def swap_out(j):
        src = pl.ds(pl.multiple_of(((1 - link.core) * half + j) * ROWS, ROWS), ROWS)
        dst = pl.ds(pl.multiple_of(j * ROWS, ROWS), ROWS)
        slot = base + 2 * half + j
        return link.remote(out_any.at[src], out_other.at[dst], slot, slot, link.sibling())

    @pl.when(i == 0)
    def _():
        if chains:
            link.meet_all()
        else:
            link.meet_plane()
        for j in range(2 * half):
            swap_dh(j).start()
        for j in range(half):
            swap_out(j).start()
        run([job.start for job in others + chains[:1]])
        acc[...] = jnp.zeros_like(acc)
        sums_ref[...] = jnp.zeros_like(sums_ref)

    for number, some in zip((2, 4), steps):

        @pl.when(i == number)
        def _():
            run(some)

    @pl.when(i == blocks - 1)
    def _():
        run([job.forward for job in others])

    mid = mid_ref[...]
    xhat, inv = standardize(mid)
    swap_dh(i).wait_recv()
    rows = pl.ds(pl.multiple_of(i * ROWS, ROWS), ROWS)
    dh = dh_ref[...].astype(f32) + dh_other[rows, :].astype(f32)
    dx = dh * vec_ref[GAIN2]
    dz = dz_ref[...].astype(f32)
    dmid = dz + inv * (
        dx - jnp.mean(dx, axis=-1, keepdims=True) - xhat * jnp.mean(dx * xhat, axis=-1, keepdims=True)
    )
    dmid_ref[...] = dmid
    dy = dmid.astype(bf16)
    do_ref[:, :width] = dot_nt(dy, w_ref[...]).astype(bf16)
    do_ref[:, width:] = jnp.zeros((do_ref.shape[0], do_ref.shape[1] - width), bf16)
    acc[...] += dot_tn(o_ref[...], dy)
    for row, value in enumerate((dh * xhat, dh, dy.astype(f32), dz)):
        sums_ref[row : row + 1, :] += jnp.sum(value, axis=0, keepdims=True)

    j = i - link.core * half

    @pl.when((j >= 0) & (j < half))
    def _():
        swap_out(j).wait_recv()
        here = pl.ds(pl.multiple_of(j * ROWS, ROWS), ROWS)
        layer_ref[here, :] = (
            mid + (out_ref[...].astype(f32) + out_other[here, :].astype(f32) + vec_ref[DBIAS])
        ).astype(bf16)

    @pl.when(i == blocks - 1)
    def _():
        dw_ref[...] = acc[...].astype(bf16)
        for j in range(2 * half):
            swap_dh(j).wait_send()
        for j in range(half):
            swap_out(j).wait_send()
        for some in steps[2:]:
            run(some)
        run([job.outward for job in chains] + [job.finish for job in others + chains])


def second_back_call(mid, dh, out, dz, vec, w, o, wide, jobs, number):
    n, d = mid.shape
    width = w.shape[0]
    block = row_block(ROWS, d)
    count = 3 * n // ROWS // 2
    return pl.pallas_call(
        functools.partial(second_back_kernel, jobs=jobs),
        grid=(n // ROWS,),
        in_specs=[block] * 4
        + [whole(vec.shape), whole(w.shape), row_block(ROWS, width)]
        + [pl.BlockSpec(memory_space=pl.ANY)] * 2
        + jobs.in_specs(),
        out_specs=[block, row_block(ROWS, wide), whole((width, d)), whole((8, d)), whole((n // 2, d))]
        + jobs.in_specs(),
        out_shape=[
            jax.ShapeDtypeStruct((n, d), f32),
            jax.ShapeDtypeStruct((n, wide), bf16),
            jax.ShapeDtypeStruct((width, d), bf16),
            jax.ShapeDtypeStruct((8, d), f32),
            jax.ShapeDtypeStruct((n // 2, d), bf16),
        ]
        + jobs.out_shapes(),
        scratch_shapes=[
            pltpu.VMEM((width, d), f32),
            pltpu.VMEM((n, d), bf16),
            pltpu.VMEM((n // 2, d), bf16),
        ]
        + jobs.scratch(count),
        compiler_params=comm_params(number),
        cost_estimate=cost(4 * n * d * width, 14 * n * d),
        name="second_back",
    )(mid, dh, out, dz, vec, w, o, dh, out, *jobs.sources())


def dw_kernel(h_ref, g_ref, out_ref):
    out_ref[...] = dot_tn(h_ref[...], g_ref[...]).astype(bf16)


def dw_call(h, grads):
    n, d = h.shape
    cols = grads.shape[1]
    return pl.pallas_call(
        dw_kernel,
        grid=(d // 256,),
        in_specs=[pl.BlockSpec((n, 256), lambda i: (0, i)), whole((n, cols))],
        out_specs=row_block(256, cols),
        out_shape=jax.ShapeDtypeStruct((d, cols), bf16),
        compiler_params=params(),
        cost_estimate=cost(2 * n * d * cols, 2 * (n * d + n * cols + d * cols)),
        name="project_grad",
    )(h, grads)


def first_back_kernel(*refs, jobs):
    count = len(jobs.jobs)
    g_ref, w_ref, vec_ref, x_any, dmid_any = refs[:5]
    dx_ref, sums_ref = refs[5 + count : 7 + count]
    x, dmid, mine, other = refs[7 + 2 * count : 11 + 2 * count]
    link, bound, _ = jobs.bind(refs[11 + 2 * count :], refs[5 : 5 + count], refs[7 + count : 7 + 2 * count])
    size = dx_ref.shape[0]
    half = size // ROWS
    base = link.slots(half)
    keep = link.local_slots(2)
    own = pl.ds(pl.multiple_of(link.core * size, size), size)
    loads = [link.here(x_any.at[own], x, keep), link.here(dmid_any.at[own], dmid, keep + 1)]
    for c in loads:
        c.start()
    link.meet_plane(jobs.pairs)
    for job in bound:
        job.start()

    def product(j):
        rows = pl.ds(pl.multiple_of(j * ROWS, ROWS), ROWS)
        return dot_nt(g_ref[rows, :], w_ref[...])

    def swap(j):
        rows = pl.ds(pl.multiple_of(j * ROWS, ROWS), ROWS)
        return rows, link.remote(mine.at[rows], other.at[rows], base + j, base + j, link.sibling())

    def send(j, carry):
        rows, copy = swap(j)
        mine[rows, :] = product((1 - link.core) * half + j).astype(bf16)
        copy.start()
        return carry

    def norm(j, carry):
        rows, copy = swap(j)
        part = product(link.core * half + j)
        copy.wait_recv()
        xhat, inv = standardize(x[rows, :].astype(f32))
        dh = part + other[rows, :].astype(f32)
        dx = dh * vec_ref[GAIN1]
        dx_ref[rows, :] = (
            dmid[rows, :]
            + inv
            * (dx - jnp.mean(dx, axis=-1, keepdims=True) - xhat * jnp.mean(dx * xhat, axis=-1, keepdims=True))
        ).astype(bf16)
        for row, value in enumerate((dh * xhat, dh)):
            sums_ref[row : row + 1, :] += jnp.sum(value, axis=0, keepdims=True)
        return carry

    sums_ref[...] = jnp.zeros_like(sums_ref)
    lax.fori_loop(0, half, send, 0)
    for c in loads:
        c.wait()
    lax.fori_loop(0, half, norm, 0)
    for j in range(half):
        swap(j)[1].wait_send()
    for job in bound:
        job.forward()
    for job in bound:
        job.inward()
    for job in bound:
        job.finish()


def first_back_call(grads, w, vec, x, dmid, jobs, number):
    n, d = x.shape
    size = n // 2
    vmem = pl.BlockSpec(memory_space=pltpu.VMEM)
    hbm = pl.BlockSpec(memory_space=pl.ANY)
    return pl.pallas_call(
        functools.partial(first_back_kernel, jobs=jobs),
        in_specs=[vmem] * 3 + [hbm] * 2 + jobs.in_specs(),
        out_specs=[vmem] * 2 + jobs.in_specs(),
        out_shape=[jax.ShapeDtypeStruct((size, d), bf16), jax.ShapeDtypeStruct((8, d), f32)] + jobs.out_shapes(),
        scratch_shapes=[
            pltpu.VMEM((size, d), bf16),
            pltpu.VMEM((size, d), f32),
            pltpu.VMEM((size, d), bf16),
            pltpu.VMEM((size, d), bf16),
        ]
        + jobs.scratch(size // ROWS),
        compiler_params=comm_params(number),
        cost_estimate=cost(2 * n * w.size, 12 * n * d),
        name="first_back",
    )(grads, w, vec, x, dmid, *jobs.sources())


class Blocks:
    def __init__(self, ref, stride, first):
        self.ref, self.stride, self.first = ref, stride, first

    @property
    def at(self):
        return self

    def __getitem__(self, index):
        block, part = index
        start = pl.multiple_of(block * self.stride + (self.first + part.start), 16)
        return self.ref.at[pl.ds(start, part.size)]


def back_kernel(*refs, jobs):
    count = len(jobs.jobs)
    g_ref, vec_ref, h_ref, early_ref, *w_refs = refs[:7]
    x_any, dmid_any = refs[7:9]
    tokens_any, small_ref, both_any = refs[9 + count : 12 + count]
    rest = list(refs[12 + 2 * count :])
    x, dmid, mine, other, dx, dw, own, total, came, stage = rest[:10]
    rest = rest[10:]
    small_bufs, rest = rest[:3], rest[3:]
    reduce_bufs, rest = [rest[10 * i : 10 * i + 10] for i in range(3)], rest[30:]
    chain_bufs, rest = [rest[3 * i : 3 * i + 3] for i in range(6)], rest[18:]
    link, bound, _ = jobs.bind(rest, refs[9 : 9 + count], refs[12 + count : 12 + 2 * count])
    ready = [job for job in bound if isinstance(job, Chain)]
    others = [job for job in bound if job not in ready]
    size, d = dx.shape
    half = size // ROWS
    _, owned, width = own.shape
    order = (2, 1, 0)
    reduces = [Reduce(link, Blocks(dw.at[c], owned, 0), own.at[c], reduce_bufs[c]) for c in order]
    last = []
    for c in order:
        for i in range(2):
            rows, cols = pl.ds(i * (owned // 2), owned // 2), pl.ds(c * width, width)
            last.append(Chain(link, own.at[c, rows], both_any.at[:, rows, cols], chain_bufs[len(last)]))
    to_owners = FromClip(link, dx, tokens_any, [stage])
    base = link.slots(half)
    keep = link.local_slots(2)
    swap_base = link.slots(3)
    peers = [link.sibling()] + [(link.rep, link.shard ^ bit) for bit in (1, 2)]
    swaps = [link.remote(total, came.at[i], swap_base + i, swap_base + i, to) for i, to in enumerate(peers)]
    small = Chain(link, total, small_ref, small_bufs)
    mine_rows = pl.ds(pl.multiple_of(link.core * size, size), size)
    loads = [link.here(x_any.at[mine_rows], x, keep), link.here(dmid_any.at[mine_rows], dmid, keep + 1)]
    for c in loads:
        c.start()
    link.meet_all()
    ready[0].start()
    for c, job in zip(order, reduces):

        def weight(i, carry):
            part = pl.ds(pl.multiple_of(i * 256, 256), 256)
            dw[c, part, :] = dot_tn(h_ref[:, part], g_ref[:, c * width : (c + 1) * width]).astype(bf16)
            return carry

        lax.fori_loop(0, d // 256, weight, 0)
        job.start()

    def product(j):
        rows = pl.ds(pl.multiple_of(j * ROWS, ROWS), ROWS)
        parts = [dot_nt(g_ref[rows, c * width : (c + 1) * width], w_refs[c][...]) for c in range(3)]
        return parts[0] + parts[1] + parts[2]

    def swap(j):
        rows = pl.ds(pl.multiple_of(j * ROWS, ROWS), ROWS)
        return rows, link.remote(mine.at[rows], other.at[rows], base + j, base + j, link.sibling())

    def send(j, carry):
        rows, copy = swap(j)
        mine[rows, :] = product((1 - link.core) * half + j).astype(bf16)
        copy.start()
        return carry

    first = early_ref.shape[0]

    def norm(j, carry):
        rows, copy = swap(j)
        part = product(link.core * half + j)
        copy.wait_recv()
        xhat, inv = standardize(x[rows, :].astype(f32))
        dh = part + other[rows, :].astype(f32)
        slope = dh * vec_ref[GAIN1]
        dx[rows, :] = (
            dmid[rows, :]
            + inv
            * (
                slope
                - jnp.mean(slope, axis=-1, keepdims=True)
                - xhat * jnp.mean(slope * xhat, axis=-1, keepdims=True)
            )
        ).astype(bf16)
        for row, value in enumerate((dh * xhat, dh)):
            total[first + row : first + row + 1, :] += jnp.sum(value, axis=0, keepdims=True)
        return carry

    steps = chain_steps(ready)
    run(steps[0])
    total[:first, :] = early_ref[...]
    total[first:, :] = jnp.zeros((total.shape[0] - first, d), f32)
    lax.fori_loop(0, half, send, 0)
    for c in loads:
        c.wait()
    reduces[0].forward()
    after = {0: steps[1] + [reduces[1].forward], 1: [reduces[2].forward]}
    for j in range(half):
        norm(j, 0)
        run(after.get(j, []))
    swaps[0].start()
    run(steps[2])
    reduces[0].collect()
    last[0].start()
    reduces[1].collect()
    swaps[0].wait()
    total[...] += came[0]
    swaps[1].start()
    reduces[2].collect()
    for some in steps[3:]:
        run(some)
    swaps[1].wait()
    total[...] += came[1]
    swaps[2].start()
    for number, some in enumerate(chain_steps(last)):
        run(some)
        if number == 0:
            swaps[2].wait()
            total[...] += came[2]
            small.start()
        if number == 2:
            run([job.start for job in [to_owners] + others])
        if number == 3:
            small.inward()
            small.sent()
        if number == 5:
            small.across()
    for c in ready + last:
        c.outward()
    small.outward()
    for job in ready + last + [small]:
        job.finish()
    for job in reduces:
        job.close()
    for j in range(half):
        swap(j)[1].wait_send()
    run([job.finish for job in [to_owners] + others])


def back_call(grads, weights, vec, h, early, x, dmid, jobs, clips, number):
    n, d = x.shape
    size = n // 2
    width = grads.shape[1] // 3
    groups = lax.axis_size("shard")
    owned = d // groups
    rows = early.shape[0] + 8
    small = pltpu.VMEM((rows, d), f32)
    vmem = pl.BlockSpec(memory_space=pltpu.VMEM)
    hbm = pl.BlockSpec(memory_space=pl.ANY)
    return pl.pallas_call(
        functools.partial(back_kernel, jobs=jobs),
        in_specs=[vmem] * 7 + [hbm] * 2 + jobs.in_specs(),
        out_specs=[hbm, vmem, hbm] + jobs.in_specs(),
        out_shape=[
            jax.ShapeDtypeStruct((clips, size // clips, d), bf16),
            jax.ShapeDtypeStruct((2, rows, d), f32),
            jax.ShapeDtypeStruct((2, owned, 3 * width), bf16),
        ]
        + jobs.out_shapes(),
        scratch_shapes=[
            pltpu.VMEM((size, d), bf16),
            pltpu.VMEM((size, d), f32),
            pltpu.VMEM((size, d), bf16),
            pltpu.VMEM((size, d), bf16),
            pltpu.VMEM((size, d), bf16),
            pltpu.VMEM((3, d, width), bf16),
            pltpu.VMEM((3, owned, width), bf16),
            small,
            pltpu.VMEM((3, rows, d), f32),
            pltpu.VMEM((size // clips, d), bf16),
        ]
        + [small] * 3
        + [pltpu.VMEM((owned // 2, width), bf16)] * 48
        + jobs.scratch(80),
        compiler_params=comm_params(number, 62),
        cost_estimate=cost(12 * n * weights[0].size, 20 * n * d),
        name="back",
    )(grads, vec, h, early, *weights, x, dmid, *jobs.sources())


def place_kernel(*refs, groups):
    up_refs, down_refs = refs[:4], refs[4:8]
    out_ref, in_ref = refs[8:10]
    up, down, wo = refs[10:13]
    qkv = refs[13:16]

    def put(target, axis, pieces):
        first = 0
        for value in pieces:
            size = value.shape[axis]
            span = slice(first, first + size)
            if axis:
                target[:, span] = value.astype(f32)
            else:
                target[span, :] = value.astype(f32)
            first += size

    cut = up_refs[0].shape[1]
    for part in range(2):
        put(up.at[pl.ds(part * cut, cut)], 1, [r[c] for c in range(2) for r in (up_refs[part], up_refs[2 + part])])
    put(down, 0, [r[c] for c in range(2) for r in down_refs])
    put(wo, 0, [out_ref[c] for c in range(2)])
    rows = in_ref.shape[1]
    width = in_ref.shape[2] // 3
    part = width // groups

    for i, out in enumerate(qkv):
        for c in range(2):
            value = in_ref[c, :, i * width : (i + 1) * width].astype(f32)
            for s in range(groups):
                first = (2 * s + c) * part
                out[:, first : first + part] = value[:, s * part : (s + 1) * part]


def place_call(ups, downs, wo, qkv, groups):
    steps = 5
    own_d, cols = qkv.shape[1:]
    d = downs[0].shape[2]
    own_f = 2 * sum(a.shape[1] for a in downs)
    take = [pl.BlockSpec((2, a.shape[1], a.shape[2] // groups), lambda i: (0, 0, jnp.minimum(i, groups - 1))) for a in ups]
    wide = d // steps
    per = own_d // steps
    ff = 2 * ups[0].shape[2] + 2 * ups[2].shape[2]
    return pl.pallas_call(
        functools.partial(place_kernel, groups=groups),
        grid=(steps,),
        in_specs=take
        + [pl.BlockSpec((2, a.shape[1], wide), lambda i: (0, 0, i)) for a in downs]
        + [
            pl.BlockSpec((2, wo.shape[1], wide), lambda i: (0, 0, i)),
            pl.BlockSpec((2, per, cols), lambda i: (0, i, 0)),
        ],
        out_specs=[
            pl.BlockSpec((own_d, ff // groups), lambda i: (0, jnp.minimum(i, groups - 1))),
            pl.BlockSpec((own_f, wide), lambda i: (0, i)),
            pl.BlockSpec((own_d, wide), lambda i: (0, i)),
        ]
        + [pl.BlockSpec((per, d), lambda i: (i, 0))] * 3,
        out_shape=[
            jax.ShapeDtypeStruct((own_d, ff), f32),
            jax.ShapeDtypeStruct((own_f, d), f32),
            jax.ShapeDtypeStruct((own_d, d), f32),
        ]
        + [jax.ShapeDtypeStruct((own_d, d), f32)] * 3,
        compiler_params=params(),
        name="place",
    )(*ups, *downs, wo, qkv)


def own_sum(blocks, others):
    shard = lax.axis_index("shard")
    total = lax.dynamic_index_in_dim(blocks, shard, 0, keepdims=False).astype(f32)
    for i in range(others.shape[0]):
        total = total + others[i].astype(f32)
    return total.astype(bf16)


def over_reps(own):
    planes = lax.axis_size("rep") // 2
    sums = lax.psum_scatter(
        own,
        "rep",
        scatter_dimension=0,
        tiled=True,
        axis_index_groups=[[2 * z + c for z in range(planes)] for c in range(2)],
    )
    both = lax.all_gather(sums, "rep", axis=0)
    rows, cols = sums.shape
    return both.reshape(planes, 2, rows, cols).transpose(1, 0, 2, 3).reshape(2, planes * rows, cols)


def on_device(
    tokens,
    lengths,
    cotangent,
    first_gain,
    first_shift,
    query_weight,
    query_bias,
    key_weight,
    value_weight,
    value_bias,
    out_weight,
    out_bias,
    second_gain,
    second_shift,
    up_weight,
    up_bias,
    down_weight,
    down_bias,
):
    g = lax.axis_size("shard")
    shard = lax.axis_index("shard")
    core = lax.rem(lax.axis_index("rep"), 2)
    cl, rows, d = tokens.shape
    n = 2 * cl * rows
    ff = up_weight.shape[1]
    own_d = d // g
    own_f = ff // g
    attn_cols = own_d // 2
    ffn_cols = own_f // 2
    width = d // 2
    heads = width // HEAD
    wide = pl.cdiv(width, 128) * 128 + 128
    first_n = ffn_cols * 2 // 5
    pieces = ((0, first_n), (first_n, ffn_cols))

    fast = g == 4 and lax.axis_size("rep") == 8
    weights = PairGather if fast else Gather
    positions = shard * rows + jnp.arange(rows, dtype=jnp.int32)
    live = positions[None, :] < lengths[:, None]
    masked = jnp.where(live[:, :, None], cotangent, jnp.zeros_like(cotangent))

    def core_of():
        return lax.rem(lax.axis_index("rep"), 2)

    def core_cols(w, size, a, b):
        def of(c):
            return jnp.concatenate([w[:, (2 * s + c) * size + a : (2 * s + c) * size + b] for s in range(g)], axis=1)

        return jnp.where(core == 0, of(0), of(1))

    vectors = (first_gain, first_shift, query_bias, value_bias, out_bias, second_gain, second_shift, down_bias)
    lens = jnp.pad(lengths, (0, own_d - cl)).astype(f32)
    flat = jnp.concatenate([*vectors, up_bias]).astype(f32)
    cut = len(vectors) * own_d
    flat = jnp.concatenate([flat[:cut], lens, flat[cut:], jnp.zeros((16 * own_d - flat.shape[0] - own_d,), f32)])
    small = jnp.pad(flat.reshape(16, own_d), ((0, 0), (0, -own_d % 128)))
    own = [core_cols(w, attn_cols, 0, attn_cols) for w in (query_weight, key_weight, value_weight)]
    jobs = Jobs(
        (ToClip, tokens, (n, d)),
        (Gather, small, (g,) + small.shape),
        *[(weights, w, (g,) + w.shape) for w in own],
    )
    x, smalls, *w_qkv, other_small = exchange_call(jobs, small, 0, "first_exchange")
    w_qkv = [w.reshape(d, width) for w in w_qkv]
    vec = smalls[:, :, :own_d].transpose(1, 0, 2).reshape(16, d)
    near = lax.div(shard, cl) == core
    lens = jnp.where(near, small[LENGTHS], other_small[LENGTHS])[0]
    length = lens[lax.rem(shard, cl)].astype(jnp.int32).reshape(1)

    def bias_cols(b):
        return lax.dynamic_index_in_dim(vec[b].reshape(1, g, 2, attn_cols), core, 2).reshape(1, width)

    bias = jnp.concatenate([bias_cols(QBIAS), jnp.zeros((1, width), f32), bias_cols(VBIAS)], axis=1)
    ubias = lax.dynamic_index_in_dim(
        vec[UBIAS : UBIAS + own_f // own_d].reshape(-1, g, own_d).transpose(1, 0, 2).reshape(g, 2, ffn_cols),
        core,
        1,
        keepdims=False,
    )
    ups = [core_cols(up_weight, ffn_cols, a, b) for a, b in pieces]

    def half_rows(w, first=0, last=None):
        half = w.shape[0] // 2
        size = (half if last is None else last) - first

        def view(ref):
            return ref.at[pl.ds(pl.multiple_of(core_of() * half + first, 16), size)]

        return size, view

    def gathered(a, part=None):
        if part is None:
            return (weights, a, (g,) + a.shape)
        return (weights, a, (g, part[0]) + a.shape[1:], part[1])

    h1, q, k, v = qkv_call(x, vec, bias, w_qkv, wide)
    jobs = Jobs(
        gathered(ups[0]),
        gathered(down_weight, half_rows(down_weight, *pieces[0])),
        gathered(out_weight, half_rows(out_weight)),
    )
    o, lse, up, down, w_out = attn_fwd_call(length, q, k, v, width, heads, jobs, 1)
    w_out = w_out.reshape(width, d)
    jobs = Jobs((ToClip, masked, (n, d)))
    mid, h2, o_wide, dz = middle_call(o, w_out, x, vec, wide, jobs, 2)

    def hidden_bias(piece):
        return ubias[:, piece[0] : piece[1]].reshape(1, -1)


    def to_owners(a):
        if fast:
            return (Reduce, a, a.shape[1:])
        return (Owners, a, (g - 1,) + a.shape[1:])

    def owned(a, came):
        return came if fast else own_sum(a, came)

    def chained(a):
        return (Chain, a, (2,) + a.shape)

    def chained_halves(a):
        half = a.shape[0] // 2

        def part(i):
            return lambda ref: ref.at[pl.ds(i * half, half)]

        return [(Chain, a, (2, half, a.shape[1]), part(i)) for i in range(2)]

    jobs = Jobs(gathered(ups[1]), gathered(down_weight, half_rows(down_weight, *pieces[1])))
    out, dh2, dup0, ddn0, dub0, up1, down1 = ffn_call(
        h2, dz, up.reshape(d, -1), hidden_bias(pieces[0]), down.reshape(-1, d), None, False, jobs, 3, "hidden0"
    )
    dup0, ddn0 = dup0.reshape(g, own_d, -1), ddn0.reshape(g, -1, d)
    jobs = Jobs(to_owners(dup0), to_owners(ddn0))
    out, dh2, dup1, ddn1, dub1, dup0_in, ddn0_in = ffn_call(
        h2, dz, up1.reshape(d, -1), hidden_bias(pieces[1]), down1.reshape(-1, d), (out, dh2), True, jobs, 4, "hidden1"
    )
    dup1, ddn1 = dup1.reshape(g, own_d, -1), ddn1.reshape(g, -1, d)
    up0_own, down0_own = owned(dup0, dup0_in), owned(ddn0, ddn0_in)

    jobs = [to_owners(dup1)]
    if fast:
        jobs += chained_halves(up0_own)
    dmid, do, dwo, sums2, layer_own, dup1_in, *sums0 = second_back_call(
        mid, dh2, out, dz, vec, w_out, o, wide, Jobs(*jobs), 5
    )
    dwo = dwo.reshape(g, -1, d)
    up1_own = owned(dup1, dup1_in)

    to_tokens = (FromClip, layer_own, (cl, rows, d))
    jobs = [to_owners(ddn1), to_owners(dwo), to_tokens]
    if fast:
        jobs += chained_halves(down0_own) + chained_halves(up1_own)
    grads, bias_sums, ddn1_in, dwo_in, layer_out, *later = attn_bwd_call(
        length, q, k, v, o_wide, do, lse, width, heads, Jobs(*jobs), 6
    )
    down1_own, out_own_grad = owned(ddn1, ddn1_in), owned(dwo, dwo_in)

    def spread(v, size):
        out = jnp.zeros((g, 2, size), f32)
        return lax.dynamic_update_index_in_dim(out, v.reshape(g, size), core, 1)

    ub_sums = jnp.concatenate([dub0.reshape(g, -1), dub1.reshape(g, -1)], axis=1)
    early = jnp.concatenate(
        [
            spread(bias_sums[0, :width], attn_cols).reshape(1, d),
            spread(bias_sums[0, 2 * width :], attn_cols).reshape(1, d),
            sums2[:4] * 0.5,
            spread(ub_sums, ffn_cols).reshape(-1, d),
        ],
        axis=0,
    )
    early = jnp.pad(early, ((0, -early.shape[0] % 8), (0, 0)))

    if fast:
        jobs = Jobs(*chained_halves(down1_own), chained(out_own_grad))
        tokens_grad, smalls, qkv_all, *sums = back_call(grads, w_qkv, vec, h1, early, x, dmid, jobs, cl, 7)
        up_grad, down_grad, out_grad, *qkv_grads = place_call(
            (*sums0, *later[2:]), (*later[:2], *sums[:2]), sums[2], qkv_all, g
        )
        smalls = lax.dynamic_index_in_dim(smalls, core, 0, keepdims=False)
    else:
        dwqkv = dw_call(h1, grads).reshape(g, own_d, 3 * width)
        jobs = Jobs(to_owners(dwqkv))
        dx, sums1, dwqkv_in = first_back_call(grads, jnp.concatenate(w_qkv, axis=1), vec, x, dmid, jobs, 7)
        jobs = Jobs((FromClip, dx, (cl, rows, d)))
        tokens_grad, _ = exchange_call(jobs, sums1, 8, "last_exchange")
        ups_all = [over_reps(a).reshape(2, own_d, g, -1) for a in (up0_own, up1_own)]
        up_grad = jnp.concatenate(ups_all, axis=3).transpose(1, 2, 0, 3).reshape(own_d, ff).astype(f32)
        downs_all = [over_reps(a) for a in (down0_own, down1_own)]
        down_grad = jnp.concatenate(downs_all, axis=1).reshape(own_f, d).astype(f32)
        out_grad = over_reps(out_own_grad).reshape(own_d, d).astype(f32)
        qkv_all = over_reps(owned(dwqkv, dwqkv_in)).reshape(2, own_d, 3, g, attn_cols)
        qkv_grads = [qkv_all[:, :, i].transpose(1, 2, 0, 3).reshape(own_d, d).astype(f32) for i in range(3)]
        smalls = lax.psum(jnp.concatenate([early, sums1], axis=0), ("rep", "shard"))

    mine = lax.dynamic_slice_in_dim(smalls, shard * own_d, own_d, 1)
    s_qb, s_vb, s_gain2, s_shift2, s_ob, s_db = [mine[i] for i in range(6)]
    s_gain1, s_shift1 = [mine[early.shape[0] + i] for i in range(2)]
    s_ub = lax.dynamic_slice_in_dim(smalls[6 : 6 + ff // d].reshape(-1), shard * own_f, own_f, 0)

    return (
        layer_out,
        tokens_grad,
        s_gain1,
        s_shift1,
        qkv_grads[0],
        s_qb,
        qkv_grads[1],
        qkv_grads[2],
        s_vb,
        out_grad,
        s_ob,
        s_gain2,
        s_shift2,
        up_grad,
        s_ub,
        down_grad,
        s_db,
    )


def solution(mesh):
    row, mat, vec = P("rep", "shard", None), P("shard", None), P("shard")
    return jax.shard_map(
        on_device,
        mesh=mesh,
        in_specs=(row, P("rep"), row, vec, vec, mat, vec, mat, mat, vec, mat, vec, vec, vec, mat, vec, mat, vec),
        out_specs=(row, row, vec, vec, mat, vec, mat, mat, vec, mat, vec, vec, vec, mat, vec, mat, vec),
        check_vma=False,
    )
```

```python
import functools
import math

import jax
import jax.numpy as jnp
from jax import lax
from jax.experimental import pallas as pl
from jax.experimental.pallas import tpu as pltpu
from jax.sharding import PartitionSpec as P

HEAD = 80
WIN = 256
AUG = 192
EPS = 1e-5
SCALE = HEAD**-0.5
SCALE2 = SCALE * math.log2(math.e)
DEAD = -1e30
ROWS = 256
GAIN1, SHIFT1, QBIAS, VBIAS, OBIAS, GAIN2, SHIFT2, DBIAS, LENGTHS = [slice(i, i + 1) for i in range(9)]
UBIAS = 9
FFN_TILE = 512
FFN_ROWS = 768
PAIR_SHARE = 3
f32 = jnp.float32
bf16 = jnp.bfloat16
MESH = pl.DeviceIdType.MESH

ERF_P = 0.35
ERF_C = (0.19458996, 0.23381038, -0.00165479, 0.67243411, -0.66868964, 0.76616445, -0.19665448)


def params(limit=60):
    return pltpu.CompilerParams(vmem_limit_bytes=limit * 2**20)


def cost(flops, size):
    return pl.CostEstimate(flops=int(flops), bytes_accessed=int(size), transcendentals=0)


def dot(a, b):
    return jnp.dot(a, b, preferred_element_type=f32)


def dot_nt(a, b):
    return lax.dot_general(a, b, (((1,), (1,)), ((), ())), preferred_element_type=f32)


def dot_tn(a, b):
    return lax.dot_general(a, b, (((0,), (0,)), ((), ())), preferred_element_type=f32)


def gelu_pair(a):
    expo = jnp.exp2(a * a * (-0.5 * math.log2(math.e)))
    t = 1.0 / (1.0 + jnp.abs(a) * (ERF_P * math.sqrt(0.5)))
    total = ERF_C[-1]
    for c in ERF_C[-2::-1]:
        total = total * t + c
    tail = 0.5 * expo * (total * t)
    cdf = jnp.where(a >= 0, 1.0 - tail, tail)
    return a * cdf, cdf + a * (expo * (1.0 / math.sqrt(2.0 * math.pi)))


def whole(shape):
    return pl.BlockSpec(shape, lambda *_: (0,) * len(shape))


def once(shape):
    return pl.BlockSpec(shape, lambda *_: (0,) * len(shape), pipeline_mode=pl.Buffered(1))


def row_block(rows, cols):
    return pl.BlockSpec((rows, cols), lambda i: (i, 0))


def standardize(x):
    centred = x - jnp.mean(x, axis=-1, keepdims=True)
    inv = lax.rsqrt(jnp.mean(centred * centred, axis=-1, keepdims=True) + EPS)
    return centred * inv, inv


class Link:
    def __init__(self, sems):
        self.send, self.recv, self.local = sems
        self.next = 0
        self.next_local = 0
        self.groups = lax.axis_size("shard")
        self.rep = lax.axis_index("rep")
        self.shard = lax.axis_index("shard")
        self.core = lax.rem(self.rep, 2)
        self.half = self.groups // 2

    def meet_plane(self, pair=False):
        barrier = pltpu.get_barrier_semaphore()
        base = self.rep - self.core
        for c in range(2):
            for p in range(self.groups):
                if c or p:
                    to = (base + (self.core ^ c), self.shard ^ p)
                    pl.semaphore_signal(barrier, inc=1, device_id=to, device_id_type=MESH)
        if pair:
            pl.semaphore_signal(barrier, inc=1, device_id=self.pair(), device_id_type=MESH)
        pl.semaphore_wait(barrier, 2 * self.groups - 1 + int(pair))

    def pair(self):
        return (self.rep ^ 2, self.shard)

    def meet_all(self):
        barrier = pltpu.get_barrier_semaphore()
        base = self.rep - self.core
        for c in range(2):
            for p in range(self.groups):
                if c or p:
                    to = (base + (self.core ^ c), self.shard ^ p)
                    pl.semaphore_signal(barrier, inc=1, device_id=to, device_id_type=MESH)
        pl.semaphore_signal(barrier, inc=1, device_id=self.inward(), device_id_type=MESH)

        @pl.when(self.inner())
        def _():
            pl.semaphore_signal(barrier, inc=1, device_id=self.outward(), device_id_type=MESH)
            pl.semaphore_wait(barrier, 2 * self.groups + 1)

        @pl.when(jnp.logical_not(self.inner()))
        def _():
            pl.semaphore_wait(barrier, 2 * self.groups)

    def inner(self):
        plane = lax.div(self.rep, 2)
        return (plane == 1) | (plane == 2)

    def inward(self):
        return (self.rep + jnp.where(self.rep < 4, 2, -2), self.shard)

    def outward(self):
        return (self.rep - jnp.where(self.rep < 4, 2, -2), self.shard)

    def meet_core(self):
        barrier = pltpu.get_barrier_semaphore()
        pl.semaphore_signal(barrier, inc=1, device_id=self.sibling(), device_id_type=MESH)
        pl.semaphore_wait(barrier, 1)

    def sibling(self):
        return (self.rep ^ 1, self.shard)

    def slots(self, count):
        first = self.next
        self.next += count
        return first

    def local_slots(self, count):
        first = self.next_local
        self.next_local += count
        return first

    def remote(self, src, dst, send, recv, to):
        return pltpu.make_async_remote_copy(
            src_ref=src,
            dst_ref=dst,
            send_sem=self.send.at[send],
            recv_sem=self.recv.at[recv],
            device_id=to,
            device_id_type=MESH,
        )

    def here(self, src, dst, slot):
        return pltpu.make_async_copy(src, dst, self.local.at[slot])


class Job:
    @staticmethod
    def buffers(source, shape):
        return []

    def forward(self):
        pass

    def inward(self):
        pass

    def across(self):
        pass

    def outward(self):
        pass


class Staged:
    def __init__(self, link, src, dst, buf):
        slot = link.local_slots(1)
        self.load = link.here(src, buf, slot)
        self.store = link.here(buf, dst, slot)

    def start(self):
        self.load.start()

    def turn(self):
        self.load.wait()
        self.store.start()

    def wait(self):
        self.store.wait()


class Gather(Job):
    def __init__(self, link, src, dst, bufs):
        self.link, self.src, self.dst = link, src, dst
        self.rows = src.shape[0]
        self.base = link.slots(max(4, link.groups - 1))
        self.keep = Staged(link, src, dst.at[link.shard], bufs[0])

    @staticmethod
    def buffers(source, shape):
        return [pltpu.VMEM(shape[1:], source.dtype)]

    def first(self):
        link = self.link
        peers = (1, 2) if link.groups == 4 else range(1, link.groups)
        return [
            link.remote(self.src, self.dst.at[link.shard], self.base + i, self.base + i, (link.rep, link.shard ^ p))
            for i, p in enumerate(peers)
        ]

    def second(self):
        link = self.link
        if link.groups != 4:
            return []
        cut = self.rows // 2
        parts = ((1, 2, pl.ds(0, cut)), (2, 1, pl.ds(cut, self.rows - cut)))
        out = []
        for i, (origin, to, rows) in enumerate(parts):
            ref = self.dst.at[link.shard ^ origin, rows]
            out.append(link.remote(ref, ref, self.base + 2 + i, self.base + 2 + i, (link.rep, link.shard ^ to)))
        return out

    def start(self):
        self.keep.start()
        for c in self.first():
            c.start()

    def forward(self):
        self.keep.turn()
        for c, d in zip(self.first(), self.second()):
            c.wait_recv()
            d.start()

    def finish(self):
        second = self.second()
        for c in self.first():
            if not second:
                c.wait_recv()
            c.wait_send()
        for c in second:
            c.wait()
        self.keep.wait()


class PairGather(Job):
    def __init__(self, link, src, dst, bufs):
        self.link, self.src, self.dst = link, src, dst
        rows = src.shape[0]
        outer = max(rows // PAIR_SHARE // 16, 1) * 16
        second = lax.rem(lax.div(link.rep, 2), 2)
        self.part = pl.ds(pl.multiple_of(second * outer, 16), rows - outer)
        self.alone = pl.ds(pl.multiple_of(second * (rows - outer), 16), outer)
        self.both = pl.ds(outer, rows - 2 * outer)
        self.base = link.slots(7)
        self.keep = Staged(link, src, dst.at[link.shard], bufs[0])

    @staticmethod
    def buffers(source, shape):
        return [pltpu.VMEM(shape[1:], source.dtype)]

    def step(self, src, dst, slot, to):
        return self.link.remote(src, dst, self.base + slot, self.base + slot, to)

    def near(self, bit):
        return (self.link.rep, self.link.shard ^ bit)

    def first(self):
        mine = self.dst.at[self.link.shard, self.part]
        return [self.step(self.src.at[self.part], mine, i, self.near(i + 1)) for i in range(2)]

    def second(self):
        one = self.dst.at[self.link.shard ^ 1, self.alone]
        two = self.dst.at[self.link.shard ^ 2, self.both]
        return [self.step(one, one, 2, self.near(2)), self.step(two, two, 3, self.near(1))]

    def third(self):
        out = []
        for i in range(3):
            ref = self.dst.at[self.link.shard ^ (i + 1), self.alone]
            out.append(self.step(ref, ref, 4 + i, self.link.pair()))
        return out

    def start(self):
        self.keep.start()
        for c in self.first():
            c.start()

    def forward(self):
        self.keep.turn()
        for c, d, e in zip(self.first(), self.second(), self.third()):
            c.wait_recv()
            d.start()
            e.start()

    def inward(self):
        self.second()[0].wait_recv()
        self.third()[2].start()

    def finish(self):
        for c in self.first():
            c.wait_send()
        one, two = self.second()
        one.wait_send()
        two.wait()
        for c in self.third():
            c.wait()
        self.keep.wait()


class ToClip(Job):
    def __init__(self, link, src, dst, bufs):
        self.link, self.src, self.dst = link, src, dst
        self.rows = src.shape[1]
        self.base = link.slots(link.half + 1)
        self.keep = link.local_slots(1)
        self.buf = bufs[0]

    @staticmethod
    def buffers(source, shape):
        return [pltpu.VMEM(source.shape[1:], source.dtype)]

    def copy(self, j):
        link = self.link
        core = lax.div(link.shard, link.half)
        to = (link.rep - link.core + core, link.core * link.half + j)
        mine = (core == link.core) & (link.core * link.half + j == link.shard)
        dst = self.dst.at[pl.ds(pl.multiple_of(link.shard * self.rows, self.rows), self.rows)]
        there = link.remote(self.src.at[j], dst, self.base + j, self.base + lax.rem(link.shard, link.half), to)
        return mine, there, link.here(self.src.at[j], self.buf, self.keep)

    def arrival(self, t):
        link = self.link
        source = link.core * link.half + t
        mine = (lax.div(link.shard, link.half) == link.core) & (source == link.shard)
        dst = self.dst.at[pl.ds(pl.multiple_of(source * self.rows, self.rows), self.rows)]
        there = link.remote(self.src.at[0], dst, self.base, self.base + t, link.sibling())
        return mine, there, link.here(self.buf, dst, self.keep)

    def to_sibling(self):
        link = self.link
        size = link.half * self.rows
        rows = pl.ds(pl.multiple_of(link.core * size, size), size)
        slot = self.base + link.half
        return link.remote(self.dst.at[rows], self.dst.at[rows], slot, slot, link.sibling())

    def start(self):
        for j in range(self.link.half):
            mine, there, here = self.copy(j)
            pl.when(mine)(here.start)
            pl.when(jnp.logical_not(mine))(there.start)

    def forward(self):
        for t in range(self.link.half):
            mine, there, here = self.arrival(t)

            @pl.when(mine)
            def _():
                self.copy(0)[2].wait()
                here.start()
                here.wait()

            pl.when(jnp.logical_not(mine))(there.wait_recv)
        self.to_sibling().start()

    def finish(self):
        self.to_sibling().wait()
        for j in range(self.link.half):
            mine, there, _ = self.copy(j)
            pl.when(jnp.logical_not(mine))(there.wait_send)


class FromClip(Job):
    def __init__(self, link, src, dst, bufs):
        self.link, self.src, self.dst = link, src, dst
        self.rows = dst.shape[1]
        self.base = link.slots(link.half)
        self.keep = link.local_slots(1)
        self.buf = bufs[0]

    @staticmethod
    def buffers(source, shape):
        return [pltpu.VMEM(shape[1:], source.dtype)]

    def copy(self, t):
        link = self.link
        core = lax.div(link.shard, link.half)
        shard = link.core * link.half + t
        mine = (core == link.core) & (shard == link.shard)
        clip = lax.rem(link.shard, link.half)
        src = self.src.at[pl.ds(t * self.rows, self.rows)]
        dst = self.dst.at[clip]
        there = link.remote(src, dst, self.base + t, self.base + clip, (link.rep - link.core + core, shard))
        return mine, there, link.here(src, self.buf, self.keep)

    def arrival(self, j):
        link = self.link
        mine = (lax.div(link.shard, link.half) == link.core) & (link.core * link.half + j == link.shard)
        src = self.src.at[pl.ds(0, self.rows)]
        there = link.remote(src, self.dst.at[j], self.base, self.base + j, link.sibling())
        return mine, there, link.here(self.buf, self.dst.at[j], self.keep)

    def start(self):
        for t in range(self.link.half):
            mine, there, here = self.copy(t)
            pl.when(mine)(here.start)
            pl.when(jnp.logical_not(mine))(there.start)

    def finish(self):
        for t in range(self.link.half):
            mine, there, here = self.copy(t)
            pl.when(jnp.logical_not(mine))(there.wait_send)
        for j in range(self.link.half):
            mine, there, here = self.arrival(j)

            @pl.when(mine)
            def _():
                self.copy(0)[2].wait()
                here.start()
                here.wait()

            pl.when(jnp.logical_not(mine))(there.wait_recv)


class Owners(Job):
    def __init__(self, link, src, dst, bufs):
        self.link, self.src, self.dst = link, src, dst
        self.base = link.slots(link.groups - 1)

    def copies(self):
        link = self.link
        return [
            link.remote(
                self.src.at[link.shard ^ p],
                self.dst.at[p - 1],
                self.base + p - 1,
                self.base + p - 1,
                (link.rep, link.shard ^ p),
            )
            for p in range(1, link.groups)
        ]

    def start(self):
        for c in self.copies():
            c.start()

    def finish(self):
        for c in self.copies():
            c.wait()


def add_low(a, b):
    return (a.astype(f32) + b.astype(f32)).astype(bf16)


class Reduce(Job):
    def __init__(self, link, src, dst, bufs):
        self.link, self.src, self.dst = link, src, dst
        self.base = link.slots(6)
        self.keep = link.local_slots(4)
        self.half = dst.shape[0] // 2
        self.pass_in, self.pass_sum, self.near, self.far, self.own = (bufs[2 * i : 2 * i + 2] for i in range(5))

    @staticmethod
    def buffers(source, shape):
        half = pltpu.VMEM((source.shape[1] // 2, source.shape[2]), source.dtype)
        return [half] * 10

    def block(self, i, part):
        rows = pl.ds(part * self.half, self.half)
        return self.src.at[self.link.shard ^ i, rows]

    def hops(self):
        link = self.link
        x, y = (link.rep, link.shard ^ 1), (link.rep, link.shard ^ 2)
        plan = (
            (self.block(3, 0), self.pass_in[0], x),
            (self.block(3, 1), self.pass_in[1], y),
            (self.block(1, 0), self.near[0], x),
            (self.block(2, 1), self.near[1], y),
        )
        return [link.remote(s, d, self.base + i, self.base + i, to) for i, (s, d, to) in enumerate(plan)]

    def later(self):
        link = self.link
        x, y = (link.rep, link.shard ^ 1), (link.rep, link.shard ^ 2)
        plan = zip(self.pass_sum, self.far, (y, x))
        return [link.remote(s, d, self.base + 4 + i, self.base + 4 + i, to) for i, (s, d, to) in enumerate(plan)]

    def loads(self):
        plan = (
            (self.block(2, 0), self.pass_sum[0]),
            (self.block(1, 1), self.pass_sum[1]),
            (self.block(0, 0), self.own[0]),
            (self.block(0, 1), self.own[1]),
        )
        return [self.link.here(s, d, self.keep + i) for i, (s, d) in enumerate(plan)]

    def store(self, part):
        rows = pl.ds(part * self.half, self.half)
        return self.link.here(self.own[part], self.dst.at[rows], self.keep + part)

    def start(self):
        for c in self.hops():
            c.start()
        for c in self.loads():
            c.start()

    def forward(self):
        hops, loads, later = self.hops(), self.loads(), self.later()
        for i in range(2):
            loads[i].wait()
            hops[i].wait_recv()
            self.pass_sum[i][...] = add_low(self.pass_sum[i][...], self.pass_in[i][...])
            later[i].start()

    def collect(self):
        hops, loads, later = self.hops(), self.loads(), self.later()
        for i in range(2):
            loads[2 + i].wait()
            hops[2 + i].wait_recv()
            later[i].wait_recv()
            total = self.own[i][...].astype(f32) + self.near[i][...].astype(f32) + self.far[i][...].astype(f32)
            self.own[i][...] = total.astype(bf16)
            self.store(i).start()
        for i in range(2):
            self.store(i).wait()

    def finish(self):
        self.collect()
        self.close()

    def close(self):
        for c in self.hops() + self.later():
            c.wait_send()


class Chain(Job):
    def __init__(self, link, src, dst, bufs):
        self.link, self.src, self.dst = link, src, dst
        self.own, self.one, self.two = bufs
        self.base = link.slots(4)
        self.keep = link.local_slots(2)

    @staticmethod
    def buffers(source, shape):
        return [pltpu.VMEM(shape[1:], source.dtype)] * 3

    def step(self, src, dst, slot, to):
        return self.link.remote(src, dst, self.base + slot, self.base + slot, to)

    def steps(self):
        link = self.link
        return (
            self.step(self.src, self.one, 0, link.inward()),
            self.step(self.own, self.two, 1, link.inward()),
            self.step(self.one, self.two, 2, link.outward()),
        )

    def share(self, ref):
        link = self.link
        place = self.dst.at[link.core]
        return self.step(ref, place, 3, link.sibling()), link.here(ref, place, self.keep + 1)

    def start(self):
        inner = self.link.inner()
        pl.when(inner)(self.link.here(self.src, self.own, self.keep).start)
        pl.when(jnp.logical_not(inner))(self.steps()[0].start)

    def add(self, a, b):
        return (a[...].astype(f32) + b[...].astype(f32)).astype(a.dtype)

    def sent(self):
        pl.when(jnp.logical_not(self.link.inner()))(self.steps()[0].wait_send)

    def inward(self):
        @pl.when(self.link.inner())
        def _():
            steps = self.steps()
            self.link.here(self.src, self.own, self.keep).wait()
            steps[0].wait_recv()
            self.own[...] = self.add(self.own, self.one)
            steps[1].start()

    def across(self):
        @pl.when(self.link.inner())
        def _():
            steps = self.steps()
            steps[1].wait_recv()
            self.one[...] = self.add(self.own, self.two)
            steps[2].start()
            for c in self.share(self.one):
                c.start()

    def outward(self):
        @pl.when(jnp.logical_not(self.link.inner()))
        def _():
            self.steps()[2].wait_recv()
            for c in self.share(self.two):
                c.start()

    def finish(self):
        swap, here = self.share(self.one)
        swap.wait()
        here.wait()
        inner = self.link.inner()

        @pl.when(inner)
        def _():
            self.steps()[1].wait_send()
            self.steps()[2].wait_send()


def chain_steps(chains):
    lists = []
    for i in range(len(chains) + 1):
        lists.append(
            [step for c in chains[i : i + 1] for step in (c.inward, c.sent)]
            + [c.start for c in chains[i + 1 : i + 2]]
            + [c.across for c in chains[max(i - 1, 0) : i]]
        )
    return lists


def gather_steps(gathers):
    lists = []
    for i in range(len(gathers) + 2):
        lists.append(
            [c.start for c in gathers[i : i + 1]]
            + [c.forward for c in gathers[max(i - 1, 0) : i]]
            + [c.inward for c in gathers[max(i - 2, 0) : max(i - 1, 0)]]
        )
    return lists


def run(steps):
    for step in steps:
        step()


def split_gathers(bound):
    gathers = [job for job in bound if isinstance(job, (Gather, PairGather))]
    return gathers, [job for job in bound if job not in gathers]


class Jobs:
    def __init__(self, *jobs):
        self.jobs = [(job + (None,))[:4] for job in jobs]
        self.pairs = any(job[0] is PairGather for job in jobs)
        self.bufs = [kind.buffers(a, shape) for kind, a, shape, _ in self.jobs]

    def sources(self):
        return [a for _, a, _, _ in self.jobs]

    def in_specs(self):
        return [pl.BlockSpec(memory_space=pl.ANY)] * len(self.jobs)

    def out_shapes(self):
        return [jax.ShapeDtypeStruct(shape, a.dtype) for _, a, shape, _ in self.jobs]

    def scratch(self, extra=0):
        groups = lax.axis_size("shard")
        remote = len(self.jobs) * max(7, groups) + extra
        return [b for bufs in self.bufs for b in bufs] + [
            pltpu.SemaphoreType.DMA((remote,)),
            pltpu.SemaphoreType.DMA((remote,)),
            pltpu.SemaphoreType.DMA((4 * len(self.jobs) + extra + 1,)),
        ]

    def bind(self, rest, srcs, dsts):
        rest = list(rest)
        bufs = []
        for shapes in self.bufs:
            bufs.append([rest.pop(0) for _ in shapes])
        link = Link(rest[:3])
        bound = [
            kind(link, view(a) if view else a, b, c) for (kind, _, _, view), a, b, c in zip(self.jobs, srcs, dsts, bufs)
        ]
        return link, bound, rest[3:]


def comm_params(number, limit=60):
    return pltpu.CompilerParams(
        vmem_limit_bytes=limit * 2**20, collective_id=number, has_side_effects=True
    )


def exchange_call(jobs, sibling, number, name):
    count = len(jobs.jobs)

    def kernel(*refs):
        srcs, mine = refs[:count], refs[count]
        dsts, other = refs[count + 1 : 2 * count + 1], refs[2 * count + 1]
        link, bound, _ = jobs.bind(refs[2 * count + 2 :], srcs, dsts)
        slot = link.slots(1)
        swap = link.remote(mine, other, slot, slot, link.sibling())
        link.meet_plane(jobs.pairs)
        swap.start()
        gathers, others = split_gathers(bound)
        steps = gather_steps(gathers)
        run([job.start for job in others] + steps[0])
        for i, some in enumerate(steps[1:]):
            if i == 1:
                run([job.forward for job in others])
            run(some)
        run([job.finish for job in bound])
        swap.wait()

    return pl.pallas_call(
        kernel,
        in_specs=jobs.in_specs() + [pl.BlockSpec(memory_space=pl.ANY)],
        out_specs=[pl.BlockSpec(memory_space=pl.ANY)] * (count + 1),
        out_shape=jobs.out_shapes() + [jax.ShapeDtypeStruct(sibling.shape, sibling.dtype)],
        scratch_shapes=jobs.scratch(1),
        compiler_params=comm_params(number),
        name=name,
    )(*jobs.sources(), sibling)


def pack_kernel(*refs, count):
    out_ref = refs[-1]
    lens_ref = refs[count]
    out_ref[...] = jnp.zeros_like(out_ref)
    row = 0
    for ref in refs[:count]:
        size = refs[0].shape[0]
        for part in range(ref.shape[0] // size):
            value = ref[part * size : (part + 1) * size].astype(f32)
            out_ref[row : row + 1, :size] = value.reshape(1, size)
            row += 1
        if row == LENGTHS.start:
            lane = lax.broadcasted_iota(jnp.int32, (1, out_ref.shape[1]), 1)
            value = jnp.zeros(lane.shape, f32)
            for clip in range(lens_ref.shape[0]):
                value = jnp.where(lane == clip, lens_ref[clip].astype(f32), value)
            out_ref[row : row + 1, :] = value
            row += 1


def pack_call(vectors, lengths):
    vmem = pl.BlockSpec(memory_space=pltpu.VMEM)
    lanes = pl.cdiv(vectors[0].shape[0], 128) * 128
    return pl.pallas_call(
        functools.partial(pack_kernel, count=len(vectors)),
        in_specs=[vmem] * len(vectors) + [pl.BlockSpec(memory_space=pltpu.SMEM)],
        out_specs=vmem,
        out_shape=jax.ShapeDtypeStruct((16, lanes), f32),
        name="pack",
    )(*vectors, lengths)


def first_kernel(*refs, jobs, size):
    count = len(jobs.jobs)
    srcs, mine = refs[:count], refs[count]
    h_ref, *heads, vec_ref = refs[count + 1 : count + 6]
    dsts, other = refs[count + 6 : 2 * count + 6], refs[2 * count + 6]
    x, small, weight, bias, sems = refs[2 * count + 7 : 2 * count + 12]
    link, bound, _ = jobs.bind(refs[2 * count + 12 :], srcs, dsts)
    tokens, smalls, *gathers = bound
    slot = link.slots(1)
    swap = link.remote(mine, other, slot, slot, link.sibling())
    n = x.shape[0]
    width = weight.shape[2]
    part = size // 2

    def load(src, dst, i):
        return pltpu.make_async_copy(src, dst, sems.at[i])

    link.meet_plane(jobs.pairs)
    steps = gather_steps(gathers)
    swap.start()
    run([smalls.start, tokens.start] + steps[0])
    run([smalls.forward, smalls.finish])
    load(dsts[1], small, 0).start()
    run(steps[1])
    load(dsts[1], small, 0).wait()
    bias[...] = jnp.zeros_like(bias)
    for s in range(small.shape[0]):
        vec_ref[:, s * size : (s + 1) * size] = small[s][:, :size]
        for row, first in ((QBIAS, 0), (VBIAS, 2 * width)):
            value = jnp.where(link.core == 0, small[s, row, :part], small[s, row, part:size])
            bias[:, first + s * part : first + (s + 1) * part] = value
    tokens.forward()
    run(steps[2])
    tokens.finish()
    load(dsts[0], x, 0).start()
    load(dsts[0], x, 0).wait()

    def norm(i, carry):
        rows = pl.ds(pl.multiple_of(i * ROWS, ROWS), ROWS)
        xhat, _ = standardize(x[rows, :].astype(f32))
        h_ref[rows, :] = (xhat * vec_ref[GAIN1] + vec_ref[SHIFT1]).astype(bf16)
        return carry

    lax.fori_loop(0, n // ROWS, norm, 0)
    for ref in heads:
        ref[:, width:] = jnp.zeros((n, ref.shape[1] - width), bf16)
    for i, (gather, ref) in enumerate(zip(gathers, heads)):
        run(steps[3 + i] if 3 + i < len(steps) else [])
        gather.finish()
        for s in range(small.shape[0]):
            load(dsts[2 + i].at[s], weight.at[i, pl.ds(s * size, size)], 1 + s).start()
        for s in range(small.shape[0]):
            load(dsts[2 + i].at[s], weight.at[i, pl.ds(s * size, size)], 1 + s).wait()

        def project(j, carry):
            rows = pl.ds(pl.multiple_of(j * ROWS, ROWS), ROWS)
            z = dot(h_ref[rows, :], weight[i]) + bias[:, i * width : (i + 1) * width]
            ref[rows, :width] = z.astype(bf16)
            return carry

        lax.fori_loop(0, n // ROWS, project, 0)
    swap.wait()


def first_call(jobs, small, wide, number):
    (n, d), groups = jobs.jobs[0][2], lax.axis_size("shard")
    width = jobs.jobs[2][2][2]
    vmem = pl.BlockSpec(memory_space=pltpu.VMEM)
    hbm = pl.BlockSpec(memory_space=pl.ANY)
    head = jax.ShapeDtypeStruct((n, wide), bf16)
    return pl.pallas_call(
        functools.partial(first_kernel, jobs=jobs, size=d // groups),
        in_specs=jobs.in_specs() + [hbm],
        out_specs=[vmem] * 5 + jobs.in_specs() + [hbm],
        out_shape=[jax.ShapeDtypeStruct((n, d), bf16), head, head, head, jax.ShapeDtypeStruct((16, d), f32)]
        + jobs.out_shapes()
        + [jax.ShapeDtypeStruct(small.shape, small.dtype)],
        scratch_shapes=[
            pltpu.VMEM((n, d), bf16),
            pltpu.VMEM((groups,) + small.shape, f32),
            pltpu.VMEM((3, d, width), bf16),
            pltpu.VMEM((1, 3 * width), f32),
            pltpu.SemaphoreType.DMA((1 + groups,)),
        ]
        + jobs.scratch(1),
        compiler_params=comm_params(number),
        cost_estimate=cost(6 * n * d * width, 12 * n * d),
        name="first",
    )(*jobs.sources(), small)


def head_window(h):
    start = h * HEAD
    base = (start // 128) * 128
    off = start - base
    lane = lax.broadcasted_iota(jnp.int32, (1, WIN), 1)
    keep = jnp.where((lane >= off) & (lane < off + HEAD), 1.0, 0.0)
    return pl.ds(pl.multiple_of(base, 128), WIN), keep, lane


def put3(x, lane, first, value):
    hi = value.astype(bf16).astype(f32)
    rest = value - hi
    mid = rest.astype(bf16).astype(f32)
    low = rest - mid
    return jnp.where(
        lane == first,
        hi,
        jnp.where(lane == first + 1, mid, jnp.where(lane == first + 2, low, x)),
    )


def key_extra(rows, length):
    lane = lax.broadcasted_iota(jnp.int32, (rows, WIN), 1)
    row = lax.broadcasted_iota(jnp.int32, (rows, WIN), 0)
    dead = jnp.where(row >= length, DEAD, 0.0)
    minus = jnp.where((lane > AUG) & (lane <= AUG + 3), -1.0, 0.0)
    return jnp.where(lane == AUG, dead, minus).astype(bf16)


def attn_fwd_kernel(*refs, bq, jobs):
    count = len(jobs.jobs)
    len_ref, q_ref, k_ref, v_ref = refs[:4]
    o_ref, lse_ref = refs[4 + count : 6 + count]
    acc, kx = refs[6 + 2 * count : 8 + 2 * count]
    link, bound, _ = jobs.bind(refs[8 + 2 * count :], refs[4 : 4 + count], refs[6 + count : 6 + 2 * count])
    h = pl.program_id(0)
    heads = pl.num_programs(0)
    n = q_ref.shape[0]
    width = o_ref.shape[1]

    gathers, others = split_gathers(bound)
    steps = gather_steps(gathers)

    @pl.when(h == 0)
    def _():
        link.meet_plane(jobs.pairs)
        run([job.start for job in others] + steps[0])
        acc[...] = jnp.zeros_like(acc)
        lse_ref[...] = jnp.zeros_like(lse_ref)
        kx[...] = key_extra(n, len_ref[0])

    for number, some in zip((2, 4, 6, 7), steps[1:]):

        @pl.when(h == number * heads // 8)
        def _():
            run(some)

    win, keep, lane = head_window(h)
    low = keep.astype(bf16)
    q_one = jnp.where(lane == AUG, 1.0, 0.0).astype(bf16)
    v_one = jnp.where((lane >= AUG) & (lane < AUG + 3), 1.0, 0.0).astype(bf16)
    k = k_ref[:, win] * low + kx[...]
    v = v_ref[:, win] * low + v_one
    for i in range(n // bq):
        rows = slice(i * bq, (i + 1) * bq)
        s = dot_nt(q_ref[rows, win] * low + q_one, k)
        peak = jnp.max(s, axis=-1, keepdims=True)
        p = jnp.exp2((s - peak) * SCALE2).astype(bf16)
        o = dot(p, v)
        total = o[:, AUG : AUG + 1]
        acc[rows, win] += o * (keep * (1.0 / total))
        here = lax.broadcasted_iota(jnp.int32, (bq, 128), 1) == h
        lse = peak + jnp.log(total) * (1.0 / SCALE)
        lse_ref[rows, :] = jnp.where(here, lse, lse_ref[rows, :])

    @pl.when(h == heads - 1)
    def _():
        o_ref[:, :width] = acc[:, :width].astype(bf16)
        for some in steps[5:]:
            run(some)
        run([job.finish for job in bound])


def attn_fwd_call(length, q, k, v, width, heads, jobs, number):
    n, wide = q.shape
    return pl.pallas_call(
        functools.partial(attn_fwd_kernel, bq=256, jobs=jobs),
        grid=(heads,),
        in_specs=[pl.BlockSpec(memory_space=pltpu.SMEM)] + [whole((n, wide))] * 3 + jobs.in_specs(),
        out_specs=[whole((n, width)), whole((n, 128))] + jobs.in_specs(),
        out_shape=[jax.ShapeDtypeStruct((n, width), bf16), jax.ShapeDtypeStruct((n, 128), f32)] + jobs.out_shapes(),
        scratch_shapes=[pltpu.VMEM((n, wide), f32), pltpu.VMEM((n, WIN), bf16)] + jobs.scratch(),
        compiler_params=comm_params(number),
        cost_estimate=cost(4 * n * n * WIN * heads, 8 * n * wide),
        name="attend",
    )(length, q, k, v, *jobs.sources())


def attn_bwd_kernel(*refs, bk, jobs):
    count = len(jobs.jobs)
    len_ref, q_ref, k_ref, v_ref, o_ref, do_ref, lse_ref = refs[:7]
    g_ref, sum_ref = refs[7 + count : 9 + count]
    dq, dk, dv, part, qa, da, kx = refs[9 + 2 * count : 16 + 2 * count]
    link, bound, _ = jobs.bind(refs[16 + 2 * count :], refs[7 : 7 + count], refs[9 + count : 9 + 2 * count])
    chains = [job for job in bound if isinstance(job, Chain)]
    h = pl.program_id(0)
    n = q_ref.shape[0]

    @pl.when(h == 0)
    def _():
        if chains:
            link.meet_all()
        else:
            link.meet_plane(jobs.pairs)
        for job in bound:
            if job not in chains[1:]:
                job.start()
        for ref in (dq, dk, dv):
            ref[...] = jnp.zeros_like(ref)
        kx[...] = key_extra(n, len_ref[0])

    heads = pl.num_programs(0)

    def at_head(number, steps):
        @pl.when(h == number)
        def _():
            for step in steps:
                step()

    steps = chain_steps(chains) if chains else []
    for number, some in zip((1, 2, 4, 6, 7), steps):
        at_head(number, some)
    at_head(heads - 3, [job.forward for job in bound])

    win, keep, lane = head_window(h)
    low = keep.astype(bf16)
    v_one = jnp.where((lane >= AUG) & (lane < AUG + 3), 1.0, 0.0).astype(bf16)
    for i in range(n // ROWS):
        rows = slice(i * ROWS, (i + 1) * ROWS)
        here = lax.broadcasted_iota(jnp.int32, (ROWS, 128), 1) == h
        lse = jnp.sum(jnp.where(here, lse_ref[rows, :], 0.0), axis=-1, keepdims=True)
        q = q_ref[rows, win].astype(f32) * keep
        qa[rows, :] = jnp.where(lane == AUG, 1.0, put3(q, lane, AUG + 1, lse)).astype(bf16)
        d = do_ref[rows, win].astype(f32) * keep
        delta = jnp.sum(d * o_ref[rows, win].astype(f32), axis=-1, keepdims=True)
        da[rows, :] = put3(d, lane, AUG, -delta).astype(bf16)
    for i in range(n // bk):
        rows = slice(i * bk, (i + 1) * bk)
        k = k_ref[rows, win] * low + kx[rows, :]
        v = v_ref[rows, win] * low + v_one
        p = jnp.exp2(dot_nt(k, qa[...]) * SCALE2)
        ds = (p * dot_nt(v, da[...])).astype(bf16)
        dv[rows, win] += dot(p.astype(bf16), da[...]) * keep
        dk[rows, win] += dot(ds, qa[...]) * keep
        new = dot_tn(ds, k)
        part[...] = new if i == 0 else part[...] + new
    dq[:, win] += part[...] * keep

    @pl.when(h == heads - 1)
    def _():
        for i, (ref, factor) in enumerate(((dq, SCALE), (dk, SCALE), (dv, 1.0))):
            value = (ref[:, : g_ref.shape[1] // 3] * factor).astype(bf16)
            cols = slice(i * value.shape[1], (i + 1) * value.shape[1])
            g_ref[:, cols] = value
            sum_ref[:, cols] = jnp.sum(value.astype(f32), axis=0, keepdims=True)
        for some in steps[5:]:
            run(some)
        for job in bound:
            job.outward()
        for job in bound:
            job.finish()


def attn_bwd_call(length, q, k, v, o, do, lse, width, heads, jobs, number):
    n, wide = q.shape
    return pl.pallas_call(
        functools.partial(attn_bwd_kernel, bk=256, jobs=jobs),
        grid=(heads,),
        in_specs=[pl.BlockSpec(memory_space=pltpu.SMEM)]
        + [once((n, wide))] * 5
        + [once((n, 128))]
        + jobs.in_specs(),
        out_specs=[once((n, 3 * width)), whole((1, 3 * width))] + jobs.in_specs(),
        out_shape=[
            jax.ShapeDtypeStruct((n, 3 * width), bf16),
            jax.ShapeDtypeStruct((1, 3 * width), f32),
        ]
        + jobs.out_shapes(),
        scratch_shapes=[pltpu.VMEM((n, wide), f32)] * 3
        + [pltpu.VMEM((n, WIN), f32)]
        + [pltpu.VMEM((n, WIN), bf16)] * 3
        + jobs.scratch(),
        compiler_params=comm_params(number),
        cost_estimate=cost(10 * n * n * WIN * heads, 20 * n * wide),
        name="attend_back",
    )(length, q, k, v, o, do, lse, *jobs.sources())


def middle_kernel(*refs, jobs):
    count = len(jobs.jobs)
    o_ref, w_ref, x_ref, vec_ref = refs[:4]
    mid_ref, h_ref, owide_ref = refs[4 + count : 7 + count]
    mine, other = refs[7 + 2 * count : 9 + 2 * count]
    link, bound, _ = jobs.bind(refs[9 + 2 * count :], refs[4 : 4 + count], refs[7 + count : 7 + 2 * count])
    n = x_ref.shape[0]
    width = o_ref.shape[1]
    base = link.slots(n // ROWS)
    link.meet_plane(jobs.pairs)
    for job in bound:
        job.start()

    def swap(i):
        rows = pl.ds(pl.multiple_of(i * ROWS, ROWS), ROWS)
        return rows, link.remote(mine.at[rows], other.at[rows], base + i, base + i, link.sibling())

    def project(i, carry):
        rows, copy = swap(i)
        mine[rows, :] = dot(o_ref[rows, :], w_ref[...]).astype(bf16)
        copy.start()
        return carry

    def norm(i, carry):
        rows, copy = swap(i)
        copy.wait_recv()
        mid = x_ref[rows, :].astype(f32) + (
            mine[rows, :].astype(f32) + other[rows, :].astype(f32) + vec_ref[OBIAS]
        )
        mid_ref[rows, :] = mid
        xhat, _ = standardize(mid)
        h_ref[rows, :] = (xhat * vec_ref[GAIN2] + vec_ref[SHIFT2]).astype(bf16)
        return carry

    lax.fori_loop(0, n // ROWS, project, 0)
    owide_ref[:, :width] = o_ref[...]
    owide_ref[:, width:] = jnp.zeros((n, owide_ref.shape[1] - width), bf16)
    lax.fori_loop(0, n // ROWS, norm, 0)
    for i in range(n // ROWS):
        swap(i)[1].wait_send()
    for job in bound:
        job.forward()
    for job in bound:
        job.inward()
    for job in bound:
        job.finish()


def middle_call(o, w, x, vec, wide, jobs, number):
    n, d = x.shape
    vmem = pl.BlockSpec(memory_space=pltpu.VMEM)
    return pl.pallas_call(
        functools.partial(middle_kernel, jobs=jobs),
        in_specs=[vmem] * 4 + jobs.in_specs(),
        out_specs=[vmem] * 3 + jobs.in_specs(),
        out_shape=[
            jax.ShapeDtypeStruct((n, d), f32),
            jax.ShapeDtypeStruct((n, d), bf16),
            jax.ShapeDtypeStruct((n, wide), bf16),
        ]
        + jobs.out_shapes(),
        scratch_shapes=[pltpu.VMEM((n, d), bf16)] * 2 + jobs.scratch(n // ROWS),
        compiler_params=comm_params(number),
        cost_estimate=cost(2 * n * w.size, 14 * n * d),
        name="middle",
    )(o, w, x, vec, *jobs.sources())


def ffn_kernel(*refs, chained, last, mc, jobs):
    count = len(jobs.jobs)
    h_ref, dz_ref, up_ref, ub_ref, dn_ref = refs[:5]
    refs = refs[5:]
    if chained:
        old_out, old_dh = refs[:2]
        refs = refs[2:]
    srcs, refs = refs[:count], refs[count:]
    out_ref, dh_ref, dup_ref, ddn_ref, dub_ref = refs[:5]
    dsts, refs = refs[5 : 5 + count], refs[5 + count :]
    ht, act, grad = refs[:3]
    acc, dh = refs[3:5] if last else (out_ref, dh_ref)
    refs = refs[5:] if last else refs[3:]
    link, bound, refs = jobs.bind(refs, srcs, dsts)
    gathers, others = split_gathers(bound)
    steps = gather_steps(gathers)
    t = pl.program_id(0)
    tiles = pl.num_programs(0)
    n = h_ref.shape[0]

    @pl.when(t == 0)
    def _():
        link.meet_plane(jobs.pairs)
        run([job.start for job in others] + steps[0])
        if chained:
            sem = refs[0]
            copies = [
                pltpu.make_async_copy(src, dst, sem.at[i])
                for i, (src, dst) in enumerate(((old_out, acc), (old_dh, dh)))
            ]
            for c in copies:
                c.start()
            ht[...] = h_ref[...].T
            for c in copies:
                c.wait()
        else:
            ht[...] = h_ref[...].T
            acc[...] = jnp.zeros_like(acc)
            dh[...] = jnp.zeros_like(dh)

    def at_tile(number, some):
        if some:

            @pl.when(t == number)
            def _():
                run(some)

    at_tile(tiles - 1, [job.forward for job in others])

    def step(i, carry):
        rows = pl.ds(pl.multiple_of(i * mc, mc), mc)
        g, slope = gelu_pair(dot(h_ref[rows, :], up_ref[...]) + ub_ref[...])
        g = g.astype(bf16)
        da = (dot_nt(dz_ref[rows, :], dn_ref[...]) * slope).astype(bf16)
        act[rows, :] = g
        grad[rows, :] = da
        acc[rows, :] += dot(g, dn_ref[...])
        dh[rows, :] += dot_nt(da, up_ref[...])
        return carry

    lax.fori_loop(0, n // mc, step, 0)

    at_tile(0, steps[1] if gathers else [])
    dub_ref[...] = jnp.sum(grad[...].astype(f32), axis=0, keepdims=True)
    dup_ref[...] = dot(ht[...], grad[...]).astype(bf16)
    at_tile(tiles - 1, steps[2] if gathers else [])
    ddn_ref[...] = dot_tn(act[...], dz_ref[...]).astype(bf16)

    @pl.when(t == tiles - 1)
    def _():
        if last:
            out_ref[...] = acc[...].astype(out_ref.dtype)
            dh_ref[...] = dh[...].astype(dh_ref.dtype)
        for some in steps[3:]:
            run(some)
        run([job.finish for job in bound])


def ffn_call(h, dz, up, bias, down, old, last, jobs, number, name):
    n, d = h.shape
    hidden = up.shape[1]
    bt = FFN_TILE
    out = jax.ShapeDtypeStruct((n, d), bf16 if last else f32)
    chained = old is not None
    kept = once((n, d))
    return pl.pallas_call(
        functools.partial(ffn_kernel, chained=chained, last=last, mc=FFN_ROWS, jobs=jobs),
        grid=(hidden // bt,),
        in_specs=[
            kept,
            kept,
            pl.BlockSpec((d, bt), lambda t: (0, t)),
            pl.BlockSpec((1, bt), lambda t: (0, t)),
            pl.BlockSpec((bt, d), lambda t: (t, 0)),
        ]
        + ([pl.BlockSpec(memory_space=pl.ANY)] * 2 if chained else [])
        + jobs.in_specs(),
        out_specs=[
            kept,
            kept,
            pl.BlockSpec((d, bt), lambda t: (0, t)),
            pl.BlockSpec((bt, d), lambda t: (t, 0)),
            pl.BlockSpec((1, bt), lambda t: (0, t)),
        ]
        + jobs.in_specs(),
        out_shape=[
            out,
            out,
            jax.ShapeDtypeStruct((d, hidden), bf16),
            jax.ShapeDtypeStruct((hidden, d), bf16),
            jax.ShapeDtypeStruct((1, hidden), f32),
        ]
        + jobs.out_shapes(),
        scratch_shapes=[pltpu.VMEM((d, n), bf16)]
        + [pltpu.VMEM((n, bt), bf16)] * 2
        + ([pltpu.VMEM((n, d), f32)] * 2 if last else [])
        + jobs.scratch()
        + ([pltpu.SemaphoreType.DMA((2,))] if chained else []),
        compiler_params=comm_params(number),
        cost_estimate=cost(12 * n * d * hidden, 8 * d * hidden + 12 * n * d),
        name=name,
    )(h, dz, up, bias, down, *(old if chained else ()), *jobs.sources())


def second_back_kernel(*refs, jobs):
    count = len(jobs.jobs)
    mid_ref, dh_ref, out_ref, dz_ref, vec_ref, w_ref, o_ref, dh_any, out_any = refs[:9]
    dmid_ref, do_ref, dw_ref, sums_ref, layer_ref = refs[9 + count : 14 + count]
    acc, dh_other, out_other = refs[14 + 2 * count : 17 + 2 * count]
    link, bound, _ = jobs.bind(refs[17 + 2 * count :], refs[9 : 9 + count], refs[14 + count : 14 + 2 * count])
    chains = [job for job in bound if isinstance(job, Chain)]
    others = [job for job in bound if job not in chains]
    steps = chain_steps(chains) if chains else []
    i = pl.program_id(0)
    blocks = pl.num_programs(0)
    half = layer_ref.shape[0] // ROWS
    width = w_ref.shape[0]
    base = link.slots(3 * half)

    def swap_dh(j):
        rows = pl.ds(pl.multiple_of(j * ROWS, ROWS), ROWS)
        return link.remote(dh_any.at[rows], dh_other.at[rows], base + j, base + j, link.sibling())

    def swap_out(j):
        src = pl.ds(pl.multiple_of(((1 - link.core) * half + j) * ROWS, ROWS), ROWS)
        dst = pl.ds(pl.multiple_of(j * ROWS, ROWS), ROWS)
        slot = base + 2 * half + j
        return link.remote(out_any.at[src], out_other.at[dst], slot, slot, link.sibling())

    @pl.when(i == 0)
    def _():
        if chains:
            link.meet_all()
        else:
            link.meet_plane()
        for j in range(2 * half):
            swap_dh(j).start()
        for j in range(half):
            swap_out(j).start()
        run([job.start for job in others + chains[:1]])
        acc[...] = jnp.zeros_like(acc)
        sums_ref[...] = jnp.zeros_like(sums_ref)

    for number, some in zip((2, 4), steps):

        @pl.when(i == number)
        def _():
            run(some)

    @pl.when(i == blocks - 1)
    def _():
        run([job.forward for job in others])

    mid = mid_ref[...]
    xhat, inv = standardize(mid)
    swap_dh(i).wait_recv()
    rows = pl.ds(pl.multiple_of(i * ROWS, ROWS), ROWS)
    dh = dh_ref[...].astype(f32) + dh_other[rows, :].astype(f32)
    dx = dh * vec_ref[GAIN2]
    dz = dz_ref[...].astype(f32)
    dmid = dz + inv * (
        dx - jnp.mean(dx, axis=-1, keepdims=True) - xhat * jnp.mean(dx * xhat, axis=-1, keepdims=True)
    )
    dmid_ref[...] = dmid
    dy = dmid.astype(bf16)
    do_ref[:, :width] = dot_nt(dy, w_ref[...]).astype(bf16)
    do_ref[:, width:] = jnp.zeros((do_ref.shape[0], do_ref.shape[1] - width), bf16)
    acc[...] += dot_tn(o_ref[...], dy)
    for row, value in enumerate((dh * xhat, dh, dy.astype(f32), dz)):
        sums_ref[row : row + 1, :] += jnp.sum(value, axis=0, keepdims=True)

    j = i - link.core * half

    @pl.when((j >= 0) & (j < half))
    def _():
        swap_out(j).wait_recv()
        here = pl.ds(pl.multiple_of(j * ROWS, ROWS), ROWS)
        layer_ref[here, :] = (
            mid + (out_ref[...].astype(f32) + out_other[here, :].astype(f32) + vec_ref[DBIAS])
        ).astype(bf16)

    @pl.when(i == blocks - 1)
    def _():
        dw_ref[...] = acc[...].astype(bf16)
        for j in range(2 * half):
            swap_dh(j).wait_send()
        for j in range(half):
            swap_out(j).wait_send()
        for some in steps[2:]:
            run(some)
        run([job.outward for job in chains] + [job.finish for job in others + chains])


def second_back_call(mid, dh, out, dz, vec, w, o, wide, jobs, number):
    n, d = mid.shape
    width = w.shape[0]
    block = row_block(ROWS, d)
    count = 3 * n // ROWS // 2
    return pl.pallas_call(
        functools.partial(second_back_kernel, jobs=jobs),
        grid=(n // ROWS,),
        in_specs=[block] * 4
        + [whole(vec.shape), whole(w.shape), row_block(ROWS, width)]
        + [pl.BlockSpec(memory_space=pl.ANY)] * 2
        + jobs.in_specs(),
        out_specs=[block, row_block(ROWS, wide), whole((width, d)), whole((8, d)), whole((n // 2, d))]
        + jobs.in_specs(),
        out_shape=[
            jax.ShapeDtypeStruct((n, d), f32),
            jax.ShapeDtypeStruct((n, wide), bf16),
            jax.ShapeDtypeStruct((width, d), bf16),
            jax.ShapeDtypeStruct((8, d), f32),
            jax.ShapeDtypeStruct((n // 2, d), bf16),
        ]
        + jobs.out_shapes(),
        scratch_shapes=[
            pltpu.VMEM((width, d), f32),
            pltpu.VMEM((n, d), bf16),
            pltpu.VMEM((n // 2, d), bf16),
        ]
        + jobs.scratch(count),
        compiler_params=comm_params(number),
        cost_estimate=cost(4 * n * d * width, 14 * n * d),
        name="second_back",
    )(mid, dh, out, dz, vec, w, o, dh, out, *jobs.sources())


def dw_kernel(h_ref, g_ref, out_ref):
    out_ref[...] = dot_tn(h_ref[...], g_ref[...]).astype(bf16)


def dw_call(h, grads):
    n, d = h.shape
    cols = grads.shape[1]
    return pl.pallas_call(
        dw_kernel,
        grid=(d // 256,),
        in_specs=[pl.BlockSpec((n, 256), lambda i: (0, i)), whole((n, cols))],
        out_specs=row_block(256, cols),
        out_shape=jax.ShapeDtypeStruct((d, cols), bf16),
        compiler_params=params(),
        cost_estimate=cost(2 * n * d * cols, 2 * (n * d + n * cols + d * cols)),
        name="project_grad",
    )(h, grads)


def first_back_kernel(*refs, jobs):
    count = len(jobs.jobs)
    g_ref, w_ref, vec_ref, x_any, dmid_any = refs[:5]
    dx_ref, sums_ref = refs[5 + count : 7 + count]
    x, dmid, mine, other = refs[7 + 2 * count : 11 + 2 * count]
    link, bound, _ = jobs.bind(refs[11 + 2 * count :], refs[5 : 5 + count], refs[7 + count : 7 + 2 * count])
    size = dx_ref.shape[0]
    half = size // ROWS
    base = link.slots(half)
    keep = link.local_slots(2)
    own = pl.ds(pl.multiple_of(link.core * size, size), size)
    loads = [link.here(x_any.at[own], x, keep), link.here(dmid_any.at[own], dmid, keep + 1)]
    for c in loads:
        c.start()
    link.meet_plane(jobs.pairs)
    for job in bound:
        job.start()

    def product(j):
        rows = pl.ds(pl.multiple_of(j * ROWS, ROWS), ROWS)
        return dot_nt(g_ref[rows, :], w_ref[...])

    def swap(j):
        rows = pl.ds(pl.multiple_of(j * ROWS, ROWS), ROWS)
        return rows, link.remote(mine.at[rows], other.at[rows], base + j, base + j, link.sibling())

    def send(j, carry):
        rows, copy = swap(j)
        mine[rows, :] = product((1 - link.core) * half + j).astype(bf16)
        copy.start()
        return carry

    def norm(j, carry):
        rows, copy = swap(j)
        part = product(link.core * half + j)
        copy.wait_recv()
        xhat, inv = standardize(x[rows, :].astype(f32))
        dh = part + other[rows, :].astype(f32)
        dx = dh * vec_ref[GAIN1]
        dx_ref[rows, :] = (
            dmid[rows, :]
            + inv
            * (dx - jnp.mean(dx, axis=-1, keepdims=True) - xhat * jnp.mean(dx * xhat, axis=-1, keepdims=True))
        ).astype(bf16)
        for row, value in enumerate((dh * xhat, dh)):
            sums_ref[row : row + 1, :] += jnp.sum(value, axis=0, keepdims=True)
        return carry

    sums_ref[...] = jnp.zeros_like(sums_ref)
    lax.fori_loop(0, half, send, 0)
    for c in loads:
        c.wait()
    lax.fori_loop(0, half, norm, 0)
    for j in range(half):
        swap(j)[1].wait_send()
    for job in bound:
        job.forward()
    for job in bound:
        job.inward()
    for job in bound:
        job.finish()


def first_back_call(grads, w, vec, x, dmid, jobs, number):
    n, d = x.shape
    size = n // 2
    vmem = pl.BlockSpec(memory_space=pltpu.VMEM)
    hbm = pl.BlockSpec(memory_space=pl.ANY)
    return pl.pallas_call(
        functools.partial(first_back_kernel, jobs=jobs),
        in_specs=[vmem] * 3 + [hbm] * 2 + jobs.in_specs(),
        out_specs=[vmem] * 2 + jobs.in_specs(),
        out_shape=[jax.ShapeDtypeStruct((size, d), bf16), jax.ShapeDtypeStruct((8, d), f32)] + jobs.out_shapes(),
        scratch_shapes=[
            pltpu.VMEM((size, d), bf16),
            pltpu.VMEM((size, d), f32),
            pltpu.VMEM((size, d), bf16),
            pltpu.VMEM((size, d), bf16),
        ]
        + jobs.scratch(size // ROWS),
        compiler_params=comm_params(number),
        cost_estimate=cost(2 * n * w.size, 12 * n * d),
        name="first_back",
    )(grads, w, vec, x, dmid, *jobs.sources())


class Blocks:
    def __init__(self, ref, stride, first):
        self.ref, self.stride, self.first = ref, stride, first

    @property
    def at(self):
        return self

    def __getitem__(self, index):
        block, part = index
        start = pl.multiple_of(block * self.stride + (self.first + part.start), 16)
        return self.ref.at[pl.ds(start, part.size)]


def back_kernel(*refs, jobs):
    count = len(jobs.jobs)
    g_ref, vec_ref, h_ref, early_ref, *w_refs = refs[:7]
    x_any, dmid_any = refs[7:9]
    tokens_any, small_ref, both_any = refs[9 + count : 12 + count]
    rest = list(refs[12 + 2 * count :])
    x, dmid, mine, other, dx, dw, own, total, came, stage = rest[:10]
    rest = rest[10:]
    small_bufs, rest = rest[:3], rest[3:]
    reduce_bufs, rest = [rest[10 * i : 10 * i + 10] for i in range(3)], rest[30:]
    chain_bufs, rest = [rest[3 * i : 3 * i + 3] for i in range(6)], rest[18:]
    link, bound, _ = jobs.bind(rest, refs[9 : 9 + count], refs[12 + count : 12 + 2 * count])
    ready = [job for job in bound if isinstance(job, Chain)]
    others = [job for job in bound if job not in ready]
    size, d = dx.shape
    half = size // ROWS
    _, owned, width = own.shape
    order = (2, 1, 0)
    reduces = [Reduce(link, Blocks(dw.at[c], owned, 0), own.at[c], reduce_bufs[c]) for c in order]
    last = []
    for c in order:
        for i in range(2):
            rows, cols = pl.ds(i * (owned // 2), owned // 2), pl.ds(c * width, width)
            last.append(Chain(link, own.at[c, rows], both_any.at[:, rows, cols], chain_bufs[len(last)]))
    to_owners = FromClip(link, dx, tokens_any, [stage])
    base = link.slots(half)
    keep = link.local_slots(2)
    swap_base = link.slots(3)
    peers = [link.sibling()] + [(link.rep, link.shard ^ bit) for bit in (1, 2)]
    swaps = [link.remote(total, came.at[i], swap_base + i, swap_base + i, to) for i, to in enumerate(peers)]
    small = Chain(link, total, small_ref, small_bufs)
    mine_rows = pl.ds(pl.multiple_of(link.core * size, size), size)
    loads = [link.here(x_any.at[mine_rows], x, keep), link.here(dmid_any.at[mine_rows], dmid, keep + 1)]
    for c in loads:
        c.start()
    link.meet_all()
    ready[0].start()
    for c, job in zip(order, reduces):

        def weight(i, carry):
            part = pl.ds(pl.multiple_of(i * 256, 256), 256)
            dw[c, part, :] = dot_tn(h_ref[:, part], g_ref[:, c * width : (c + 1) * width]).astype(bf16)
            return carry

        lax.fori_loop(0, d // 256, weight, 0)
        job.start()

    def product(j):
        rows = pl.ds(pl.multiple_of(j * ROWS, ROWS), ROWS)
        parts = [dot_nt(g_ref[rows, c * width : (c + 1) * width], w_refs[c][...]) for c in range(3)]
        return parts[0] + parts[1] + parts[2]

    def swap(j):
        rows = pl.ds(pl.multiple_of(j * ROWS, ROWS), ROWS)
        return rows, link.remote(mine.at[rows], other.at[rows], base + j, base + j, link.sibling())

    def send(j, carry):
        rows, copy = swap(j)
        mine[rows, :] = product((1 - link.core) * half + j).astype(bf16)
        copy.start()
        return carry

    first = early_ref.shape[0]

    def norm(j, carry):
        rows, copy = swap(j)
        part = product(link.core * half + j)
        copy.wait_recv()
        xhat, inv = standardize(x[rows, :].astype(f32))
        dh = part + other[rows, :].astype(f32)
        slope = dh * vec_ref[GAIN1]
        dx[rows, :] = (
            dmid[rows, :]
            + inv
            * (
                slope
                - jnp.mean(slope, axis=-1, keepdims=True)
                - xhat * jnp.mean(slope * xhat, axis=-1, keepdims=True)
            )
        ).astype(bf16)
        for row, value in enumerate((dh * xhat, dh)):
            total[first + row : first + row + 1, :] += jnp.sum(value, axis=0, keepdims=True)
        return carry

    steps = chain_steps(ready)
    run(steps[0])
    total[:first, :] = early_ref[...]
    total[first:, :] = jnp.zeros((total.shape[0] - first, d), f32)
    lax.fori_loop(0, half, send, 0)
    for c in loads:
        c.wait()
    reduces[0].forward()
    after = {0: steps[1] + [reduces[1].forward], 1: [reduces[2].forward]}
    for j in range(half):
        norm(j, 0)
        run(after.get(j, []))
    swaps[0].start()
    run(steps[2])
    reduces[0].collect()
    last[0].start()
    reduces[1].collect()
    swaps[0].wait()
    total[...] += came[0]
    swaps[1].start()
    reduces[2].collect()
    for some in steps[3:]:
        run(some)
    swaps[1].wait()
    total[...] += came[1]
    swaps[2].start()
    for number, some in enumerate(chain_steps(last)):
        run(some)
        if number == 0:
            swaps[2].wait()
            total[...] += came[2]
            small.start()
        if number == 2:
            run([job.start for job in [to_owners] + others])
        if number == 3:
            small.inward()
            small.sent()
        if number == 5:
            small.across()
    for c in ready + last:
        c.outward()
    small.outward()
    for job in ready + last + [small]:
        job.finish()
    for job in reduces:
        job.close()
    for j in range(half):
        swap(j)[1].wait_send()
    run([job.finish for job in [to_owners] + others])


def back_call(grads, weights, vec, h, early, x, dmid, jobs, clips, number):
    n, d = x.shape
    size = n // 2
    width = grads.shape[1] // 3
    groups = lax.axis_size("shard")
    owned = d // groups
    rows = early.shape[0] + 8
    small = pltpu.VMEM((rows, d), f32)
    vmem = pl.BlockSpec(memory_space=pltpu.VMEM)
    hbm = pl.BlockSpec(memory_space=pl.ANY)
    return pl.pallas_call(
        functools.partial(back_kernel, jobs=jobs),
        in_specs=[vmem] * 7 + [hbm] * 2 + jobs.in_specs(),
        out_specs=[hbm, vmem, hbm] + jobs.in_specs(),
        out_shape=[
            jax.ShapeDtypeStruct((clips, size // clips, d), bf16),
            jax.ShapeDtypeStruct((2, rows, d), f32),
            jax.ShapeDtypeStruct((2, owned, 3 * width), bf16),
        ]
        + jobs.out_shapes(),
        scratch_shapes=[
            pltpu.VMEM((size, d), bf16),
            pltpu.VMEM((size, d), f32),
            pltpu.VMEM((size, d), bf16),
            pltpu.VMEM((size, d), bf16),
            pltpu.VMEM((size, d), bf16),
            pltpu.VMEM((3, d, width), bf16),
            pltpu.VMEM((3, owned, width), bf16),
            small,
            pltpu.VMEM((3, rows, d), f32),
            pltpu.VMEM((size // clips, d), bf16),
        ]
        + [small] * 3
        + [pltpu.VMEM((owned // 2, width), bf16)] * 48
        + jobs.scratch(80),
        compiler_params=comm_params(number, 62),
        cost_estimate=cost(12 * n * weights[0].size, 20 * n * d),
        name="back",
    )(grads, vec, h, early, *weights, x, dmid, *jobs.sources())


def place_kernel(*refs, groups):
    up_refs, down_refs = refs[:4], refs[4:8]
    out_ref, in_ref = refs[8:10]
    up, down, wo = refs[10:13]
    qkv = refs[13:16]

    def put(target, axis, pieces):
        first = 0
        for value in pieces:
            size = value.shape[axis]
            span = slice(first, first + size)
            if axis:
                target[:, span] = value.astype(f32)
            else:
                target[span, :] = value.astype(f32)
            first += size

    cut = up_refs[0].shape[1]
    for part in range(2):
        put(up.at[pl.ds(part * cut, cut)], 1, [r[c] for c in range(2) for r in (up_refs[part], up_refs[2 + part])])
    put(down, 0, [r[c] for c in range(2) for r in down_refs])
    put(wo, 0, [out_ref[c] for c in range(2)])
    rows = in_ref.shape[1]
    width = in_ref.shape[2] // 3
    part = width // groups

    for i, out in enumerate(qkv):
        for c in range(2):
            value = in_ref[c, :, i * width : (i + 1) * width].astype(f32)
            for s in range(groups):
                first = (2 * s + c) * part
                out[:, first : first + part] = value[:, s * part : (s + 1) * part]


def place_call(ups, downs, wo, qkv, groups):
    steps = 5
    own_d, cols = qkv.shape[1:]
    d = downs[0].shape[2]
    own_f = 2 * sum(a.shape[1] for a in downs)
    take = [pl.BlockSpec((2, a.shape[1], a.shape[2] // groups), lambda i: (0, 0, jnp.minimum(i, groups - 1))) for a in ups]
    wide = d // steps
    per = own_d // steps
    ff = 2 * ups[0].shape[2] + 2 * ups[2].shape[2]
    return pl.pallas_call(
        functools.partial(place_kernel, groups=groups),
        grid=(steps,),
        in_specs=take
        + [pl.BlockSpec((2, a.shape[1], wide), lambda i: (0, 0, i)) for a in downs]
        + [
            pl.BlockSpec((2, wo.shape[1], wide), lambda i: (0, 0, i)),
            pl.BlockSpec((2, per, cols), lambda i: (0, i, 0)),
        ],
        out_specs=[
            pl.BlockSpec((own_d, ff // groups), lambda i: (0, jnp.minimum(i, groups - 1))),
            pl.BlockSpec((own_f, wide), lambda i: (0, i)),
            pl.BlockSpec((own_d, wide), lambda i: (0, i)),
        ]
        + [pl.BlockSpec((per, d), lambda i: (i, 0))] * 3,
        out_shape=[
            jax.ShapeDtypeStruct((own_d, ff), f32),
            jax.ShapeDtypeStruct((own_f, d), f32),
            jax.ShapeDtypeStruct((own_d, d), f32),
        ]
        + [jax.ShapeDtypeStruct((own_d, d), f32)] * 3,
        compiler_params=params(),
        name="place",
    )(*ups, *downs, wo, qkv)


def own_sum(blocks, others):
    shard = lax.axis_index("shard")
    total = lax.dynamic_index_in_dim(blocks, shard, 0, keepdims=False).astype(f32)
    for i in range(others.shape[0]):
        total = total + others[i].astype(f32)
    return total.astype(bf16)


def over_reps(own):
    planes = lax.axis_size("rep") // 2
    sums = lax.psum_scatter(
        own,
        "rep",
        scatter_dimension=0,
        tiled=True,
        axis_index_groups=[[2 * z + c for z in range(planes)] for c in range(2)],
    )
    both = lax.all_gather(sums, "rep", axis=0)
    rows, cols = sums.shape
    return both.reshape(planes, 2, rows, cols).transpose(1, 0, 2, 3).reshape(2, planes * rows, cols)


def on_device(
    tokens,
    lengths,
    cotangent,
    first_gain,
    first_shift,
    query_weight,
    query_bias,
    key_weight,
    value_weight,
    value_bias,
    out_weight,
    out_bias,
    second_gain,
    second_shift,
    up_weight,
    up_bias,
    down_weight,
    down_bias,
):
    g = lax.axis_size("shard")
    shard = lax.axis_index("shard")
    core = lax.rem(lax.axis_index("rep"), 2)
    cl, rows, d = tokens.shape
    n = 2 * cl * rows
    ff = up_weight.shape[1]
    own_d = d // g
    own_f = ff // g
    attn_cols = own_d // 2
    ffn_cols = own_f // 2
    width = d // 2
    heads = width // HEAD
    wide = pl.cdiv(width, 128) * 128 + 128
    first_n = ffn_cols * 2 // 5
    pieces = ((0, first_n), (first_n, ffn_cols))

    fast = g == 4 and lax.axis_size("rep") == 8
    weights = PairGather if fast else Gather
    positions = shard * rows + jnp.arange(rows, dtype=jnp.int32)
    live = positions[None, :] < lengths[:, None]
    masked = jnp.where(live[:, :, None], cotangent, jnp.zeros_like(cotangent))

    def core_of():
        return lax.rem(lax.axis_index("rep"), 2)

    def core_cols(w, size, a, b):
        def of(c):
            return jnp.concatenate([w[:, (2 * s + c) * size + a : (2 * s + c) * size + b] for s in range(g)], axis=1)

        return jnp.where(core == 0, of(0), of(1))

    vectors = (first_gain, first_shift, query_bias, value_bias, out_bias, second_gain, second_shift, down_bias)
    small = pack_call((*vectors, up_bias), lengths)
    own = [core_cols(w, attn_cols, 0, attn_cols) for w in (query_weight, key_weight, value_weight)]
    jobs = Jobs(
        (ToClip, tokens, (n, d)),
        (Gather, small, (g,) + small.shape),
        *[(weights, w, (g,) + w.shape) for w in own],
    )
    h1, q, k, v, vec, x, _, *w_qkv, other_small = first_call(jobs, small, wide, 0)
    w_qkv = [w.reshape(d, width) for w in w_qkv]
    near = lax.div(shard, cl) == core
    lens = jnp.where(near, small[LENGTHS], other_small[LENGTHS])[0]
    length = lens[lax.rem(shard, cl)].astype(jnp.int32).reshape(1)

    ubias = lax.dynamic_index_in_dim(
        vec[UBIAS : UBIAS + own_f // own_d].reshape(-1, g, own_d).transpose(1, 0, 2).reshape(g, 2, ffn_cols),
        core,
        1,
        keepdims=False,
    )
    ups = [core_cols(up_weight, ffn_cols, a, b) for a, b in pieces]

    def half_rows(w, first=0, last=None):
        half = w.shape[0] // 2
        size = (half if last is None else last) - first

        def view(ref):
            return ref.at[pl.ds(pl.multiple_of(core_of() * half + first, 16), size)]

        return size, view

    def gathered(a, part=None):
        if part is None:
            return (weights, a, (g,) + a.shape)
        return (weights, a, (g, part[0]) + a.shape[1:], part[1])

    jobs = Jobs(
        gathered(ups[0]),
        gathered(down_weight, half_rows(down_weight, *pieces[0])),
        gathered(out_weight, half_rows(out_weight)),
    )
    o, lse, up, down, w_out = attn_fwd_call(length, q, k, v, width, heads, jobs, 1)
    w_out = w_out.reshape(width, d)
    jobs = Jobs((ToClip, masked, (n, d)))
    mid, h2, o_wide, dz = middle_call(o, w_out, x, vec, wide, jobs, 2)

    def hidden_bias(piece):
        return ubias[:, piece[0] : piece[1]].reshape(1, -1)


    def to_owners(a):
        if fast:
            return (Reduce, a, a.shape[1:])
        return (Owners, a, (g - 1,) + a.shape[1:])

    def owned(a, came):
        return came if fast else own_sum(a, came)

    def chained(a):
        return (Chain, a, (2,) + a.shape)

    def chained_halves(a):
        half = a.shape[0] // 2

        def part(i):
            return lambda ref: ref.at[pl.ds(i * half, half)]

        return [(Chain, a, (2, half, a.shape[1]), part(i)) for i in range(2)]

    jobs = Jobs(gathered(ups[1]), gathered(down_weight, half_rows(down_weight, *pieces[1])))
    out, dh2, dup0, ddn0, dub0, up1, down1 = ffn_call(
        h2, dz, up.reshape(d, -1), hidden_bias(pieces[0]), down.reshape(-1, d), None, False, jobs, 3, "hidden0"
    )
    dup0, ddn0 = dup0.reshape(g, own_d, -1), ddn0.reshape(g, -1, d)
    jobs = Jobs(to_owners(dup0), to_owners(ddn0))
    out, dh2, dup1, ddn1, dub1, dup0_in, ddn0_in = ffn_call(
        h2, dz, up1.reshape(d, -1), hidden_bias(pieces[1]), down1.reshape(-1, d), (out, dh2), True, jobs, 4, "hidden1"
    )
    dup1, ddn1 = dup1.reshape(g, own_d, -1), ddn1.reshape(g, -1, d)
    up0_own, down0_own = owned(dup0, dup0_in), owned(ddn0, ddn0_in)

    jobs = [to_owners(dup1)]
    if fast:
        jobs += chained_halves(up0_own)
    dmid, do, dwo, sums2, layer_own, dup1_in, *sums0 = second_back_call(
        mid, dh2, out, dz, vec, w_out, o, wide, Jobs(*jobs), 5
    )
    dwo = dwo.reshape(g, -1, d)
    up1_own = owned(dup1, dup1_in)

    to_tokens = (FromClip, layer_own, (cl, rows, d))
    jobs = [to_owners(ddn1), to_owners(dwo), to_tokens]
    if fast:
        jobs += chained_halves(down0_own) + chained_halves(up1_own)
    grads, bias_sums, ddn1_in, dwo_in, layer_out, *later = attn_bwd_call(
        length, q, k, v, o_wide, do, lse, width, heads, Jobs(*jobs), 6
    )
    down1_own, out_own_grad = owned(ddn1, ddn1_in), owned(dwo, dwo_in)

    def spread(v, size):
        out = jnp.zeros((g, 2, size), f32)
        return lax.dynamic_update_index_in_dim(out, v.reshape(g, size), core, 1)

    ub_sums = jnp.concatenate([dub0.reshape(g, -1), dub1.reshape(g, -1)], axis=1)
    early = jnp.concatenate(
        [
            spread(bias_sums[0, :width], attn_cols).reshape(1, d),
            spread(bias_sums[0, 2 * width :], attn_cols).reshape(1, d),
            sums2[:4] * 0.5,
            spread(ub_sums, ffn_cols).reshape(-1, d),
        ],
        axis=0,
    )
    early = jnp.pad(early, ((0, -early.shape[0] % 8), (0, 0)))

    if fast:
        jobs = Jobs(*chained_halves(down1_own), chained(out_own_grad))
        tokens_grad, smalls, qkv_all, *sums = back_call(grads, w_qkv, vec, h1, early, x, dmid, jobs, cl, 7)
        up_grad, down_grad, out_grad, *qkv_grads = place_call(
            (*sums0, *later[2:]), (*later[:2], *sums[:2]), sums[2], qkv_all, g
        )
        smalls = lax.dynamic_index_in_dim(smalls, core, 0, keepdims=False)
    else:
        dwqkv = dw_call(h1, grads).reshape(g, own_d, 3 * width)
        jobs = Jobs(to_owners(dwqkv))
        dx, sums1, dwqkv_in = first_back_call(grads, jnp.concatenate(w_qkv, axis=1), vec, x, dmid, jobs, 7)
        jobs = Jobs((FromClip, dx, (cl, rows, d)))
        tokens_grad, _ = exchange_call(jobs, sums1, 8, "last_exchange")
        ups_all = [over_reps(a).reshape(2, own_d, g, -1) for a in (up0_own, up1_own)]
        up_grad = jnp.concatenate(ups_all, axis=3).transpose(1, 2, 0, 3).reshape(own_d, ff).astype(f32)
        downs_all = [over_reps(a) for a in (down0_own, down1_own)]
        down_grad = jnp.concatenate(downs_all, axis=1).reshape(own_f, d).astype(f32)
        out_grad = over_reps(out_own_grad).reshape(own_d, d).astype(f32)
        qkv_all = over_reps(owned(dwqkv, dwqkv_in)).reshape(2, own_d, 3, g, attn_cols)
        qkv_grads = [qkv_all[:, :, i].transpose(1, 2, 0, 3).reshape(own_d, d).astype(f32) for i in range(3)]
        smalls = lax.psum(jnp.concatenate([early, sums1], axis=0), ("rep", "shard"))

    mine = lax.dynamic_slice_in_dim(smalls, shard * own_d, own_d, 1)
    s_qb, s_vb, s_gain2, s_shift2, s_ob, s_db = [mine[i] for i in range(6)]
    s_gain1, s_shift1 = [mine[early.shape[0] + i] for i in range(2)]
    s_ub = lax.dynamic_slice_in_dim(smalls[6 : 6 + ff // d].reshape(-1), shard * own_f, own_f, 0)

    return (
        layer_out,
        tokens_grad,
        s_gain1,
        s_shift1,
        qkv_grads[0],
        s_qb,
        qkv_grads[1],
        qkv_grads[2],
        s_vb,
        out_grad,
        s_ob,
        s_gain2,
        s_shift2,
        up_grad,
        s_ub,
        down_grad,
        s_db,
    )


def solution(mesh):
    row, mat, vec = P("rep", "shard", None), P("shard", None), P("shard")
    return jax.shard_map(
        on_device,
        mesh=mesh,
        in_specs=(row, P("rep"), row, vec, vec, mat, vec, mat, mat, vec, mat, vec, vec, vec, mat, vec, mat, vec),
        out_specs=(row, row, vec, vec, mat, vec, mat, mat, vec, mat, vec, vec, vec, mat, vec, mat, vec),
        check_vma=False,
    )
```

```python
import functools
import math

import jax
import jax.numpy as jnp
from jax import lax
from jax.experimental import pallas as pl
from jax.experimental.pallas import tpu as pltpu
from jax.sharding import PartitionSpec as P

HEAD = 80
WIN = 256
AUG = 192
EPS = 1e-5
SCALE = HEAD**-0.5
SCALE2 = SCALE * math.log2(math.e)
DEAD = -1e30
ROWS = 256
GAIN1, SHIFT1, QBIAS, VBIAS, OBIAS, GAIN2, SHIFT2, DBIAS, LENGTHS = [slice(i, i + 1) for i in range(9)]
UBIAS = 9
FFN_TILE = 512
FFN_ROWS = 768
PAIR_SHARE = 3
f32 = jnp.float32
bf16 = jnp.bfloat16
MESH = pl.DeviceIdType.MESH

ERF_P = 0.35
ERF_C = (0.19458996, 0.23381038, -0.00165479, 0.67243411, -0.66868964, 0.76616445, -0.19665448)


def params(limit=60):
    return pltpu.CompilerParams(vmem_limit_bytes=limit * 2**20)


def cost(flops, size):
    return pl.CostEstimate(flops=int(flops), bytes_accessed=int(size), transcendentals=0)


def dot(a, b):
    return jnp.dot(a, b, preferred_element_type=f32)


def dot_nt(a, b):
    return lax.dot_general(a, b, (((1,), (1,)), ((), ())), preferred_element_type=f32)


def dot_tn(a, b):
    return lax.dot_general(a, b, (((0,), (0,)), ((), ())), preferred_element_type=f32)


def gelu_pair(a):
    expo = jnp.exp2(a * a * (-0.5 * math.log2(math.e)))
    t = 1.0 / (1.0 + jnp.abs(a) * (ERF_P * math.sqrt(0.5)))
    total = ERF_C[-1]
    for c in ERF_C[-2::-1]:
        total = total * t + c
    tail = 0.5 * expo * (total * t)
    cdf = jnp.where(a >= 0, 1.0 - tail, tail)
    return a * cdf, cdf + a * (expo * (1.0 / math.sqrt(2.0 * math.pi)))


def whole(shape):
    return pl.BlockSpec(shape, lambda *_: (0,) * len(shape))


def once(shape):
    return pl.BlockSpec(shape, lambda *_: (0,) * len(shape), pipeline_mode=pl.Buffered(1))


def row_block(rows, cols):
    return pl.BlockSpec((rows, cols), lambda i: (i, 0))


def standardize(x):
    centred = x - jnp.mean(x, axis=-1, keepdims=True)
    inv = lax.rsqrt(jnp.mean(centred * centred, axis=-1, keepdims=True) + EPS)
    return centred * inv, inv


class Link:
    def __init__(self, sems):
        self.send, self.recv, self.local = sems
        self.next = 0
        self.next_local = 0
        self.groups = lax.axis_size("shard")
        self.rep = lax.axis_index("rep")
        self.shard = lax.axis_index("shard")
        self.core = lax.rem(self.rep, 2)
        self.half = self.groups // 2

    def meet_plane(self, pair=False):
        barrier = pltpu.get_barrier_semaphore()
        base = self.rep - self.core
        for c in range(2):
            for p in range(self.groups):
                if c or p:
                    to = (base + (self.core ^ c), self.shard ^ p)
                    pl.semaphore_signal(barrier, inc=1, device_id=to, device_id_type=MESH)
        if pair:
            pl.semaphore_signal(barrier, inc=1, device_id=self.pair(), device_id_type=MESH)
        pl.semaphore_wait(barrier, 2 * self.groups - 1 + int(pair))

    def pair(self):
        return (self.rep ^ 2, self.shard)

    def meet_all(self):
        barrier = pltpu.get_barrier_semaphore()
        base = self.rep - self.core
        for c in range(2):
            for p in range(self.groups):
                if c or p:
                    to = (base + (self.core ^ c), self.shard ^ p)
                    pl.semaphore_signal(barrier, inc=1, device_id=to, device_id_type=MESH)
        pl.semaphore_signal(barrier, inc=1, device_id=self.inward(), device_id_type=MESH)

        @pl.when(self.inner())
        def _():
            pl.semaphore_signal(barrier, inc=1, device_id=self.outward(), device_id_type=MESH)
            pl.semaphore_wait(barrier, 2 * self.groups + 1)

        @pl.when(jnp.logical_not(self.inner()))
        def _():
            pl.semaphore_wait(barrier, 2 * self.groups)

    def inner(self):
        plane = lax.div(self.rep, 2)
        return (plane == 1) | (plane == 2)

    def inward(self):
        return (self.rep + jnp.where(self.rep < 4, 2, -2), self.shard)

    def outward(self):
        return (self.rep - jnp.where(self.rep < 4, 2, -2), self.shard)

    def meet_core(self):
        barrier = pltpu.get_barrier_semaphore()
        pl.semaphore_signal(barrier, inc=1, device_id=self.sibling(), device_id_type=MESH)
        pl.semaphore_wait(barrier, 1)

    def sibling(self):
        return (self.rep ^ 1, self.shard)

    def slots(self, count):
        first = self.next
        self.next += count
        return first

    def local_slots(self, count):
        first = self.next_local
        self.next_local += count
        return first

    def remote(self, src, dst, send, recv, to):
        return pltpu.make_async_remote_copy(
            src_ref=src,
            dst_ref=dst,
            send_sem=self.send.at[send],
            recv_sem=self.recv.at[recv],
            device_id=to,
            device_id_type=MESH,
        )

    def here(self, src, dst, slot):
        return pltpu.make_async_copy(src, dst, self.local.at[slot])


class Job:
    @staticmethod
    def buffers(source, shape):
        return []

    def forward(self):
        pass

    def inward(self):
        pass

    def across(self):
        pass

    def outward(self):
        pass


class Staged:
    def __init__(self, link, src, dst, buf):
        slot = link.local_slots(1)
        self.load = link.here(src, buf, slot)
        self.store = link.here(buf, dst, slot)

    def start(self):
        self.load.start()

    def turn(self):
        self.load.wait()
        self.store.start()

    def wait(self):
        self.store.wait()


class Gather(Job):
    def __init__(self, link, src, dst, bufs):
        self.link, self.src, self.dst = link, src, dst
        self.rows = src.shape[0]
        self.base = link.slots(max(4, link.groups - 1))
        self.keep = Staged(link, src, dst.at[link.shard], bufs[0])

    @staticmethod
    def buffers(source, shape):
        return [pltpu.VMEM(shape[1:], source.dtype)]

    def first(self):
        link = self.link
        peers = (1, 2) if link.groups == 4 else range(1, link.groups)
        return [
            link.remote(self.src, self.dst.at[link.shard], self.base + i, self.base + i, (link.rep, link.shard ^ p))
            for i, p in enumerate(peers)
        ]

    def second(self):
        link = self.link
        if link.groups != 4:
            return []
        cut = self.rows // 2
        parts = ((1, 2, pl.ds(0, cut)), (2, 1, pl.ds(cut, self.rows - cut)))
        out = []
        for i, (origin, to, rows) in enumerate(parts):
            ref = self.dst.at[link.shard ^ origin, rows]
            out.append(link.remote(ref, ref, self.base + 2 + i, self.base + 2 + i, (link.rep, link.shard ^ to)))
        return out

    def start(self):
        self.keep.start()
        for c in self.first():
            c.start()

    def forward(self):
        self.keep.turn()
        for c, d in zip(self.first(), self.second()):
            c.wait_recv()
            d.start()

    def finish(self):
        second = self.second()
        for c in self.first():
            if not second:
                c.wait_recv()
            c.wait_send()
        for c in second:
            c.wait()
        self.keep.wait()


class PairGather(Job):
    def __init__(self, link, src, dst, bufs):
        self.link, self.src, self.dst = link, src, dst
        rows = src.shape[0]
        outer = max(rows // PAIR_SHARE // 16, 1) * 16
        second = lax.rem(lax.div(link.rep, 2), 2)
        self.part = pl.ds(pl.multiple_of(second * outer, 16), rows - outer)
        self.alone = pl.ds(pl.multiple_of(second * (rows - outer), 16), outer)
        self.both = pl.ds(outer, rows - 2 * outer)
        self.base = link.slots(7)
        self.keep = Staged(link, src, dst.at[link.shard], bufs[0])

    @staticmethod
    def buffers(source, shape):
        return [pltpu.VMEM(shape[1:], source.dtype)]

    def step(self, src, dst, slot, to):
        return self.link.remote(src, dst, self.base + slot, self.base + slot, to)

    def near(self, bit):
        return (self.link.rep, self.link.shard ^ bit)

    def first(self):
        mine = self.dst.at[self.link.shard, self.part]
        return [self.step(self.src.at[self.part], mine, i, self.near(i + 1)) for i in range(2)]

    def second(self):
        one = self.dst.at[self.link.shard ^ 1, self.alone]
        two = self.dst.at[self.link.shard ^ 2, self.both]
        return [self.step(one, one, 2, self.near(2)), self.step(two, two, 3, self.near(1))]

    def third(self):
        out = []
        for i in range(3):
            ref = self.dst.at[self.link.shard ^ (i + 1), self.alone]
            out.append(self.step(ref, ref, 4 + i, self.link.pair()))
        return out

    def start(self):
        self.keep.start()
        for c in self.first():
            c.start()

    def forward(self):
        self.keep.turn()
        for c, d, e in zip(self.first(), self.second(), self.third()):
            c.wait_recv()
            d.start()
            e.start()

    def inward(self):
        self.second()[0].wait_recv()
        self.third()[2].start()

    def finish(self):
        for c in self.first():
            c.wait_send()
        one, two = self.second()
        one.wait_send()
        two.wait()
        for c in self.third():
            c.wait()
        self.keep.wait()


class ToClip(Job):
    def __init__(self, link, src, dst, bufs):
        self.link, self.src, self.dst = link, src, dst
        self.rows = src.shape[1]
        self.base = link.slots(link.half + 1)
        self.keep = link.local_slots(1)
        self.buf = bufs[0]

    @staticmethod
    def buffers(source, shape):
        return [pltpu.VMEM(source.shape[1:], source.dtype)]

    def copy(self, j):
        link = self.link
        core = lax.div(link.shard, link.half)
        to = (link.rep - link.core + core, link.core * link.half + j)
        mine = (core == link.core) & (link.core * link.half + j == link.shard)
        dst = self.dst.at[pl.ds(pl.multiple_of(link.shard * self.rows, self.rows), self.rows)]
        there = link.remote(self.src.at[j], dst, self.base + j, self.base + lax.rem(link.shard, link.half), to)
        return mine, there, link.here(self.src.at[j], self.buf, self.keep)

    def arrival(self, t):
        link = self.link
        source = link.core * link.half + t
        mine = (lax.div(link.shard, link.half) == link.core) & (source == link.shard)
        dst = self.dst.at[pl.ds(pl.multiple_of(source * self.rows, self.rows), self.rows)]
        there = link.remote(self.src.at[0], dst, self.base, self.base + t, link.sibling())
        return mine, there, link.here(self.buf, dst, self.keep)

    def to_sibling(self):
        link = self.link
        size = link.half * self.rows
        rows = pl.ds(pl.multiple_of(link.core * size, size), size)
        slot = self.base + link.half
        return link.remote(self.dst.at[rows], self.dst.at[rows], slot, slot, link.sibling())

    def start(self):
        for j in range(self.link.half):
            mine, there, here = self.copy(j)
            pl.when(mine)(here.start)
            pl.when(jnp.logical_not(mine))(there.start)

    def forward(self):
        for t in range(self.link.half):
            mine, there, here = self.arrival(t)

            @pl.when(mine)
            def _():
                self.copy(0)[2].wait()
                here.start()
                here.wait()

            pl.when(jnp.logical_not(mine))(there.wait_recv)
        self.to_sibling().start()

    def finish(self):
        self.to_sibling().wait()
        for j in range(self.link.half):
            mine, there, _ = self.copy(j)
            pl.when(jnp.logical_not(mine))(there.wait_send)


class FromClip(Job):
    def __init__(self, link, src, dst, bufs):
        self.link, self.src, self.dst = link, src, dst
        self.rows = dst.shape[1]
        self.base = link.slots(link.half)
        self.keep = link.local_slots(1)
        self.buf = bufs[0]

    @staticmethod
    def buffers(source, shape):
        return [pltpu.VMEM(shape[1:], source.dtype)]

    def copy(self, t):
        link = self.link
        core = lax.div(link.shard, link.half)
        shard = link.core * link.half + t
        mine = (core == link.core) & (shard == link.shard)
        clip = lax.rem(link.shard, link.half)
        src = self.src.at[pl.ds(t * self.rows, self.rows)]
        dst = self.dst.at[clip]
        there = link.remote(src, dst, self.base + t, self.base + clip, (link.rep - link.core + core, shard))
        return mine, there, link.here(src, self.buf, self.keep)

    def arrival(self, j):
        link = self.link
        mine = (lax.div(link.shard, link.half) == link.core) & (link.core * link.half + j == link.shard)
        src = self.src.at[pl.ds(0, self.rows)]
        there = link.remote(src, self.dst.at[j], self.base, self.base + j, link.sibling())
        return mine, there, link.here(self.buf, self.dst.at[j], self.keep)

    def start(self):
        for t in range(self.link.half):
            mine, there, here = self.copy(t)
            pl.when(mine)(here.start)
            pl.when(jnp.logical_not(mine))(there.start)

    def finish(self):
        for t in range(self.link.half):
            mine, there, here = self.copy(t)
            pl.when(jnp.logical_not(mine))(there.wait_send)
        for j in range(self.link.half):
            mine, there, here = self.arrival(j)

            @pl.when(mine)
            def _():
                self.copy(0)[2].wait()
                here.start()
                here.wait()

            pl.when(jnp.logical_not(mine))(there.wait_recv)


class Owners(Job):
    def __init__(self, link, src, dst, bufs):
        self.link, self.src, self.dst = link, src, dst
        self.base = link.slots(link.groups - 1)

    def copies(self):
        link = self.link
        return [
            link.remote(
                self.src.at[link.shard ^ p],
                self.dst.at[p - 1],
                self.base + p - 1,
                self.base + p - 1,
                (link.rep, link.shard ^ p),
            )
            for p in range(1, link.groups)
        ]

    def start(self):
        for c in self.copies():
            c.start()

    def finish(self):
        for c in self.copies():
            c.wait()


def add_low(a, b):
    return (a.astype(f32) + b.astype(f32)).astype(bf16)


class Reduce(Job):
    def __init__(self, link, src, dst, bufs):
        self.link, self.src, self.dst = link, src, dst
        self.base = link.slots(6)
        self.keep = link.local_slots(4)
        self.half = dst.shape[0] // 2
        self.pass_in, self.pass_sum, self.near, self.far, self.own = (bufs[2 * i : 2 * i + 2] for i in range(5))

    @staticmethod
    def buffers(source, shape):
        half = pltpu.VMEM((source.shape[1] // 2, source.shape[2]), source.dtype)
        return [half] * 10

    def block(self, i, part):
        rows = pl.ds(part * self.half, self.half)
        return self.src.at[self.link.shard ^ i, rows]

    def hops(self):
        link = self.link
        x, y = (link.rep, link.shard ^ 1), (link.rep, link.shard ^ 2)
        plan = (
            (self.block(3, 0), self.pass_in[0], x),
            (self.block(3, 1), self.pass_in[1], y),
            (self.block(1, 0), self.near[0], x),
            (self.block(2, 1), self.near[1], y),
        )
        return [link.remote(s, d, self.base + i, self.base + i, to) for i, (s, d, to) in enumerate(plan)]

    def later(self):
        link = self.link
        x, y = (link.rep, link.shard ^ 1), (link.rep, link.shard ^ 2)
        plan = zip(self.pass_sum, self.far, (y, x))
        return [link.remote(s, d, self.base + 4 + i, self.base + 4 + i, to) for i, (s, d, to) in enumerate(plan)]

    def loads(self):
        plan = (
            (self.block(2, 0), self.pass_sum[0]),
            (self.block(1, 1), self.pass_sum[1]),
            (self.block(0, 0), self.own[0]),
            (self.block(0, 1), self.own[1]),
        )
        return [self.link.here(s, d, self.keep + i) for i, (s, d) in enumerate(plan)]

    def store(self, part):
        rows = pl.ds(part * self.half, self.half)
        return self.link.here(self.own[part], self.dst.at[rows], self.keep + part)

    def start(self):
        for c in self.hops():
            c.start()
        for c in self.loads():
            c.start()

    def forward(self):
        hops, loads, later = self.hops(), self.loads(), self.later()
        for i in range(2):
            loads[i].wait()
            hops[i].wait_recv()
            self.pass_sum[i][...] = add_low(self.pass_sum[i][...], self.pass_in[i][...])
            later[i].start()

    def collect(self):
        hops, loads, later = self.hops(), self.loads(), self.later()
        for i in range(2):
            loads[2 + i].wait()
            hops[2 + i].wait_recv()
            later[i].wait_recv()
            total = self.own[i][...].astype(f32) + self.near[i][...].astype(f32) + self.far[i][...].astype(f32)
            self.own[i][...] = total.astype(bf16)
            self.store(i).start()
        for i in range(2):
            self.store(i).wait()

    def finish(self):
        self.collect()
        self.close()

    def close(self):
        for c in self.hops() + self.later():
            c.wait_send()


class Chain(Job):
    def __init__(self, link, src, dst, bufs):
        self.link, self.src, self.dst = link, src, dst
        self.own, self.one, self.two = bufs
        self.base = link.slots(4)
        self.keep = link.local_slots(2)

    @staticmethod
    def buffers(source, shape):
        return [pltpu.VMEM(shape[1:], source.dtype)] * 3

    def step(self, src, dst, slot, to):
        return self.link.remote(src, dst, self.base + slot, self.base + slot, to)

    def steps(self):
        link = self.link
        return (
            self.step(self.src, self.one, 0, link.inward()),
            self.step(self.own, self.two, 1, link.inward()),
            self.step(self.one, self.two, 2, link.outward()),
        )

    def share(self, ref):
        link = self.link
        place = self.dst.at[link.core]
        return self.step(ref, place, 3, link.sibling()), link.here(ref, place, self.keep + 1)

    def start(self):
        inner = self.link.inner()
        pl.when(inner)(self.link.here(self.src, self.own, self.keep).start)
        pl.when(jnp.logical_not(inner))(self.steps()[0].start)

    def add(self, a, b):
        return (a[...].astype(f32) + b[...].astype(f32)).astype(a.dtype)

    def sent(self):
        pl.when(jnp.logical_not(self.link.inner()))(self.steps()[0].wait_send)

    def inward(self):
        @pl.when(self.link.inner())
        def _():
            steps = self.steps()
            self.link.here(self.src, self.own, self.keep).wait()
            steps[0].wait_recv()
            self.own[...] = self.add(self.own, self.one)
            steps[1].start()

    def across(self):
        @pl.when(self.link.inner())
        def _():
            steps = self.steps()
            steps[1].wait_recv()
            self.one[...] = self.add(self.own, self.two)
            steps[2].start()
            for c in self.share(self.one):
                c.start()

    def outward(self):
        @pl.when(jnp.logical_not(self.link.inner()))
        def _():
            self.steps()[2].wait_recv()
            for c in self.share(self.two):
                c.start()

    def finish(self):
        swap, here = self.share(self.one)
        swap.wait()
        here.wait()
        inner = self.link.inner()

        @pl.when(inner)
        def _():
            self.steps()[1].wait_send()
            self.steps()[2].wait_send()


def chain_steps(chains):
    lists = []
    for i in range(len(chains) + 1):
        lists.append(
            [step for c in chains[i : i + 1] for step in (c.inward, c.sent)]
            + [c.start for c in chains[i + 1 : i + 2]]
            + [c.across for c in chains[max(i - 1, 0) : i]]
        )
    return lists


def gather_steps(gathers):
    lists = []
    for i in range(len(gathers) + 2):
        lists.append(
            [c.start for c in gathers[i : i + 1]]
            + [c.forward for c in gathers[max(i - 1, 0) : i]]
            + [c.inward for c in gathers[max(i - 2, 0) : max(i - 1, 0)]]
        )
    return lists


def run(steps):
    for step in steps:
        step()


def split_gathers(bound):
    gathers = [job for job in bound if isinstance(job, (Gather, PairGather))]
    return gathers, [job for job in bound if job not in gathers]


class Jobs:
    def __init__(self, *jobs):
        self.jobs = [(job + (None,))[:4] for job in jobs]
        self.pairs = any(job[0] is PairGather for job in jobs)
        self.bufs = [kind.buffers(a, shape) for kind, a, shape, _ in self.jobs]

    def sources(self):
        return [a for _, a, _, _ in self.jobs]

    def in_specs(self):
        return [pl.BlockSpec(memory_space=pl.ANY)] * len(self.jobs)

    def out_shapes(self):
        return [jax.ShapeDtypeStruct(shape, a.dtype) for _, a, shape, _ in self.jobs]

    def scratch(self, extra=0):
        groups = lax.axis_size("shard")
        remote = len(self.jobs) * max(7, groups) + extra
        return [b for bufs in self.bufs for b in bufs] + [
            pltpu.SemaphoreType.DMA((remote,)),
            pltpu.SemaphoreType.DMA((remote,)),
            pltpu.SemaphoreType.DMA((4 * len(self.jobs) + extra + 1,)),
        ]

    def bind(self, rest, srcs, dsts):
        rest = list(rest)
        bufs = []
        for shapes in self.bufs:
            bufs.append([rest.pop(0) for _ in shapes])
        link = Link(rest[:3])
        bound = [
            kind(link, view(a) if view else a, b, c) for (kind, _, _, view), a, b, c in zip(self.jobs, srcs, dsts, bufs)
        ]
        return link, bound, rest[3:]


def comm_params(number, limit=60):
    return pltpu.CompilerParams(
        vmem_limit_bytes=limit * 2**20, collective_id=number, has_side_effects=True
    )


def exchange_call(jobs, sibling, number, name):
    count = len(jobs.jobs)

    def kernel(*refs):
        srcs, mine = refs[:count], refs[count]
        dsts, other = refs[count + 1 : 2 * count + 1], refs[2 * count + 1]
        link, bound, _ = jobs.bind(refs[2 * count + 2 :], srcs, dsts)
        slot = link.slots(1)
        swap = link.remote(mine, other, slot, slot, link.sibling())
        link.meet_plane(jobs.pairs)
        swap.start()
        gathers, others = split_gathers(bound)
        steps = gather_steps(gathers)
        run([job.start for job in others] + steps[0])
        for i, some in enumerate(steps[1:]):
            if i == 1:
                run([job.forward for job in others])
            run(some)
        run([job.finish for job in bound])
        swap.wait()

    return pl.pallas_call(
        kernel,
        in_specs=jobs.in_specs() + [pl.BlockSpec(memory_space=pl.ANY)],
        out_specs=[pl.BlockSpec(memory_space=pl.ANY)] * (count + 1),
        out_shape=jobs.out_shapes() + [jax.ShapeDtypeStruct(sibling.shape, sibling.dtype)],
        scratch_shapes=jobs.scratch(1),
        compiler_params=comm_params(number),
        name=name,
    )(*jobs.sources(), sibling)


def pack_kernel(*refs, count):
    out_ref = refs[-1]
    lens_ref = refs[count]
    out_ref[...] = jnp.zeros_like(out_ref)
    row = 0
    for ref in refs[:count]:
        size = refs[0].shape[0]
        for part in range(ref.shape[0] // size):
            value = ref[part * size : (part + 1) * size].astype(f32)
            out_ref[row : row + 1, :size] = value.reshape(1, size)
            row += 1
        if row == LENGTHS.start:
            lane = lax.broadcasted_iota(jnp.int32, (1, out_ref.shape[1]), 1)
            value = jnp.zeros(lane.shape, f32)
            for clip in range(lens_ref.shape[0]):
                value = jnp.where(lane == clip, lens_ref[clip].astype(f32), value)
            out_ref[row : row + 1, :] = value
            row += 1


def pack_call(vectors, lengths):
    vmem = pl.BlockSpec(memory_space=pltpu.VMEM)
    lanes = pl.cdiv(vectors[0].shape[0], 128) * 128
    return pl.pallas_call(
        functools.partial(pack_kernel, count=len(vectors)),
        in_specs=[vmem] * len(vectors) + [pl.BlockSpec(memory_space=pltpu.SMEM)],
        out_specs=vmem,
        out_shape=jax.ShapeDtypeStruct((16, lanes), f32),
        name="pack",
    )(*vectors, lengths)


def first_kernel(*refs, jobs, size):
    count = len(jobs.jobs)
    srcs, mine = refs[:count], refs[count]
    *results, vec_ref = refs[count + 1 : count + 6]
    dsts, other = refs[count + 6 : 2 * count + 6], refs[2 * count + 6]
    x, small, weight, bias, sems, h_ref, *heads = refs[2 * count + 7 : 2 * count + 16]
    link, bound, _ = jobs.bind(refs[2 * count + 16 :], srcs, dsts)
    tokens, smalls, *gathers = bound
    slot = link.slots(1)
    swap = link.remote(mine, other, slot, slot, link.sibling())
    n = x.shape[0]
    width = weight.shape[2]
    part = size // 2

    def load(src, dst, i):
        return pltpu.make_async_copy(src, dst, sems.at[i])

    first_store = 1 + small.shape[0]
    stores = [load(a, b, first_store + i) for i, (a, b) in enumerate(zip([h_ref] + heads, results))]
    link.meet_plane(jobs.pairs)
    steps = gather_steps(gathers)
    swap.start()
    run([smalls.start, tokens.start] + steps[0])
    run([smalls.forward, smalls.finish])
    load(dsts[1], small, 0).start()
    run(steps[1])
    load(dsts[1], small, 0).wait()
    bias[...] = jnp.zeros_like(bias)
    for s in range(small.shape[0]):
        vec_ref[:, s * size : (s + 1) * size] = small[s][:, :size]
        for row, first in ((QBIAS, 0), (VBIAS, 2 * width)):
            value = jnp.where(link.core == 0, small[s, row, :part], small[s, row, part:size])
            bias[:, first + s * part : first + (s + 1) * part] = value
    tokens.forward()
    run(steps[2])
    tokens.finish()
    load(dsts[0], x, 0).start()
    load(dsts[0], x, 0).wait()

    def norm(i, carry):
        rows = pl.ds(pl.multiple_of(i * ROWS, ROWS), ROWS)
        xhat, _ = standardize(x[rows, :].astype(f32))
        h_ref[rows, :] = (xhat * vec_ref[GAIN1] + vec_ref[SHIFT1]).astype(bf16)
        return carry

    lax.fori_loop(0, n // ROWS, norm, 0)
    stores[0].start()
    for ref in heads:
        ref[:, width:] = jnp.zeros((n, ref.shape[1] - width), bf16)
    for i, (gather, ref) in enumerate(zip(gathers, heads)):
        run(steps[3 + i] if 3 + i < len(steps) else [])
        gather.finish()
        for s in range(small.shape[0]):
            load(dsts[2 + i].at[s], weight.at[i, pl.ds(s * size, size)], 1 + s).start()
        for s in range(small.shape[0]):
            load(dsts[2 + i].at[s], weight.at[i, pl.ds(s * size, size)], 1 + s).wait()

        def project(j, carry):
            rows = pl.ds(pl.multiple_of(j * ROWS, ROWS), ROWS)
            z = dot(h_ref[rows, :], weight[i]) + bias[:, i * width : (i + 1) * width]
            ref[rows, :width] = z.astype(bf16)
            return carry

        lax.fori_loop(0, n // ROWS, project, 0)
        stores[1 + i].start()
    swap.wait()
    for c in stores:
        c.wait()


def first_call(jobs, small, wide, number):
    (n, d), groups = jobs.jobs[0][2], lax.axis_size("shard")
    width = jobs.jobs[2][2][2]
    vmem = pl.BlockSpec(memory_space=pltpu.VMEM)
    hbm = pl.BlockSpec(memory_space=pl.ANY)
    head = jax.ShapeDtypeStruct((n, wide), bf16)
    return pl.pallas_call(
        functools.partial(first_kernel, jobs=jobs, size=d // groups),
        in_specs=jobs.in_specs() + [hbm],
        out_specs=[hbm] * 4 + [vmem] + jobs.in_specs() + [hbm],
        out_shape=[jax.ShapeDtypeStruct((n, d), bf16), head, head, head, jax.ShapeDtypeStruct((16, d), f32)]
        + jobs.out_shapes()
        + [jax.ShapeDtypeStruct(small.shape, small.dtype)],
        scratch_shapes=[
            pltpu.VMEM((n, d), bf16),
            pltpu.VMEM((groups,) + small.shape, f32),
            pltpu.VMEM((3, d, width), bf16),
            pltpu.VMEM((1, 3 * width), f32),
            pltpu.SemaphoreType.DMA((5 + groups,)),
            pltpu.VMEM((n, d), bf16),
        ]
        + [pltpu.VMEM((n, wide), bf16)] * 3
        + jobs.scratch(1),
        compiler_params=comm_params(number),
        cost_estimate=cost(6 * n * d * width, 12 * n * d),
        name="first",
    )(*jobs.sources(), small)


def head_window(h):
    start = h * HEAD
    base = (start // 128) * 128
    off = start - base
    lane = lax.broadcasted_iota(jnp.int32, (1, WIN), 1)
    keep = jnp.where((lane >= off) & (lane < off + HEAD), 1.0, 0.0)
    return pl.ds(pl.multiple_of(base, 128), WIN), keep, lane


def put3(x, lane, first, value):
    hi = value.astype(bf16).astype(f32)
    rest = value - hi
    mid = rest.astype(bf16).astype(f32)
    low = rest - mid
    return jnp.where(
        lane == first,
        hi,
        jnp.where(lane == first + 1, mid, jnp.where(lane == first + 2, low, x)),
    )


def key_extra(rows, length):
    lane = lax.broadcasted_iota(jnp.int32, (rows, WIN), 1)
    row = lax.broadcasted_iota(jnp.int32, (rows, WIN), 0)
    dead = jnp.where(row >= length, DEAD, 0.0)
    minus = jnp.where((lane > AUG) & (lane <= AUG + 3), -1.0, 0.0)
    return jnp.where(lane == AUG, dead, minus).astype(bf16)


def attn_fwd_kernel(*refs, bq, jobs):
    count = len(jobs.jobs)
    len_ref, q_ref, k_ref, v_ref = refs[:4]
    o_ref, lse_ref = refs[4 + count : 6 + count]
    acc, kx = refs[6 + 2 * count : 8 + 2 * count]
    link, bound, _ = jobs.bind(refs[8 + 2 * count :], refs[4 : 4 + count], refs[6 + count : 6 + 2 * count])
    h = pl.program_id(0)
    heads = pl.num_programs(0)
    n = q_ref.shape[0]
    width = o_ref.shape[1]

    gathers, others = split_gathers(bound)
    steps = gather_steps(gathers)

    @pl.when(h == 0)
    def _():
        link.meet_plane(jobs.pairs)
        run([job.start for job in others] + steps[0])
        acc[...] = jnp.zeros_like(acc)
        lse_ref[...] = jnp.zeros_like(lse_ref)
        kx[...] = key_extra(n, len_ref[0])

    for number, some in zip((2, 4, 6, 7), steps[1:]):

        @pl.when(h == number * heads // 8)
        def _():
            run(some)

    win, keep, lane = head_window(h)
    low = keep.astype(bf16)
    q_one = jnp.where(lane == AUG, 1.0, 0.0).astype(bf16)
    v_one = jnp.where((lane >= AUG) & (lane < AUG + 3), 1.0, 0.0).astype(bf16)
    k = k_ref[:, win] * low + kx[...]
    v = v_ref[:, win] * low + v_one
    for i in range(n // bq):
        rows = slice(i * bq, (i + 1) * bq)
        s = dot_nt(q_ref[rows, win] * low + q_one, k)
        peak = jnp.max(s, axis=-1, keepdims=True)
        p = jnp.exp2((s - peak) * SCALE2).astype(bf16)
        o = dot(p, v)
        total = o[:, AUG : AUG + 1]
        acc[rows, win] += o * (keep * (1.0 / total))
        here = lax.broadcasted_iota(jnp.int32, (bq, 128), 1) == h
        lse = peak + jnp.log(total) * (1.0 / SCALE)
        lse_ref[rows, :] = jnp.where(here, lse, lse_ref[rows, :])

    @pl.when(h == heads - 1)
    def _():
        o_ref[:, :width] = acc[:, :width].astype(bf16)
        for some in steps[5:]:
            run(some)
        run([job.finish for job in bound])


def attn_fwd_call(length, q, k, v, width, heads, jobs, number):
    n, wide = q.shape
    return pl.pallas_call(
        functools.partial(attn_fwd_kernel, bq=256, jobs=jobs),
        grid=(heads,),
        in_specs=[pl.BlockSpec(memory_space=pltpu.SMEM)] + [whole((n, wide))] * 3 + jobs.in_specs(),
        out_specs=[whole((n, width)), whole((n, 128))] + jobs.in_specs(),
        out_shape=[jax.ShapeDtypeStruct((n, width), bf16), jax.ShapeDtypeStruct((n, 128), f32)] + jobs.out_shapes(),
        scratch_shapes=[pltpu.VMEM((n, wide), f32), pltpu.VMEM((n, WIN), bf16)] + jobs.scratch(),
        compiler_params=comm_params(number),
        cost_estimate=cost(4 * n * n * WIN * heads, 8 * n * wide),
        name="attend",
    )(length, q, k, v, *jobs.sources())


def attn_bwd_kernel(*refs, bk, jobs):
    count = len(jobs.jobs)
    len_ref, q_ref, k_ref, v_ref, o_ref, do_ref, lse_ref = refs[:7]
    g_ref, sum_ref = refs[7 + count : 9 + count]
    dq, dk, dv, part, qa, da, kx = refs[9 + 2 * count : 16 + 2 * count]
    link, bound, _ = jobs.bind(refs[16 + 2 * count :], refs[7 : 7 + count], refs[9 + count : 9 + 2 * count])
    chains = [job for job in bound if isinstance(job, Chain)]
    h = pl.program_id(0)
    n = q_ref.shape[0]

    @pl.when(h == 0)
    def _():
        if chains:
            link.meet_all()
        else:
            link.meet_plane(jobs.pairs)
        for job in bound:
            if job not in chains[1:]:
                job.start()
        for ref in (dq, dk, dv):
            ref[...] = jnp.zeros_like(ref)
        kx[...] = key_extra(n, len_ref[0])

    heads = pl.num_programs(0)

    def at_head(number, steps):
        @pl.when(h == number)
        def _():
            for step in steps:
                step()

    steps = chain_steps(chains) if chains else []
    for number, some in zip((1, 2, 4, 6, 7), steps):
        at_head(number, some)
    at_head(heads - 3, [job.forward for job in bound])

    win, keep, lane = head_window(h)
    low = keep.astype(bf16)
    v_one = jnp.where((lane >= AUG) & (lane < AUG + 3), 1.0, 0.0).astype(bf16)
    for i in range(n // ROWS):
        rows = slice(i * ROWS, (i + 1) * ROWS)
        here = lax.broadcasted_iota(jnp.int32, (ROWS, 128), 1) == h
        lse = jnp.sum(jnp.where(here, lse_ref[rows, :], 0.0), axis=-1, keepdims=True)
        q = q_ref[rows, win].astype(f32) * keep
        qa[rows, :] = jnp.where(lane == AUG, 1.0, put3(q, lane, AUG + 1, lse)).astype(bf16)
        d = do_ref[rows, win].astype(f32) * keep
        delta = jnp.sum(d * o_ref[rows, win].astype(f32), axis=-1, keepdims=True)
        da[rows, :] = put3(d, lane, AUG, -delta).astype(bf16)
    for i in range(n // bk):
        rows = slice(i * bk, (i + 1) * bk)
        k = k_ref[rows, win] * low + kx[rows, :]
        v = v_ref[rows, win] * low + v_one
        p = jnp.exp2(dot_nt(k, qa[...]) * SCALE2)
        ds = (p * dot_nt(v, da[...])).astype(bf16)
        dv[rows, win] += dot(p.astype(bf16), da[...]) * keep
        dk[rows, win] += dot(ds, qa[...]) * keep
        new = dot_tn(ds, k)
        part[...] = new if i == 0 else part[...] + new
    dq[:, win] += part[...] * keep

    @pl.when(h == heads - 1)
    def _():
        for i, (ref, factor) in enumerate(((dq, SCALE), (dk, SCALE), (dv, 1.0))):
            value = (ref[:, : g_ref.shape[1] // 3] * factor).astype(bf16)
            cols = slice(i * value.shape[1], (i + 1) * value.shape[1])
            g_ref[:, cols] = value
            sum_ref[:, cols] = jnp.sum(value.astype(f32), axis=0, keepdims=True)
        for some in steps[5:]:
            run(some)
        for job in bound:
            job.outward()
        for job in bound:
            job.finish()


def attn_bwd_call(length, q, k, v, o, do, lse, width, heads, jobs, number):
    n, wide = q.shape
    return pl.pallas_call(
        functools.partial(attn_bwd_kernel, bk=256, jobs=jobs),
        grid=(heads,),
        in_specs=[pl.BlockSpec(memory_space=pltpu.SMEM)]
        + [once((n, wide))] * 5
        + [once((n, 128))]
        + jobs.in_specs(),
        out_specs=[once((n, 3 * width)), whole((1, 3 * width))] + jobs.in_specs(),
        out_shape=[
            jax.ShapeDtypeStruct((n, 3 * width), bf16),
            jax.ShapeDtypeStruct((1, 3 * width), f32),
        ]
        + jobs.out_shapes(),
        scratch_shapes=[pltpu.VMEM((n, wide), f32)] * 3
        + [pltpu.VMEM((n, WIN), f32)]
        + [pltpu.VMEM((n, WIN), bf16)] * 3
        + jobs.scratch(),
        compiler_params=comm_params(number),
        cost_estimate=cost(10 * n * n * WIN * heads, 20 * n * wide),
        name="attend_back",
    )(length, q, k, v, o, do, lse, *jobs.sources())


def middle_kernel(*refs, jobs):
    count = len(jobs.jobs)
    o_ref, w_ref, x_ref, vec_ref = refs[:4]
    results = refs[4 + count : 7 + count]
    mid_ref, h_ref, owide_ref, mine, other = refs[7 + 2 * count : 12 + 2 * count]
    link, bound, _ = jobs.bind(refs[12 + 2 * count :], refs[4 : 4 + count], refs[7 + count : 7 + 2 * count])
    n = x_ref.shape[0]
    width = o_ref.shape[1]
    base = link.slots(n // ROWS)
    keep = link.local_slots(3)
    stores = [link.here(a, b, keep + i) for i, (a, b) in enumerate(zip((mid_ref, h_ref, owide_ref), results))]
    link.meet_plane(jobs.pairs)
    for job in bound:
        job.start()

    def swap(i):
        rows = pl.ds(pl.multiple_of(i * ROWS, ROWS), ROWS)
        return rows, link.remote(mine.at[rows], other.at[rows], base + i, base + i, link.sibling())

    def project(i, carry):
        rows, copy = swap(i)
        mine[rows, :] = dot(o_ref[rows, :], w_ref[...]).astype(bf16)
        copy.start()
        return carry

    def norm(i, carry):
        rows, copy = swap(i)
        copy.wait_recv()
        mid = x_ref[rows, :].astype(f32) + (
            mine[rows, :].astype(f32) + other[rows, :].astype(f32) + vec_ref[OBIAS]
        )
        mid_ref[rows, :] = mid
        xhat, _ = standardize(mid)
        h_ref[rows, :] = (xhat * vec_ref[GAIN2] + vec_ref[SHIFT2]).astype(bf16)
        return carry

    lax.fori_loop(0, n // ROWS, project, 0)
    owide_ref[:, :width] = o_ref[...]
    owide_ref[:, width:] = jnp.zeros((n, owide_ref.shape[1] - width), bf16)
    stores[2].start()
    lax.fori_loop(0, n // ROWS, norm, 0)
    stores[0].start()
    stores[1].start()
    for i in range(n // ROWS):
        swap(i)[1].wait_send()
    for job in bound:
        job.forward()
    for job in bound:
        job.inward()
    for job in bound:
        job.finish()
    for c in stores:
        c.wait()


def middle_call(o, w, x, vec, wide, jobs, number):
    n, d = x.shape
    vmem = pl.BlockSpec(memory_space=pltpu.VMEM)
    return pl.pallas_call(
        functools.partial(middle_kernel, jobs=jobs),
        in_specs=[vmem] * 4 + jobs.in_specs(),
        out_specs=[pl.BlockSpec(memory_space=pl.ANY)] * 3 + jobs.in_specs(),
        out_shape=[
            jax.ShapeDtypeStruct((n, d), f32),
            jax.ShapeDtypeStruct((n, d), bf16),
            jax.ShapeDtypeStruct((n, wide), bf16),
        ]
        + jobs.out_shapes(),
        scratch_shapes=[pltpu.VMEM((n, d), f32), pltpu.VMEM((n, d), bf16), pltpu.VMEM((n, wide), bf16)]
        + [pltpu.VMEM((n, d), bf16)] * 2
        + jobs.scratch(n // ROWS),
        compiler_params=comm_params(number),
        cost_estimate=cost(2 * n * w.size, 14 * n * d),
        name="middle",
    )(o, w, x, vec, *jobs.sources())


def ffn_kernel(*refs, chained, last, mc, jobs):
    count = len(jobs.jobs)
    h_ref, dz_ref, up_ref, ub_ref, dn_ref = refs[:5]
    refs = refs[5:]
    if chained:
        old_out, old_dh = refs[:2]
        refs = refs[2:]
    srcs, refs = refs[:count], refs[count:]
    out_ref, dh_ref, dup_ref, ddn_ref, dub_ref = refs[:5]
    dsts, refs = refs[5 : 5 + count], refs[5 + count :]
    ht, act, grad = refs[:3]
    acc, dh = refs[3:5]
    link, bound, (sem,) = jobs.bind(refs[5:], srcs, dsts)
    loads = stores = []
    if chained:
        pairs = ((old_out, acc), (old_dh, dh))
        loads = [pltpu.make_async_copy(a, b, sem.at[i]) for i, (a, b) in enumerate(pairs)]
    if not last:
        pairs = ((acc, out_ref), (dh, dh_ref))
        stores = [pltpu.make_async_copy(a, b, sem.at[2 + i]) for i, (a, b) in enumerate(pairs)]
    gathers, others = split_gathers(bound)
    steps = gather_steps(gathers)
    t = pl.program_id(0)
    tiles = pl.num_programs(0)
    n = h_ref.shape[0]

    @pl.when(t == 0)
    def _():
        link.meet_plane(jobs.pairs)
        run([job.start for job in others] + steps[0])
        if chained:
            for c in loads:
                c.start()
            ht[...] = h_ref[...].T
        else:
            ht[...] = h_ref[...].T
            acc[...] = jnp.zeros_like(acc)
            dh[...] = jnp.zeros_like(dh)

    def at_tile(number, some):
        if some:

            @pl.when(t == number)
            def _():
                run(some)

    at_tile(tiles - 1, [job.forward for job in others])

    def step(i, carry):
        rows = pl.ds(pl.multiple_of(i * mc, mc), mc)
        g, slope = gelu_pair(dot(h_ref[rows, :], up_ref[...]) + ub_ref[...])
        g = g.astype(bf16)
        da = (dot_nt(dz_ref[rows, :], dn_ref[...]) * slope).astype(bf16)
        act[rows, :] = g
        grad[rows, :] = da
        if chained:

            @pl.when((t == 0) & (i == 0))
            def _():
                for c in loads:
                    c.wait()

        acc[rows, :] += dot(g, dn_ref[...])
        dh[rows, :] += dot_nt(da, up_ref[...])
        return carry

    lax.fori_loop(0, n // mc, step, 0)

    at_tile(0, steps[1] if gathers else [])
    dub_ref[...] = jnp.sum(grad[...].astype(f32), axis=0, keepdims=True)
    dup_ref[...] = dot(ht[...], grad[...]).astype(bf16)
    at_tile(tiles - 1, steps[2] if gathers else [])
    ddn_ref[...] = dot_tn(act[...], dz_ref[...]).astype(bf16)

    @pl.when(t == tiles - 1)
    def _():
        if last:
            out_ref[...] = acc[...].astype(out_ref.dtype)
            dh_ref[...] = dh[...].astype(dh_ref.dtype)
        for c in stores:
            c.start()
        for some in steps[3:]:
            run(some)
        run([job.finish for job in bound])
        for c in stores:
            c.wait()


def ffn_call(h, dz, up, bias, down, old, last, jobs, number, name):
    n, d = h.shape
    hidden = up.shape[1]
    bt = FFN_TILE
    out = jax.ShapeDtypeStruct((n, d), bf16 if last else f32)
    chained = old is not None
    kept = once((n, d))
    return pl.pallas_call(
        functools.partial(ffn_kernel, chained=chained, last=last, mc=FFN_ROWS, jobs=jobs),
        grid=(hidden // bt,),
        in_specs=[
            kept,
            kept,
            pl.BlockSpec((d, bt), lambda t: (0, t)),
            pl.BlockSpec((1, bt), lambda t: (0, t)),
            pl.BlockSpec((bt, d), lambda t: (t, 0)),
        ]
        + ([pl.BlockSpec(memory_space=pl.ANY)] * 2 if chained else [])
        + jobs.in_specs(),
        out_specs=([kept] * 2 if last else [pl.BlockSpec(memory_space=pl.ANY)] * 2)
        + [
            pl.BlockSpec((d, bt), lambda t: (0, t)),
            pl.BlockSpec((bt, d), lambda t: (t, 0)),
            pl.BlockSpec((1, bt), lambda t: (0, t)),
        ]
        + jobs.in_specs(),
        out_shape=[
            out,
            out,
            jax.ShapeDtypeStruct((d, hidden), bf16),
            jax.ShapeDtypeStruct((hidden, d), bf16),
            jax.ShapeDtypeStruct((1, hidden), f32),
        ]
        + jobs.out_shapes(),
        scratch_shapes=[pltpu.VMEM((d, n), bf16)]
        + [pltpu.VMEM((n, bt), bf16)] * 2
        + [pltpu.VMEM((n, d), f32)] * 2
        + jobs.scratch()
        + [pltpu.SemaphoreType.DMA((4,))],
        compiler_params=comm_params(number),
        cost_estimate=cost(12 * n * d * hidden, 8 * d * hidden + 12 * n * d),
        name=name,
    )(h, dz, up, bias, down, *(old if chained else ()), *jobs.sources())


def second_back_kernel(*refs, jobs):
    count = len(jobs.jobs)
    mid_ref, dh_ref, out_ref, dz_ref, vec_ref, w_ref, o_ref, dh_any, out_any = refs[:9]
    dmid_ref, do_ref, dw_ref, sums_ref, layer_ref = refs[9 + count : 14 + count]
    acc, dh_other, out_other = refs[14 + 2 * count : 17 + 2 * count]
    link, bound, _ = jobs.bind(refs[17 + 2 * count :], refs[9 : 9 + count], refs[14 + count : 14 + 2 * count])
    chains = [job for job in bound if isinstance(job, Chain)]
    others = [job for job in bound if job not in chains]
    steps = chain_steps(chains) if chains else []
    i = pl.program_id(0)
    blocks = pl.num_programs(0)
    half = layer_ref.shape[0] // ROWS
    width = w_ref.shape[0]
    base = link.slots(3 * half)

    def swap_dh(j):
        rows = pl.ds(pl.multiple_of(j * ROWS, ROWS), ROWS)
        return link.remote(dh_any.at[rows], dh_other.at[rows], base + j, base + j, link.sibling())

    def swap_out(j):
        src = pl.ds(pl.multiple_of(((1 - link.core) * half + j) * ROWS, ROWS), ROWS)
        dst = pl.ds(pl.multiple_of(j * ROWS, ROWS), ROWS)
        slot = base + 2 * half + j
        return link.remote(out_any.at[src], out_other.at[dst], slot, slot, link.sibling())

    @pl.when(i == 0)
    def _():
        if chains:
            link.meet_all()
        else:
            link.meet_plane()
        for j in range(2 * half):
            swap_dh(j).start()
        for j in range(half):
            swap_out(j).start()
        run([job.start for job in others + chains[:1]])
        acc[...] = jnp.zeros_like(acc)
        sums_ref[...] = jnp.zeros_like(sums_ref)

    for number, some in zip((2, 4), steps):

        @pl.when(i == number)
        def _():
            run(some)

    @pl.when(i == blocks - 1)
    def _():
        run([job.forward for job in others])

    mid = mid_ref[...]
    xhat, inv = standardize(mid)
    swap_dh(i).wait_recv()
    rows = pl.ds(pl.multiple_of(i * ROWS, ROWS), ROWS)
    dh = dh_ref[...].astype(f32) + dh_other[rows, :].astype(f32)
    dx = dh * vec_ref[GAIN2]
    dz = dz_ref[...].astype(f32)
    dmid = dz + inv * (
        dx - jnp.mean(dx, axis=-1, keepdims=True) - xhat * jnp.mean(dx * xhat, axis=-1, keepdims=True)
    )
    dmid_ref[...] = dmid
    dy = dmid.astype(bf16)
    do_ref[:, :width] = dot_nt(dy, w_ref[...]).astype(bf16)
    do_ref[:, width:] = jnp.zeros((do_ref.shape[0], do_ref.shape[1] - width), bf16)
    acc[...] += dot_tn(o_ref[...], dy)
    for row, value in enumerate((dh * xhat, dh, dy.astype(f32), dz)):
        sums_ref[row : row + 1, :] += jnp.sum(value, axis=0, keepdims=True)

    j = i - link.core * half

    @pl.when((j >= 0) & (j < half))
    def _():
        swap_out(j).wait_recv()
        here = pl.ds(pl.multiple_of(j * ROWS, ROWS), ROWS)
        layer_ref[here, :] = (
            mid + (out_ref[...].astype(f32) + out_other[here, :].astype(f32) + vec_ref[DBIAS])
        ).astype(bf16)

    @pl.when(i == blocks - 1)
    def _():
        dw_ref[...] = acc[...].astype(bf16)
        for j in range(2 * half):
            swap_dh(j).wait_send()
        for j in range(half):
            swap_out(j).wait_send()
        for some in steps[2:]:
            run(some)
        run([job.outward for job in chains] + [job.finish for job in others + chains])


def second_back_call(mid, dh, out, dz, vec, w, o, wide, jobs, number):
    n, d = mid.shape
    width = w.shape[0]
    block = row_block(ROWS, d)
    count = 3 * n // ROWS // 2
    return pl.pallas_call(
        functools.partial(second_back_kernel, jobs=jobs),
        grid=(n // ROWS,),
        in_specs=[block] * 4
        + [whole(vec.shape), whole(w.shape), row_block(ROWS, width)]
        + [pl.BlockSpec(memory_space=pl.ANY)] * 2
        + jobs.in_specs(),
        out_specs=[block, row_block(ROWS, wide), whole((width, d)), whole((8, d)), whole((n // 2, d))]
        + jobs.in_specs(),
        out_shape=[
            jax.ShapeDtypeStruct((n, d), f32),
            jax.ShapeDtypeStruct((n, wide), bf16),
            jax.ShapeDtypeStruct((width, d), bf16),
            jax.ShapeDtypeStruct((8, d), f32),
            jax.ShapeDtypeStruct((n // 2, d), bf16),
        ]
        + jobs.out_shapes(),
        scratch_shapes=[
            pltpu.VMEM((width, d), f32),
            pltpu.VMEM((n, d), bf16),
            pltpu.VMEM((n // 2, d), bf16),
        ]
        + jobs.scratch(count),
        compiler_params=comm_params(number),
        cost_estimate=cost(4 * n * d * width, 14 * n * d),
        name="second_back",
    )(mid, dh, out, dz, vec, w, o, dh, out, *jobs.sources())


def dw_kernel(h_ref, g_ref, out_ref):
    out_ref[...] = dot_tn(h_ref[...], g_ref[...]).astype(bf16)


def dw_call(h, grads):
    n, d = h.shape
    cols = grads.shape[1]
    return pl.pallas_call(
        dw_kernel,
        grid=(d // 256,),
        in_specs=[pl.BlockSpec((n, 256), lambda i: (0, i)), whole((n, cols))],
        out_specs=row_block(256, cols),
        out_shape=jax.ShapeDtypeStruct((d, cols), bf16),
        compiler_params=params(),
        cost_estimate=cost(2 * n * d * cols, 2 * (n * d + n * cols + d * cols)),
        name="project_grad",
    )(h, grads)


def first_back_kernel(*refs, jobs):
    count = len(jobs.jobs)
    g_ref, w_ref, vec_ref, x_any, dmid_any = refs[:5]
    dx_ref, sums_ref = refs[5 + count : 7 + count]
    x, dmid, mine, other = refs[7 + 2 * count : 11 + 2 * count]
    link, bound, _ = jobs.bind(refs[11 + 2 * count :], refs[5 : 5 + count], refs[7 + count : 7 + 2 * count])
    size = dx_ref.shape[0]
    half = size // ROWS
    base = link.slots(half)
    keep = link.local_slots(2)
    own = pl.ds(pl.multiple_of(link.core * size, size), size)
    loads = [link.here(x_any.at[own], x, keep), link.here(dmid_any.at[own], dmid, keep + 1)]
    for c in loads:
        c.start()
    link.meet_plane(jobs.pairs)
    for job in bound:
        job.start()

    def product(j):
        rows = pl.ds(pl.multiple_of(j * ROWS, ROWS), ROWS)
        return dot_nt(g_ref[rows, :], w_ref[...])

    def swap(j):
        rows = pl.ds(pl.multiple_of(j * ROWS, ROWS), ROWS)
        return rows, link.remote(mine.at[rows], other.at[rows], base + j, base + j, link.sibling())

    def send(j, carry):
        rows, copy = swap(j)
        mine[rows, :] = product((1 - link.core) * half + j).astype(bf16)
        copy.start()
        return carry

    def norm(j, carry):
        rows, copy = swap(j)
        part = product(link.core * half + j)
        copy.wait_recv()
        xhat, inv = standardize(x[rows, :].astype(f32))
        dh = part + other[rows, :].astype(f32)
        dx = dh * vec_ref[GAIN1]
        dx_ref[rows, :] = (
            dmid[rows, :]
            + inv
            * (dx - jnp.mean(dx, axis=-1, keepdims=True) - xhat * jnp.mean(dx * xhat, axis=-1, keepdims=True))
        ).astype(bf16)
        for row, value in enumerate((dh * xhat, dh)):
            sums_ref[row : row + 1, :] += jnp.sum(value, axis=0, keepdims=True)
        return carry

    sums_ref[...] = jnp.zeros_like(sums_ref)
    lax.fori_loop(0, half, send, 0)
    for c in loads:
        c.wait()
    lax.fori_loop(0, half, norm, 0)
    for j in range(half):
        swap(j)[1].wait_send()
    for job in bound:
        job.forward()
    for job in bound:
        job.inward()
    for job in bound:
        job.finish()


def first_back_call(grads, w, vec, x, dmid, jobs, number):
    n, d = x.shape
    size = n // 2
    vmem = pl.BlockSpec(memory_space=pltpu.VMEM)
    hbm = pl.BlockSpec(memory_space=pl.ANY)
    return pl.pallas_call(
        functools.partial(first_back_kernel, jobs=jobs),
        in_specs=[vmem] * 3 + [hbm] * 2 + jobs.in_specs(),
        out_specs=[vmem] * 2 + jobs.in_specs(),
        out_shape=[jax.ShapeDtypeStruct((size, d), bf16), jax.ShapeDtypeStruct((8, d), f32)] + jobs.out_shapes(),
        scratch_shapes=[
            pltpu.VMEM((size, d), bf16),
            pltpu.VMEM((size, d), f32),
            pltpu.VMEM((size, d), bf16),
            pltpu.VMEM((size, d), bf16),
        ]
        + jobs.scratch(size // ROWS),
        compiler_params=comm_params(number),
        cost_estimate=cost(2 * n * w.size, 12 * n * d),
        name="first_back",
    )(grads, w, vec, x, dmid, *jobs.sources())


class Blocks:
    def __init__(self, ref, stride, first):
        self.ref, self.stride, self.first = ref, stride, first

    @property
    def at(self):
        return self

    def __getitem__(self, index):
        block, part = index
        start = pl.multiple_of(block * self.stride + (self.first + part.start), 16)
        return self.ref.at[pl.ds(start, part.size)]


def back_kernel(*refs, jobs):
    count = len(jobs.jobs)
    g_ref, vec_ref, h_ref, early_ref, *w_anys = refs[:7]
    x_any, dmid_any = refs[7:9]
    tokens_any, small_ref, both_any = refs[9 + count : 12 + count]
    rest = list(refs[12 + 2 * count :])
    x, dmid, mine, other, dx, dw, own, total, came, stage = rest[:10]
    rest = rest[10:]
    w_refs, rest = rest[:3], rest[3:]
    small_bufs, rest = rest[:3], rest[3:]
    reduce_bufs, rest = [rest[10 * i : 10 * i + 10] for i in range(3)], rest[30:]
    chain_bufs, rest = [rest[3 * i : 3 * i + 3] for i in range(6)], rest[18:]
    link, bound, _ = jobs.bind(rest, refs[9 : 9 + count], refs[12 + count : 12 + 2 * count])
    ready = [job for job in bound if isinstance(job, Chain)]
    others = [job for job in bound if job not in ready]
    size, d = dx.shape
    half = size // ROWS
    _, owned, width = own.shape
    order = (2, 1, 0)
    reduces = [Reduce(link, Blocks(dw.at[c], owned, 0), own.at[c], reduce_bufs[c]) for c in order]
    last = []
    for c in order:
        for i in range(2):
            rows, cols = pl.ds(i * (owned // 2), owned // 2), pl.ds(c * width, width)
            last.append(Chain(link, own.at[c, rows], both_any.at[:, rows, cols], chain_bufs[len(last)]))
    to_owners = FromClip(link, dx, tokens_any, [stage])
    base = link.slots(half)
    keep = link.local_slots(5)
    swap_base = link.slots(3)
    peers = [link.sibling()] + [(link.rep, link.shard ^ bit) for bit in (1, 2)]
    swaps = [link.remote(total, came.at[i], swap_base + i, swap_base + i, to) for i, to in enumerate(peers)]
    small = Chain(link, total, small_ref, small_bufs)
    mine_rows = pl.ds(pl.multiple_of(link.core * size, size), size)
    loads = [link.here(x_any.at[mine_rows], x, keep), link.here(dmid_any.at[mine_rows], dmid, keep + 1)]
    loads += [link.here(a, b, keep + 2 + i) for i, (a, b) in enumerate(zip(w_anys, w_refs))]
    for c in loads:
        c.start()
    link.meet_all()
    ready[0].start()
    for c, job in zip(order, reduces):

        def weight(i, carry):
            part = pl.ds(pl.multiple_of(i * 256, 256), 256)
            dw[c, part, :] = dot_tn(h_ref[:, part], g_ref[:, c * width : (c + 1) * width]).astype(bf16)
            return carry

        lax.fori_loop(0, d // 256, weight, 0)
        job.start()

    def product(j):
        rows = pl.ds(pl.multiple_of(j * ROWS, ROWS), ROWS)
        parts = [dot_nt(g_ref[rows, c * width : (c + 1) * width], w_refs[c][...]) for c in range(3)]
        return parts[0] + parts[1] + parts[2]

    def swap(j):
        rows = pl.ds(pl.multiple_of(j * ROWS, ROWS), ROWS)
        return rows, link.remote(mine.at[rows], other.at[rows], base + j, base + j, link.sibling())

    def send(j, carry):
        rows, copy = swap(j)
        mine[rows, :] = product((1 - link.core) * half + j).astype(bf16)
        copy.start()
        return carry

    first = early_ref.shape[0]

    def norm(j, carry):
        rows, copy = swap(j)
        part = product(link.core * half + j)
        copy.wait_recv()
        xhat, inv = standardize(x[rows, :].astype(f32))
        dh = part + other[rows, :].astype(f32)
        slope = dh * vec_ref[GAIN1]
        dx[rows, :] = (
            dmid[rows, :]
            + inv
            * (
                slope
                - jnp.mean(slope, axis=-1, keepdims=True)
                - xhat * jnp.mean(slope * xhat, axis=-1, keepdims=True)
            )
        ).astype(bf16)
        for row, value in enumerate((dh * xhat, dh)):
            total[first + row : first + row + 1, :] += jnp.sum(value, axis=0, keepdims=True)
        return carry

    steps = chain_steps(ready)
    run(steps[0])
    total[:first, :] = early_ref[...]
    total[first:, :] = jnp.zeros((total.shape[0] - first, d), f32)
    for c in loads:
        c.wait()
    lax.fori_loop(0, half, send, 0)
    reduces[0].forward()
    after = {0: steps[1] + [reduces[1].forward], 1: [reduces[2].forward]}
    for j in range(half):
        norm(j, 0)
        run(after.get(j, []))
    swaps[0].start()
    run(steps[2])
    reduces[0].collect()
    last[0].start()
    reduces[1].collect()
    swaps[0].wait()
    total[...] += came[0]
    swaps[1].start()
    reduces[2].collect()
    for some in steps[3:]:
        run(some)
    swaps[1].wait()
    total[...] += came[1]
    swaps[2].start()
    for number, some in enumerate(chain_steps(last)):
        run(some)
        if number == 0:
            swaps[2].wait()
            total[...] += came[2]
            small.start()
        if number == 2:
            run([job.start for job in [to_owners] + others])
        if number == 3:
            small.inward()
            small.sent()
        if number == 5:
            small.across()
    for c in ready + last:
        c.outward()
    small.outward()
    for job in ready + last + [small]:
        job.finish()
    for job in reduces:
        job.close()
    for j in range(half):
        swap(j)[1].wait_send()
    run([job.finish for job in [to_owners] + others])


def back_call(grads, weights, vec, h, early, x, dmid, jobs, clips, number):
    n, d = x.shape
    size = n // 2
    width = grads.shape[1] // 3
    groups = lax.axis_size("shard")
    owned = d // groups
    rows = early.shape[0] + 8
    small = pltpu.VMEM((rows, d), f32)
    vmem = pl.BlockSpec(memory_space=pltpu.VMEM)
    hbm = pl.BlockSpec(memory_space=pl.ANY)
    return pl.pallas_call(
        functools.partial(back_kernel, jobs=jobs),
        in_specs=[vmem] * 4 + [hbm] * 5 + jobs.in_specs(),
        out_specs=[hbm, vmem, hbm] + jobs.in_specs(),
        out_shape=[
            jax.ShapeDtypeStruct((clips, size // clips, d), bf16),
            jax.ShapeDtypeStruct((2, rows, d), f32),
            jax.ShapeDtypeStruct((2, owned, 3 * width), bf16),
        ]
        + jobs.out_shapes(),
        scratch_shapes=[
            pltpu.VMEM((size, d), bf16),
            pltpu.VMEM((size, d), f32),
            pltpu.VMEM((size, d), bf16),
            pltpu.VMEM((size, d), bf16),
            pltpu.VMEM((size, d), bf16),
            pltpu.VMEM((3, d, width), bf16),
            pltpu.VMEM((3, owned, width), bf16),
            small,
            pltpu.VMEM((3, rows, d), f32),
            pltpu.VMEM((size // clips, d), bf16),
        ]
        + [pltpu.VMEM((d, width), bf16)] * 3
        + [small] * 3
        + [pltpu.VMEM((owned // 2, width), bf16)] * 48
        + jobs.scratch(80),
        compiler_params=comm_params(number, 62),
        cost_estimate=cost(12 * n * weights[0].size, 20 * n * d),
        name="back",
    )(grads, vec, h, early, *weights, x, dmid, *jobs.sources())


def place_kernel(*refs, groups):
    up_refs, down_refs = refs[:4], refs[4:8]
    out_ref, in_ref = refs[8:10]
    up, down, wo = refs[10:13]
    qkv = refs[13:16]

    def put(target, axis, pieces):
        first = 0
        for value in pieces:
            size = value.shape[axis]
            span = slice(first, first + size)
            if axis:
                target[:, span] = value.astype(f32)
            else:
                target[span, :] = value.astype(f32)
            first += size

    cut = up_refs[0].shape[1]
    for part in range(2):
        put(up.at[pl.ds(part * cut, cut)], 1, [r[c] for c in range(2) for r in (up_refs[part], up_refs[2 + part])])
    put(down, 0, [r[c] for c in range(2) for r in down_refs])
    put(wo, 0, [out_ref[c] for c in range(2)])
    rows = in_ref.shape[1]
    width = in_ref.shape[2] // 3
    part = width // groups

    for i, out in enumerate(qkv):
        for c in range(2):
            value = in_ref[c, :, i * width : (i + 1) * width].astype(f32)
            for s in range(groups):
                first = (2 * s + c) * part
                out[:, first : first + part] = value[:, s * part : (s + 1) * part]


def place_call(ups, downs, wo, qkv, groups):
    steps = 5
    own_d, cols = qkv.shape[1:]
    d = downs[0].shape[2]
    own_f = 2 * sum(a.shape[1] for a in downs)
    take = [pl.BlockSpec((2, a.shape[1], a.shape[2] // groups), lambda i: (0, 0, jnp.minimum(i, groups - 1))) for a in ups]
    wide = d // steps
    per = own_d // steps
    ff = 2 * ups[0].shape[2] + 2 * ups[2].shape[2]
    return pl.pallas_call(
        functools.partial(place_kernel, groups=groups),
        grid=(steps,),
        in_specs=take
        + [pl.BlockSpec((2, a.shape[1], wide), lambda i: (0, 0, i)) for a in downs]
        + [
            pl.BlockSpec((2, wo.shape[1], wide), lambda i: (0, 0, i)),
            pl.BlockSpec((2, per, cols), lambda i: (0, i, 0)),
        ],
        out_specs=[
            pl.BlockSpec((own_d, ff // groups), lambda i: (0, jnp.minimum(i, groups - 1))),
            pl.BlockSpec((own_f, wide), lambda i: (0, i)),
            pl.BlockSpec((own_d, wide), lambda i: (0, i)),
        ]
        + [pl.BlockSpec((per, d), lambda i: (i, 0))] * 3,
        out_shape=[
            jax.ShapeDtypeStruct((own_d, ff), f32),
            jax.ShapeDtypeStruct((own_f, d), f32),
            jax.ShapeDtypeStruct((own_d, d), f32),
        ]
        + [jax.ShapeDtypeStruct((own_d, d), f32)] * 3,
        compiler_params=params(),
        name="place",
    )(*ups, *downs, wo, qkv)


def own_sum(blocks, others):
    shard = lax.axis_index("shard")
    total = lax.dynamic_index_in_dim(blocks, shard, 0, keepdims=False).astype(f32)
    for i in range(others.shape[0]):
        total = total + others[i].astype(f32)
    return total.astype(bf16)


def over_reps(own):
    planes = lax.axis_size("rep") // 2
    sums = lax.psum_scatter(
        own,
        "rep",
        scatter_dimension=0,
        tiled=True,
        axis_index_groups=[[2 * z + c for z in range(planes)] for c in range(2)],
    )
    both = lax.all_gather(sums, "rep", axis=0)
    rows, cols = sums.shape
    return both.reshape(planes, 2, rows, cols).transpose(1, 0, 2, 3).reshape(2, planes * rows, cols)


def on_device(
    tokens,
    lengths,
    cotangent,
    first_gain,
    first_shift,
    query_weight,
    query_bias,
    key_weight,
    value_weight,
    value_bias,
    out_weight,
    out_bias,
    second_gain,
    second_shift,
    up_weight,
    up_bias,
    down_weight,
    down_bias,
):
    g = lax.axis_size("shard")
    shard = lax.axis_index("shard")
    core = lax.rem(lax.axis_index("rep"), 2)
    cl, rows, d = tokens.shape
    n = 2 * cl * rows
    ff = up_weight.shape[1]
    own_d = d // g
    own_f = ff // g
    attn_cols = own_d // 2
    ffn_cols = own_f // 2
    width = d // 2
    heads = width // HEAD
    wide = pl.cdiv(width, 128) * 128 + 128
    first_n = ffn_cols * 2 // 5
    pieces = ((0, first_n), (first_n, ffn_cols))

    fast = g == 4 and lax.axis_size("rep") == 8
    weights = PairGather if fast else Gather
    positions = shard * rows + jnp.arange(rows, dtype=jnp.int32)
    live = positions[None, :] < lengths[:, None]
    masked = jnp.where(live[:, :, None], cotangent, jnp.zeros_like(cotangent))

    def core_of():
        return lax.rem(lax.axis_index("rep"), 2)

    def core_cols(w, size, a, b):
        def of(c):
            return jnp.concatenate([w[:, (2 * s + c) * size + a : (2 * s + c) * size + b] for s in range(g)], axis=1)

        return jnp.where(core == 0, of(0), of(1))

    vectors = (first_gain, first_shift, query_bias, value_bias, out_bias, second_gain, second_shift, down_bias)
    small = pack_call((*vectors, up_bias), lengths)
    own = [core_cols(w, attn_cols, 0, attn_cols) for w in (query_weight, key_weight, value_weight)]
    jobs = Jobs(
        (ToClip, tokens, (n, d)),
        (Gather, small, (g,) + small.shape),
        *[(weights, w, (g,) + w.shape) for w in own],
    )
    h1, q, k, v, vec, x, _, *w_qkv, other_small = first_call(jobs, small, wide, 0)
    w_qkv = [w.reshape(d, width) for w in w_qkv]
    near = lax.div(shard, cl) == core
    lens = jnp.where(near, small[LENGTHS], other_small[LENGTHS])[0]
    length = lens[lax.rem(shard, cl)].astype(jnp.int32).reshape(1)

    ubias = lax.dynamic_index_in_dim(
        vec[UBIAS : UBIAS + own_f // own_d].reshape(-1, g, own_d).transpose(1, 0, 2).reshape(g, 2, ffn_cols),
        core,
        1,
        keepdims=False,
    )
    ups = [core_cols(up_weight, ffn_cols, a, b) for a, b in pieces]

    def half_rows(w, first=0, last=None):
        half = w.shape[0] // 2
        size = (half if last is None else last) - first

        def view(ref):
            return ref.at[pl.ds(pl.multiple_of(core_of() * half + first, 16), size)]

        return size, view

    def gathered(a, part=None):
        if part is None:
            return (weights, a, (g,) + a.shape)
        return (weights, a, (g, part[0]) + a.shape[1:], part[1])

    jobs = Jobs(
        gathered(ups[0]),
        gathered(down_weight, half_rows(down_weight, *pieces[0])),
        gathered(out_weight, half_rows(out_weight)),
    )
    o, lse, up, down, w_out = attn_fwd_call(length, q, k, v, width, heads, jobs, 1)
    w_out = w_out.reshape(width, d)
    jobs = Jobs((ToClip, masked, (n, d)))
    mid, h2, o_wide, dz = middle_call(o, w_out, x, vec, wide, jobs, 2)

    def hidden_bias(piece):
        return ubias[:, piece[0] : piece[1]].reshape(1, -1)


    def to_owners(a):
        if fast:
            return (Reduce, a, a.shape[1:])
        return (Owners, a, (g - 1,) + a.shape[1:])

    def owned(a, came):
        return came if fast else own_sum(a, came)

    def chained(a):
        return (Chain, a, (2,) + a.shape)

    def chained_halves(a):
        half = a.shape[0] // 2

        def part(i):
            return lambda ref: ref.at[pl.ds(i * half, half)]

        return [(Chain, a, (2, half, a.shape[1]), part(i)) for i in range(2)]

    jobs = Jobs(gathered(ups[1]), gathered(down_weight, half_rows(down_weight, *pieces[1])))
    out, dh2, dup0, ddn0, dub0, up1, down1 = ffn_call(
        h2, dz, up.reshape(d, -1), hidden_bias(pieces[0]), down.reshape(-1, d), None, False, jobs, 3, "hidden0"
    )
    dup0, ddn0 = dup0.reshape(g, own_d, -1), ddn0.reshape(g, -1, d)
    jobs = Jobs(to_owners(dup0), to_owners(ddn0))
    out, dh2, dup1, ddn1, dub1, dup0_in, ddn0_in = ffn_call(
        h2, dz, up1.reshape(d, -1), hidden_bias(pieces[1]), down1.reshape(-1, d), (out, dh2), True, jobs, 4, "hidden1"
    )
    dup1, ddn1 = dup1.reshape(g, own_d, -1), ddn1.reshape(g, -1, d)
    up0_own, down0_own = owned(dup0, dup0_in), owned(ddn0, ddn0_in)

    jobs = [to_owners(dup1)]
    if fast:
        jobs += chained_halves(up0_own)
    dmid, do, dwo, sums2, layer_own, dup1_in, *sums0 = second_back_call(
        mid, dh2, out, dz, vec, w_out, o, wide, Jobs(*jobs), 5
    )
    dwo = dwo.reshape(g, -1, d)
    up1_own = owned(dup1, dup1_in)

    to_tokens = (FromClip, layer_own, (cl, rows, d))
    jobs = [to_owners(ddn1), to_owners(dwo), to_tokens]
    if fast:
        jobs += chained_halves(down0_own) + chained_halves(up1_own)
    grads, bias_sums, ddn1_in, dwo_in, layer_out, *later = attn_bwd_call(
        length, q, k, v, o_wide, do, lse, width, heads, Jobs(*jobs), 6
    )
    down1_own, out_own_grad = owned(ddn1, ddn1_in), owned(dwo, dwo_in)

    def spread(v, size):
        out = jnp.zeros((g, 2, size), f32)
        return lax.dynamic_update_index_in_dim(out, v.reshape(g, size), core, 1)

    ub_sums = jnp.concatenate([dub0.reshape(g, -1), dub1.reshape(g, -1)], axis=1)
    early = jnp.concatenate(
        [
            spread(bias_sums[0, :width], attn_cols).reshape(1, d),
            spread(bias_sums[0, 2 * width :], attn_cols).reshape(1, d),
            sums2[:4] * 0.5,
            spread(ub_sums, ffn_cols).reshape(-1, d),
        ],
        axis=0,
    )
    early = jnp.pad(early, ((0, -early.shape[0] % 8), (0, 0)))

    if fast:
        jobs = Jobs(*chained_halves(down1_own), chained(out_own_grad))
        tokens_grad, smalls, qkv_all, *sums = back_call(grads, w_qkv, vec, h1, early, x, dmid, jobs, cl, 7)
        up_grad, down_grad, out_grad, *qkv_grads = place_call(
            (*sums0, *later[2:]), (*later[:2], *sums[:2]), sums[2], qkv_all, g
        )
        smalls = lax.dynamic_index_in_dim(smalls, core, 0, keepdims=False)
    else:
        dwqkv = dw_call(h1, grads).reshape(g, own_d, 3 * width)
        jobs = Jobs(to_owners(dwqkv))
        dx, sums1, dwqkv_in = first_back_call(grads, jnp.concatenate(w_qkv, axis=1), vec, x, dmid, jobs, 7)
        jobs = Jobs((FromClip, dx, (cl, rows, d)))
        tokens_grad, _ = exchange_call(jobs, sums1, 8, "last_exchange")
        ups_all = [over_reps(a).reshape(2, own_d, g, -1) for a in (up0_own, up1_own)]
        up_grad = jnp.concatenate(ups_all, axis=3).transpose(1, 2, 0, 3).reshape(own_d, ff).astype(f32)
        downs_all = [over_reps(a) for a in (down0_own, down1_own)]
        down_grad = jnp.concatenate(downs_all, axis=1).reshape(own_f, d).astype(f32)
        out_grad = over_reps(out_own_grad).reshape(own_d, d).astype(f32)
        qkv_all = over_reps(owned(dwqkv, dwqkv_in)).reshape(2, own_d, 3, g, attn_cols)
        qkv_grads = [qkv_all[:, :, i].transpose(1, 2, 0, 3).reshape(own_d, d).astype(f32) for i in range(3)]
        smalls = lax.psum(jnp.concatenate([early, sums1], axis=0), ("rep", "shard"))

    mine = lax.dynamic_slice_in_dim(smalls, shard * own_d, own_d, 1)
    s_qb, s_vb, s_gain2, s_shift2, s_ob, s_db = [mine[i] for i in range(6)]
    s_gain1, s_shift1 = [mine[early.shape[0] + i] for i in range(2)]
    s_ub = lax.dynamic_slice_in_dim(smalls[6 : 6 + ff // d].reshape(-1), shard * own_f, own_f, 0)

    return (
        layer_out,
        tokens_grad,
        s_gain1,
        s_shift1,
        qkv_grads[0],
        s_qb,
        qkv_grads[1],
        qkv_grads[2],
        s_vb,
        out_grad,
        s_ob,
        s_gain2,
        s_shift2,
        up_grad,
        s_ub,
        down_grad,
        s_db,
    )


def solution(mesh):
    row, mat, vec = P("rep", "shard", None), P("shard", None), P("shard")
    return jax.shard_map(
        on_device,
        mesh=mesh,
        in_specs=(row, P("rep"), row, vec, vec, mat, vec, mat, mat, vec, mat, vec, vec, vec, mat, vec, mat, vec),
        out_specs=(row, row, vec, vec, mat, vec, mat, mat, vec, mat, vec, vec, vec, mat, vec, mat, vec),
        check_vma=False,
    )
```

```python
import functools
import math

import jax
import jax.numpy as jnp
from jax import lax
from jax.experimental import pallas as pl
from jax.experimental.pallas import tpu as pltpu
from jax.sharding import PartitionSpec as P

HEAD = 80
WIN = 256
AUG = 192
EPS = 1e-5
SCALE = HEAD**-0.5
SCALE2 = SCALE * math.log2(math.e)
DEAD = -1e30
ROWS = 256
GAIN1, SHIFT1, QBIAS, VBIAS, OBIAS, GAIN2, SHIFT2, DBIAS, LENGTHS = [slice(i, i + 1) for i in range(9)]
UBIAS = 9
FFN_TILE = 512
FFN_ROWS = 768
PAIR_SHARE = 3
f32 = jnp.float32
bf16 = jnp.bfloat16
MESH = pl.DeviceIdType.MESH

ERF_P = 0.35
ERF_C = (0.19458996, 0.23381038, -0.00165479, 0.67243411, -0.66868964, 0.76616445, -0.19665448)


def params(limit=60):
    return pltpu.CompilerParams(vmem_limit_bytes=limit * 2**20)


def cost(flops, size):
    return pl.CostEstimate(flops=int(flops), bytes_accessed=int(size), transcendentals=0)


def dot(a, b):
    return jnp.dot(a, b, preferred_element_type=f32)


def dot_nt(a, b):
    return lax.dot_general(a, b, (((1,), (1,)), ((), ())), preferred_element_type=f32)


def dot_tn(a, b):
    return lax.dot_general(a, b, (((0,), (0,)), ((), ())), preferred_element_type=f32)


def gelu_pair(a):
    expo = jnp.exp2(a * a * (-0.5 * math.log2(math.e)))
    t = 1.0 / (1.0 + jnp.abs(a) * (ERF_P * math.sqrt(0.5)))
    total = ERF_C[-1]
    for c in ERF_C[-2::-1]:
        total = total * t + c
    tail = 0.5 * expo * (total * t)
    cdf = jnp.where(a >= 0, 1.0 - tail, tail)
    return a * cdf, cdf + a * (expo * (1.0 / math.sqrt(2.0 * math.pi)))


def whole(shape):
    return pl.BlockSpec(shape, lambda *_: (0,) * len(shape))


def once(shape):
    return pl.BlockSpec(shape, lambda *_: (0,) * len(shape), pipeline_mode=pl.Buffered(1))


def row_block(rows, cols):
    return pl.BlockSpec((rows, cols), lambda i: (i, 0))


def standardize(x):
    centred = x - jnp.mean(x, axis=-1, keepdims=True)
    inv = lax.rsqrt(jnp.mean(centred * centred, axis=-1, keepdims=True) + EPS)
    return centred * inv, inv


class Link:
    def __init__(self, sems):
        self.send, self.recv, self.local = sems
        self.next = 0
        self.next_local = 0
        self.groups = lax.axis_size("shard")
        self.rep = lax.axis_index("rep")
        self.shard = lax.axis_index("shard")
        self.core = lax.rem(self.rep, 2)
        self.half = self.groups // 2

    def meet_plane(self, pair=False):
        barrier = pltpu.get_barrier_semaphore()
        base = self.rep - self.core
        for c in range(2):
            for p in range(self.groups):
                if c or p:
                    to = (base + (self.core ^ c), self.shard ^ p)
                    pl.semaphore_signal(barrier, inc=1, device_id=to, device_id_type=MESH)
        if pair:
            pl.semaphore_signal(barrier, inc=1, device_id=self.pair(), device_id_type=MESH)
        pl.semaphore_wait(barrier, 2 * self.groups - 1 + int(pair))

    def pair(self):
        return (self.rep ^ 2, self.shard)

    def meet_all(self):
        barrier = pltpu.get_barrier_semaphore()
        base = self.rep - self.core
        for c in range(2):
            for p in range(self.groups):
                if c or p:
                    to = (base + (self.core ^ c), self.shard ^ p)
                    pl.semaphore_signal(barrier, inc=1, device_id=to, device_id_type=MESH)
        pl.semaphore_signal(barrier, inc=1, device_id=self.inward(), device_id_type=MESH)

        @pl.when(self.inner())
        def _():
            pl.semaphore_signal(barrier, inc=1, device_id=self.outward(), device_id_type=MESH)
            pl.semaphore_wait(barrier, 2 * self.groups + 1)

        @pl.when(jnp.logical_not(self.inner()))
        def _():
            pl.semaphore_wait(barrier, 2 * self.groups)

    def inner(self):
        plane = lax.div(self.rep, 2)
        return (plane == 1) | (plane == 2)

    def inward(self):
        return (self.rep + jnp.where(self.rep < 4, 2, -2), self.shard)

    def outward(self):
        return (self.rep - jnp.where(self.rep < 4, 2, -2), self.shard)

    def meet_core(self):
        barrier = pltpu.get_barrier_semaphore()
        pl.semaphore_signal(barrier, inc=1, device_id=self.sibling(), device_id_type=MESH)
        pl.semaphore_wait(barrier, 1)

    def sibling(self):
        return (self.rep ^ 1, self.shard)

    def slots(self, count):
        first = self.next
        self.next += count
        return first

    def local_slots(self, count):
        first = self.next_local
        self.next_local += count
        return first

    def remote(self, src, dst, send, recv, to):
        return pltpu.make_async_remote_copy(
            src_ref=src,
            dst_ref=dst,
            send_sem=self.send.at[send],
            recv_sem=self.recv.at[recv],
            device_id=to,
            device_id_type=MESH,
        )

    def here(self, src, dst, slot):
        return pltpu.make_async_copy(src, dst, self.local.at[slot])


class Job:
    @staticmethod
    def buffers(source, shape):
        return []

    def forward(self):
        pass

    def inward(self):
        pass

    def across(self):
        pass

    def outward(self):
        pass


class Staged:
    def __init__(self, link, src, dst, buf):
        slot = link.local_slots(1)
        self.load = link.here(src, buf, slot)
        self.store = link.here(buf, dst, slot)

    def start(self):
        self.load.start()

    def turn(self):
        self.load.wait()
        self.store.start()

    def wait(self):
        self.store.wait()


class Gather(Job):
    def __init__(self, link, src, dst, bufs):
        self.link, self.src, self.dst = link, src, dst
        self.rows = src.shape[0]
        self.base = link.slots(max(4, link.groups - 1))
        self.keep = Staged(link, src, dst.at[link.shard], bufs[0])

    @staticmethod
    def buffers(source, shape):
        return [pltpu.VMEM(shape[1:], source.dtype)]

    def first(self):
        link = self.link
        peers = (1, 2) if link.groups == 4 else range(1, link.groups)
        return [
            link.remote(self.src, self.dst.at[link.shard], self.base + i, self.base + i, (link.rep, link.shard ^ p))
            for i, p in enumerate(peers)
        ]

    def second(self):
        link = self.link
        if link.groups != 4:
            return []
        cut = self.rows // 2
        parts = ((1, 2, pl.ds(0, cut)), (2, 1, pl.ds(cut, self.rows - cut)))
        out = []
        for i, (origin, to, rows) in enumerate(parts):
            ref = self.dst.at[link.shard ^ origin, rows]
            out.append(link.remote(ref, ref, self.base + 2 + i, self.base + 2 + i, (link.rep, link.shard ^ to)))
        return out

    def start(self):
        self.keep.start()
        for c in self.first():
            c.start()

    def forward(self):
        self.keep.turn()
        for c, d in zip(self.first(), self.second()):
            c.wait_recv()
            d.start()

    def finish(self):
        second = self.second()
        for c in self.first():
            if not second:
                c.wait_recv()
            c.wait_send()
        for c in second:
            c.wait()
        self.keep.wait()


class PairGather(Job):
    def __init__(self, link, src, dst, bufs):
        self.link, self.src, self.dst = link, src, dst
        rows = src.shape[0]
        outer = max(rows // PAIR_SHARE // 16, 1) * 16
        second = lax.rem(lax.div(link.rep, 2), 2)
        self.part = pl.ds(pl.multiple_of(second * outer, 16), rows - outer)
        self.alone = pl.ds(pl.multiple_of(second * (rows - outer), 16), outer)
        self.both = pl.ds(outer, rows - 2 * outer)
        self.base = link.slots(7)
        self.keep = Staged(link, src, dst.at[link.shard], bufs[0])

    @staticmethod
    def buffers(source, shape):
        return [pltpu.VMEM(shape[1:], source.dtype)]

    def step(self, src, dst, slot, to):
        return self.link.remote(src, dst, self.base + slot, self.base + slot, to)

    def near(self, bit):
        return (self.link.rep, self.link.shard ^ bit)

    def first(self):
        mine = self.dst.at[self.link.shard, self.part]
        return [self.step(self.src.at[self.part], mine, i, self.near(i + 1)) for i in range(2)]

    def second(self):
        one = self.dst.at[self.link.shard ^ 1, self.alone]
        two = self.dst.at[self.link.shard ^ 2, self.both]
        return [self.step(one, one, 2, self.near(2)), self.step(two, two, 3, self.near(1))]

    def third(self):
        out = []
        for i in range(3):
            ref = self.dst.at[self.link.shard ^ (i + 1), self.alone]
            out.append(self.step(ref, ref, 4 + i, self.link.pair()))
        return out

    def start(self):
        self.keep.start()
        for c in self.first():
            c.start()

    def forward(self):
        self.keep.turn()
        for c, d, e in zip(self.first(), self.second(), self.third()):
            c.wait_recv()
            d.start()
            e.start()

    def inward(self):
        self.second()[0].wait_recv()
        self.third()[2].start()

    def finish(self):
        for c in self.first():
            c.wait_send()
        one, two = self.second()
        one.wait_send()
        two.wait()
        for c in self.third():
            c.wait()
        self.keep.wait()


class ToClip(Job):
    def __init__(self, link, src, dst, bufs):
        self.link, self.src, self.dst = link, src, dst
        self.rows = src.shape[1]
        self.base = link.slots(link.half + 1)
        self.keep = link.local_slots(1)
        self.buf = bufs[0]

    @staticmethod
    def buffers(source, shape):
        return [pltpu.VMEM(source.shape[1:], source.dtype)]

    def copy(self, j):
        link = self.link
        core = lax.div(link.shard, link.half)
        to = (link.rep - link.core + core, link.core * link.half + j)
        mine = (core == link.core) & (link.core * link.half + j == link.shard)
        dst = self.dst.at[pl.ds(pl.multiple_of(link.shard * self.rows, self.rows), self.rows)]
        there = link.remote(self.src.at[j], dst, self.base + j, self.base + lax.rem(link.shard, link.half), to)
        return mine, there, link.here(self.src.at[j], self.buf, self.keep)

    def arrival(self, t):
        link = self.link
        source = link.core * link.half + t
        mine = (lax.div(link.shard, link.half) == link.core) & (source == link.shard)
        dst = self.dst.at[pl.ds(pl.multiple_of(source * self.rows, self.rows), self.rows)]
        there = link.remote(self.src.at[0], dst, self.base, self.base + t, link.sibling())
        return mine, there, link.here(self.buf, dst, self.keep)

    def to_sibling(self):
        link = self.link
        size = link.half * self.rows
        rows = pl.ds(pl.multiple_of(link.core * size, size), size)
        slot = self.base + link.half
        return link.remote(self.dst.at[rows], self.dst.at[rows], slot, slot, link.sibling())

    def start(self):
        for j in range(self.link.half):
            mine, there, here = self.copy(j)
            pl.when(mine)(here.start)
            pl.when(jnp.logical_not(mine))(there.start)

    def forward(self):
        for t in range(self.link.half):
            mine, there, here = self.arrival(t)

            @pl.when(mine)
            def _():
                self.copy(0)[2].wait()
                here.start()
                here.wait()

            pl.when(jnp.logical_not(mine))(there.wait_recv)
        self.to_sibling().start()

    def finish(self):
        self.to_sibling().wait()
        for j in range(self.link.half):
            mine, there, _ = self.copy(j)
            pl.when(jnp.logical_not(mine))(there.wait_send)


class FromClip(Job):
    def __init__(self, link, src, dst, bufs):
        self.link, self.src, self.dst = link, src, dst
        self.rows = dst.shape[1]
        self.base = link.slots(link.half)
        self.keep = link.local_slots(1)
        self.buf = bufs[0]

    @staticmethod
    def buffers(source, shape):
        return [pltpu.VMEM(shape[1:], source.dtype)]

    def copy(self, t):
        link = self.link
        core = lax.div(link.shard, link.half)
        shard = link.core * link.half + t
        mine = (core == link.core) & (shard == link.shard)
        clip = lax.rem(link.shard, link.half)
        src = self.src.at[pl.ds(t * self.rows, self.rows)]
        dst = self.dst.at[clip]
        there = link.remote(src, dst, self.base + t, self.base + clip, (link.rep - link.core + core, shard))
        return mine, there, link.here(src, self.buf, self.keep)

    def arrival(self, j):
        link = self.link
        mine = (lax.div(link.shard, link.half) == link.core) & (link.core * link.half + j == link.shard)
        src = self.src.at[pl.ds(0, self.rows)]
        there = link.remote(src, self.dst.at[j], self.base, self.base + j, link.sibling())
        return mine, there, link.here(self.buf, self.dst.at[j], self.keep)

    def start(self):
        for t in range(self.link.half):
            mine, there, here = self.copy(t)
            pl.when(mine)(here.start)
            pl.when(jnp.logical_not(mine))(there.start)

    def finish(self):
        for t in range(self.link.half):
            mine, there, here = self.copy(t)
            pl.when(jnp.logical_not(mine))(there.wait_send)
        for j in range(self.link.half):
            mine, there, here = self.arrival(j)

            @pl.when(mine)
            def _():
                self.copy(0)[2].wait()
                here.start()
                here.wait()

            pl.when(jnp.logical_not(mine))(there.wait_recv)


class Owners(Job):
    def __init__(self, link, src, dst, bufs):
        self.link, self.src, self.dst = link, src, dst
        self.base = link.slots(link.groups - 1)

    def copies(self):
        link = self.link
        return [
            link.remote(
                self.src.at[link.shard ^ p],
                self.dst.at[p - 1],
                self.base + p - 1,
                self.base + p - 1,
                (link.rep, link.shard ^ p),
            )
            for p in range(1, link.groups)
        ]

    def start(self):
        for c in self.copies():
            c.start()

    def finish(self):
        for c in self.copies():
            c.wait()


def add_low(a, b):
    return (a.astype(f32) + b.astype(f32)).astype(bf16)


class Reduce(Job):
    def __init__(self, link, src, dst, bufs):
        self.link, self.src, self.dst = link, src, dst
        self.base = link.slots(6)
        self.keep = link.local_slots(4)
        self.half = dst.shape[0] // 2
        self.pass_in, self.pass_sum, self.near, self.far, self.own = (bufs[2 * i : 2 * i + 2] for i in range(5))

    @staticmethod
    def buffers(source, shape):
        half = pltpu.VMEM((source.shape[1] // 2, source.shape[2]), source.dtype)
        return [half] * 10

    def block(self, i, part):
        rows = pl.ds(part * self.half, self.half)
        return self.src.at[self.link.shard ^ i, rows]

    def hops(self):
        link = self.link
        x, y = (link.rep, link.shard ^ 1), (link.rep, link.shard ^ 2)
        plan = (
            (self.block(3, 0), self.pass_in[0], x),
            (self.block(3, 1), self.pass_in[1], y),
            (self.block(1, 0), self.near[0], x),
            (self.block(2, 1), self.near[1], y),
        )
        return [link.remote(s, d, self.base + i, self.base + i, to) for i, (s, d, to) in enumerate(plan)]

    def later(self):
        link = self.link
        x, y = (link.rep, link.shard ^ 1), (link.rep, link.shard ^ 2)
        plan = zip(self.pass_sum, self.far, (y, x))
        return [link.remote(s, d, self.base + 4 + i, self.base + 4 + i, to) for i, (s, d, to) in enumerate(plan)]

    def loads(self):
        plan = (
            (self.block(2, 0), self.pass_sum[0]),
            (self.block(1, 1), self.pass_sum[1]),
            (self.block(0, 0), self.own[0]),
            (self.block(0, 1), self.own[1]),
        )
        return [self.link.here(s, d, self.keep + i) for i, (s, d) in enumerate(plan)]

    def store(self, part):
        rows = pl.ds(part * self.half, self.half)
        return self.link.here(self.own[part], self.dst.at[rows], self.keep + part)

    def start(self):
        for c in self.hops():
            c.start()
        for c in self.loads():
            c.start()

    def forward(self):
        hops, loads, later = self.hops(), self.loads(), self.later()
        for i in range(2):
            loads[i].wait()
            hops[i].wait_recv()
            self.pass_sum[i][...] = add_low(self.pass_sum[i][...], self.pass_in[i][...])
            later[i].start()

    def collect(self):
        hops, loads, later = self.hops(), self.loads(), self.later()
        for i in range(2):
            loads[2 + i].wait()
            hops[2 + i].wait_recv()
            later[i].wait_recv()
            total = self.own[i][...].astype(f32) + self.near[i][...].astype(f32) + self.far[i][...].astype(f32)
            self.own[i][...] = total.astype(bf16)
            self.store(i).start()
        for i in range(2):
            self.store(i).wait()

    def finish(self):
        self.collect()
        self.close()

    def close(self):
        for c in self.hops() + self.later():
            c.wait_send()


class Chain(Job):
    def __init__(self, link, src, dst, bufs):
        self.link, self.src, self.dst = link, src, dst
        self.own, self.one, self.two = bufs
        self.base = link.slots(4)
        self.keep = link.local_slots(2)

    @staticmethod
    def buffers(source, shape):
        return [pltpu.VMEM(shape[1:], source.dtype)] * 3

    def step(self, src, dst, slot, to):
        return self.link.remote(src, dst, self.base + slot, self.base + slot, to)

    def steps(self):
        link = self.link
        return (
            self.step(self.src, self.one, 0, link.inward()),
            self.step(self.own, self.two, 1, link.inward()),
            self.step(self.one, self.two, 2, link.outward()),
        )

    def share(self, ref):
        link = self.link
        place = self.dst.at[link.core]
        return self.step(ref, place, 3, link.sibling()), link.here(ref, place, self.keep + 1)

    def start(self):
        inner = self.link.inner()
        pl.when(inner)(self.link.here(self.src, self.own, self.keep).start)
        pl.when(jnp.logical_not(inner))(self.steps()[0].start)

    def add(self, a, b):
        return (a[...].astype(f32) + b[...].astype(f32)).astype(a.dtype)

    def sent(self):
        pl.when(jnp.logical_not(self.link.inner()))(self.steps()[0].wait_send)

    def inward(self):
        @pl.when(self.link.inner())
        def _():
            steps = self.steps()
            self.link.here(self.src, self.own, self.keep).wait()
            steps[0].wait_recv()
            self.own[...] = self.add(self.own, self.one)
            steps[1].start()

    def across(self):
        @pl.when(self.link.inner())
        def _():
            steps = self.steps()
            steps[1].wait_recv()
            self.one[...] = self.add(self.own, self.two)
            steps[2].start()
            for c in self.share(self.one):
                c.start()

    def outward(self):
        @pl.when(jnp.logical_not(self.link.inner()))
        def _():
            self.steps()[2].wait_recv()
            for c in self.share(self.two):
                c.start()

    def finish(self):
        swap, here = self.share(self.one)
        swap.wait()
        here.wait()
        inner = self.link.inner()

        @pl.when(inner)
        def _():
            self.steps()[1].wait_send()
            self.steps()[2].wait_send()


def chain_steps(chains):
    lists = []
    for i in range(len(chains) + 1):
        lists.append(
            [step for c in chains[i : i + 1] for step in (c.inward, c.sent)]
            + [c.start for c in chains[i + 1 : i + 2]]
            + [c.across for c in chains[max(i - 1, 0) : i]]
        )
    return lists


def gather_steps(gathers):
    lists = []
    for i in range(len(gathers) + 2):
        lists.append(
            [c.start for c in gathers[i : i + 1]]
            + [c.forward for c in gathers[max(i - 1, 0) : i]]
            + [c.inward for c in gathers[max(i - 2, 0) : max(i - 1, 0)]]
        )
    return lists


def run(steps):
    for step in steps:
        step()


def split_gathers(bound):
    gathers = [job for job in bound if isinstance(job, (Gather, PairGather))]
    return gathers, [job for job in bound if job not in gathers]


class Jobs:
    def __init__(self, *jobs):
        self.jobs = [(job + (None,))[:4] for job in jobs]
        self.pairs = any(job[0] is PairGather for job in jobs)
        self.bufs = [kind.buffers(a, shape) for kind, a, shape, _ in self.jobs]

    def sources(self):
        return [a for _, a, _, _ in self.jobs]

    def in_specs(self):
        return [pl.BlockSpec(memory_space=pl.ANY)] * len(self.jobs)

    def out_shapes(self):
        return [jax.ShapeDtypeStruct(shape, a.dtype) for _, a, shape, _ in self.jobs]

    def scratch(self, extra=0):
        groups = lax.axis_size("shard")
        remote = len(self.jobs) * max(7, groups) + extra
        return [b for bufs in self.bufs for b in bufs] + [
            pltpu.SemaphoreType.DMA((remote,)),
            pltpu.SemaphoreType.DMA((remote,)),
            pltpu.SemaphoreType.DMA((4 * len(self.jobs) + extra + 1,)),
        ]

    def bind(self, rest, srcs, dsts):
        rest = list(rest)
        bufs = []
        for shapes in self.bufs:
            bufs.append([rest.pop(0) for _ in shapes])
        link = Link(rest[:3])
        bound = [
            kind(link, view(a) if view else a, b, c) for (kind, _, _, view), a, b, c in zip(self.jobs, srcs, dsts, bufs)
        ]
        return link, bound, rest[3:]


def comm_params(number, limit=60):
    return pltpu.CompilerParams(
        vmem_limit_bytes=limit * 2**20, collective_id=number, has_side_effects=True
    )


def exchange_call(jobs, sibling, number, name):
    count = len(jobs.jobs)

    def kernel(*refs):
        srcs, mine = refs[:count], refs[count]
        dsts, other = refs[count + 1 : 2 * count + 1], refs[2 * count + 1]
        link, bound, _ = jobs.bind(refs[2 * count + 2 :], srcs, dsts)
        slot = link.slots(1)
        swap = link.remote(mine, other, slot, slot, link.sibling())
        link.meet_plane(jobs.pairs)
        swap.start()
        gathers, others = split_gathers(bound)
        steps = gather_steps(gathers)
        run([job.start for job in others] + steps[0])
        for i, some in enumerate(steps[1:]):
            if i == 1:
                run([job.forward for job in others])
            run(some)
        run([job.finish for job in bound])
        swap.wait()

    return pl.pallas_call(
        kernel,
        in_specs=jobs.in_specs() + [pl.BlockSpec(memory_space=pl.ANY)],
        out_specs=[pl.BlockSpec(memory_space=pl.ANY)] * (count + 1),
        out_shape=jobs.out_shapes() + [jax.ShapeDtypeStruct(sibling.shape, sibling.dtype)],
        scratch_shapes=jobs.scratch(1),
        compiler_params=comm_params(number),
        name=name,
    )(*jobs.sources(), sibling)


def pack_kernel(*refs, count):
    out_ref = refs[-1]
    lens_ref = refs[count]
    out_ref[...] = jnp.zeros_like(out_ref)
    row = 0
    for ref in refs[:count]:
        size = refs[0].shape[0]
        for part in range(ref.shape[0] // size):
            value = ref[part * size : (part + 1) * size].astype(f32)
            out_ref[row : row + 1, :size] = value.reshape(1, size)
            row += 1
        if row == LENGTHS.start:
            lane = lax.broadcasted_iota(jnp.int32, (1, out_ref.shape[1]), 1)
            value = jnp.zeros(lane.shape, f32)
            for clip in range(lens_ref.shape[0]):
                value = jnp.where(lane == clip, lens_ref[clip].astype(f32), value)
            out_ref[row : row + 1, :] = value
            row += 1


def pack_call(vectors, lengths):
    vmem = pl.BlockSpec(memory_space=pltpu.VMEM)
    lanes = pl.cdiv(vectors[0].shape[0], 128) * 128
    return pl.pallas_call(
        functools.partial(pack_kernel, count=len(vectors)),
        in_specs=[vmem] * len(vectors) + [pl.BlockSpec(memory_space=pltpu.SMEM)],
        out_specs=vmem,
        out_shape=jax.ShapeDtypeStruct((16, lanes), f32),
        name="pack",
    )(*vectors, lengths)


def first_kernel(*refs, jobs, size):
    count = len(jobs.jobs)
    srcs, mine = refs[:count], refs[count]
    *results, vec_ref = refs[count + 1 : count + 6]
    dsts, other = refs[count + 6 : 2 * count + 6], refs[2 * count + 6]
    x, small, weight, bias, sems, h_ref, *heads = refs[2 * count + 7 : 2 * count + 16]
    link, bound, _ = jobs.bind(refs[2 * count + 16 :], srcs, dsts)
    tokens, smalls, *gathers = bound
    slot = link.slots(1)
    swap = link.remote(mine, other, slot, slot, link.sibling())
    n = x.shape[0]
    width = weight.shape[2]
    part = size // 2

    def load(src, dst, i):
        return pltpu.make_async_copy(src, dst, sems.at[i])

    first_store = 1 + small.shape[0]
    stores = [load(a, b, first_store + i) for i, (a, b) in enumerate(zip([h_ref] + heads, results))]
    link.meet_plane(jobs.pairs)
    steps = gather_steps(gathers)
    swap.start()
    run([smalls.start, tokens.start] + steps[0])
    run([smalls.forward, smalls.finish])
    load(dsts[1], small, 0).start()
    run(steps[1])
    load(dsts[1], small, 0).wait()
    bias[...] = jnp.zeros_like(bias)
    for s in range(small.shape[0]):
        vec_ref[:, s * size : (s + 1) * size] = small[s][:, :size]
        for row, first in ((QBIAS, 0), (VBIAS, 2 * width)):
            value = jnp.where(link.core == 0, small[s, row, :part], small[s, row, part:size])
            bias[:, first + s * part : first + (s + 1) * part] = value
    tokens.forward()
    run(steps[2])
    tokens.finish()
    load(dsts[0], x, 0).start()
    load(dsts[0], x, 0).wait()

    def norm(i, carry):
        rows = pl.ds(pl.multiple_of(i * ROWS, ROWS), ROWS)
        xhat, _ = standardize(x[rows, :].astype(f32))
        h_ref[rows, :] = (xhat * vec_ref[GAIN1] + vec_ref[SHIFT1]).astype(bf16)
        return carry

    lax.fori_loop(0, n // ROWS, norm, 0)
    stores[0].start()
    for ref in heads:
        ref[:, width:] = jnp.zeros((n, ref.shape[1] - width), bf16)
    for i, (gather, ref) in enumerate(zip(gathers, heads)):
        run(steps[3 + i] if 3 + i < len(steps) else [])
        gather.finish()
        for s in range(small.shape[0]):
            load(dsts[2 + i].at[s], weight.at[i, pl.ds(s * size, size)], 1 + s).start()
        for s in range(small.shape[0]):
            load(dsts[2 + i].at[s], weight.at[i, pl.ds(s * size, size)], 1 + s).wait()

        def project(j, carry):
            rows = pl.ds(pl.multiple_of(j * ROWS, ROWS), ROWS)
            z = dot(h_ref[rows, :], weight[i]) + bias[:, i * width : (i + 1) * width]
            ref[rows, :width] = z.astype(bf16)
            return carry

        lax.fori_loop(0, n // ROWS, project, 0)
        stores[1 + i].start()
    swap.wait()
    for c in stores:
        c.wait()


def first_call(jobs, small, wide, number):
    (n, d), groups = jobs.jobs[0][2], lax.axis_size("shard")
    width = jobs.jobs[2][2][2]
    vmem = pl.BlockSpec(memory_space=pltpu.VMEM)
    hbm = pl.BlockSpec(memory_space=pl.ANY)
    head = jax.ShapeDtypeStruct((n, wide), bf16)
    return pl.pallas_call(
        functools.partial(first_kernel, jobs=jobs, size=d // groups),
        in_specs=jobs.in_specs() + [hbm],
        out_specs=[hbm] * 4 + [vmem] + jobs.in_specs() + [hbm],
        out_shape=[jax.ShapeDtypeStruct((n, d), bf16), head, head, head, jax.ShapeDtypeStruct((16, d), f32)]
        + jobs.out_shapes()
        + [jax.ShapeDtypeStruct(small.shape, small.dtype)],
        scratch_shapes=[
            pltpu.VMEM((n, d), bf16),
            pltpu.VMEM((groups,) + small.shape, f32),
            pltpu.VMEM((3, d, width), bf16),
            pltpu.VMEM((1, 3 * width), f32),
            pltpu.SemaphoreType.DMA((5 + groups,)),
            pltpu.VMEM((n, d), bf16),
        ]
        + [pltpu.VMEM((n, wide), bf16)] * 3
        + jobs.scratch(1),
        compiler_params=comm_params(number),
        cost_estimate=cost(6 * n * d * width, 12 * n * d),
        name="first",
    )(*jobs.sources(), small)


def head_window(h):
    start = h * HEAD
    base = (start // 128) * 128
    off = start - base
    lane = lax.broadcasted_iota(jnp.int32, (1, WIN), 1)
    keep = jnp.where((lane >= off) & (lane < off + HEAD), 1.0, 0.0)
    return pl.ds(pl.multiple_of(base, 128), WIN), keep, lane


def put3(x, lane, first, value):
    hi = value.astype(bf16).astype(f32)
    rest = value - hi
    mid = rest.astype(bf16).astype(f32)
    low = rest - mid
    return jnp.where(
        lane == first,
        hi,
        jnp.where(lane == first + 1, mid, jnp.where(lane == first + 2, low, x)),
    )


def key_extra(rows, length):
    lane = lax.broadcasted_iota(jnp.int32, (rows, WIN), 1)
    row = lax.broadcasted_iota(jnp.int32, (rows, WIN), 0)
    dead = jnp.where(row >= length, DEAD, 0.0)
    minus = jnp.where((lane > AUG) & (lane <= AUG + 3), -1.0, 0.0)
    return jnp.where(lane == AUG, dead, minus).astype(bf16)


def attn_fwd_kernel(*refs, bq, jobs):
    count = len(jobs.jobs)
    len_ref, *sources = refs[:4]
    o_ref, lse_ref = refs[4 + count : 6 + count]
    acc, kx, q_ref, k_ref, v_ref = refs[6 + 2 * count : 11 + 2 * count]
    link, bound, _ = jobs.bind(refs[11 + 2 * count :], refs[4 : 4 + count], refs[6 + count : 6 + 2 * count])
    h = pl.program_id(0)
    heads = pl.num_programs(0)
    n = q_ref.shape[0]
    width = o_ref.shape[1]

    gathers, others = split_gathers(bound)
    steps = gather_steps(gathers)

    keep = link.local_slots(3)
    loads = [link.here(a, b, keep + i) for i, (a, b) in enumerate(zip(sources, (q_ref, k_ref, v_ref)))]

    @pl.when(h == 0)
    def _():
        for c in loads:
            c.start()
        link.meet_plane(jobs.pairs)
        run([job.start for job in others] + steps[0])
        acc[...] = jnp.zeros_like(acc)
        lse_ref[...] = jnp.zeros_like(lse_ref)
        kx[...] = key_extra(n, len_ref[0])
        for c in loads:
            c.wait()

    for number, some in zip((2, 4, 6, 7), steps[1:]):

        @pl.when(h == number * heads // 8)
        def _():
            run(some)

    win, keep, lane = head_window(h)
    low = keep.astype(bf16)
    q_one = jnp.where(lane == AUG, 1.0, 0.0).astype(bf16)
    v_one = jnp.where((lane >= AUG) & (lane < AUG + 3), 1.0, 0.0).astype(bf16)
    k = k_ref[:, win] * low + kx[...]
    v = v_ref[:, win] * low + v_one
    for i in range(n // bq):
        rows = slice(i * bq, (i + 1) * bq)
        s = dot_nt(q_ref[rows, win] * low + q_one, k)
        peak = jnp.max(s, axis=-1, keepdims=True)
        p = jnp.exp2((s - peak) * SCALE2).astype(bf16)
        o = dot(p, v)
        total = o[:, AUG : AUG + 1]
        acc[rows, win] += o * (keep * (1.0 / total))
        here = lax.broadcasted_iota(jnp.int32, (bq, 128), 1) == h
        lse = peak + jnp.log(total) * (1.0 / SCALE)
        lse_ref[rows, :] = jnp.where(here, lse, lse_ref[rows, :])

    @pl.when(h == heads - 1)
    def _():
        o_ref[:, :width] = acc[:, :width].astype(bf16)
        for some in steps[5:]:
            run(some)
        run([job.finish for job in bound])


def attn_fwd_call(length, q, k, v, width, heads, jobs, number):
    n, wide = q.shape
    return pl.pallas_call(
        functools.partial(attn_fwd_kernel, bq=256, jobs=jobs),
        grid=(heads,),
        in_specs=[pl.BlockSpec(memory_space=pltpu.SMEM)] + [pl.BlockSpec(memory_space=pl.ANY)] * 3 + jobs.in_specs(),
        out_specs=[whole((n, width)), whole((n, 128))] + jobs.in_specs(),
        out_shape=[jax.ShapeDtypeStruct((n, width), bf16), jax.ShapeDtypeStruct((n, 128), f32)] + jobs.out_shapes(),
        scratch_shapes=[pltpu.VMEM((n, wide), f32), pltpu.VMEM((n, WIN), bf16)]
        + [pltpu.VMEM((n, wide), bf16)] * 3
        + jobs.scratch(3),
        compiler_params=comm_params(number),
        cost_estimate=cost(4 * n * n * WIN * heads, 8 * n * wide),
        name="attend",
    )(length, q, k, v, *jobs.sources())


def attn_bwd_kernel(*refs, bk, jobs):
    count = len(jobs.jobs)
    len_ref, q_ref, k_ref, v_ref, o_ref, do_ref, lse_ref = refs[:7]
    g_ref, sum_ref = refs[7 + count : 9 + count]
    dq, dk, dv, part, qa, da, kx = refs[9 + 2 * count : 16 + 2 * count]
    link, bound, _ = jobs.bind(refs[16 + 2 * count :], refs[7 : 7 + count], refs[9 + count : 9 + 2 * count])
    chains = [job for job in bound if isinstance(job, Chain)]
    h = pl.program_id(0)
    n = q_ref.shape[0]

    @pl.when(h == 0)
    def _():
        if chains:
            link.meet_all()
        else:
            link.meet_plane(jobs.pairs)
        for job in bound:
            if job not in chains[1:]:
                job.start()
        for ref in (dq, dk, dv):
            ref[...] = jnp.zeros_like(ref)
        kx[...] = key_extra(n, len_ref[0])

    heads = pl.num_programs(0)

    def at_head(number, steps):
        @pl.when(h == number)
        def _():
            for step in steps:
                step()

    steps = chain_steps(chains) if chains else []
    for number, some in zip((1, 2, 4, 6, 7), steps):
        at_head(number, some)
    at_head(heads - 3, [job.forward for job in bound])

    win, keep, lane = head_window(h)
    low = keep.astype(bf16)
    v_one = jnp.where((lane >= AUG) & (lane < AUG + 3), 1.0, 0.0).astype(bf16)
    for i in range(n // ROWS):
        rows = slice(i * ROWS, (i + 1) * ROWS)
        here = lax.broadcasted_iota(jnp.int32, (ROWS, 128), 1) == h
        lse = jnp.sum(jnp.where(here, lse_ref[rows, :], 0.0), axis=-1, keepdims=True)
        q = q_ref[rows, win].astype(f32) * keep
        qa[rows, :] = jnp.where(lane == AUG, 1.0, put3(q, lane, AUG + 1, lse)).astype(bf16)
        d = do_ref[rows, win].astype(f32) * keep
        delta = jnp.sum(d * o_ref[rows, win].astype(f32), axis=-1, keepdims=True)
        da[rows, :] = put3(d, lane, AUG, -delta).astype(bf16)
    for i in range(n // bk):
        rows = slice(i * bk, (i + 1) * bk)
        k = k_ref[rows, win] * low + kx[rows, :]
        v = v_ref[rows, win] * low + v_one
        p = jnp.exp2(dot_nt(k, qa[...]) * SCALE2)
        ds = (p * dot_nt(v, da[...])).astype(bf16)
        dv[rows, win] += dot(p.astype(bf16), da[...]) * keep
        dk[rows, win] += dot(ds, qa[...]) * keep
        new = dot_tn(ds, k)
        part[...] = new if i == 0 else part[...] + new
    dq[:, win] += part[...] * keep

    @pl.when(h == heads - 1)
    def _():
        for i, (ref, factor) in enumerate(((dq, SCALE), (dk, SCALE), (dv, 1.0))):
            value = (ref[:, : g_ref.shape[1] // 3] * factor).astype(bf16)
            cols = slice(i * value.shape[1], (i + 1) * value.shape[1])
            g_ref[:, cols] = value
            sum_ref[:, cols] = jnp.sum(value.astype(f32), axis=0, keepdims=True)
        for some in steps[5:]:
            run(some)
        for job in bound:
            job.outward()
        for job in bound:
            job.finish()


def attn_bwd_call(length, q, k, v, o, do, lse, width, heads, jobs, number):
    n, wide = q.shape
    return pl.pallas_call(
        functools.partial(attn_bwd_kernel, bk=256, jobs=jobs),
        grid=(heads,),
        in_specs=[pl.BlockSpec(memory_space=pltpu.SMEM)]
        + [once((n, wide))] * 5
        + [once((n, 128))]
        + jobs.in_specs(),
        out_specs=[once((n, 3 * width)), whole((1, 3 * width))] + jobs.in_specs(),
        out_shape=[
            jax.ShapeDtypeStruct((n, 3 * width), bf16),
            jax.ShapeDtypeStruct((1, 3 * width), f32),
        ]
        + jobs.out_shapes(),
        scratch_shapes=[pltpu.VMEM((n, wide), f32)] * 3
        + [pltpu.VMEM((n, WIN), f32)]
        + [pltpu.VMEM((n, WIN), bf16)] * 3
        + jobs.scratch(),
        compiler_params=comm_params(number),
        cost_estimate=cost(10 * n * n * WIN * heads, 20 * n * wide),
        name="attend_back",
    )(length, q, k, v, o, do, lse, *jobs.sources())


def middle_kernel(*refs, jobs):
    count = len(jobs.jobs)
    *sources, vec_ref = refs[:4]
    results = refs[4 + count : 7 + count]
    mid_ref, h_ref, owide_ref, mine, other, o_ref, w_ref, x_ref = refs[7 + 2 * count : 15 + 2 * count]
    link, bound, _ = jobs.bind(refs[15 + 2 * count :], refs[4 : 4 + count], refs[7 + count : 7 + 2 * count])
    n = x_ref.shape[0]
    width = o_ref.shape[1]
    base = link.slots(n // ROWS)
    keep = link.local_slots(6)
    loads = [link.here(a, b, keep + 3 + i) for i, (a, b) in enumerate(zip(sources, (o_ref, w_ref, x_ref)))]
    for c in loads:
        c.start()
    stores = [link.here(a, b, keep + i) for i, (a, b) in enumerate(zip((mid_ref, h_ref, owide_ref), results))]
    link.meet_plane(jobs.pairs)
    for job in bound:
        job.start()

    def swap(i):
        rows = pl.ds(pl.multiple_of(i * ROWS, ROWS), ROWS)
        return rows, link.remote(mine.at[rows], other.at[rows], base + i, base + i, link.sibling())

    def project(i, carry):
        rows, copy = swap(i)
        mine[rows, :] = dot(o_ref[rows, :], w_ref[...]).astype(bf16)
        copy.start()
        return carry

    def norm(i, carry):
        rows, copy = swap(i)
        copy.wait_recv()
        mid = x_ref[rows, :].astype(f32) + (
            mine[rows, :].astype(f32) + other[rows, :].astype(f32) + vec_ref[OBIAS]
        )
        mid_ref[rows, :] = mid
        xhat, _ = standardize(mid)
        h_ref[rows, :] = (xhat * vec_ref[GAIN2] + vec_ref[SHIFT2]).astype(bf16)
        return carry

    for c in loads:
        c.wait()
    lax.fori_loop(0, n // ROWS, project, 0)
    owide_ref[:, :width] = o_ref[...]
    owide_ref[:, width:] = jnp.zeros((n, owide_ref.shape[1] - width), bf16)
    stores[2].start()
    lax.fori_loop(0, n // ROWS, norm, 0)
    stores[0].start()
    stores[1].start()
    for i in range(n // ROWS):
        swap(i)[1].wait_send()
    for job in bound:
        job.forward()
    for job in bound:
        job.inward()
    for job in bound:
        job.finish()
    for c in stores:
        c.wait()


def middle_call(o, w, x, vec, wide, jobs, number):
    n, d = x.shape
    vmem = pl.BlockSpec(memory_space=pltpu.VMEM)
    return pl.pallas_call(
        functools.partial(middle_kernel, jobs=jobs),
        in_specs=[pl.BlockSpec(memory_space=pl.ANY)] * 3 + [vmem] + jobs.in_specs(),
        out_specs=[pl.BlockSpec(memory_space=pl.ANY)] * 3 + jobs.in_specs(),
        out_shape=[
            jax.ShapeDtypeStruct((n, d), f32),
            jax.ShapeDtypeStruct((n, d), bf16),
            jax.ShapeDtypeStruct((n, wide), bf16),
        ]
        + jobs.out_shapes(),
        scratch_shapes=[pltpu.VMEM((n, d), f32), pltpu.VMEM((n, d), bf16), pltpu.VMEM((n, wide), bf16)]
        + [pltpu.VMEM((n, d), bf16)] * 2
        + [pltpu.VMEM(o.shape, bf16), pltpu.VMEM(w.shape, bf16), pltpu.VMEM((n, d), bf16)]
        + jobs.scratch(n // ROWS),
        compiler_params=comm_params(number),
        cost_estimate=cost(2 * n * w.size, 14 * n * d),
        name="middle",
    )(o, w, x, vec, *jobs.sources())


def ffn_kernel(*refs, chained, last, mc, jobs):
    count = len(jobs.jobs)
    h_any, dz_any, up_ref, ub_ref, dn_ref = refs[:5]
    refs = refs[5:]
    if chained:
        old_out, old_dh = refs[:2]
        refs = refs[2:]
    srcs, refs = refs[:count], refs[count:]
    out_ref, dh_ref, dup_ref, ddn_ref, dub_ref = refs[:5]
    dsts, refs = refs[5 : 5 + count], refs[5 + count :]
    ht, act, grad = refs[:3]
    acc, dh, h_ref, dz_ref = refs[3:7]
    link, bound, (sem,) = jobs.bind(refs[7:], srcs, dsts)
    fetch = [pltpu.make_async_copy(a, b, sem.at[4 + i]) for i, (a, b) in enumerate(((h_any, h_ref), (dz_any, dz_ref)))]
    loads = stores = []
    if chained:
        pairs = ((old_out, acc), (old_dh, dh))
        loads = [pltpu.make_async_copy(a, b, sem.at[i]) for i, (a, b) in enumerate(pairs)]
    if not last:
        pairs = ((acc, out_ref), (dh, dh_ref))
        stores = [pltpu.make_async_copy(a, b, sem.at[2 + i]) for i, (a, b) in enumerate(pairs)]
    gathers, others = split_gathers(bound)
    steps = gather_steps(gathers)
    t = pl.program_id(0)
    tiles = pl.num_programs(0)
    n = h_any.shape[0]

    @pl.when(t == 0)
    def _():
        for c in fetch:
            c.start()
        link.meet_plane(jobs.pairs)
        run([job.start for job in others] + steps[0])
        if chained:
            for c in loads:
                c.start()
            fetch[0].wait()
            ht[...] = h_ref[...].T
        else:
            acc[...] = jnp.zeros_like(acc)
            dh[...] = jnp.zeros_like(dh)
            fetch[0].wait()
            ht[...] = h_ref[...].T
        fetch[1].wait()

    def at_tile(number, some):
        if some:

            @pl.when(t == number)
            def _():
                run(some)

    at_tile(tiles - 1, [job.forward for job in others])

    def step(i, carry):
        rows = pl.ds(pl.multiple_of(i * mc, mc), mc)
        g, slope = gelu_pair(dot(h_ref[rows, :], up_ref[...]) + ub_ref[...])
        g = g.astype(bf16)
        da = (dot_nt(dz_ref[rows, :], dn_ref[...]) * slope).astype(bf16)
        act[rows, :] = g
        grad[rows, :] = da
        if chained:

            @pl.when((t == 0) & (i == 0))
            def _():
                for c in loads:
                    c.wait()

        acc[rows, :] += dot(g, dn_ref[...])
        dh[rows, :] += dot_nt(da, up_ref[...])
        return carry

    lax.fori_loop(0, n // mc, step, 0)

    at_tile(0, steps[1] if gathers else [])
    dub_ref[...] = jnp.sum(grad[...].astype(f32), axis=0, keepdims=True)
    dup_ref[...] = dot(ht[...], grad[...]).astype(bf16)
    at_tile(tiles - 1, steps[2] if gathers else [])
    ddn_ref[...] = dot_tn(act[...], dz_ref[...]).astype(bf16)

    @pl.when(t == tiles - 1)
    def _():
        if last:
            out_ref[...] = acc[...].astype(out_ref.dtype)
            dh_ref[...] = dh[...].astype(dh_ref.dtype)
        for c in stores:
            c.start()
        for some in steps[3:]:
            run(some)
        run([job.finish for job in bound])
        for c in stores:
            c.wait()


def ffn_call(h, dz, up, bias, down, old, last, jobs, number, name):
    n, d = h.shape
    hidden = up.shape[1]
    bt = FFN_TILE
    out = jax.ShapeDtypeStruct((n, d), bf16 if last else f32)
    chained = old is not None
    kept = once((n, d))
    return pl.pallas_call(
        functools.partial(ffn_kernel, chained=chained, last=last, mc=FFN_ROWS, jobs=jobs),
        grid=(hidden // bt,),
        in_specs=[
            pl.BlockSpec(memory_space=pl.ANY),
            pl.BlockSpec(memory_space=pl.ANY),
            pl.BlockSpec((d, bt), lambda t: (0, t)),
            pl.BlockSpec((1, bt), lambda t: (0, t)),
            pl.BlockSpec((bt, d), lambda t: (t, 0)),
        ]
        + ([pl.BlockSpec(memory_space=pl.ANY)] * 2 if chained else [])
        + jobs.in_specs(),
        out_specs=([kept] * 2 if last else [pl.BlockSpec(memory_space=pl.ANY)] * 2)
        + [
            pl.BlockSpec((d, bt), lambda t: (0, t)),
            pl.BlockSpec((bt, d), lambda t: (t, 0)),
            pl.BlockSpec((1, bt), lambda t: (0, t)),
        ]
        + jobs.in_specs(),
        out_shape=[
            out,
            out,
            jax.ShapeDtypeStruct((d, hidden), bf16),
            jax.ShapeDtypeStruct((hidden, d), bf16),
            jax.ShapeDtypeStruct((1, hidden), f32),
        ]
        + jobs.out_shapes(),
        scratch_shapes=[pltpu.VMEM((d, n), bf16)]
        + [pltpu.VMEM((n, bt), bf16)] * 2
        + [pltpu.VMEM((n, d), f32)] * 2
        + [pltpu.VMEM((n, d), bf16)] * 2
        + jobs.scratch()
        + [pltpu.SemaphoreType.DMA((6,))],
        compiler_params=comm_params(number),
        cost_estimate=cost(12 * n * d * hidden, 8 * d * hidden + 12 * n * d),
        name=name,
    )(h, dz, up, bias, down, *(old if chained else ()), *jobs.sources())


def second_back_kernel(*refs, jobs):
    count = len(jobs.jobs)
    mid_ref, dh_ref, out_ref, dz_ref, vec_ref, w_ref, o_ref, dh_any, out_any = refs[:9]
    dmid_ref, do_ref, dw_ref, sums_ref, layer_ref = refs[9 + count : 14 + count]
    acc, dh_other, out_other = refs[14 + 2 * count : 17 + 2 * count]
    link, bound, _ = jobs.bind(refs[17 + 2 * count :], refs[9 : 9 + count], refs[14 + count : 14 + 2 * count])
    chains = [job for job in bound if isinstance(job, Chain)]
    others = [job for job in bound if job not in chains]
    steps = chain_steps(chains) if chains else []
    i = pl.program_id(0)
    blocks = pl.num_programs(0)
    half = layer_ref.shape[0] // ROWS
    width = w_ref.shape[0]
    base = link.slots(3 * half)

    def swap_dh(j):
        rows = pl.ds(pl.multiple_of(j * ROWS, ROWS), ROWS)
        return link.remote(dh_any.at[rows], dh_other.at[rows], base + j, base + j, link.sibling())

    def swap_out(j):
        src = pl.ds(pl.multiple_of(((1 - link.core) * half + j) * ROWS, ROWS), ROWS)
        dst = pl.ds(pl.multiple_of(j * ROWS, ROWS), ROWS)
        slot = base + 2 * half + j
        return link.remote(out_any.at[src], out_other.at[dst], slot, slot, link.sibling())

    @pl.when(i == 0)
    def _():
        if chains:
            link.meet_all()
        else:
            link.meet_plane()
        for j in range(2 * half):
            swap_dh(j).start()
        for j in range(half):
            swap_out(j).start()
        run([job.start for job in others + chains[:1]])
        acc[...] = jnp.zeros_like(acc)
        sums_ref[...] = jnp.zeros_like(sums_ref)

    for number, some in zip((2, 4), steps):

        @pl.when(i == number)
        def _():
            run(some)

    @pl.when(i == blocks - 1)
    def _():
        run([job.forward for job in others])

    mid = mid_ref[...]
    xhat, inv = standardize(mid)
    swap_dh(i).wait_recv()
    rows = pl.ds(pl.multiple_of(i * ROWS, ROWS), ROWS)
    dh = dh_ref[...].astype(f32) + dh_other[rows, :].astype(f32)
    dx = dh * vec_ref[GAIN2]
    dz = dz_ref[...].astype(f32)
    dmid = dz + inv * (
        dx - jnp.mean(dx, axis=-1, keepdims=True) - xhat * jnp.mean(dx * xhat, axis=-1, keepdims=True)
    )
    dmid_ref[...] = dmid
    dy = dmid.astype(bf16)
    do_ref[:, :width] = dot_nt(dy, w_ref[...]).astype(bf16)
    do_ref[:, width:] = jnp.zeros((do_ref.shape[0], do_ref.shape[1] - width), bf16)
    acc[...] += dot_tn(o_ref[...], dy)
    for row, value in enumerate((dh * xhat, dh, dy.astype(f32), dz)):
        sums_ref[row : row + 1, :] += jnp.sum(value, axis=0, keepdims=True)

    j = i - link.core * half

    @pl.when((j >= 0) & (j < half))
    def _():
        swap_out(j).wait_recv()
        here = pl.ds(pl.multiple_of(j * ROWS, ROWS), ROWS)
        layer_ref[here, :] = (
            mid + (out_ref[...].astype(f32) + out_other[here, :].astype(f32) + vec_ref[DBIAS])
        ).astype(bf16)

    @pl.when(i == blocks - 1)
    def _():
        dw_ref[...] = acc[...].astype(bf16)
        for j in range(2 * half):
            swap_dh(j).wait_send()
        for j in range(half):
            swap_out(j).wait_send()
        for some in steps[2:]:
            run(some)
        run([job.outward for job in chains] + [job.finish for job in others + chains])


def second_back_call(mid, dh, out, dz, vec, w, o, wide, jobs, number):
    n, d = mid.shape
    width = w.shape[0]
    block = row_block(ROWS, d)
    count = 3 * n // ROWS // 2
    return pl.pallas_call(
        functools.partial(second_back_kernel, jobs=jobs),
        grid=(n // ROWS,),
        in_specs=[block] * 4
        + [whole(vec.shape), whole(w.shape), row_block(ROWS, width)]
        + [pl.BlockSpec(memory_space=pl.ANY)] * 2
        + jobs.in_specs(),
        out_specs=[block, row_block(ROWS, wide), whole((width, d)), whole((8, d)), whole((n // 2, d))]
        + jobs.in_specs(),
        out_shape=[
            jax.ShapeDtypeStruct((n, d), f32),
            jax.ShapeDtypeStruct((n, wide), bf16),
            jax.ShapeDtypeStruct((width, d), bf16),
            jax.ShapeDtypeStruct((8, d), f32),
            jax.ShapeDtypeStruct((n // 2, d), bf16),
        ]
        + jobs.out_shapes(),
        scratch_shapes=[
            pltpu.VMEM((width, d), f32),
            pltpu.VMEM((n, d), bf16),
            pltpu.VMEM((n // 2, d), bf16),
        ]
        + jobs.scratch(count),
        compiler_params=comm_params(number),
        cost_estimate=cost(4 * n * d * width, 14 * n * d),
        name="second_back",
    )(mid, dh, out, dz, vec, w, o, dh, out, *jobs.sources())


def dw_kernel(h_ref, g_ref, out_ref):
    out_ref[...] = dot_tn(h_ref[...], g_ref[...]).astype(bf16)


def dw_call(h, grads):
    n, d = h.shape
    cols = grads.shape[1]
    return pl.pallas_call(
        dw_kernel,
        grid=(d // 256,),
        in_specs=[pl.BlockSpec((n, 256), lambda i: (0, i)), whole((n, cols))],
        out_specs=row_block(256, cols),
        out_shape=jax.ShapeDtypeStruct((d, cols), bf16),
        compiler_params=params(),
        cost_estimate=cost(2 * n * d * cols, 2 * (n * d + n * cols + d * cols)),
        name="project_grad",
    )(h, grads)


def first_back_kernel(*refs, jobs):
    count = len(jobs.jobs)
    g_ref, w_ref, vec_ref, x_any, dmid_any = refs[:5]
    dx_ref, sums_ref = refs[5 + count : 7 + count]
    x, dmid, mine, other = refs[7 + 2 * count : 11 + 2 * count]
    link, bound, _ = jobs.bind(refs[11 + 2 * count :], refs[5 : 5 + count], refs[7 + count : 7 + 2 * count])
    size = dx_ref.shape[0]
    half = size // ROWS
    base = link.slots(half)
    keep = link.local_slots(2)
    own = pl.ds(pl.multiple_of(link.core * size, size), size)
    loads = [link.here(x_any.at[own], x, keep), link.here(dmid_any.at[own], dmid, keep + 1)]
    for c in loads:
        c.start()
    link.meet_plane(jobs.pairs)
    for job in bound:
        job.start()

    def product(j):
        rows = pl.ds(pl.multiple_of(j * ROWS, ROWS), ROWS)
        return dot_nt(g_ref[rows, :], w_ref[...])

    def swap(j):
        rows = pl.ds(pl.multiple_of(j * ROWS, ROWS), ROWS)
        return rows, link.remote(mine.at[rows], other.at[rows], base + j, base + j, link.sibling())

    def send(j, carry):
        rows, copy = swap(j)
        mine[rows, :] = product((1 - link.core) * half + j).astype(bf16)
        copy.start()
        return carry

    def norm(j, carry):
        rows, copy = swap(j)
        part = product(link.core * half + j)
        copy.wait_recv()
        xhat, inv = standardize(x[rows, :].astype(f32))
        dh = part + other[rows, :].astype(f32)
        dx = dh * vec_ref[GAIN1]
        dx_ref[rows, :] = (
            dmid[rows, :]
            + inv
            * (dx - jnp.mean(dx, axis=-1, keepdims=True) - xhat * jnp.mean(dx * xhat, axis=-1, keepdims=True))
        ).astype(bf16)
        for row, value in enumerate((dh * xhat, dh)):
            sums_ref[row : row + 1, :] += jnp.sum(value, axis=0, keepdims=True)
        return carry

    sums_ref[...] = jnp.zeros_like(sums_ref)
    lax.fori_loop(0, half, send, 0)
    for c in loads:
        c.wait()
    lax.fori_loop(0, half, norm, 0)
    for j in range(half):
        swap(j)[1].wait_send()
    for job in bound:
        job.forward()
    for job in bound:
        job.inward()
    for job in bound:
        job.finish()


def first_back_call(grads, w, vec, x, dmid, jobs, number):
    n, d = x.shape
    size = n // 2
    vmem = pl.BlockSpec(memory_space=pltpu.VMEM)
    hbm = pl.BlockSpec(memory_space=pl.ANY)
    return pl.pallas_call(
        functools.partial(first_back_kernel, jobs=jobs),
        in_specs=[vmem] * 3 + [hbm] * 2 + jobs.in_specs(),
        out_specs=[vmem] * 2 + jobs.in_specs(),
        out_shape=[jax.ShapeDtypeStruct((size, d), bf16), jax.ShapeDtypeStruct((8, d), f32)] + jobs.out_shapes(),
        scratch_shapes=[
            pltpu.VMEM((size, d), bf16),
            pltpu.VMEM((size, d), f32),
            pltpu.VMEM((size, d), bf16),
            pltpu.VMEM((size, d), bf16),
        ]
        + jobs.scratch(size // ROWS),
        compiler_params=comm_params(number),
        cost_estimate=cost(2 * n * w.size, 12 * n * d),
        name="first_back",
    )(grads, w, vec, x, dmid, *jobs.sources())


class Blocks:
    def __init__(self, ref, stride, first):
        self.ref, self.stride, self.first = ref, stride, first

    @property
    def at(self):
        return self

    def __getitem__(self, index):
        block, part = index
        start = pl.multiple_of(block * self.stride + (self.first + part.start), 16)
        return self.ref.at[pl.ds(start, part.size)]


def back_kernel(*refs, jobs):
    count = len(jobs.jobs)
    g_any, vec_ref, h_any, early_ref, *w_anys = refs[:7]
    x_any, dmid_any = refs[7:9]
    tokens_any, small_ref, both_any = refs[9 + count : 12 + count]
    rest = list(refs[12 + 2 * count :])
    x, dmid, mine, other, dx, dw, own, total, came, stage = rest[:10]
    rest = rest[10:]
    w_refs, rest = rest[:3], rest[3:]
    (g_ref, h_ref), rest = rest[:2], rest[2:]
    small_bufs, rest = rest[:3], rest[3:]
    reduce_bufs, rest = [rest[10 * i : 10 * i + 10] for i in range(3)], rest[30:]
    chain_bufs, rest = [rest[3 * i : 3 * i + 3] for i in range(6)], rest[18:]
    link, bound, _ = jobs.bind(rest, refs[9 : 9 + count], refs[12 + count : 12 + 2 * count])
    ready = [job for job in bound if isinstance(job, Chain)]
    others = [job for job in bound if job not in ready]
    size, d = dx.shape
    half = size // ROWS
    _, owned, width = own.shape
    order = (2, 1, 0)
    reduces = [Reduce(link, Blocks(dw.at[c], owned, 0), own.at[c], reduce_bufs[c]) for c in order]
    last = []
    for c in order:
        for i in range(2):
            rows, cols = pl.ds(i * (owned // 2), owned // 2), pl.ds(c * width, width)
            last.append(Chain(link, own.at[c, rows], both_any.at[:, rows, cols], chain_bufs[len(last)]))
    to_owners = FromClip(link, dx, tokens_any, [stage])
    base = link.slots(half)
    keep = link.local_slots(7)
    rows_in = [link.here(a, b, keep + 5 + i) for i, (a, b) in enumerate(((g_any, g_ref), (h_any, h_ref)))]
    for c in rows_in:
        c.start()
    swap_base = link.slots(3)
    peers = [link.sibling()] + [(link.rep, link.shard ^ bit) for bit in (1, 2)]
    swaps = [link.remote(total, came.at[i], swap_base + i, swap_base + i, to) for i, to in enumerate(peers)]
    small = Chain(link, total, small_ref, small_bufs)
    mine_rows = pl.ds(pl.multiple_of(link.core * size, size), size)
    loads = [link.here(x_any.at[mine_rows], x, keep), link.here(dmid_any.at[mine_rows], dmid, keep + 1)]
    loads += [link.here(a, b, keep + 2 + i) for i, (a, b) in enumerate(zip(w_anys, w_refs))]
    for c in loads:
        c.start()
    link.meet_all()
    ready[0].start()
    for c in rows_in:
        c.wait()
    for c, job in zip(order, reduces):

        def weight(i, carry):
            part = pl.ds(pl.multiple_of(i * 256, 256), 256)
            dw[c, part, :] = dot_tn(h_ref[:, part], g_ref[:, c * width : (c + 1) * width]).astype(bf16)
            return carry

        lax.fori_loop(0, d // 256, weight, 0)
        job.start()

    def product(j):
        rows = pl.ds(pl.multiple_of(j * ROWS, ROWS), ROWS)
        parts = [dot_nt(g_ref[rows, c * width : (c + 1) * width], w_refs[c][...]) for c in range(3)]
        return parts[0] + parts[1] + parts[2]

    def swap(j):
        rows = pl.ds(pl.multiple_of(j * ROWS, ROWS), ROWS)
        return rows, link.remote(mine.at[rows], other.at[rows], base + j, base + j, link.sibling())

    def send(j, carry):
        rows, copy = swap(j)
        mine[rows, :] = product((1 - link.core) * half + j).astype(bf16)
        copy.start()
        return carry

    first = early_ref.shape[0]

    def norm(j, carry):
        rows, copy = swap(j)
        part = product(link.core * half + j)
        copy.wait_recv()
        xhat, inv = standardize(x[rows, :].astype(f32))
        dh = part + other[rows, :].astype(f32)
        slope = dh * vec_ref[GAIN1]
        dx[rows, :] = (
            dmid[rows, :]
            + inv
            * (
                slope
                - jnp.mean(slope, axis=-1, keepdims=True)
                - xhat * jnp.mean(slope * xhat, axis=-1, keepdims=True)
            )
        ).astype(bf16)
        for row, value in enumerate((dh * xhat, dh)):
            total[first + row : first + row + 1, :] += jnp.sum(value, axis=0, keepdims=True)
        return carry

    steps = chain_steps(ready)
    run(steps[0])
    total[:first, :] = early_ref[...]
    total[first:, :] = jnp.zeros((total.shape[0] - first, d), f32)
    for c in loads:
        c.wait()
    lax.fori_loop(0, half, send, 0)
    reduces[0].forward()
    after = {0: steps[1] + [reduces[1].forward], 1: [reduces[2].forward]}
    for j in range(half):
        norm(j, 0)
        run(after.get(j, []))
    swaps[0].start()
    run(steps[2])
    reduces[0].collect()
    last[0].start()
    reduces[1].collect()
    swaps[0].wait()
    total[...] += came[0]
    swaps[1].start()
    reduces[2].collect()
    for some in steps[3:]:
        run(some)
    swaps[1].wait()
    total[...] += came[1]
    swaps[2].start()
    for number, some in enumerate(chain_steps(last)):
        run(some)
        if number == 0:
            swaps[2].wait()
            total[...] += came[2]
            small.start()
        if number == 2:
            run([job.start for job in [to_owners] + others])
        if number == 3:
            small.inward()
            small.sent()
        if number == 5:
            small.across()
    for c in ready + last:
        c.outward()
    small.outward()
    for job in ready + last + [small]:
        job.finish()
    for job in reduces:
        job.close()
    for j in range(half):
        swap(j)[1].wait_send()
    run([job.finish for job in [to_owners] + others])


def back_call(grads, weights, vec, h, early, x, dmid, jobs, clips, number):
    n, d = x.shape
    size = n // 2
    width = grads.shape[1] // 3
    groups = lax.axis_size("shard")
    owned = d // groups
    rows = early.shape[0] + 8
    small = pltpu.VMEM((rows, d), f32)
    vmem = pl.BlockSpec(memory_space=pltpu.VMEM)
    hbm = pl.BlockSpec(memory_space=pl.ANY)
    return pl.pallas_call(
        functools.partial(back_kernel, jobs=jobs),
        in_specs=[hbm, vmem, hbm, vmem] + [hbm] * 5 + jobs.in_specs(),
        out_specs=[hbm, vmem, hbm] + jobs.in_specs(),
        out_shape=[
            jax.ShapeDtypeStruct((clips, size // clips, d), bf16),
            jax.ShapeDtypeStruct((2, rows, d), f32),
            jax.ShapeDtypeStruct((2, owned, 3 * width), bf16),
        ]
        + jobs.out_shapes(),
        scratch_shapes=[
            pltpu.VMEM((size, d), bf16),
            pltpu.VMEM((size, d), f32),
            pltpu.VMEM((size, d), bf16),
            pltpu.VMEM((size, d), bf16),
            pltpu.VMEM((size, d), bf16),
            pltpu.VMEM((3, d, width), bf16),
            pltpu.VMEM((3, owned, width), bf16),
            small,
            pltpu.VMEM((3, rows, d), f32),
            pltpu.VMEM((size // clips, d), bf16),
        ]
        + [pltpu.VMEM((d, width), bf16)] * 3
        + [pltpu.VMEM(grads.shape, bf16), pltpu.VMEM((n, d), bf16)]
        + [small] * 3
        + [pltpu.VMEM((owned // 2, width), bf16)] * 48
        + jobs.scratch(80),
        compiler_params=comm_params(number, 62),
        cost_estimate=cost(12 * n * weights[0].size, 20 * n * d),
        name="back",
    )(grads, vec, h, early, *weights, x, dmid, *jobs.sources())


def place_kernel(*refs, groups):
    up_refs, down_refs = refs[:4], refs[4:8]
    out_ref, in_ref = refs[8:10]
    up, down, wo = refs[10:13]
    qkv = refs[13:16]

    def put(target, axis, pieces):
        first = 0
        for value in pieces:
            size = value.shape[axis]
            span = slice(first, first + size)
            if axis:
                target[:, span] = value.astype(f32)
            else:
                target[span, :] = value.astype(f32)
            first += size

    cut = up_refs[0].shape[1]
    for part in range(2):
        put(up.at[pl.ds(part * cut, cut)], 1, [r[c] for c in range(2) for r in (up_refs[part], up_refs[2 + part])])
    put(down, 0, [r[c] for c in range(2) for r in down_refs])
    put(wo, 0, [out_ref[c] for c in range(2)])
    rows = in_ref.shape[1]
    width = in_ref.shape[2] // 3
    part = width // groups

    for i, out in enumerate(qkv):
        for c in range(2):
            value = in_ref[c, :, i * width : (i + 1) * width].astype(f32)
            for s in range(groups):
                first = (2 * s + c) * part
                out[:, first : first + part] = value[:, s * part : (s + 1) * part]


def place_call(ups, downs, wo, qkv, groups):
    steps = 5
    own_d, cols = qkv.shape[1:]
    d = downs[0].shape[2]
    own_f = 2 * sum(a.shape[1] for a in downs)
    take = [pl.BlockSpec((2, a.shape[1], a.shape[2] // groups), lambda i: (0, 0, jnp.minimum(i, groups - 1))) for a in ups]
    wide = d // steps
    per = own_d // steps
    ff = 2 * ups[0].shape[2] + 2 * ups[2].shape[2]
    return pl.pallas_call(
        functools.partial(place_kernel, groups=groups),
        grid=(steps,),
        in_specs=take
        + [pl.BlockSpec((2, a.shape[1], wide), lambda i: (0, 0, i)) for a in downs]
        + [
            pl.BlockSpec((2, wo.shape[1], wide), lambda i: (0, 0, i)),
            pl.BlockSpec((2, per, cols), lambda i: (0, i, 0)),
        ],
        out_specs=[
            pl.BlockSpec((own_d, ff // groups), lambda i: (0, jnp.minimum(i, groups - 1))),
            pl.BlockSpec((own_f, wide), lambda i: (0, i)),
            pl.BlockSpec((own_d, wide), lambda i: (0, i)),
        ]
        + [pl.BlockSpec((per, d), lambda i: (i, 0))] * 3,
        out_shape=[
            jax.ShapeDtypeStruct((own_d, ff), f32),
            jax.ShapeDtypeStruct((own_f, d), f32),
            jax.ShapeDtypeStruct((own_d, d), f32),
        ]
        + [jax.ShapeDtypeStruct((own_d, d), f32)] * 3,
        compiler_params=params(),
        name="place",
    )(*ups, *downs, wo, qkv)


def own_sum(blocks, others):
    shard = lax.axis_index("shard")
    total = lax.dynamic_index_in_dim(blocks, shard, 0, keepdims=False).astype(f32)
    for i in range(others.shape[0]):
        total = total + others[i].astype(f32)
    return total.astype(bf16)


def over_reps(own):
    planes = lax.axis_size("rep") // 2
    sums = lax.psum_scatter(
        own,
        "rep",
        scatter_dimension=0,
        tiled=True,
        axis_index_groups=[[2 * z + c for z in range(planes)] for c in range(2)],
    )
    both = lax.all_gather(sums, "rep", axis=0)
    rows, cols = sums.shape
    return both.reshape(planes, 2, rows, cols).transpose(1, 0, 2, 3).reshape(2, planes * rows, cols)


def on_device(
    tokens,
    lengths,
    cotangent,
    first_gain,
    first_shift,
    query_weight,
    query_bias,
    key_weight,
    value_weight,
    value_bias,
    out_weight,
    out_bias,
    second_gain,
    second_shift,
    up_weight,
    up_bias,
    down_weight,
    down_bias,
):
    g = lax.axis_size("shard")
    shard = lax.axis_index("shard")
    core = lax.rem(lax.axis_index("rep"), 2)
    cl, rows, d = tokens.shape
    n = 2 * cl * rows
    ff = up_weight.shape[1]
    own_d = d // g
    own_f = ff // g
    attn_cols = own_d // 2
    ffn_cols = own_f // 2
    width = d // 2
    heads = width // HEAD
    wide = pl.cdiv(width, 128) * 128 + 128
    first_n = ffn_cols * 2 // 5
    pieces = ((0, first_n), (first_n, ffn_cols))

    fast = g == 4 and lax.axis_size("rep") == 8
    weights = PairGather if fast else Gather
    positions = shard * rows + jnp.arange(rows, dtype=jnp.int32)
    live = positions[None, :] < lengths[:, None]
    masked = jnp.where(live[:, :, None], cotangent, jnp.zeros_like(cotangent))

    def core_of():
        return lax.rem(lax.axis_index("rep"), 2)

    def core_cols(w, size, a, b):
        def of(c):
            return jnp.concatenate([w[:, (2 * s + c) * size + a : (2 * s + c) * size + b] for s in range(g)], axis=1)

        return jnp.where(core == 0, of(0), of(1))

    vectors = (first_gain, first_shift, query_bias, value_bias, out_bias, second_gain, second_shift, down_bias)
    small = pack_call((*vectors, up_bias), lengths)
    own = [core_cols(w, attn_cols, 0, attn_cols) for w in (query_weight, key_weight, value_weight)]
    jobs = Jobs(
        (ToClip, tokens, (n, d)),
        (Gather, small, (g,) + small.shape),
        *[(weights, w, (g,) + w.shape) for w in own],
    )
    h1, q, k, v, vec, x, _, *w_qkv, other_small = first_call(jobs, small, wide, 0)
    w_qkv = [w.reshape(d, width) for w in w_qkv]
    near = lax.div(shard, cl) == core
    lens = jnp.where(near, small[LENGTHS], other_small[LENGTHS])[0]
    length = lens[lax.rem(shard, cl)].astype(jnp.int32).reshape(1)

    ubias = lax.dynamic_index_in_dim(
        vec[UBIAS : UBIAS + own_f // own_d].reshape(-1, g, own_d).transpose(1, 0, 2).reshape(g, 2, ffn_cols),
        core,
        1,
        keepdims=False,
    )
    ups = [core_cols(up_weight, ffn_cols, a, b) for a, b in pieces]

    def half_rows(w, first=0, last=None):
        half = w.shape[0] // 2
        size = (half if last is None else last) - first

        def view(ref):
            return ref.at[pl.ds(pl.multiple_of(core_of() * half + first, 16), size)]

        return size, view

    def gathered(a, part=None):
        if part is None:
            return (weights, a, (g,) + a.shape)
        return (weights, a, (g, part[0]) + a.shape[1:], part[1])

    jobs = Jobs(
        gathered(ups[0]),
        gathered(down_weight, half_rows(down_weight, *pieces[0])),
        gathered(out_weight, half_rows(out_weight)),
    )
    o, lse, up, down, w_out = attn_fwd_call(length, q, k, v, width, heads, jobs, 1)
    w_out = w_out.reshape(width, d)
    jobs = Jobs((ToClip, masked, (n, d)))
    mid, h2, o_wide, dz = middle_call(o, w_out, x, vec, wide, jobs, 2)

    def hidden_bias(piece):
        return ubias[:, piece[0] : piece[1]].reshape(1, -1)


    def to_owners(a):
        if fast:
            return (Reduce, a, a.shape[1:])
        return (Owners, a, (g - 1,) + a.shape[1:])

    def owned(a, came):
        return came if fast else own_sum(a, came)

    def chained(a):
        return (Chain, a, (2,) + a.shape)

    def chained_halves(a):
        half = a.shape[0] // 2

        def part(i):
            return lambda ref: ref.at[pl.ds(i * half, half)]

        return [(Chain, a, (2, half, a.shape[1]), part(i)) for i in range(2)]

    jobs = Jobs(gathered(ups[1]), gathered(down_weight, half_rows(down_weight, *pieces[1])))
    out, dh2, dup0, ddn0, dub0, up1, down1 = ffn_call(
        h2, dz, up.reshape(d, -1), hidden_bias(pieces[0]), down.reshape(-1, d), None, False, jobs, 3, "hidden0"
    )
    dup0, ddn0 = dup0.reshape(g, own_d, -1), ddn0.reshape(g, -1, d)
    jobs = Jobs(to_owners(dup0), to_owners(ddn0))
    out, dh2, dup1, ddn1, dub1, dup0_in, ddn0_in = ffn_call(
        h2, dz, up1.reshape(d, -1), hidden_bias(pieces[1]), down1.reshape(-1, d), (out, dh2), True, jobs, 4, "hidden1"
    )
    dup1, ddn1 = dup1.reshape(g, own_d, -1), ddn1.reshape(g, -1, d)
    up0_own, down0_own = owned(dup0, dup0_in), owned(ddn0, ddn0_in)

    jobs = [to_owners(dup1)]
    if fast:
        jobs += chained_halves(up0_own)
    dmid, do, dwo, sums2, layer_own, dup1_in, *sums0 = second_back_call(
        mid, dh2, out, dz, vec, w_out, o, wide, Jobs(*jobs), 5
    )
    dwo = dwo.reshape(g, -1, d)
    up1_own = owned(dup1, dup1_in)

    to_tokens = (FromClip, layer_own, (cl, rows, d))
    jobs = [to_owners(ddn1), to_owners(dwo), to_tokens]
    if fast:
        jobs += chained_halves(down0_own) + chained_halves(up1_own)
    grads, bias_sums, ddn1_in, dwo_in, layer_out, *later = attn_bwd_call(
        length, q, k, v, o_wide, do, lse, width, heads, Jobs(*jobs), 6
    )
    down1_own, out_own_grad = owned(ddn1, ddn1_in), owned(dwo, dwo_in)

    def spread(v, size):
        out = jnp.zeros((g, 2, size), f32)
        return lax.dynamic_update_index_in_dim(out, v.reshape(g, size), core, 1)

    ub_sums = jnp.concatenate([dub0.reshape(g, -1), dub1.reshape(g, -1)], axis=1)
    early = jnp.concatenate(
        [
            spread(bias_sums[0, :width], attn_cols).reshape(1, d),
            spread(bias_sums[0, 2 * width :], attn_cols).reshape(1, d),
            sums2[:4] * 0.5,
            spread(ub_sums, ffn_cols).reshape(-1, d),
        ],
        axis=0,
    )
    early = jnp.pad(early, ((0, -early.shape[0] % 8), (0, 0)))

    if fast:
        jobs = Jobs(*chained_halves(down1_own), chained(out_own_grad))
        tokens_grad, smalls, qkv_all, *sums = back_call(grads, w_qkv, vec, h1, early, x, dmid, jobs, cl, 7)
        up_grad, down_grad, out_grad, *qkv_grads = place_call(
            (*sums0, *later[2:]), (*later[:2], *sums[:2]), sums[2], qkv_all, g
        )
        smalls = lax.dynamic_index_in_dim(smalls, core, 0, keepdims=False)
    else:
        dwqkv = dw_call(h1, grads).reshape(g, own_d, 3 * width)
        jobs = Jobs(to_owners(dwqkv))
        dx, sums1, dwqkv_in = first_back_call(grads, jnp.concatenate(w_qkv, axis=1), vec, x, dmid, jobs, 7)
        jobs = Jobs((FromClip, dx, (cl, rows, d)))
        tokens_grad, _ = exchange_call(jobs, sums1, 8, "last_exchange")
        ups_all = [over_reps(a).reshape(2, own_d, g, -1) for a in (up0_own, up1_own)]
        up_grad = jnp.concatenate(ups_all, axis=3).transpose(1, 2, 0, 3).reshape(own_d, ff).astype(f32)
        downs_all = [over_reps(a) for a in (down0_own, down1_own)]
        down_grad = jnp.concatenate(downs_all, axis=1).reshape(own_f, d).astype(f32)
        out_grad = over_reps(out_own_grad).reshape(own_d, d).astype(f32)
        qkv_all = over_reps(owned(dwqkv, dwqkv_in)).reshape(2, own_d, 3, g, attn_cols)
        qkv_grads = [qkv_all[:, :, i].transpose(1, 2, 0, 3).reshape(own_d, d).astype(f32) for i in range(3)]
        smalls = lax.psum(jnp.concatenate([early, sums1], axis=0), ("rep", "shard"))

    mine = lax.dynamic_slice_in_dim(smalls, shard * own_d, own_d, 1)
    s_qb, s_vb, s_gain2, s_shift2, s_ob, s_db = [mine[i] for i in range(6)]
    s_gain1, s_shift1 = [mine[early.shape[0] + i] for i in range(2)]
    s_ub = lax.dynamic_slice_in_dim(smalls[6 : 6 + ff // d].reshape(-1), shard * own_f, own_f, 0)

    return (
        layer_out,
        tokens_grad,
        s_gain1,
        s_shift1,
        qkv_grads[0],
        s_qb,
        qkv_grads[1],
        qkv_grads[2],
        s_vb,
        out_grad,
        s_ob,
        s_gain2,
        s_shift2,
        up_grad,
        s_ub,
        down_grad,
        s_db,
    )


def solution(mesh):
    row, mat, vec = P("rep", "shard", None), P("shard", None), P("shard")
    return jax.shard_map(
        on_device,
        mesh=mesh,
        in_specs=(row, P("rep"), row, vec, vec, mat, vec, mat, mat, vec, mat, vec, vec, vec, mat, vec, mat, vec),
        out_specs=(row, row, vec, vec, mat, vec, mat, mat, vec, mat, vec, vec, vec, mat, vec, mat, vec),
        check_vma=False,
    )
```
